32 devices in a mesh: angle: 2 (over x), gx: 4 (over y, core), gy: 4 (over z).
Axes of the slice: x: 2, y: 2, z: 4, core: 2. Of those that a mesh axis runs over, the one named last changes fastest.
Arguments:
- forward_fields: float32 [2, 12, 32, 64, 128], P('angle', None, 'gx', 'gy'), may hold values from -6 to 6
- adjoint_fields: float32 [2, 12, 32, 64, 128], P('angle', None, 'gx', 'gy'), may hold values from -6 to 6
- forward_spectrum: float32 [2, 6, 32, 64, 128], P('angle', None, 'gx', 'gy'), may hold values from -6 to 6
- adjoint_spectrum: float32 [2, 6, 32, 64, 128], P('angle', None, 'gx', 'gy'), may hold values from -6 to 6
- permittivity: float32 [32, 64, 128], P('gx', 'gy'), may hold values from 1 to 12
- phase_table: float32 [2, 2], replicated, may hold values from -3.140625 to 3.140625
- angle_index: int32 [2], P('angle'), may hold values from 0 to 1, each once
- design_tiles: int32 [4], replicated, may hold values from 0 to 15, as said below
Outputs:
- forward_transform: float32 [2, 6, 32, 64, 128], P('angle', None, 'gx', 'gy')
- adjoint_transform: float32 [2, 6, 32, 64, 128], P('angle', None, 'gx', 'gy')
- gradient: float32 [32, 64, 128], P('gx', 'gy', 'angle')
The draws below stay inside these ranges and needn't reach their ends.
Inputs may be any that keep to these rules, and one draw needn't show every extreme that they name: `angle_index`: every row of phase_table is used by exactly one angle. `design_tiles`: 4 distinct tile numbers; tiles 0 and 15 are always among them.
All inputs are finite; a program needn't handle non-finite values.
Results may differ from the reference program's by a relative error of at most 0.0001.
Values sent between devices are 32-bit elements; how exact they have to be, the bound alone decides.
No kernel may reach another device: no remote copies, remote signals or barrier semaphores. Data moves between devices by JAX's collectives and lax.ppermute only.
A program may use at most 64 MiB of HBM per device.

```python
import math
import jax
import jax.numpy as jnp
from jax import lax

CX = 8
CY = 16
NZ = 128
STEPS = 3
ANGLES = 2
NX = 32
NY = 64
TILES = 16
NDES = 4
N_GY = 4


def draw_design_tiles(key, part):
    others = jax.random.permutation(jax.random.fold_in(key, 7), TILES - 2)[:NDES - 2] + 1
    chosen = jnp.concatenate([jnp.array([0, TILES - 1], dtype=jnp.int32), others.astype(jnp.int32)])
    order = jax.random.permutation(jax.random.fold_in(key, 11), NDES)
    return chosen[order].astype(jnp.int32)


def block_scale(own_key, shape, cuts, least, high):
    level, own = 1.0, jax.random.fold_in(own_key, 6)
    for position, shards_of in cuts:
        draws = jnp.exp(jax.random.uniform(jax.random.fold_in(own, position), (shards_of,), jnp.float32, least / len(cuts), high / len(cuts)))
        level = level * jnp.repeat(draws, shape[position] // shards_of).reshape([-1 if axis == position else 1 for axis in range(len(shape))])
    return level


def bell_draw(stream_key, shape, scale, limit, pieces=(), kind=jnp.bfloat16):
    entries = scale * jax.random.normal(stream_key, shape, jnp.float32)
    if pieces:
        entries = entries * block_scale(stream_key, shape, pieces, -0.22, 0.18)
    return jnp.clip(entries, -limit, limit).astype(kind)


def setup_inputs(seed: int = 0) -> dict:
    streams_of = jax.random.split(jax.random.key(seed), 9)
    return {
        "forward_fields": bell_draw(streams_of[0], (ANGLES, 12, NX, NY, NZ), 1.0, 6.0, ((0, 2), (2, 4), (3, 4)), jnp.float32),
        "adjoint_fields": bell_draw(streams_of[1], (ANGLES, 12, NX, NY, NZ), 1.0, 6.0, ((0, 2), (2, 4), (3, 4)), jnp.float32),
        "forward_spectrum": bell_draw(streams_of[2], (ANGLES, 6, NX, NY, NZ), 1.0, 6.0, ((0, 2), (2, 4), (3, 4)), jnp.float32),
        "adjoint_spectrum": bell_draw(streams_of[3], (ANGLES, 6, NX, NY, NZ), 1.0, 6.0, ((0, 2), (2, 4), (3, 4)), jnp.float32),
        "permittivity": jnp.clip(1.0 + 11.0 * jax.random.uniform(streams_of[4], (NX, NY, NZ), jnp.float32) ** block_scale(streams_of[4], (NX, NY, NZ), ((0, 4), (1, 4)), -0.2, 0.2), 1.0, 12.0),
        "phase_table": jnp.clip(jax.random.uniform(streams_of[5], (ANGLES, 2), jnp.float32, -3.140625, 3.140625), -3.140625, 3.140625),
        "angle_index": jax.random.permutation(streams_of[6], ANGLES).astype(jnp.int32),
        "design_tiles": draw_design_tiles(jax.random.fold_in(streams_of[8], 71), 0),
    }


courant = 0.5
omega_step = 0.7


def rotate_pair(pair, cosine, sine):
    real_part = pair[0]
    imag_part = pair[1]
    return jnp.stack([real_part * cosine - imag_part * sine, real_part * sine + imag_part * cosine])


def next_along(pair, axis, cosine, sine):
    rolled = jnp.roll(pair, -1, axis)
    count = pair.shape[axis]
    edge = lax.broadcasted_iota(jnp.int32, pair.shape, axis) == count - 1
    return jnp.where(edge, rotate_pair(rolled, cosine, sine), rolled)


def prev_along(pair, axis, cosine, sine):
    rolled = jnp.roll(pair, 1, axis)
    edge = lax.broadcasted_iota(jnp.int32, pair.shape, axis) == 0
    return jnp.where(edge, rotate_pair(rolled, cosine, -sine), rolled)


def next_depth(field):
    return jnp.concatenate([field[..., 1:], jnp.zeros_like(field[..., :1])], axis=-1)


def prev_depth(field):
    return jnp.concatenate([jnp.zeros_like(field[..., :1]), field[..., :-1]], axis=-1)


def curl_forward(efield, cos_x, sin_x, cos_y, sin_y):
    comp_x = efield[:, 0]
    comp_y = efield[:, 1]
    comp_z = efield[:, 2]
    dz_dy = next_along(comp_z, 2, cos_y, sin_y) - comp_z
    dy_dz = next_depth(comp_y) - comp_y
    dx_dz = next_depth(comp_x) - comp_x
    dz_dx = next_along(comp_z, 1, cos_x, sin_x) - comp_z
    dy_dx = next_along(comp_y, 1, cos_x, sin_x) - comp_y
    dx_dy = next_along(comp_x, 2, cos_y, sin_y) - comp_x
    return jnp.stack([dz_dy - dy_dz, dx_dz - dz_dx, dy_dx - dx_dy], axis=1)


def curl_backward(hfield, cos_x, sin_x, cos_y, sin_y):
    comp_x = hfield[:, 0]
    comp_y = hfield[:, 1]
    comp_z = hfield[:, 2]
    first = (comp_z - prev_along(comp_z, 2, cos_y, sin_y)) - (comp_y - prev_depth(comp_y))
    second = (comp_x - prev_depth(comp_x)) - (comp_z - prev_along(comp_z, 1, cos_x, sin_x))
    third = (comp_y - prev_along(comp_y, 1, cos_x, sin_x)) - (comp_x - prev_along(comp_x, 2, cos_y, sin_y))
    return jnp.stack([first, second, third], axis=1)


def advance(fields, spectrum, permittivity, cos_x, sin_x, cos_y, sin_y):
    cells = fields.shape[1:]
    efield = fields[0:6].reshape((2, 3) + cells)
    hfield = fields[6:12].reshape((2, 3) + cells)
    spectrum = spectrum.reshape((2, 3) + cells)
    coef = courant / permittivity
    for step in range(STEPS):
        hfield = hfield - courant * curl_forward(efield, cos_x, sin_x, cos_y, sin_y)
        efield = efield + coef * curl_backward(hfield, cos_x, sin_x, cos_y, sin_y)
        theta = omega_step * (step + 1)
        spectrum = spectrum + rotate_pair(efield, math.cos(theta), math.sin(theta))
    return spectrum


def reference(forward_fields, adjoint_fields, forward_spectrum, adjoint_spectrum, permittivity, phase_table, angle_index, design_tiles):
    total = jnp.zeros((NX, NY, NZ), jnp.float32)
    forward_list = []
    adjoint_list = []
    for angle in range(ANGLES):
        row = phase_table[angle_index[angle]]
        cos_x = jnp.cos(row[0])
        sin_x = jnp.sin(row[0])
        cos_y = jnp.cos(row[1])
        sin_y = jnp.sin(row[1])
        forward_out = advance(forward_fields[angle], forward_spectrum[angle], permittivity, cos_x, sin_x, cos_y, sin_y)
        adjoint_out = advance(adjoint_fields[angle], adjoint_spectrum[angle], permittivity, cos_x, -sin_x, cos_y, -sin_y)
        total = total + jnp.sum(forward_out[0] * adjoint_out[0] - forward_out[1] * adjoint_out[1], axis=0)
        forward_list.append(forward_out.reshape((6, NX, NY, NZ)))
        adjoint_list.append(adjoint_out.reshape((6, NX, NY, NZ)))
    tile_x = (jnp.arange(NX) // CX).astype(jnp.int32)
    tile_y = (jnp.arange(NY) // CY).astype(jnp.int32)
    tiles = tile_x[:, None] * N_GY + tile_y[None, :]
    inside = jnp.any(tiles[:, :, None] == design_tiles[None, None, :], axis=-1).astype(jnp.float32)
    gradient = total * inside[:, :, None] * (1.0 / ANGLES)
    return jnp.stack(forward_list), jnp.stack(adjoint_list), gradient
```

```python
import functools
import math

import jax
import jax.numpy as jnp
from jax import lax
from jax.experimental import pallas as pl
from jax.experimental.pallas import tpu as pltpu
from jax.sharding import PartitionSpec as P

STEPS = 3
SUB = 8

courant = 0.5
omega_step = 0.7

VMEM = pl.BlockSpec(memory_space=pltpu.VMEM)
SMEM = pl.BlockSpec(memory_space=pltpu.SMEM)
ANY = pl.BlockSpec(memory_space=pl.ANY)


def moved(cells, dx, dy):
    return {(x + dx, y + dy) for x, y in cells}


def cone(nx, ny):
    block = {(x, y) for x in range(nx) for y in range(ny)}
    ex, ey, ez = block, block, block
    hx, hy, hz, eps = set(), set(), set(), set()
    for _ in range(STEPS):
        eps = eps | ex | ey | ez
        hx, hy, hz = (
            hx | ey | ez | moved(ez, 0, -1),
            hy | ex | ez | moved(ez, -1, 0),
            hz | ex | moved(ex, 0, -1) | ey | moved(ey, -1, 0),
        )
        ex, ey, ez = (
            ex | hy | hz | moved(hz, 0, 1),
            ey | hx | hz | moved(hz, 1, 0),
            ez | hx | moved(hx, 0, 1) | hy | moved(hy, 1, 0),
        )
    return (ex, ey, ez), (hx, hy, hz), eps


PLANES = [(run, kind, part, comp) for run in (0, 1) for kind in (0, 1) for comp in (0, 1, 2) for part in (0, 1)]


class Plan:
    def __init__(self, nx, ny):
        efield, hfield, eps = cone(nx, ny)
        self.nx, self.ny = nx, ny

        def cells(plane):
            if plane is None:
                return eps
            return (efield, hfield)[plane[1]][plane[3]]

        planes = PLANES + [None]
        self.x_low, self.x_high, self.y_low, self.y_high = [], [], [], []
        for plane in planes:
            need = cells(plane)
            self.x_low += [(plane, x) for x in range(-STEPS, 0) if any((x, y) in need for y in range(ny))]
            self.x_high += [(plane, x) for x in range(nx, nx + STEPS) if any((x, y) in need for y in range(ny))]
            self.y_low += [(plane, y) for y in range(-STEPS, 0) if any((x, y) in need for x in range(nx))]
            self.y_high += [(plane, y) for y in range(ny, ny + STEPS) if any((x, y) in need for x in range(nx))]
        self.corner_low, self.corner_high = [], []
        for out, layers in ((self.corner_low, range(-STEPS, 0)), (self.corner_high, range(nx, nx + STEPS))):
            for rows in (range(-STEPS, 0), range(ny, ny + STEPS)):
                for plane in planes:
                    need = cells(plane)
                    out += [(plane, x, y) for x in layers for y in rows if (x, y) in need]


def row_of(plane, nx, ny, x, y):
    _, kind, part, comp = plane
    return ((kind * 6 + part * 3 + comp) * nx + x) * ny + y


def pack_kernel(plan, fwd, adj, eps, x_up, x_down, z_up, z_down):
    nx, ny = plan.nx, plan.ny

    def source(plane, x, y):
        if plane is None:
            return eps, x * ny + y
        return (fwd, adj)[plane[0]], row_of(plane, nx, ny, x, y)

    for entries, shift, out in ((plan.y_low, ny, z_up), (plan.y_high, -ny, z_down)):
        for i, (plane, y) in enumerate(entries):
            ref, row = source(plane, 0, y + shift)
            out[pl.ds(i * nx, nx), :] = ref[pl.ds(row, nx, stride=ny), :]
    for entries, shift, out in ((plan.x_low, nx, x_up), (plan.x_high, -nx, x_down)):
        for i, (plane, x) in enumerate(entries):
            ref, row = source(plane, x + shift, 0)
            out[pl.ds(i * ny, ny), :] = ref[pl.ds(row, ny), :]


def corner_kernel(plan, z_low, z_high, c_up, c_down):
    nx, ny = plan.nx, plan.ny
    low = {entry: i for i, entry in enumerate(plan.y_low)}
    high = {entry: i for i, entry in enumerate(plan.y_high)}
    for entries, shift, out in ((plan.corner_low, nx, c_up), (plan.corner_high, -nx, c_down)):
        for i, (plane, x, y) in enumerate(entries):
            ref, at = (z_low, low[plane, y]) if y < 0 else (z_high, high[plane, y])
            out[pl.ds(i, 1), :] = ref[pl.ds(at * nx + x + shift, 1), :]


def turned(real, imag, cosine, sine):
    return real * cosine - imag * sine, real * sine + imag * cosine


def advance_kernel(plan, groups, fwd, adj, spec_f, spec_a, eps, x_low, x_high, z_low, z_high, c_low, c_high,
                   table, index, tiles, out_f, out_a, parts, state, coef, turns):
    nx, ny = plan.nx, plan.ny
    wide_x, ring = nx + 2 * STEPS, ny + SUB

    def base(level, kind, run, part, comp):
        return (((level * 2 + kind) * 2 + run) * 6 + part * 3 + comp) * wide_x * ring

    def place(plane, x, y):
        start = 0 if plane is None else base(0, plane[1], plane[0], plane[2], plane[3])
        return (coef if plane is None else state), start + (x + STEPS) * ring + y % ring

    for run, ref in enumerate((fwd, adj)):
        for kind in (0, 1):
            for part in (0, 1):
                for comp in (0, 1, 2):
                    for x in range(nx):
                        source = row_of((run, kind, part, comp), nx, ny, x, 0)
                        target = base(0, kind, run, part, comp) + (x + STEPS) * ring
                        state[pl.ds(target, ny), :] = ref[pl.ds(source, ny), :]
    for x in range(nx):
        coef[pl.ds((x + STEPS) * ring, ny), :] = eps[pl.ds(x * ny, ny), :]

    row = index[0]
    phi_x, phi_y = table[row, 0], table[row, 1]
    at_x, at_y = lax.axis_index("gx"), lax.axis_index("gy")
    none = jnp.float32(0.0)
    ax_low = jnp.where(at_x == 0, -phi_x, none)
    ax_high = jnp.where(at_x == lax.axis_size("gx") - 1, phi_x, none)
    ay_low = jnp.where(at_y == 0, -phi_y, none)
    ay_high = jnp.where(at_y == lax.axis_size("gy") - 1, phi_y, none)
    sub = lax.broadcasted_iota(jnp.int32, (SUB, 128), 0)
    angles = jnp.zeros((SUB, 128), jnp.float32)
    for i, angle in enumerate((ax_low, ax_high, ay_low, ay_high, ax_low + ay_low, ax_low + ay_high,
                               ax_high + ay_low, ax_high + ay_high)):
        angles = jnp.where(sub == i, angle, angles)
    turns[pl.ds(0, SUB), :] = jnp.cos(angles)
    turns[pl.ds(SUB, SUB), :] = jnp.sin(angles)

    def turn(i, run):
        cosine = turns[pl.ds(i, 1), :]
        sine = turns[pl.ds(SUB + i, 1), :]
        return cosine, (sine if run == 0 else -sine)

    for which, entries, ref in ((0, plan.x_low, x_low), (1, plan.x_high, x_high)):
        at = {entry: i for i, entry in enumerate(entries)}
        for (plane, x), i in at.items():
            if plane is None:
                target, row = place(plane, x, 0)
                target[pl.ds(row, ny), :] = ref[pl.ds(i * ny, ny), :]
            elif plane[2] == 0:
                twin = plane[:2] + (1,) + plane[3:]
                cosine, sine = turn(which, plane[0])
                real, imag = turned(ref[pl.ds(i * ny, ny), :], ref[pl.ds(at[twin, x] * ny, ny), :], cosine, sine)
                state[pl.ds(place(plane, x, 0)[1], ny), :] = real
                state[pl.ds(place(twin, x, 0)[1], ny), :] = imag
    for which, entries, ref in ((2, plan.y_low, z_low), (3, plan.y_high, z_high)):
        at = {entry: i for i, entry in enumerate(entries)}
        for (plane, y), i in at.items():
            if plane is None:
                target, row = place(plane, 0, y)
                target[pl.ds(row, nx, stride=ring), :] = ref[pl.ds(i * nx, nx), :]
            elif plane[2] == 0:
                twin = plane[:2] + (1,) + plane[3:]
                cosine, sine = turn(which, plane[0])
                real, imag = turned(ref[pl.ds(i * nx, nx), :], ref[pl.ds(at[twin, y] * nx, nx), :], cosine, sine)
                state[pl.ds(place(plane, 0, y)[1], nx, stride=ring), :] = real
                state[pl.ds(place(twin, 0, y)[1], nx, stride=ring), :] = imag
    for which, entries, ref in ((4, plan.corner_low, c_low), (6, plan.corner_high, c_high)):
        at = {entry: i for i, entry in enumerate(entries)}
        for (plane, x, y), i in at.items():
            target, row = place(plane, x, y)
            if plane is None:
                target[pl.ds(row, 1), :] = ref[pl.ds(i, 1), :]
            elif plane[2] == 0:
                twin = plane[:2] + (1,) + plane[3:]
                cosine, sine = turn(which + (y >= 0), plane[0])
                real, imag = turned(ref[pl.ds(i, 1), :], ref[pl.ds(at[twin, x, y], 1), :], cosine, sine)
                state[pl.ds(row, 1), :] = real
                state[pl.ds(place(twin, x, y)[1], 1), :] = imag

    @pl.loop(0, wide_x)
    def _(x):
        rows = pl.ds(pl.multiple_of(x * ring, SUB), ring)
        coef[rows, :] = (0.5 * courant) / coef[rows, :]

    lane = lax.broadcasted_iota(jnp.int32, (ring, 128), 1)
    first, last = lane == 0, lane == 127

    def next_z(value):
        return jnp.where(last, 0.0, pltpu.roll(value, 127, 1))

    def prev_z(value):
        return jnp.where(first, 0.0, pltpu.roll(value, 1, 1))

    def next_y(value):
        return pltpu.roll(value, ring - 1, 0)

    def prev_y(value):
        return pltpu.roll(value, 1, 0)

    for step in range(STEPS):

        def rows(level, kind, run, part, comp, x):
            return pl.ds(pl.multiple_of(base(level, kind, run, part, comp) + x * ring, SUB), ring)

        def get(level, kind, run, part, comp, x):
            return state[rows(level, kind, run, part, comp, x), :]

        def update_h(run, part, x):
            ex, ey, ez = (get(step, 0, run, part, comp, x) for comp in range(3))
            ey_x, ez_x = get(step, 0, run, part, 1, x + 1), get(step, 0, run, part, 2, x + 1)
            hx, hy, hz = (get(step, 1, run, part, comp, x) for comp in range(3))
            if step == 0:
                hx, hy, hz = hx + hx, hy + hy, hz + hz
            hx = hx - ((next_y(ez) - ez) - (next_z(ey) - ey))
            hy = hy - ((next_z(ex) - ex) - (ez_x - ez))
            hz = hz - ((ey_x - ey) - (next_y(ex) - ex))
            for comp, value in enumerate((hx, hy, hz)):
                state[rows(step + 1, 1, run, part, comp, x), :] = value
            return (ex, ey, ez), (hx, hy, hz)

        def update_e(run, part, x, efield, hfield):
            ex, ey, ez = efield
            hx, hy, hz = hfield
            hy_x, hz_x = get(step + 1, 1, run, part, 1, x - 1), get(step + 1, 1, run, part, 2, x - 1)
            scale = coef[pl.ds(pl.multiple_of(x * ring, SUB), ring), :]
            ex = ex + scale * ((hz - prev_y(hz)) - (hy - prev_z(hy)))
            ey = ey + scale * ((hx - prev_z(hx)) - (hz - hz_x))
            ez = ez + scale * ((hy - hy_x) - (hx - prev_y(hx)))
            for comp, value in enumerate((ex, ey, ez)):
                state[rows(step + 1, 0, run, part, comp, x), :] = value

        for run in (0, 1):
            for part in (0, 1):
                update_h(run, part, step)

        @pl.loop(step + 1, wide_x - step - 1)
        def _(x):
            for run in (0, 1):
                for part in (0, 1):
                    efield, hfield = update_h(run, part, x)
                    update_e(run, part, x, efield, hfield)

    own_tile = at_x * lax.axis_size("gy") + at_y
    chosen = tiles[0] == own_tile
    for i in range(1, tiles.shape[0]):
        chosen = jnp.logical_or(chosen, tiles[i] == own_tile)
    weight = jnp.where(chosen, jnp.float32(1.0 / groups), none)
    share = parts.shape[2]
    shift = lax.rem(groups - lax.axis_index("angle"), groups) * share

    @pl.loop(0, nx * (ny // SUB))
    def _(i):
        x, tile = i // (ny // SUB), lax.rem(i, ny // SUB)
        total = jnp.zeros((SUB, 128), jnp.float32)
        for comp in range(3):
            ends = []
            for run, (spec, out) in enumerate(((spec_f, out_f), (spec_a, out_a))):
                at = [pl.ds(pl.multiple_of(((part * 3 + comp) * nx + x) * ny + tile * SUB, SUB), SUB) for part in (0, 1)]
                real, imag = spec[at[0], :], spec[at[1], :]
                for step in range(STEPS):
                    theta = omega_step * (step + 1)
                    efield = [
                        state[pl.ds(pl.multiple_of(base(step + 1, 0, run, part, comp) + (x + STEPS) * ring + tile * SUB, SUB), SUB), :]
                        for part in (0, 1)
                    ]
                    more = turned(efield[0], efield[1], math.cos(theta), math.sin(theta))
                    real, imag = real + more[0], imag + more[1]
                out[at[0], :], out[at[1], :] = real, imag
                ends.append((real, imag))
            total = total + (ends[0][0] * ends[1][0] - ends[0][1] * ends[1][1])
        total = pltpu.roll(total * weight, shift, 1)
        for k in range(groups):
            parts[k, pl.ds(pl.multiple_of(i * SUB, SUB), SUB), :] = total[:, k * share : (k + 1) * share]


def ring_pairs(axis, offset):
    size = lax.axis_size(axis)
    return [(i, (i + offset) % size) for i in range(size)]


def shards(
    forward_fields,
    adjoint_fields,
    forward_spectrum,
    adjoint_spectrum,
    permittivity,
    phase_table,
    angle_index,
    design_tiles,
):
    nx, ny, depth = permittivity.shape
    plan = Plan(nx, ny)
    groups = lax.axis_size("angle")
    wide_x, ring = nx + 2 * STEPS, ny + SUB

    def rows(array):
        return array.reshape((-1, depth))

    def lines(count):
        return jax.ShapeDtypeStruct((count, depth), jnp.float32)

    fwd, adj, eps = rows(forward_fields), rows(adjoint_fields), rows(permittivity)
    params = pltpu.CompilerParams(vmem_limit_bytes=40 * 2**20)
    with jax.named_scope("pack_faces"):
        x_up, x_down, z_up, z_down = pl.pallas_call(
            functools.partial(pack_kernel, plan),
            out_shape=(
                lines(len(plan.x_low) * ny),
                lines(len(plan.x_high) * ny),
                lines(len(plan.y_low) * nx),
                lines(len(plan.y_high) * nx),
            ),
            in_specs=[VMEM] * 3,
            out_specs=[VMEM] * 4,
            compiler_params=params,
        )(fwd, adj, eps)
    with jax.named_scope("send_faces"):
        z_low = lax.ppermute(z_up, "gy", ring_pairs("gy", 1))
        z_high = lax.ppermute(z_down, "gy", ring_pairs("gy", -1))
        x_low = lax.ppermute(x_up, "gx", ring_pairs("gx", 1))
        x_high = lax.ppermute(x_down, "gx", ring_pairs("gx", -1))
    with jax.named_scope("relay_corners"):
        c_up, c_down = pl.pallas_call(
            functools.partial(corner_kernel, plan),
            out_shape=(lines(-(-len(plan.corner_low) // SUB) * SUB), lines(-(-len(plan.corner_high) // SUB) * SUB)),
            in_specs=[VMEM] * 2,
            out_specs=[VMEM] * 2,
            compiler_params=params,
        )(z_low, z_high)
        c_low = lax.ppermute(c_up, "gx", ring_pairs("gx", 1))
        c_high = lax.ppermute(c_down, "gx", ring_pairs("gx", -1))
    with jax.named_scope("advance"):
        out_f, out_a, parts = pl.pallas_call(
            functools.partial(advance_kernel, plan, groups),
            out_shape=(
                lines(6 * nx * ny),
                lines(6 * nx * ny),
                jax.ShapeDtypeStruct((groups, nx * ny, depth // groups), jnp.float32),
            ),
            in_specs=[VMEM] * 11 + [SMEM] * 3,
            out_specs=[VMEM] * 3,
            scratch_shapes=[
                pltpu.VMEM(((STEPS + 1) * 24 * wide_x * ring, depth), jnp.float32),
                pltpu.VMEM((wide_x * ring, depth), jnp.float32),
                pltpu.VMEM((2 * SUB, depth), jnp.float32),
            ],
            compiler_params=params,
        )(fwd, adj, rows(forward_spectrum), rows(adjoint_spectrum), eps, x_low, x_high, z_low, z_high, c_low, c_high,
          phase_table, angle_index, design_tiles)
    with jax.named_scope("sum_angles"):
        gradient = parts[0]
        for k in range(1, groups):
            gradient = gradient + lax.ppermute(parts[k], "angle", ring_pairs("angle", k))
    return (
        out_f.reshape(forward_spectrum.shape),
        out_a.reshape(adjoint_spectrum.shape),
        gradient.reshape((nx, ny, depth // groups)),
    )


def solution(mesh):
    in_specs = (
        P("angle", None, "gx", "gy", None),
        P("angle", None, "gx", "gy", None),
        P("angle", None, "gx", "gy", None),
        P("angle", None, "gx", "gy", None),
        P("gx", "gy", None),
        P(),
        P("angle"),
        P(),
    )
    out_specs = (
        P("angle", None, "gx", "gy", None),
        P("angle", None, "gx", "gy", None),
        P("gx", "gy", "angle"),
    )
    return jax.shard_map(shards, mesh=mesh, in_specs=in_specs, out_specs=out_specs, check_vma=False)
```

```python
import functools
import math

import jax
import jax.numpy as jnp
from jax import lax
from jax.experimental import pallas as pl
from jax.experimental.pallas import tpu as pltpu
from jax.sharding import PartitionSpec as P

STEPS = 3
SUB = 8

courant = 0.5
omega_step = 0.7

VMEM = pl.BlockSpec(memory_space=pltpu.VMEM)
SMEM = pl.BlockSpec(memory_space=pltpu.SMEM)
HBM = pl.BlockSpec(memory_space=pltpu.HBM)


def moved(cells, dx, dy):
    return {(x + dx, y + dy) for x, y in cells}


def cone(nx, ny):
    block = {(x, y) for x in range(nx) for y in range(ny)}
    ex, ey, ez = block, block, block
    hx, hy, hz, eps = set(), set(), set(), set()
    for _ in range(STEPS):
        eps = eps | ex | ey | ez
        hx, hy, hz = (
            hx | ey | ez | moved(ez, 0, -1),
            hy | ex | ez | moved(ez, -1, 0),
            hz | ex | moved(ex, 0, -1) | ey | moved(ey, -1, 0),
        )
        ex, ey, ez = (
            ex | hy | hz | moved(hz, 0, 1),
            ey | hx | hz | moved(hz, 1, 0),
            ez | hx | moved(hx, 0, 1) | hy | moved(hy, 1, 0),
        )
    return (ex, ey, ez), (hx, hy, hz), eps


PLANES = [(run, kind, part, comp) for run in (0, 1) for kind in (0, 1) for comp in (0, 1, 2) for part in (0, 1)]


class Plan:
    def __init__(self, nx, ny):
        efield, hfield, eps = cone(nx, ny)
        self.nx, self.ny = nx, ny
        self.wide, self.ring = nx + 2 * STEPS, ny + SUB

        def cells(plane):
            if plane is None:
                return eps
            return (efield, hfield)[plane[1]][plane[3]]

        planes = PLANES + [None]
        self.x_low, self.x_high, self.y_low, self.y_high = [], [], [], []
        for plane in planes:
            need = cells(plane)
            self.x_low += [(plane, x) for x in range(-STEPS, 0) if any((x, y) in need for y in range(ny))]
            self.x_high += [(plane, x) for x in range(nx, nx + STEPS) if any((x, y) in need for y in range(ny))]
            self.y_low += [(plane, y) for y in range(-STEPS, 0) if any((x, y) in need for x in range(nx))]
            self.y_high += [(plane, y) for y in range(ny, ny + STEPS) if any((x, y) in need for x in range(nx))]
        self.corner_low, self.corner_high = [], []
        for out, layers in ((self.corner_low, range(-STEPS, 0)), (self.corner_high, range(nx, nx + STEPS))):
            for rows in (range(-STEPS, 0), range(ny, ny + STEPS)):
                for plane in planes:
                    need = cells(plane)
                    out += [(plane, x, y) for x in layers for y in rows if (x, y) in need]

    def row(self, x, y, plane=(0, 0, 0, 0)):
        run, _, part, comp = plane
        return ((run * 6 + part * 3 + comp) * self.wide + x + STEPS) * self.ring + y % self.ring


def pack_y_kernel(plan, fwd, adj, eps, e0, h0, coef, z_up, z_down, sems):
    nx, ny = plan.nx, plan.ny
    own = (pl.ds(STEPS, nx), pl.ds(0, ny), slice(None))
    copies = []
    for run, ref in enumerate((fwd, adj)):
        for kind, state in enumerate((e0, h0)):
            for i in range(6):
                copies.append(
                    pltpu.make_async_copy(ref.at[kind * 6 + i], state.at[(run * 6 + i, *own)], sems.at[len(copies)])
                )
    copies.append(pltpu.make_async_copy(eps, coef.at[own], sems.at[len(copies)]))
    for copy in copies:
        copy.start()
    for copy in copies:
        copy.wait()
    for x in range(nx):
        coef[STEPS + x, pl.ds(0, ny), :] = (0.5 * courant) / coef[STEPS + x, pl.ds(0, ny), :]
    flat = [state.reshape((-1, state.shape[-1])) for state in (e0, h0)]
    flat_coef = coef.reshape((-1, coef.shape[-1]))
    for entries, shift, out in ((plan.y_low, ny, z_up), (plan.y_high, -ny, z_down)):
        for i, (plane, y) in enumerate(entries):
            ref, row = (flat_coef, plan.row(0, y + shift)) if plane is None else (flat[plane[1]], plan.row(0, y + shift, plane))
            out[pl.ds(i * nx, nx), :] = ref[pl.ds(row, nx, stride=plan.ring), :]


def pack_x_kernel(plan, e0, h0, coef, x_up, x_down):
    nx, ny = plan.nx, plan.ny
    for entries, shift, out in ((plan.x_low, nx, x_up), (plan.x_high, -nx, x_down)):
        for i, (plane, x) in enumerate(entries):
            ref, row = (coef, plan.row(x + shift, 0)) if plane is None else ((e0, h0)[plane[1]], plan.row(x + shift, 0, plane))
            out[pl.ds(i * ny, ny), :] = ref[pl.ds(row, ny), :]


def turns_kernel(groups, table, index, tiles, turns):
    row = index[0]
    phi_x, phi_y = table[row, 0], table[row, 1]
    at_x, at_y = lax.axis_index("gx"), lax.axis_index("gy")
    none = jnp.float32(0.0)
    ax_low = jnp.where(at_x == 0, -phi_x, none)
    ax_high = jnp.where(at_x == lax.axis_size("gx") - 1, phi_x, none)
    ay_low = jnp.where(at_y == 0, -phi_y, none)
    ay_high = jnp.where(at_y == lax.axis_size("gy") - 1, phi_y, none)
    sub = lax.broadcasted_iota(jnp.int32, (SUB, turns.shape[1]), 0)
    angles = jnp.zeros(sub.shape, jnp.float32)
    for i, angle in enumerate((ax_low, ax_high, ay_low, ay_high, ax_low + ay_low, ax_low + ay_high,
                               ax_high + ay_low, ax_high + ay_high)):
        angles = jnp.where(sub == i, angle, angles)
    turns[pl.ds(0, SUB), :] = jnp.cos(angles)
    turns[pl.ds(SUB, SUB), :] = jnp.sin(angles)
    own_tile = at_x * lax.axis_size("gy") + at_y
    chosen = tiles[0] == own_tile
    for i in range(1, tiles.shape[0]):
        chosen = jnp.logical_or(chosen, tiles[i] == own_tile)
    weight = jnp.where(chosen, jnp.float32(1.0 / groups), none)
    turns[pl.ds(2 * SUB, SUB), :] = jnp.full(sub.shape, weight, jnp.float32)


def corner_kernel(plan, z_low, z_high, c_up, c_down):
    nx = plan.nx
    low = {entry: i for i, entry in enumerate(plan.y_low)}
    high = {entry: i for i, entry in enumerate(plan.y_high)}
    for entries, shift, out in ((plan.corner_low, nx, c_up), (plan.corner_high, -nx, c_down)):
        for i, (plane, x, y) in enumerate(entries):
            ref, at = (z_low, low[plane, y]) if y < 0 else (z_high, high[plane, y])
            out[pl.ds(i, 1), :] = ref[pl.ds(at * nx + x + shift, 1), :]


def turned(real, imag, cosine, sine):
    return real * cosine - imag * sine, real * sine + imag * cosine


def unpack(entries, ref, count, which, turns, target):
    at = {entry: i for i, entry in enumerate(entries)}
    for entry, i in at.items():
        plane = entry[0]
        own = ref[pl.ds(i * count, count), :]
        if plane is None:
            array, rows = target(entry)
            array[rows, :] = own
        elif plane[2] == 0:
            twin = (plane[:2] + (1,) + plane[3:], *entry[1:])
            row = which(entry)
            cosine, sine = turns[pl.ds(row, 1), :], turns[pl.ds(SUB + row, 1), :]
            if plane[0] == 1:
                sine = -sine
            real, imag = turned(own, ref[pl.ds(at[twin] * count, count), :], cosine, sine)
            for what, value in ((entry, real), (twin, imag)):
                array, rows = target(what)
                array[rows, :] = value


class Sweeps:
    def __init__(self, plan, efield, hfield, coef):
        self.plan, self.efield, self.hfield, self.coef = plan, efield, hfield, coef
        lane = lax.broadcasted_iota(jnp.int32, (plan.ring, coef.shape[1]), 1)
        self.first, self.last = lane == 0, lane == coef.shape[1] - 1

    def rows(self, group, comp, x):
        plan = self.plan
        start = (group * 3 + comp) * plan.wide * plan.ring + (x + STEPS) * plan.ring
        return pl.ds(start if isinstance(start, int) else pl.multiple_of(start, SUB), plan.ring)

    def next_z(self, value):
        return jnp.where(self.last, 0.0, pltpu.roll(value, value.shape[1] - 1, 1))

    def prev_z(self, value):
        return jnp.where(self.first, 0.0, pltpu.roll(value, 1, 1))

    def next_y(self, value):
        return pltpu.roll(value, self.plan.ring - 1, 0)

    def prev_y(self, value):
        return pltpu.roll(value, 1, 0)

    def update_h(self, step, group, x):
        efield, old, new = self.efield[step - 1], self.hfield[step - 1], self.hfield[step]
        ex, ey, ez = (efield[self.rows(group, comp, x), :] for comp in range(3))
        ey_x, ez_x = (efield[self.rows(group, comp, x + 1), :] for comp in (1, 2))
        hx, hy, hz = (old[self.rows(group, comp, x), :] for comp in range(3))
        if step == 1:
            hx, hy, hz = hx + hx, hy + hy, hz + hz
        new[self.rows(group, 0, x), :] = hx - ((self.next_y(ez) - ez) - (self.next_z(ey) - ey))
        new[self.rows(group, 1, x), :] = hy - ((self.next_z(ex) - ex) - (ez_x - ez))
        new[self.rows(group, 2, x), :] = hz - ((ey_x - ey) - (self.next_y(ex) - ex))

    def update_e(self, step, group, x):
        old, new, hfield = self.efield[step - 1], self.efield[step], self.hfield[step]
        ex, ey, ez = (old[self.rows(group, comp, x), :] for comp in range(3))
        hx, hy, hz = (hfield[self.rows(group, comp, x), :] for comp in range(3))
        hy_x, hz_x = (hfield[self.rows(group, comp, x - 1), :] for comp in (1, 2))
        scale = self.coef[self.rows(0, 0, x), :]
        new[self.rows(group, 0, x), :] = ex + scale * ((hz - self.prev_y(hz)) - (hy - self.prev_z(hy)))
        new[self.rows(group, 1, x), :] = ey + scale * ((hx - self.prev_z(hx)) - (hz - hz_x))
        new[self.rows(group, 2, x), :] = ez + scale * ((hy - hy_x) - (hx - self.prev_y(hx)))

    def both(self, step, h_layers, e_layers):
        for update, layers in ((self.update_h, h_layers), (self.update_e, e_layers)):

            @pl.loop(0, 2)
            def _(run):
                for part in (0, 1):
                    for x in layers:
                        update(step, run * 2 + part, x)


def middle_kernel(plan, e0_in, h0_in, coef_in, z_low, z_high, turns, *state):
    nx = plan.nx
    efield, hfield, coef = state[: STEPS + 1], state[STEPS + 1 : 2 * STEPS + 2], state[-1]

    def target(entry):
        plane, y = entry
        if plane is None:
            return coef, pl.ds(plan.row(0, y), nx, stride=plan.ring)
        return (efield, hfield)[plane[1]][0], pl.ds(plan.row(0, y, plane), nx, stride=plan.ring)

    unpack(plan.y_low, z_low, nx, lambda entry: 2, turns, target)
    unpack(plan.y_high, z_high, nx, lambda entry: 3, turns, target)
    sweeps = Sweeps(plan, efield, hfield, coef)
    for step in range(1, STEPS + 1):
        sweeps.both(step, range(step - 1, nx - step), range(step, nx - step))


def edges_kernel(plan, groups, *refs):
    nx, ny = plan.nx, plan.ny
    count = 2 * STEPS + 3
    x_low, x_high, c_low, c_high, turns, spec_f, spec_a = refs[count : count + 7]
    state = refs[count + 7 : 2 * count + 7]
    out_f, out_a, parts = refs[2 * count + 7 :]
    efield, hfield, coef = state[: STEPS + 1], state[STEPS + 1 : 2 * STEPS + 2], state[-1]

    def target(entry):
        plane, x = entry[:2]
        y, size = (0, ny) if len(entry) == 2 else (entry[2], 1)
        if plane is None:
            return coef, pl.ds(plan.row(x, y), size)
        return (efield, hfield)[plane[1]][0], pl.ds(plan.row(x, y, plane), size)

    unpack(plan.x_low, x_low, ny, lambda entry: 0, turns, target)
    unpack(plan.x_high, x_high, ny, lambda entry: 1, turns, target)
    unpack(plan.corner_low, c_low, 1, lambda entry: 4 + (entry[2] >= 0), turns, target)
    unpack(plan.corner_high, c_high, 1, lambda entry: 6 + (entry[2] >= 0), turns, target)
    sweeps = Sweeps(plan, efield, hfield, coef)
    for step in range(1, STEPS + 1):
        low, high = step - STEPS, nx - step
        sweeps.both(
            step,
            [*range(low - 1, step - 1), *range(high, nx + STEPS - step)],
            [*range(low, step), *range(high, nx + STEPS - step)],
        )

    share = parts.shape[2]
    shift = lax.rem(groups - lax.axis_index("angle"), groups) * share
    weight = turns[pl.ds(2 * SUB, SUB), :]
    tiles = ny // SUB

    @pl.loop(0, nx * tiles)
    def _(i):
        x, tile = i // tiles, lax.rem(i, tiles)
        total = jnp.zeros(weight.shape, jnp.float32)
        for comp in range(3):
            ends = []
            for run, (spec, out) in enumerate(((spec_f, out_f), (spec_a, out_a))):
                at = [pl.ds(pl.multiple_of(((part * 3 + comp) * nx + x) * ny + tile * SUB, SUB), SUB) for part in (0, 1)]
                real, imag = spec[at[0], :], spec[at[1], :]
                for step in range(1, STEPS + 1):
                    theta = omega_step * step
                    ends_e = [
                        efield[step][pl.ds(pl.multiple_of(plan.row(x, 0, (run, 0, part, comp)) + tile * SUB, SUB), SUB), :]
                        for part in (0, 1)
                    ]
                    more = turned(*ends_e, math.cos(theta), math.sin(theta))
                    real, imag = real + more[0], imag + more[1]
                out[at[0], :], out[at[1], :] = real, imag
                ends.append((real, imag))
            total = total + (ends[0][0] * ends[1][0] - ends[0][1] * ends[1][1])
        total = pltpu.roll(total * weight, shift, 1)
        for k in range(groups):
            parts[k, pl.ds(pl.multiple_of(i * SUB, SUB), SUB), :] = total[:, k * share : (k + 1) * share]


def write_kernel(tr_f, tr_a, out_f, out_a, sems):
    copies = []
    for source, target in ((tr_f, out_f), (tr_a, out_a)):
        for i in range(source.shape[0]):
            copies.append(pltpu.make_async_copy(source.at[i], target.at[i], sems.at[len(copies)]))
    for copy in copies:
        copy.start()
    for copy in copies:
        copy.wait()


def ring_pairs(axis, offset):
    size = lax.axis_size(axis)
    return [(i, (i + offset) % size) for i in range(size)]


def shards(
    forward_fields,
    adjoint_fields,
    forward_spectrum,
    adjoint_spectrum,
    permittivity,
    phase_table,
    angle_index,
    design_tiles,
):
    nx, ny, depth = permittivity.shape
    plan = Plan(nx, ny)
    groups = lax.axis_size("angle")
    wide, ring = plan.wide, plan.ring

    def array(*shape):
        return jax.ShapeDtypeStruct(shape, jnp.float32)

    def lines(count):
        return array(count, depth)

    def params(mib):
        return pltpu.CompilerParams(vmem_limit_bytes=mib * 2**20)

    def cost(size):
        return pl.CostEstimate(flops=size, bytes_accessed=size, transcendentals=0)

    with jax.named_scope("pack_y"):
        e0, h0, coef, z_up, z_down = pl.pallas_call(
            functools.partial(pack_y_kernel, plan),
            out_shape=(
                array(12, wide, ring, depth),
                array(12, wide, ring, depth),
                array(wide, ring, depth),
                lines(len(plan.y_low) * nx),
                lines(len(plan.y_high) * nx),
            ),
            in_specs=[HBM] * 3,
            out_specs=[VMEM] * 5,
            scratch_shapes=[pltpu.SemaphoreType.DMA((25,))],
            compiler_params=params(16),
        )(forward_fields[0], adjoint_fields[0], permittivity)
    e0, h0, coef = (state.reshape((-1, depth)) for state in (e0, h0, coef))
    with jax.named_scope("send_y"):
        z_low = lax.ppermute(z_up, "gy", ring_pairs("gy", 1))
        z_high = lax.ppermute(z_down, "gy", ring_pairs("gy", -1))
    with jax.named_scope("pack_x"):
        x_up, x_down = pl.pallas_call(
            functools.partial(pack_x_kernel, plan),
            out_shape=(lines(len(plan.x_low) * ny), lines(len(plan.x_high) * ny)),
            in_specs=[VMEM] * 3,
            out_specs=[VMEM] * 2,
            compiler_params=params(8),
            cost_estimate=cost(40 * 2**20),
        )(e0, h0, coef)
    with jax.named_scope("send_x"):
        x_low = lax.ppermute(x_up, "gx", ring_pairs("gx", 1))
        x_high = lax.ppermute(x_down, "gx", ring_pairs("gx", -1))
    with jax.named_scope("turns"):
        turns = pl.pallas_call(
            functools.partial(turns_kernel, groups),
            out_shape=lines(3 * SUB),
            in_specs=[SMEM] * 3,
            out_specs=VMEM,
            compiler_params=params(4),
        )(phase_table, angle_index, design_tiles)
    with jax.named_scope("relay_corners"):
        c_up, c_down = pl.pallas_call(
            functools.partial(corner_kernel, plan),
            out_shape=(lines(-(-len(plan.corner_low) // SUB) * SUB), lines(-(-len(plan.corner_high) // SUB) * SUB)),
            in_specs=[VMEM] * 2,
            out_specs=[VMEM] * 2,
            compiler_params=params(4),
        )(z_low, z_high)
        c_low = lax.ppermute(c_up, "gx", ring_pairs("gx", 1))
        c_high = lax.ppermute(c_down, "gx", ring_pairs("gx", -1))
    level = lines(12 * wide * ring)
    count = 2 * STEPS + 3
    levels = [level] * (count - 1) + [lines(wide * ring)]
    with jax.named_scope("middle"):
        state = pl.pallas_call(
            functools.partial(middle_kernel, plan),
            out_shape=levels,
            in_specs=[VMEM] * 6,
            out_specs=[VMEM] * count,
            input_output_aliases={0: 0, 1: STEPS + 1, 2: count - 1},
            compiler_params=params(8),
            cost_estimate=cost(20 * 2**20),
        )(e0, h0, coef, z_low, z_high, turns)
    with jax.named_scope("edges"):
        spectra = [spectrum.reshape((-1, depth)) for spectrum in (forward_spectrum, adjoint_spectrum)]
        *_, tr_f, tr_a, parts = pl.pallas_call(
            functools.partial(edges_kernel, plan, groups),
            out_shape=[*levels, lines(6 * nx * ny), lines(6 * nx * ny), array(groups, nx * ny, depth // groups)],
            in_specs=[VMEM] * (count + 7),
            out_specs=[VMEM] * (count + 3),
            input_output_aliases={i: i for i in range(count)},
            compiler_params=params(8),
        )(*state, x_low, x_high, c_low, c_high, turns, *spectra)
    with jax.named_scope("sum_angles"):
        gradient = parts[0]
        for k in range(1, groups):
            gradient = gradient + lax.ppermute(parts[k], "angle", ring_pairs("angle", k))
    with jax.named_scope("write"):
        out_f, out_a = pl.pallas_call(
            write_kernel,
            out_shape=[array(6, nx, ny, depth)] * 2,
            in_specs=[VMEM] * 2,
            out_specs=[HBM] * 2,
            scratch_shapes=[pltpu.SemaphoreType.DMA((12,))],
            compiler_params=params(4),
        )(tr_f.reshape((6, nx, ny, depth)), tr_a.reshape((6, nx, ny, depth)))
    return (
        out_f.reshape(forward_spectrum.shape),
        out_a.reshape(adjoint_spectrum.shape),
        gradient.reshape((nx, ny, depth // groups)),
    )


def solution(mesh):
    in_specs = (
        P("angle", None, "gx", "gy", None),
        P("angle", None, "gx", "gy", None),
        P("angle", None, "gx", "gy", None),
        P("angle", None, "gx", "gy", None),
        P("gx", "gy", None),
        P(),
        P("angle"),
        P(),
    )
    out_specs = (
        P("angle", None, "gx", "gy", None),
        P("angle", None, "gx", "gy", None),
        P("gx", "gy", "angle"),
    )
    return jax.shard_map(shards, mesh=mesh, in_specs=in_specs, out_specs=out_specs, check_vma=False)
```

```python
import functools
import math

import jax
import jax.numpy as jnp
from jax import lax
from jax.experimental import pallas as pl
from jax.experimental.pallas import tpu as pltpu
from jax.sharding import PartitionSpec as P

STEPS = 3
SUB = 8

courant = 0.5
omega_step = 0.7

VMEM = pl.BlockSpec(memory_space=pltpu.VMEM)
SMEM = pl.BlockSpec(memory_space=pltpu.SMEM)
HBM = pl.BlockSpec(memory_space=pltpu.HBM)


def moved(cells, dx, dy):
    return {(x + dx, y + dy) for x, y in cells}


def cone(nx, ny):
    block = {(x, y) for x in range(nx) for y in range(ny)}
    ex, ey, ez = block, block, block
    hx, hy, hz, eps = set(), set(), set(), set()
    for _ in range(STEPS):
        eps = eps | ex | ey | ez
        hx, hy, hz = (
            hx | ey | ez | moved(ez, 0, -1),
            hy | ex | ez | moved(ez, -1, 0),
            hz | ex | moved(ex, 0, -1) | ey | moved(ey, -1, 0),
        )
        ex, ey, ez = (
            ex | hy | hz | moved(hz, 0, 1),
            ey | hx | hz | moved(hz, 1, 0),
            ez | hx | moved(hx, 0, 1) | hy | moved(hy, 1, 0),
        )
    return (ex, ey, ez), (hx, hy, hz), eps


PLANES = [(run, kind, part, comp) for run in (0, 1) for kind in (0, 1) for comp in (0, 1, 2) for part in (0, 1)]


class Plan:
    def __init__(self, nx, ny):
        efield, hfield, eps = cone(nx, ny)
        self.nx, self.ny = nx, ny
        self.wide, self.ring = nx + 2 * STEPS, ny + SUB

        def cells(plane):
            if plane is None:
                return eps
            return (efield, hfield)[plane[1]][plane[3]]

        planes = PLANES + [None]
        self.x_low, self.x_high, self.y_low, self.y_high = [], [], [], []
        for plane in planes:
            need = cells(plane)
            self.x_low += [(plane, x) for x in range(-STEPS, 0) if any((x, y) in need for y in range(ny))]
            self.x_high += [(plane, x) for x in range(nx, nx + STEPS) if any((x, y) in need for y in range(ny))]
            self.y_low += [(plane, y) for y in range(-STEPS, 0) if any((x, y) in need for x in range(nx))]
            self.y_high += [(plane, y) for y in range(ny, ny + STEPS) if any((x, y) in need for x in range(nx))]
        self.corner_low, self.corner_high = [], []
        for out, layers in ((self.corner_low, range(-STEPS, 0)), (self.corner_high, range(nx, nx + STEPS))):
            for rows in (range(-STEPS, 0), range(ny, ny + STEPS)):
                for plane in planes:
                    need = cells(plane)
                    out += [(plane, x, y) for x in layers for y in rows if (x, y) in need]

    def row(self, x, y, plane=(0, 0, 0, 0)):
        run, _, part, comp = plane
        return ((run * 6 + part * 3 + comp) * self.wide + x + STEPS) * self.ring + y % self.ring


def pack_y_kernel(plan, fwd, adj, eps, e0, h0, coef, z_up, z_down, sems):
    nx, ny = plan.nx, plan.ny
    own = (pl.ds(STEPS, nx), pl.ds(0, ny), slice(None))
    copies = []
    for run, ref in enumerate((fwd, adj)):
        for kind, state in enumerate((e0, h0)):
            for i in range(6):
                copies.append(
                    pltpu.make_async_copy(ref.at[kind * 6 + i], state.at[(run * 6 + i, *own)], sems.at[len(copies)])
                )
    copies.append(pltpu.make_async_copy(eps, coef.at[own], sems.at[len(copies)]))
    for copy in copies:
        copy.start()
    for copy in copies:
        copy.wait()
    for x in range(nx):
        coef[STEPS + x, pl.ds(0, ny), :] = (0.5 * courant) / coef[STEPS + x, pl.ds(0, ny), :]
    flat = [state.reshape((-1, state.shape[-1])) for state in (e0, h0)]
    flat_coef = coef.reshape((-1, coef.shape[-1]))
    for entries, shift, out in ((plan.y_low, ny, z_up), (plan.y_high, -ny, z_down)):
        for i, (plane, y) in enumerate(entries):
            ref, row = (flat_coef, plan.row(0, y + shift)) if plane is None else (flat[plane[1]], plan.row(0, y + shift, plane))
            out[pl.ds(i * nx, nx), :] = ref[pl.ds(row, nx, stride=plan.ring), :]


def pack_x_kernel(plan, e0, h0, coef, x_up, x_down):
    nx, ny = plan.nx, plan.ny
    for entries, shift, out in ((plan.x_low, nx, x_up), (plan.x_high, -nx, x_down)):
        for i, (plane, x) in enumerate(entries):
            ref, row = (coef, plan.row(x + shift, 0)) if plane is None else ((e0, h0)[plane[1]], plan.row(x + shift, 0, plane))
            out[pl.ds(i * ny, ny), :] = ref[pl.ds(row, ny), :]


def turns_kernel(groups, table, index, tiles, turns):
    row = index[0]
    phi_x, phi_y = table[row, 0], table[row, 1]
    at_x, at_y = lax.axis_index("gx"), lax.axis_index("gy")
    none = jnp.float32(0.0)
    ax_low = jnp.where(at_x == 0, -phi_x, none)
    ax_high = jnp.where(at_x == lax.axis_size("gx") - 1, phi_x, none)
    ay_low = jnp.where(at_y == 0, -phi_y, none)
    ay_high = jnp.where(at_y == lax.axis_size("gy") - 1, phi_y, none)
    sub = lax.broadcasted_iota(jnp.int32, (SUB, turns.shape[1]), 0)
    angles = jnp.zeros(sub.shape, jnp.float32)
    for i, angle in enumerate((ax_low, ax_high, ay_low, ay_high, ax_low + ay_low, ax_low + ay_high,
                               ax_high + ay_low, ax_high + ay_high)):
        angles = jnp.where(sub == i, angle, angles)
    turns[pl.ds(0, SUB), :] = jnp.cos(angles)
    turns[pl.ds(SUB, SUB), :] = jnp.sin(angles)
    own_tile = at_x * lax.axis_size("gy") + at_y
    chosen = tiles[0] == own_tile
    for i in range(1, tiles.shape[0]):
        chosen = jnp.logical_or(chosen, tiles[i] == own_tile)
    weight = jnp.where(chosen, jnp.float32(1.0 / groups), none)
    turns[pl.ds(2 * SUB, SUB), :] = jnp.full(sub.shape, weight, jnp.float32)


def corner_kernel(plan, z_low, z_high, c_up, c_down):
    nx = plan.nx
    low = {entry: i for i, entry in enumerate(plan.y_low)}
    high = {entry: i for i, entry in enumerate(plan.y_high)}
    for entries, shift, out in ((plan.corner_low, nx, c_up), (plan.corner_high, -nx, c_down)):
        for i, (plane, x, y) in enumerate(entries):
            ref, at = (z_low, low[plane, y]) if y < 0 else (z_high, high[plane, y])
            out[pl.ds(i, 1), :] = ref[pl.ds(at * nx + x + shift, 1), :]


def turned(real, imag, cosine, sine):
    return real * cosine - imag * sine, real * sine + imag * cosine


def unpack(entries, ref, count, which, turns, target):
    at = {entry: i for i, entry in enumerate(entries)}
    for entry, i in at.items():
        plane = entry[0]
        own = ref[pl.ds(i * count, count), :]
        if plane is None:
            array, rows = target(entry)
            array[rows, :] = own
        elif plane[2] == 0:
            twin = (plane[:2] + (1,) + plane[3:], *entry[1:])
            row = which(entry)
            cosine, sine = turns[pl.ds(row, 1), :], turns[pl.ds(SUB + row, 1), :]
            if plane[0] == 1:
                sine = -sine
            real, imag = turned(own, ref[pl.ds(at[twin] * count, count), :], cosine, sine)
            for what, value in ((entry, real), (twin, imag)):
                array, rows = target(what)
                array[rows, :] = value


class Sweeps:
    def __init__(self, plan, efield, hfield, coef):
        self.plan, self.efield, self.hfield, self.coef = plan, efield, hfield, coef
        lane = lax.broadcasted_iota(jnp.int32, (plan.ring, coef.shape[1]), 1)
        self.first, self.last = lane == 0, lane == coef.shape[1] - 1

    def rows(self, group, comp, x):
        plan = self.plan
        start = (group * 3 + comp) * plan.wide * plan.ring + (x + STEPS) * plan.ring
        return pl.ds(start if isinstance(start, int) else pl.multiple_of(start, SUB), plan.ring)

    def next_z(self, value):
        return jnp.where(self.last, 0.0, pltpu.roll(value, value.shape[1] - 1, 1))

    def prev_z(self, value):
        return jnp.where(self.first, 0.0, pltpu.roll(value, 1, 1))

    def next_y(self, value):
        return pltpu.roll(value, self.plan.ring - 1, 0)

    def prev_y(self, value):
        return pltpu.roll(value, 1, 0)

    def update_h(self, step, group, x):
        efield, old, new = self.efield[step - 1], self.hfield[step - 1], self.hfield[step]
        ex, ey, ez = (efield[self.rows(group, comp, x), :] for comp in range(3))
        ey_x, ez_x = (efield[self.rows(group, comp, x + 1), :] for comp in (1, 2))
        hx, hy, hz = (old[self.rows(group, comp, x), :] for comp in range(3))
        if step == 1:
            hx, hy, hz = hx + hx, hy + hy, hz + hz
        new[self.rows(group, 0, x), :] = hx - ((self.next_y(ez) - ez) - (self.next_z(ey) - ey))
        new[self.rows(group, 1, x), :] = hy - ((self.next_z(ex) - ex) - (ez_x - ez))
        new[self.rows(group, 2, x), :] = hz - ((ey_x - ey) - (self.next_y(ex) - ex))

    def update_e(self, step, group, x):
        old, new, hfield = self.efield[step - 1], self.efield[step], self.hfield[step]
        ex, ey, ez = (old[self.rows(group, comp, x), :] for comp in range(3))
        hx, hy, hz = (hfield[self.rows(group, comp, x), :] for comp in range(3))
        hy_x, hz_x = (hfield[self.rows(group, comp, x - 1), :] for comp in (1, 2))
        scale = self.coef[self.rows(0, 0, x), :]
        new[self.rows(group, 0, x), :] = ex + scale * ((hz - self.prev_y(hz)) - (hy - self.prev_z(hy)))
        new[self.rows(group, 1, x), :] = ey + scale * ((hx - self.prev_z(hx)) - (hz - hz_x))
        new[self.rows(group, 2, x), :] = ez + scale * ((hy - hy_x) - (hx - self.prev_y(hx)))

    def both(self, step, h_layers, e_layers):
        for update, layers in ((self.update_h, h_layers), (self.update_e, e_layers)):

            @pl.loop(0, 2)
            def _(run):
                for part in (0, 1):
                    for x in layers:
                        update(step, run * 2 + part, x)


def middle_kernel(plan, e0_in, h0_in, coef_in, z_low, z_high, turns, *state):
    nx = plan.nx
    efield, hfield, coef = state[: STEPS + 1], state[STEPS + 1 : 2 * STEPS + 2], state[-1]

    def target(entry):
        plane, y = entry
        if plane is None:
            return coef, pl.ds(plan.row(0, y), nx, stride=plan.ring)
        return (efield, hfield)[plane[1]][0], pl.ds(plan.row(0, y, plane), nx, stride=plan.ring)

    unpack(plan.y_low, z_low, nx, lambda entry: 2, turns, target)
    unpack(plan.y_high, z_high, nx, lambda entry: 3, turns, target)
    sweeps = Sweeps(plan, efield, hfield, coef)
    for step in range(1, STEPS + 1):
        sweeps.both(step, range(step - 1, nx - step), range(step, nx - step))


def edges_kernel(plan, groups, *refs):
    nx, ny = plan.nx, plan.ny
    count = 2 * STEPS + 3
    x_low, x_high, c_low, c_high, turns, spec_f, spec_a = refs[count : count + 7]
    state = refs[count + 7 : 2 * count + 7]
    out_f, out_a, parts = refs[2 * count + 7 :]
    efield, hfield, coef = state[: STEPS + 1], state[STEPS + 1 : 2 * STEPS + 2], state[-1]

    def target(entry):
        plane, x = entry[:2]
        y, size = (0, ny) if len(entry) == 2 else (entry[2], 1)
        if plane is None:
            return coef, pl.ds(plan.row(x, y), size)
        return (efield, hfield)[plane[1]][0], pl.ds(plan.row(x, y, plane), size)

    unpack(plan.x_low, x_low, ny, lambda entry: 0, turns, target)
    unpack(plan.x_high, x_high, ny, lambda entry: 1, turns, target)
    unpack(plan.corner_low, c_low, 1, lambda entry: 4 + (entry[2] >= 0), turns, target)
    unpack(plan.corner_high, c_high, 1, lambda entry: 6 + (entry[2] >= 0), turns, target)
    sweeps = Sweeps(plan, efield, hfield, coef)
    for step in range(1, STEPS + 1):
        low, high = step - STEPS, nx - step
        sweeps.both(
            step,
            [*range(low - 1, step - 1), *range(high, nx + STEPS - step)],
            [*range(low, step), *range(high, nx + STEPS - step)],
        )

    share = parts.shape[2]
    shift = lax.rem(groups - lax.axis_index("angle"), groups) * share
    weight = turns[pl.ds(2 * SUB, SUB), :]
    tiles = ny // SUB

    @pl.loop(0, nx * tiles)
    def _(i):
        x, tile = i // tiles, lax.rem(i, tiles)
        total = jnp.zeros(weight.shape, jnp.float32)
        for comp in range(3):
            ends = []
            for run, (spec, out) in enumerate(((spec_f, out_f), (spec_a, out_a))):
                at = [pl.ds(pl.multiple_of(((part * 3 + comp) * nx + x) * ny + tile * SUB, SUB), SUB) for part in (0, 1)]
                real, imag = spec[at[0], :], spec[at[1], :]
                for step in range(1, STEPS + 1):
                    theta = omega_step * step
                    ends_e = [
                        efield[step][pl.ds(pl.multiple_of(plan.row(x, 0, (run, 0, part, comp)) + tile * SUB, SUB), SUB), :]
                        for part in (0, 1)
                    ]
                    more = turned(*ends_e, math.cos(theta), math.sin(theta))
                    real, imag = real + more[0], imag + more[1]
                out[at[0], :], out[at[1], :] = real, imag
                ends.append((real, imag))
            total = total + (ends[0][0] * ends[1][0] - ends[0][1] * ends[1][1])
        total = pltpu.roll(total * weight, shift, 1)
        for k in range(groups):
            parts[k, pl.ds(pl.multiple_of(i * SUB, SUB), SUB), :] = total[:, k * share : (k + 1) * share]


def write_kernel(tr_f, tr_a, out_f, out_a, sems):
    copies = []
    for source, target in ((tr_f, out_f), (tr_a, out_a)):
        for i in range(source.shape[0]):
            copies.append(pltpu.make_async_copy(source.at[i], target.at[i], sems.at[len(copies)]))
    for copy in copies:
        copy.start()
    for copy in copies:
        copy.wait()


def ring_pairs(axis, offset):
    size = lax.axis_size(axis)
    return [(i, (i + offset) % size) for i in range(size)]


def shards(
    forward_fields,
    adjoint_fields,
    forward_spectrum,
    adjoint_spectrum,
    permittivity,
    phase_table,
    angle_index,
    design_tiles,
):
    nx, ny, depth = permittivity.shape
    plan = Plan(nx, ny)
    groups = lax.axis_size("angle")
    wide, ring = plan.wide, plan.ring

    def array(*shape):
        return jax.ShapeDtypeStruct(shape, jnp.float32)

    def lines(count):
        return array(count, depth)

    def params(mib):
        return pltpu.CompilerParams(vmem_limit_bytes=mib * 2**20)

    def cost(size):
        return pl.CostEstimate(flops=size, bytes_accessed=size, transcendentals=0)

    with jax.named_scope("pack_y"):
        e0, h0, coef, z_up, z_down = pl.pallas_call(
            functools.partial(pack_y_kernel, plan),
            out_shape=(
                array(12, wide, ring, depth),
                array(12, wide, ring, depth),
                array(wide, ring, depth),
                lines(len(plan.y_low) * nx),
                lines(len(plan.y_high) * nx),
            ),
            in_specs=[HBM] * 3,
            out_specs=[VMEM] * 5,
            scratch_shapes=[pltpu.SemaphoreType.DMA((25,))],
            compiler_params=params(16),
        )(*(pltpu.with_memory_space_constraint(array, pltpu.HBM) for array in (forward_fields[0], adjoint_fields[0], permittivity)))
    e0, h0, coef = (state.reshape((-1, depth)) for state in (e0, h0, coef))
    with jax.named_scope("send_y"):
        z_low = lax.ppermute(z_up, "gy", ring_pairs("gy", 1))
        z_high = lax.ppermute(z_down, "gy", ring_pairs("gy", -1))
    with jax.named_scope("pack_x"):
        x_up, x_down = pl.pallas_call(
            functools.partial(pack_x_kernel, plan),
            out_shape=(lines(len(plan.x_low) * ny), lines(len(plan.x_high) * ny)),
            in_specs=[VMEM] * 3,
            out_specs=[VMEM] * 2,
            compiler_params=params(8),
            cost_estimate=cost(40 * 2**20),
        )(e0, h0, coef)
    with jax.named_scope("send_x"):
        x_low = lax.ppermute(x_up, "gx", ring_pairs("gx", 1))
        x_high = lax.ppermute(x_down, "gx", ring_pairs("gx", -1))
    with jax.named_scope("turns"):
        turns = pl.pallas_call(
            functools.partial(turns_kernel, groups),
            out_shape=lines(3 * SUB),
            in_specs=[SMEM] * 3,
            out_specs=VMEM,
            compiler_params=params(4),
        )(phase_table, angle_index, design_tiles)
    with jax.named_scope("relay_corners"):
        c_up, c_down = pl.pallas_call(
            functools.partial(corner_kernel, plan),
            out_shape=(lines(-(-len(plan.corner_low) // SUB) * SUB), lines(-(-len(plan.corner_high) // SUB) * SUB)),
            in_specs=[VMEM] * 2,
            out_specs=[VMEM] * 2,
            compiler_params=params(4),
        )(z_low, z_high)
        c_low = lax.ppermute(c_up, "gx", ring_pairs("gx", 1))
        c_high = lax.ppermute(c_down, "gx", ring_pairs("gx", -1))
    level = lines(12 * wide * ring)
    count = 2 * STEPS + 3
    levels = [level] * (count - 1) + [lines(wide * ring)]
    with jax.named_scope("middle"):
        state = pl.pallas_call(
            functools.partial(middle_kernel, plan),
            out_shape=levels,
            in_specs=[VMEM] * 6,
            out_specs=[VMEM] * count,
            input_output_aliases={0: 0, 1: STEPS + 1, 2: count - 1},
            compiler_params=params(8),
            cost_estimate=cost(2**32),
        )(e0, h0, coef, z_low, z_high, turns)
    with jax.named_scope("edges"):
        spectra = [spectrum.reshape((-1, depth)) for spectrum in (forward_spectrum, adjoint_spectrum)]
        *_, tr_f, tr_a, parts = pl.pallas_call(
            functools.partial(edges_kernel, plan, groups),
            out_shape=[*levels, lines(6 * nx * ny), lines(6 * nx * ny), array(groups, nx * ny, depth // groups)],
            in_specs=[VMEM] * (count + 7),
            out_specs=[VMEM] * (count + 3),
            input_output_aliases={i: i for i in range(count)},
            compiler_params=params(8),
        )(*state, x_low, x_high, c_low, c_high, turns, *spectra)
    with jax.named_scope("sum_angles"):
        gradient = parts[0]
        for k in range(1, groups):
            gradient = gradient + lax.ppermute(parts[k], "angle", ring_pairs("angle", k))
    with jax.named_scope("write"):
        out_f, out_a = pl.pallas_call(
            write_kernel,
            out_shape=[array(6, nx, ny, depth)] * 2,
            in_specs=[VMEM] * 2,
            out_specs=[HBM] * 2,
            scratch_shapes=[pltpu.SemaphoreType.DMA((12,))],
            compiler_params=params(4),
        )(tr_f.reshape((6, nx, ny, depth)), tr_a.reshape((6, nx, ny, depth)))
    return (
        out_f.reshape(forward_spectrum.shape),
        out_a.reshape(adjoint_spectrum.shape),
        gradient.reshape((nx, ny, depth // groups)),
    )


def solution(mesh):
    in_specs = (
        P("angle", None, "gx", "gy", None),
        P("angle", None, "gx", "gy", None),
        P("angle", None, "gx", "gy", None),
        P("angle", None, "gx", "gy", None),
        P("gx", "gy", None),
        P(),
        P("angle"),
        P(),
    )
    out_specs = (
        P("angle", None, "gx", "gy", None),
        P("angle", None, "gx", "gy", None),
        P("gx", "gy", "angle"),
    )
    return jax.shard_map(shards, mesh=mesh, in_specs=in_specs, out_specs=out_specs, check_vma=False)
```

```python
import functools
import math

import jax
import jax.numpy as jnp
from jax import lax
from jax.experimental import pallas as pl
from jax.experimental.pallas import tpu as pltpu
from jax.sharding import PartitionSpec as P

STEPS = 3
SUB = 8

courant = 0.5
omega_step = 0.7

VMEM = pl.BlockSpec(memory_space=pltpu.VMEM)
SMEM = pl.BlockSpec(memory_space=pltpu.SMEM)
HBM = pl.BlockSpec(memory_space=pltpu.HBM)


def reads(node):
    kind, level, comp, x, y = node
    others = [c for c in range(3) if c != comp]
    if kind == "E":
        found = [("E", level - 1, comp, x, y), ("C", 0, 0, x, y)] + [("H", level, c, x, y) for c in others]
        if comp != 1:
            found.append(("H", level, 2 - comp, x, y - 1))
        if comp != 0:
            found.append(("H", level, 3 - comp, x - 1, y))
        return found
    found = [("H", level - 1, comp, x, y)] + [("E", level - 1, c, x, y) for c in others]
    if comp != 1:
        found.append(("E", level - 1, 2 - comp, x, y + 1))
    if comp != 0:
        found.append(("E", level - 1, 3 - comp, x + 1, y))
    return found


def wanted(nx, ny):
    def block(node):
        return node[3] // nx, node[4] // ny

    @functools.cache
    def alone(node):
        if node[1] == 0:
            return True
        return node[1] == 1 and all(block(other) == block(node) and alone(other) for other in reads(node))

    found, seen = set(), set()
    todo = [("E", STEPS, comp, x, y) for comp in range(3) for x in range(nx) for y in range(ny)]
    while todo:
        node = todo.pop()
        if node in seen:
            continue
        seen.add(node)
        if block(node) != (0, 0) and alone(node):
            found.add(node)
        elif node[1]:
            todo += reads(node)
    return found


class Message:
    def __init__(self, nodes, axis):
        self.axis, self.runs, self.at, self.size = axis, [], {}, 0
        stretches = []
        for node in sorted(nodes):
            before = list(node)
            before[3 + axis] -= 1
            if tuple(before) in nodes:
                continue
            count = 1
            while (*node[:3], node[3] + count * (axis == 0), node[4] + count * (axis == 1)) in nodes:
                count += 1
            stretches.append((count, node))
        for count, (kind, level, comp, x, y) in sorted(stretches, key=lambda item: (-item[0], item[1])):
            for run in (0, 1) if kind != "C" else (0,):
                for part in (0, 1) if kind != "C" else (0,):
                    what = (kind, level, comp, run, part)
                    self.runs.append((what, x, y, count, self.size))
                    for i in range(count):
                        self.at[what, x + i * (axis == 0), y + i * (axis == 1)] = self.size + i
                    self.size += count
        self.lines = -(-self.size // SUB) * SUB


class Plan:
    def __init__(self, nx, ny):
        self.nx, self.ny = nx, ny
        self.wide, self.ring = nx + 2 * STEPS, ny + SUB
        nodes = wanted(nx, ny)
        sides = {}
        for node in nodes:
            sides.setdefault((node[3] // nx, node[4] // ny), set()).add(node)

        def shifted(found, dx):
            return {(*node[:3], node[3] + dx, node[4]) for node in found}

        self.x_low, self.x_high = Message(sides[-1, 0], 1), Message(sides[1, 0], 1)
        self.y_low, self.y_high = (
            Message(sides[0, side] | shifted(sides[-1, side], nx) | shifted(sides[1, side], -nx), 0) for side in (-1, 1)
        )
        self.corner_low, self.corner_high = (Message(sides[side, -1] | sides[side, 1], 1) for side in (-1, 1))

    def row(self, x, y, run=0, part=0, comp=0):
        return ((run * 6 + part * 3 + comp) * self.wide + x + STEPS) * self.ring + y % self.ring

    def rows(self, what, x, y, axis, count):
        _, _, comp, run, part = what
        start = self.row(x, y, run, part, comp)
        return pl.ds(start, count, stride=self.ring) if axis == 0 and count > 1 else pl.ds(start, count)


class State:
    def __init__(self, efield, hfield, coef):
        self.by_kind = {"E": efield, "H": hfield, "C": [coef]}

    def __call__(self, what):
        return self.by_kind[what[0]][what[1]]


def pack(plan, message, state, dx, dy, out):
    for what, x, y, count, at in message.runs:
        out[pl.ds(at, count), :] = state(what)[plan.rows(what, x + dx, y + dy, message.axis, count), :]


def pack_y_kernel(plan, fwd, adj, eps, e0, h0, e1, h1, coef, z_up, z_down, sems):
    nx, ny = plan.nx, plan.ny
    own = (pl.ds(STEPS, nx), pl.ds(0, ny), slice(None))
    copies = []
    for run, ref in enumerate((fwd, adj)):
        for kind, array in enumerate((e0, h0)):
            for i in range(6):
                copies.append(
                    pltpu.make_async_copy(ref.at[kind * 6 + i], array.at[(run * 6 + i, *own)], sems.at[len(copies)])
                )
    copies.append(pltpu.make_async_copy(eps, coef.at[own], sems.at[len(copies)]))
    for copy in copies:
        copy.start()
    for copy in copies:
        copy.wait()
    for x in range(nx):
        coef[STEPS + x, pl.ds(0, ny), :] = (0.5 * courant) / coef[STEPS + x, pl.ds(0, ny), :]
    e0, h0, e1, h1, coef = (array.reshape((-1, array.shape[-1])) for array in (e0, h0, e1, h1, coef))
    Sweeps(plan, [e0, e1], [h0, h1], coef, ny).both(1, range(nx), range(nx - 1))
    state = State([e0, e1], [h0, h1], coef)
    pack(plan, plan.y_low, state, 0, ny, z_up)
    pack(plan, plan.y_high, state, 0, -ny, z_down)


def pack_x_kernel(plan, e0, h0, e1, h1, coef, x_up, x_down):
    state = State([e0, e1], [h0, h1], coef)
    pack(plan, plan.x_low, state, plan.nx, 0, x_up)
    pack(plan, plan.x_high, state, -plan.nx, 0, x_down)


def turns_kernel(groups, table, index, tiles, turns):
    row = index[0]
    phi_x, phi_y = table[row, 0], table[row, 1]
    at_x, at_y = lax.axis_index("gx"), lax.axis_index("gy")
    none = jnp.float32(0.0)
    ax_low = jnp.where(at_x == 0, -phi_x, none)
    ax_high = jnp.where(at_x == lax.axis_size("gx") - 1, phi_x, none)
    ay_low = jnp.where(at_y == 0, -phi_y, none)
    ay_high = jnp.where(at_y == lax.axis_size("gy") - 1, phi_y, none)
    sub = lax.broadcasted_iota(jnp.int32, (SUB, turns.shape[1]), 0)
    angles = jnp.zeros(sub.shape, jnp.float32)
    for i, angle in enumerate((ax_low, ax_high, ay_low, ay_high, ax_low + ay_low, ax_low + ay_high,
                               ax_high + ay_low, ax_high + ay_high)):
        angles = jnp.where(sub == i, angle, angles)
    turns[pl.ds(0, SUB), :] = jnp.cos(angles)
    turns[pl.ds(SUB, SUB), :] = jnp.sin(angles)
    own_tile = at_x * lax.axis_size("gy") + at_y
    chosen = tiles[0] == own_tile
    for i in range(1, tiles.shape[0]):
        chosen = jnp.logical_or(chosen, tiles[i] == own_tile)
    weight = jnp.where(chosen, jnp.float32(1.0 / groups), none)
    turns[pl.ds(2 * SUB, SUB), :] = jnp.full(sub.shape, weight, jnp.float32)


def corner_kernel(plan, z_low, z_high, c_up, c_down):
    for message, dx, out in ((plan.corner_low, plan.nx, c_up), (plan.corner_high, -plan.nx, c_down)):
        for (what, x, y), row in message.at.items():
            ref, source = (z_low, plan.y_low) if y < 0 else (z_high, plan.y_high)
            out[pl.ds(row, 1), :] = ref[pl.ds(source.at[what, x + dx, y], 1), :]


def turned(real, imag, cosine, sine):
    return real * cosine - imag * sine, real * sine + imag * cosine


def unpack(plan, message, ref, which, turns, state, kinds, level, layers=None):
    axis = message.axis
    for (kind, at_level, comp, run, part), x, y, count, at in message.runs:
        if kind not in kinds or at_level != level or part == 1:
            continue
        pieces = [(x, y, count, at)]
        if layers is not None:
            pieces = [(x + i, y, 1, at + i) for i in range(count) if x + i in layers]
        for cell_x, cell_y, size, row in pieces:
            what = (kind, at_level, comp, run, 0)
            real = ref[pl.ds(row, size), :]
            if kind == "C":
                state(what)[plan.rows(what, cell_x, cell_y, axis, size), :] = real
                continue
            twin = (kind, at_level, comp, run, 1)
            imag = ref[pl.ds(message.at[twin, cell_x, cell_y], size), :]
            turn = which(y)
            cosine, sine = turns[pl.ds(turn, 1), :], turns[pl.ds(SUB + turn, 1), :]
            real, imag = turned(real, imag, cosine, sine if run == 0 else -sine)
            state(what)[plan.rows(what, cell_x, cell_y, axis, size), :] = real
            state(twin)[plan.rows(twin, cell_x, cell_y, axis, size), :] = imag


class Sweeps:
    def __init__(self, plan, efield, hfield, coef, height):
        self.plan, self.efield, self.hfield, self.coef, self.height = plan, efield, hfield, coef, height
        lane = lax.broadcasted_iota(jnp.int32, (height, coef.shape[1]), 1)
        self.first, self.last = lane == 0, lane == coef.shape[1] - 1

    def rows(self, group, comp, x):
        plan = self.plan
        start = (group * 3 + comp) * plan.wide * plan.ring + (x + STEPS) * plan.ring
        return pl.ds(start if isinstance(start, int) else pl.multiple_of(start, SUB), self.height)

    def next_z(self, value):
        return jnp.where(self.last, 0.0, pltpu.roll(value, value.shape[1] - 1, 1))

    def prev_z(self, value):
        return jnp.where(self.first, 0.0, pltpu.roll(value, 1, 1))

    def next_y(self, value):
        return pltpu.roll(value, self.height - 1, 0)

    def prev_y(self, value):
        return pltpu.roll(value, 1, 0)

    def update_h(self, step, group, x):
        efield, old, new = self.efield[step - 1], self.hfield[step - 1], self.hfield[step]
        ex, ey, ez = (efield[self.rows(group, comp, x), :] for comp in range(3))
        ey_x, ez_x = (efield[self.rows(group, comp, x + 1), :] for comp in (1, 2))
        hx, hy, hz = (old[self.rows(group, comp, x), :] for comp in range(3))
        if step == 1:
            hx, hy, hz = hx + hx, hy + hy, hz + hz
        new[self.rows(group, 0, x), :] = hx - ((self.next_y(ez) - ez) - (self.next_z(ey) - ey))
        new[self.rows(group, 1, x), :] = hy - ((self.next_z(ex) - ex) - (ez_x - ez))
        new[self.rows(group, 2, x), :] = hz - ((ey_x - ey) - (self.next_y(ex) - ex))

    def update_e(self, step, group, x):
        old, new, hfield = self.efield[step - 1], self.efield[step], self.hfield[step]
        ex, ey, ez = (old[self.rows(group, comp, x), :] for comp in range(3))
        hx, hy, hz = (hfield[self.rows(group, comp, x), :] for comp in range(3))
        hy_x, hz_x = (hfield[self.rows(group, comp, x - 1), :] for comp in (1, 2))
        scale = self.coef[self.rows(0, 0, x), :]
        new[self.rows(group, 0, x), :] = ex + scale * ((hz - self.prev_y(hz)) - (hy - self.prev_z(hy)))
        new[self.rows(group, 1, x), :] = ey + scale * ((hx - self.prev_z(hx)) - (hz - hz_x))
        new[self.rows(group, 2, x), :] = ez + scale * ((hy - hy_x) - (hx - self.prev_y(hx)))

    def both(self, step, h_layers, e_layers, after_h=None, after_e=None):
        for update, layers, after in ((self.update_h, h_layers, after_h), (self.update_e, e_layers, after_e)):

            @pl.loop(0, 2)
            def _(run):
                for part in (0, 1):
                    for x in layers:
                        update(step, run * 2 + part, x)

            if after is not None:
                after()


def middle_kernel(plan, e0_in, h0_in, e1_in, h1_in, coef_in, z_low, z_high, turns, *arrays):
    nx = plan.nx
    efield, hfield, coef = arrays[: STEPS + 1], arrays[STEPS + 1 : 2 * STEPS + 2], arrays[-1]
    state = State(efield, hfield, coef)

    def take(kinds, level):
        unpack(plan, plan.y_low, z_low, lambda y: 2, turns, state, kinds, level)
        unpack(plan, plan.y_high, z_high, lambda y: 3, turns, state, kinds, level)

    take("EHC", 0)
    sweeps = Sweeps(plan, efield, hfield, coef, plan.ring)
    for step in range(1, STEPS + 1):
        after = [lambda: take("H", 1), lambda: take("E", 1)] if step == 1 else []
        sweeps.both(step, range(step - 1, nx - step), range(step, nx - step), *after)


def edges_kernel(plan, groups, *refs):
    nx, ny = plan.nx, plan.ny
    count = 2 * STEPS + 3
    x_low, x_high, c_low, c_high, z_low, z_high, turns, spec_f, spec_a = refs[count : count + 9]
    arrays = refs[count + 9 : 2 * count + 9]
    out_f, out_a, parts = refs[2 * count + 9 :]
    efield, hfield, coef = arrays[: STEPS + 1], arrays[STEPS + 1 : 2 * STEPS + 2], arrays[-1]
    state = State(efield, hfield, coef)

    def take(kinds, level, layers=()):
        unpack(plan, plan.x_low, x_low, lambda y: 0, turns, state, kinds, level)
        unpack(plan, plan.x_high, x_high, lambda y: 1, turns, state, kinds, level)
        unpack(plan, plan.corner_low, c_low, lambda y: 4 + (y >= 0), turns, state, kinds, level)
        unpack(plan, plan.corner_high, c_high, lambda y: 6 + (y >= 0), turns, state, kinds, level)
        unpack(plan, plan.y_low, z_low, lambda y: 2, turns, state, kinds, level, layers)
        unpack(plan, plan.y_high, z_high, lambda y: 3, turns, state, kinds, level, layers)

    take("EHC", 0)
    sweeps = Sweeps(plan, efield, hfield, coef, plan.ring)
    for step in range(1, STEPS + 1):
        low, high = step - STEPS, nx - step
        h_layers = [*range(low - 1, step - 1), *range(high, nx + STEPS - step)]
        e_layers = [*range(low, step), *range(high, nx + STEPS - step)]
        after = []
        if step == 1:
            after = [functools.partial(take, "H", 1, h_layers), functools.partial(take, "E", 1, e_layers)]
        sweeps.both(step, h_layers, e_layers, *after)

    share = parts.shape[2]
    shift = lax.rem(groups - lax.axis_index("angle"), groups) * share
    weight = turns[pl.ds(2 * SUB, SUB), :]
    tiles = ny // SUB

    @pl.loop(0, nx * tiles)
    def _(i):
        x, tile = i // tiles, lax.rem(i, tiles)
        total = jnp.zeros(weight.shape, jnp.float32)
        for comp in range(3):
            ends = []
            for run, (spec, out) in enumerate(((spec_f, out_f), (spec_a, out_a))):
                at = [pl.ds(pl.multiple_of(((part * 3 + comp) * nx + x) * ny + tile * SUB, SUB), SUB) for part in (0, 1)]
                real, imag = spec[at[0], :], spec[at[1], :]
                for step in range(1, STEPS + 1):
                    theta = omega_step * step
                    ends_e = [
                        efield[step][pl.ds(pl.multiple_of(plan.row(x, 0, run, part, comp) + tile * SUB, SUB), SUB), :]
                        for part in (0, 1)
                    ]
                    more = turned(*ends_e, math.cos(theta), math.sin(theta))
                    real, imag = real + more[0], imag + more[1]
                out[at[0], :], out[at[1], :] = real, imag
                ends.append((real, imag))
            total = total + (ends[0][0] * ends[1][0] - ends[0][1] * ends[1][1])
        total = pltpu.roll(total * weight, shift, 1)
        for k in range(groups):
            parts[k, pl.ds(pl.multiple_of(i * SUB, SUB), SUB), :] = total[:, k * share : (k + 1) * share]


def write_kernel(tr_f, tr_a, out_f, out_a, sems):
    copies = []
    for source, target in ((tr_f, out_f), (tr_a, out_a)):
        for i in range(source.shape[0]):
            copies.append(pltpu.make_async_copy(source.at[i], target.at[i], sems.at[len(copies)]))
    for copy in copies:
        copy.start()
    for copy in copies:
        copy.wait()


def ring_pairs(axis, offset):
    size = lax.axis_size(axis)
    return [(i, (i + offset) % size) for i in range(size)]


def shards(
    forward_fields,
    adjoint_fields,
    forward_spectrum,
    adjoint_spectrum,
    permittivity,
    phase_table,
    angle_index,
    design_tiles,
):
    nx, ny, depth = permittivity.shape
    plan = Plan(nx, ny)
    groups = lax.axis_size("angle")
    wide, ring = plan.wide, plan.ring

    def array(*shape):
        return jax.ShapeDtypeStruct(shape, jnp.float32)

    def lines(count):
        return array(count, depth)

    def params(mib):
        return pltpu.CompilerParams(vmem_limit_bytes=mib * 2**20)

    def cost(size):
        return pl.CostEstimate(flops=size, bytes_accessed=size, transcendentals=0)

    with jax.named_scope("pack_y"):
        *first, coef, z_up, z_down = pl.pallas_call(
            functools.partial(pack_y_kernel, plan),
            out_shape=(
                *[array(12, wide, ring, depth)] * 4,
                array(wide, ring, depth),
                lines(plan.y_low.lines),
                lines(plan.y_high.lines),
            ),
            in_specs=[HBM] * 3,
            out_specs=[VMEM] * 7,
            scratch_shapes=[pltpu.SemaphoreType.DMA((25,))],
            compiler_params=params(8),
        )(*(pltpu.with_memory_space_constraint(array, pltpu.HBM) for array in (forward_fields[0], adjoint_fields[0], permittivity)))
    e0, h0, e1, h1, coef = (state.reshape((-1, depth)) for state in (*first, coef))
    with jax.named_scope("send_y"):
        z_low = lax.ppermute(z_up, "gy", ring_pairs("gy", 1))
        z_high = lax.ppermute(z_down, "gy", ring_pairs("gy", -1))
    with jax.named_scope("pack_x"):
        x_up, x_down = pl.pallas_call(
            functools.partial(pack_x_kernel, plan),
            out_shape=(lines(plan.x_low.lines), lines(plan.x_high.lines)),
            in_specs=[VMEM] * 5,
            out_specs=[VMEM] * 2,
            compiler_params=params(8),
            cost_estimate=cost(40 * 2**20),
        )(e0, h0, e1, h1, coef)
    with jax.named_scope("send_x"):
        x_low = lax.ppermute(x_up, "gx", ring_pairs("gx", 1))
        x_high = lax.ppermute(x_down, "gx", ring_pairs("gx", -1))
    with jax.named_scope("turns"):
        turns = pl.pallas_call(
            functools.partial(turns_kernel, groups),
            out_shape=lines(3 * SUB),
            in_specs=[SMEM] * 3,
            out_specs=VMEM,
            compiler_params=params(4),
        )(phase_table, angle_index, design_tiles)
    with jax.named_scope("relay_corners"):
        c_up, c_down = pl.pallas_call(
            functools.partial(corner_kernel, plan),
            out_shape=(lines(plan.corner_low.lines), lines(plan.corner_high.lines)),
            in_specs=[VMEM] * 2,
            out_specs=[VMEM] * 2,
            compiler_params=params(4),
        )(z_low, z_high)
        c_low = lax.ppermute(c_up, "gx", ring_pairs("gx", 1))
        c_high = lax.ppermute(c_down, "gx", ring_pairs("gx", -1))
    level = lines(12 * wide * ring)
    count = 2 * STEPS + 3
    levels = [level] * (count - 1) + [lines(wide * ring)]
    with jax.named_scope("middle"):
        state = pl.pallas_call(
            functools.partial(middle_kernel, plan),
            out_shape=levels,
            in_specs=[VMEM] * 8,
            out_specs=[VMEM] * count,
            input_output_aliases={0: 0, 1: STEPS + 1, 2: 1, 3: STEPS + 2, 4: count - 1},
            compiler_params=params(8),
            cost_estimate=cost(2**32),
        )(e0, h0, e1, h1, coef, z_low, z_high, turns)
    with jax.named_scope("edges"):
        spectra = [spectrum.reshape((-1, depth)) for spectrum in (forward_spectrum, adjoint_spectrum)]
        *_, tr_f, tr_a, parts = pl.pallas_call(
            functools.partial(edges_kernel, plan, groups),
            out_shape=[*levels, lines(6 * nx * ny), lines(6 * nx * ny), array(groups, nx * ny, depth // groups)],
            in_specs=[VMEM] * (count + 9),
            out_specs=[VMEM] * (count + 3),
            input_output_aliases={i: i for i in range(count)},
            compiler_params=params(8),
        )(*state, x_low, x_high, c_low, c_high, z_low, z_high, turns, *spectra)
    with jax.named_scope("sum_angles"):
        gradient = parts[0]
        for k in range(1, groups):
            gradient = gradient + lax.ppermute(parts[k], "angle", ring_pairs("angle", k))
    with jax.named_scope("write"):
        out_f, out_a = pl.pallas_call(
            write_kernel,
            out_shape=[array(6, nx, ny, depth)] * 2,
            in_specs=[VMEM] * 2,
            out_specs=[HBM] * 2,
            scratch_shapes=[pltpu.SemaphoreType.DMA((12,))],
            compiler_params=params(4),
        )(tr_f.reshape((6, nx, ny, depth)), tr_a.reshape((6, nx, ny, depth)))
    return (
        out_f.reshape(forward_spectrum.shape),
        out_a.reshape(adjoint_spectrum.shape),
        gradient.reshape((nx, ny, depth // groups)),
    )


def solution(mesh):
    in_specs = (
        P("angle", None, "gx", "gy", None),
        P("angle", None, "gx", "gy", None),
        P("angle", None, "gx", "gy", None),
        P("angle", None, "gx", "gy", None),
        P("gx", "gy", None),
        P(),
        P("angle"),
        P(),
    )
    out_specs = (
        P("angle", None, "gx", "gy", None),
        P("angle", None, "gx", "gy", None),
        P("gx", "gy", "angle"),
    )
    return jax.shard_map(shards, mesh=mesh, in_specs=in_specs, out_specs=out_specs, check_vma=False)
```

```python
import functools
import math

import jax
import jax.numpy as jnp
from jax import lax
from jax.experimental import pallas as pl
from jax.experimental.pallas import tpu as pltpu
from jax.sharding import PartitionSpec as P

STEPS = 3
SUB = 8

courant = 0.5
omega_step = 0.7

VMEM = pl.BlockSpec(memory_space=pltpu.VMEM)
SMEM = pl.BlockSpec(memory_space=pltpu.SMEM)
HBM = pl.BlockSpec(memory_space=pltpu.HBM)


def reads(node):
    kind, level, comp, x, y = node
    others = [c for c in range(3) if c != comp]
    if kind == "E":
        found = [("E", level - 1, comp, x, y), ("C", 0, 0, x, y)] + [("H", level, c, x, y) for c in others]
        if comp != 1:
            found.append(("H", level, 2 - comp, x, y - 1))
        if comp != 0:
            found.append(("H", level, 3 - comp, x - 1, y))
        return found
    found = [("H", level - 1, comp, x, y)] + [("E", level - 1, c, x, y) for c in others]
    if comp != 1:
        found.append(("E", level - 1, 2 - comp, x, y + 1))
    if comp != 0:
        found.append(("E", level - 1, 3 - comp, x + 1, y))
    return found


def wanted(nx, ny):
    def block(node):
        return node[3] // nx, node[4] // ny

    @functools.cache
    def alone(node):
        if node[1] == 0:
            return True
        return node[1] == 1 and all(block(other) == block(node) and alone(other) for other in reads(node))

    found, seen = set(), set()
    todo = [("E", STEPS, comp, x, y) for comp in range(3) for x in range(nx) for y in range(ny)]
    while todo:
        node = todo.pop()
        if node in seen:
            continue
        seen.add(node)
        if block(node) != (0, 0) and alone(node):
            found.add(node)
        elif node[1]:
            todo += reads(node)
    return found


class Message:
    def __init__(self, nodes, axis):
        self.axis, self.runs, self.at, self.size = axis, [], {}, 0
        stretches = []
        for node in sorted(nodes):
            before = list(node)
            before[3 + axis] -= 1
            if tuple(before) in nodes:
                continue
            count = 1
            while (*node[:3], node[3] + count * (axis == 0), node[4] + count * (axis == 1)) in nodes:
                count += 1
            stretches.append((count, node))
        for count, (kind, level, comp, x, y) in sorted(stretches, key=lambda item: (-item[0], item[1])):
            for run in (0, 1) if kind != "C" else (0,):
                for part in (0, 1) if kind != "C" else (0,):
                    what = (kind, level, comp, run, part)
                    self.runs.append((what, x, y, count, self.size))
                    for i in range(count):
                        self.at[what, x + i * (axis == 0), y + i * (axis == 1)] = self.size + i
                    self.size += count
        self.lines = -(-self.size // SUB) * SUB


class Plan:
    def __init__(self, nx, ny):
        self.nx, self.ny = nx, ny
        self.wide, self.ring = nx + 2 * STEPS, ny + SUB
        nodes = wanted(nx, ny)
        sides = {}
        for node in nodes:
            sides.setdefault((node[3] // nx, node[4] // ny), set()).add(node)

        def shifted(found, dx):
            return {(*node[:3], node[3] + dx, node[4]) for node in found}

        self.x_low, self.x_high = Message(sides[-1, 0], 1), Message(sides[1, 0], 1)
        self.y_low, self.y_high = (
            Message(sides[0, side] | shifted(sides[-1, side], nx) | shifted(sides[1, side], -nx), 0) for side in (-1, 1)
        )
        self.corner_low, self.corner_high = (Message(sides[side, -1] | sides[side, 1], 1) for side in (-1, 1))

    def row(self, x, y, run=0, part=0, comp=0):
        return ((run * 6 + part * 3 + comp) * self.wide + x + STEPS) * self.ring + y % self.ring

    def rows(self, what, x, y, axis, count):
        _, _, comp, run, part = what
        start = self.row(x, y, run, part, comp)
        return pl.ds(start, count, stride=self.ring) if axis == 0 and count > 1 else pl.ds(start, count)


class State:
    def __init__(self, efield, hfield, coef):
        self.by_kind = {"E": efield, "H": hfield, "C": [coef]}

    def __call__(self, what):
        return self.by_kind[what[0]][what[1]]


def pack(plan, message, state, dx, dy, out):
    for what, x, y, count, at in message.runs:
        out[pl.ds(at, count), :] = state(what)[plan.rows(what, x + dx, y + dy, message.axis, count), :]


def pack_y_kernel(plan, fwd, adj, eps, e0, h0, e1, h1, coef, z_up, z_down, sems):
    nx, ny = plan.nx, plan.ny
    own = (pl.ds(STEPS, nx), pl.ds(0, ny), slice(None))
    copies = [pltpu.make_async_copy(eps, coef.at[own], sems.at[0])]
    for run, ref in enumerate((fwd, adj)):
        for kind, array in enumerate((e0, h0)):
            for i in range(6):
                copies.append(
                    pltpu.make_async_copy(ref.at[kind * 6 + i], array.at[(run * 6 + i, *own)], sems.at[len(copies)])
                )
    for copy in copies:
        copy.start()
    copies[0].wait()
    for x in range(nx):
        coef[STEPS + x, pl.ds(0, ny), :] = (0.5 * courant) / coef[STEPS + x, pl.ds(0, ny), :]
    e0, h0, e1, h1, coef = (array.reshape((-1, array.shape[-1])) for array in (e0, h0, e1, h1, coef))
    sweeps = Sweeps(plan, [e0, e1], [h0, h1], coef, ny)
    for run in (0, 1):
        for copy in copies[1 + 12 * run : 13 + 12 * run]:
            copy.wait()
        sweeps.both(1, range(nx), range(nx - 1), runs=(run,))
    state = State([e0, e1], [h0, h1], coef)
    pack(plan, plan.y_low, state, 0, ny, z_up)
    pack(plan, plan.y_high, state, 0, -ny, z_down)


def pack_x_kernel(plan, e0, h0, e1, h1, coef, x_up, x_down):
    state = State([e0, e1], [h0, h1], coef)
    pack(plan, plan.x_low, state, plan.nx, 0, x_up)
    pack(plan, plan.x_high, state, -plan.nx, 0, x_down)


def turns_kernel(groups, table, index, tiles, turns):
    row = index[0]
    phi_x, phi_y = table[row, 0], table[row, 1]
    at_x, at_y = lax.axis_index("gx"), lax.axis_index("gy")
    none = jnp.float32(0.0)
    ax_low = jnp.where(at_x == 0, -phi_x, none)
    ax_high = jnp.where(at_x == lax.axis_size("gx") - 1, phi_x, none)
    ay_low = jnp.where(at_y == 0, -phi_y, none)
    ay_high = jnp.where(at_y == lax.axis_size("gy") - 1, phi_y, none)
    sub = lax.broadcasted_iota(jnp.int32, (SUB, turns.shape[1]), 0)
    angles = jnp.zeros(sub.shape, jnp.float32)
    for i, angle in enumerate((ax_low, ax_high, ay_low, ay_high, ax_low + ay_low, ax_low + ay_high,
                               ax_high + ay_low, ax_high + ay_high)):
        angles = jnp.where(sub == i, angle, angles)
    turns[pl.ds(0, SUB), :] = jnp.cos(angles)
    turns[pl.ds(SUB, SUB), :] = jnp.sin(angles)
    own_tile = at_x * lax.axis_size("gy") + at_y
    chosen = tiles[0] == own_tile
    for i in range(1, tiles.shape[0]):
        chosen = jnp.logical_or(chosen, tiles[i] == own_tile)
    weight = jnp.where(chosen, jnp.float32(1.0 / groups), none)
    turns[pl.ds(2 * SUB, SUB), :] = jnp.full(sub.shape, weight, jnp.float32)


def corner_kernel(plan, z_low, z_high, c_up, c_down):
    for message, dx, out in ((plan.corner_low, plan.nx, c_up), (plan.corner_high, -plan.nx, c_down)):
        for (what, x, y), row in message.at.items():
            ref, source = (z_low, plan.y_low) if y < 0 else (z_high, plan.y_high)
            out[pl.ds(row, 1), :] = ref[pl.ds(source.at[what, x + dx, y], 1), :]


def turned(real, imag, cosine, sine):
    return real * cosine - imag * sine, real * sine + imag * cosine


def unpack(plan, message, ref, which, turns, state, kinds, level, layers=None):
    axis = message.axis
    for (kind, at_level, comp, run, part), x, y, count, at in message.runs:
        if kind not in kinds or at_level != level or part == 1:
            continue
        pieces = [(x, y, count, at)]
        if layers is not None:
            pieces = [(x + i, y, 1, at + i) for i in range(count) if x + i in layers]
        for cell_x, cell_y, size, row in pieces:
            what = (kind, at_level, comp, run, 0)
            real = ref[pl.ds(row, size), :]
            if kind == "C":
                state(what)[plan.rows(what, cell_x, cell_y, axis, size), :] = real
                continue
            twin = (kind, at_level, comp, run, 1)
            imag = ref[pl.ds(message.at[twin, cell_x, cell_y], size), :]
            turn = which(y)
            cosine, sine = turns[pl.ds(turn, 1), :], turns[pl.ds(SUB + turn, 1), :]
            real, imag = turned(real, imag, cosine, sine if run == 0 else -sine)
            state(what)[plan.rows(what, cell_x, cell_y, axis, size), :] = real
            state(twin)[plan.rows(twin, cell_x, cell_y, axis, size), :] = imag


class Sweeps:
    def __init__(self, plan, efield, hfield, coef, height):
        self.plan, self.efield, self.hfield, self.coef, self.height = plan, efield, hfield, coef, height

    def rows(self, run, part, comp, x, height=None):
        return pl.ds(self.plan.row(x, 0, run, part, comp), height or self.height)

    def next_z(self, value):
        lane = lax.broadcasted_iota(jnp.int32, value.shape, 1)
        return jnp.where(lane == value.shape[1] - 1, 0.0, pltpu.roll(value, value.shape[1] - 1, 1))

    def prev_z(self, value):
        lane = lax.broadcasted_iota(jnp.int32, value.shape, 1)
        return jnp.where(lane == 0, 0.0, pltpu.roll(value, 1, 1))

    def next_y(self, value):
        return pltpu.roll(value, self.height - 1, 0)

    def prev_y(self, value):
        return pltpu.roll(value, 1, 0)

    def update_h(self, step, run, part, x):
        efield, old, new = self.efield[step - 1], self.hfield[step - 1], self.hfield[step]
        ex, ey, ez = (efield[self.rows(run, part, comp, x), :] for comp in range(3))
        ey_x, ez_x = (efield[self.rows(run, part, comp, x + 1), :] for comp in (1, 2))
        hx, hy, hz = (old[self.rows(run, part, comp, x), :] for comp in range(3))
        if step == 1:
            hx, hy, hz = hx + hx, hy + hy, hz + hz
        new[self.rows(run, part, 0, x), :] = hx - ((self.next_y(ez) - ez) - (self.next_z(ey) - ey))
        new[self.rows(run, part, 2, x), :] = hz - ((ey_x - ey) - (self.next_y(ex) - ex))
        height = self.last_height(step)
        ex, ez, ez_x, hy = (value[:height] for value in (ex, ez, ez_x, hy))
        new[self.rows(run, part, 1, x, height), :] = hy - ((self.next_z(ex) - ex) - (ez_x - ez))

    def update_e(self, step, run, part, x):
        old, new, hfield = self.efield[step - 1], self.efield[step], self.hfield[step]
        height = self.last_height(step)
        ex, ey, ez = (old[self.rows(run, part, comp, x, height), :] for comp in range(3))
        hx, hz = (hfield[self.rows(run, part, comp, x), :] for comp in (0, 2))
        hx_y, hz_y = self.prev_y(hx)[:height], self.prev_y(hz)[:height]
        hx, hz = hx[:height], hz[:height]
        hy = hfield[self.rows(run, part, 1, x, height), :]
        hy_x, hz_x = (hfield[self.rows(run, part, comp, x - 1, height), :] for comp in (1, 2))
        scale = self.coef[self.rows(0, 0, 0, x, height), :]
        new[self.rows(run, part, 0, x, height), :] = ex + scale * ((hz - hz_y) - (hy - self.prev_z(hy)))
        new[self.rows(run, part, 1, x, height), :] = ey + scale * ((hx - self.prev_z(hx)) - (hz - hz_x))
        new[self.rows(run, part, 2, x, height), :] = ez + scale * ((hy - hy_x) - (hx - hx_y))

    def last_height(self, step):
        return self.plan.ny if step == STEPS else self.height

    def both(self, step, h_layers, e_layers, after_h=None, after_e=None, runs=(0, 1)):
        for update, layers, after in ((self.update_h, h_layers, after_h), (self.update_e, e_layers, after_e)):
            for x in layers:
                for run in runs:
                    for part in (0, 1):
                        update(step, run, part, x)
            if after is not None:
                after()


def middle_kernel(plan, e0_in, h0_in, e1_in, h1_in, coef_in, z_low, z_high, turns, *arrays):
    nx = plan.nx
    efield, hfield, coef = arrays[: STEPS + 1], arrays[STEPS + 1 : 2 * STEPS + 2], arrays[-1]
    state = State(efield, hfield, coef)

    def take(kinds, level):
        unpack(plan, plan.y_low, z_low, lambda y: 2, turns, state, kinds, level)
        unpack(plan, plan.y_high, z_high, lambda y: 3, turns, state, kinds, level)

    take("EHC", 0)
    sweeps = Sweeps(plan, efield, hfield, coef, plan.ring)
    for step in range(1, STEPS + 1):
        after = [lambda: take("H", 1), lambda: take("E", 1)] if step == 1 else []
        sweeps.both(step, range(step - 1, nx - step), range(step, nx - step), *after)


def edges_kernel(plan, groups, *refs):
    nx, ny = plan.nx, plan.ny
    count = 2 * STEPS + 3
    x_low, x_high, c_low, c_high, z_low, z_high, turns, spec_f, spec_a = refs[count : count + 9]
    arrays = refs[count + 9 : 2 * count + 9]
    out_f, out_a, parts = refs[2 * count + 9 :]
    efield, hfield, coef = arrays[: STEPS + 1], arrays[STEPS + 1 : 2 * STEPS + 2], arrays[-1]
    state = State(efield, hfield, coef)

    def take(kinds, level, layers=()):
        unpack(plan, plan.x_low, x_low, lambda y: 0, turns, state, kinds, level)
        unpack(plan, plan.x_high, x_high, lambda y: 1, turns, state, kinds, level)
        unpack(plan, plan.corner_low, c_low, lambda y: 4 + (y >= 0), turns, state, kinds, level)
        unpack(plan, plan.corner_high, c_high, lambda y: 6 + (y >= 0), turns, state, kinds, level)
        unpack(plan, plan.y_low, z_low, lambda y: 2, turns, state, kinds, level, layers)
        unpack(plan, plan.y_high, z_high, lambda y: 3, turns, state, kinds, level, layers)

    take("EHC", 0)
    sweeps = Sweeps(plan, efield, hfield, coef, plan.ring)
    for step in range(1, STEPS + 1):
        low, high = step - STEPS, nx - step
        h_layers = [*range(low - 1, step - 1), *range(high, nx + STEPS - step)]
        e_layers = [*range(low, step), *range(high, nx + STEPS - step)]
        after = []
        if step == 1:
            after = [functools.partial(take, "H", 1, h_layers), functools.partial(take, "E", 1, e_layers)]
        sweeps.both(step, h_layers, e_layers, *after)

    share = parts.shape[2]
    shift = lax.rem(groups - lax.axis_index("angle"), groups) * share
    weight = turns[pl.ds(2 * SUB, SUB), :]
    tiles = ny // SUB

    for i in range(nx * tiles):
        x, tile = i // tiles, i % tiles
        total = jnp.zeros(weight.shape, jnp.float32)
        for comp in range(3):
            ends = []
            for run, (spec, out) in enumerate(((spec_f, out_f), (spec_a, out_a))):
                at = [pl.ds(((part * 3 + comp) * nx + x) * ny + tile * SUB, SUB) for part in (0, 1)]
                real, imag = spec[at[0], :], spec[at[1], :]
                for step in range(1, STEPS + 1):
                    theta = omega_step * step
                    ends_e = [
                        efield[step][pl.ds(plan.row(x, tile * SUB, run, part, comp), SUB), :]
                        for part in (0, 1)
                    ]
                    more = turned(*ends_e, math.cos(theta), math.sin(theta))
                    real, imag = real + more[0], imag + more[1]
                out[at[0], :], out[at[1], :] = real, imag
                ends.append((real, imag))
            total = total + (ends[0][0] * ends[1][0] - ends[0][1] * ends[1][1])
        total = pltpu.roll(total * weight, shift, 1)
        for k in range(groups):
            parts[k, pl.ds(i * SUB, SUB), :] = total[:, k * share : (k + 1) * share]


def write_kernel(tr_f, tr_a, out_f, out_a, sems):
    copies = []
    for source, target in ((tr_f, out_f), (tr_a, out_a)):
        for i in range(source.shape[0]):
            copies.append(pltpu.make_async_copy(source.at[i], target.at[i], sems.at[len(copies)]))
    for copy in copies:
        copy.start()
    for copy in copies:
        copy.wait()


def ring_pairs(axis, offset):
    size = lax.axis_size(axis)
    return [(i, (i + offset) % size) for i in range(size)]


def shards(
    forward_fields,
    adjoint_fields,
    forward_spectrum,
    adjoint_spectrum,
    permittivity,
    phase_table,
    angle_index,
    design_tiles,
):
    nx, ny, depth = permittivity.shape
    plan = Plan(nx, ny)
    groups = lax.axis_size("angle")
    wide, ring = plan.wide, plan.ring

    def array(*shape):
        return jax.ShapeDtypeStruct(shape, jnp.float32)

    def lines(count):
        return array(count, depth)

    def params(mib):
        return pltpu.CompilerParams(vmem_limit_bytes=mib * 2**20)

    def cost(size):
        return pl.CostEstimate(flops=size, bytes_accessed=size, transcendentals=0)

    with jax.named_scope("pack_y"):
        *first, coef, z_up, z_down = pl.pallas_call(
            functools.partial(pack_y_kernel, plan),
            out_shape=(
                *[array(12, wide, ring, depth)] * 4,
                array(wide, ring, depth),
                lines(plan.y_low.lines),
                lines(plan.y_high.lines),
            ),
            in_specs=[HBM] * 3,
            out_specs=[VMEM] * 7,
            scratch_shapes=[pltpu.SemaphoreType.DMA((25,))],
            compiler_params=params(8),
        )(*(pltpu.with_memory_space_constraint(array, pltpu.HBM) for array in (forward_fields[0], adjoint_fields[0], permittivity)))
    e0, h0, e1, h1, coef = (state.reshape((-1, depth)) for state in (*first, coef))
    with jax.named_scope("send_y"):
        z_low = lax.ppermute(z_up, "gy", ring_pairs("gy", 1))
        z_high = lax.ppermute(z_down, "gy", ring_pairs("gy", -1))
    with jax.named_scope("pack_x"):
        x_up, x_down = pl.pallas_call(
            functools.partial(pack_x_kernel, plan),
            out_shape=(lines(plan.x_low.lines), lines(plan.x_high.lines)),
            in_specs=[VMEM] * 5,
            out_specs=[VMEM] * 2,
            compiler_params=params(8),
            cost_estimate=cost(40 * 2**20),
        )(e0, h0, e1, h1, coef)
    with jax.named_scope("send_x"):
        x_low = lax.ppermute(x_up, "gx", ring_pairs("gx", 1))
        x_high = lax.ppermute(x_down, "gx", ring_pairs("gx", -1))
    with jax.named_scope("turns"):
        turns = pl.pallas_call(
            functools.partial(turns_kernel, groups),
            out_shape=lines(3 * SUB),
            in_specs=[SMEM] * 3,
            out_specs=VMEM,
            compiler_params=params(4),
        )(phase_table, angle_index, design_tiles)
    with jax.named_scope("relay_corners"):
        c_up, c_down = pl.pallas_call(
            functools.partial(corner_kernel, plan),
            out_shape=(lines(plan.corner_low.lines), lines(plan.corner_high.lines)),
            in_specs=[VMEM] * 2,
            out_specs=[VMEM] * 2,
            compiler_params=params(4),
        )(z_low, z_high)
        c_low = lax.ppermute(c_up, "gx", ring_pairs("gx", 1))
        c_high = lax.ppermute(c_down, "gx", ring_pairs("gx", -1))
    level = lines(12 * wide * ring)
    count = 2 * STEPS + 3
    levels = [level] * (count - 1) + [lines(wide * ring)]
    with jax.named_scope("middle"):
        state = pl.pallas_call(
            functools.partial(middle_kernel, plan),
            out_shape=levels,
            in_specs=[VMEM] * 8,
            out_specs=[VMEM] * count,
            input_output_aliases={0: 0, 1: STEPS + 1, 2: 1, 3: STEPS + 2, 4: count - 1},
            compiler_params=params(8),
            cost_estimate=cost(2**32),
        )(e0, h0, e1, h1, coef, z_low, z_high, turns)
    with jax.named_scope("edges"):
        spectra = [spectrum.reshape((-1, depth)) for spectrum in (forward_spectrum, adjoint_spectrum)]
        *_, tr_f, tr_a, parts = pl.pallas_call(
            functools.partial(edges_kernel, plan, groups),
            out_shape=[*levels, lines(6 * nx * ny), lines(6 * nx * ny), array(groups, nx * ny, depth // groups)],
            in_specs=[VMEM] * (count + 9),
            out_specs=[VMEM] * (count + 3),
            input_output_aliases={i: i for i in range(count)},
            compiler_params=params(8),
        )(*state, x_low, x_high, c_low, c_high, z_low, z_high, turns, *spectra)
    with jax.named_scope("sum_angles"):
        gradient = parts[0]
        for k in range(1, groups):
            gradient = gradient + lax.ppermute(parts[k], "angle", ring_pairs("angle", k))
    with jax.named_scope("write"):
        out_f, out_a = pl.pallas_call(
            write_kernel,
            out_shape=[array(6, nx, ny, depth)] * 2,
            in_specs=[VMEM] * 2,
            out_specs=[HBM] * 2,
            scratch_shapes=[pltpu.SemaphoreType.DMA((12,))],
            compiler_params=params(4),
        )(tr_f.reshape((6, nx, ny, depth)), tr_a.reshape((6, nx, ny, depth)))
    return (
        out_f.reshape(forward_spectrum.shape),
        out_a.reshape(adjoint_spectrum.shape),
        gradient.reshape((nx, ny, depth // groups)),
    )


def solution(mesh):
    in_specs = (
        P("angle", None, "gx", "gy", None),
        P("angle", None, "gx", "gy", None),
        P("angle", None, "gx", "gy", None),
        P("angle", None, "gx", "gy", None),
        P("gx", "gy", None),
        P(),
        P("angle"),
        P(),
    )
    out_specs = (
        P("angle", None, "gx", "gy", None),
        P("angle", None, "gx", "gy", None),
        P("gx", "gy", "angle"),
    )
    return jax.shard_map(shards, mesh=mesh, in_specs=in_specs, out_specs=out_specs, check_vma=False)
```

```python
import functools
import math

import jax
import jax.numpy as jnp
from jax import lax
from jax.experimental import pallas as pl
from jax.experimental.pallas import tpu as pltpu
from jax.sharding import PartitionSpec as P

STEPS = 3
SUB = 8

courant = 0.5
omega_step = 0.7

VMEM = pl.BlockSpec(memory_space=pltpu.VMEM)
SMEM = pl.BlockSpec(memory_space=pltpu.SMEM)
HBM = pl.BlockSpec(memory_space=pltpu.HBM)


def reads(node):
    kind, level, comp, x, y = node
    others = [c for c in range(3) if c != comp]
    if kind == "E":
        found = [("E", level - 1, comp, x, y), ("C", 0, 0, x, y)] + [("H", level, c, x, y) for c in others]
        if comp != 1:
            found.append(("H", level, 2 - comp, x, y - 1))
        if comp != 0:
            found.append(("H", level, 3 - comp, x - 1, y))
        return found
    found = [("H", level - 1, comp, x, y)] + [("E", level - 1, c, x, y) for c in others]
    if comp != 1:
        found.append(("E", level - 1, 2 - comp, x, y + 1))
    if comp != 0:
        found.append(("E", level - 1, 3 - comp, x + 1, y))
    return found


def wanted(nx, ny):
    def block(node):
        return node[3] // nx, node[4] // ny

    @functools.cache
    def alone(node):
        if node[1] == 0:
            return True
        return node[1] == 1 and all(block(other) == block(node) and alone(other) for other in reads(node))

    found, seen = set(), set()
    todo = [("E", STEPS, comp, x, y) for comp in range(3) for x in range(nx) for y in range(ny)]
    while todo:
        node = todo.pop()
        if node in seen:
            continue
        seen.add(node)
        if block(node) != (0, 0) and alone(node):
            found.add(node)
        elif node[1]:
            todo += reads(node)
    return found


class Message:
    def __init__(self, nodes, axis):
        self.axis, self.runs, self.at, self.size = axis, [], {}, 0
        stretches = []
        for node in sorted(nodes):
            before = list(node)
            before[3 + axis] -= 1
            if tuple(before) in nodes:
                continue
            count = 1
            while (*node[:3], node[3] + count * (axis == 0), node[4] + count * (axis == 1)) in nodes:
                count += 1
            stretches.append((count, node))
        for count, (kind, level, comp, x, y) in sorted(stretches, key=lambda item: (-item[0], item[1])):
            for run in (0, 1) if kind != "C" else (0,):
                for part in (0, 1) if kind != "C" else (0,):
                    what = (kind, level, comp, run, part)
                    self.runs.append((what, x, y, count, self.size))
                    for i in range(count):
                        self.at[what, x + i * (axis == 0), y + i * (axis == 1)] = self.size + i
                    self.size += count
        self.lines = -(-self.size // SUB) * SUB


class Plan:
    def __init__(self, nx, ny):
        self.nx, self.ny = nx, ny
        self.wide, self.ring = nx + 2 * STEPS, ny + SUB
        nodes = wanted(nx, ny)
        sides = {}
        for node in nodes:
            sides.setdefault((node[3] // nx, node[4] // ny), set()).add(node)

        def shifted(found, dx):
            return {(*node[:3], node[3] + dx, node[4]) for node in found}

        self.y_low, self.y_high = (
            Message(sides[0, side] | shifted(sides[-1, side], nx) | shifted(sides[1, side], -nx), 0) for side in (-1, 1)
        )
        self.mate_side, self.far_side = (1, -1), (-1, 1)
        self.x_mate, self.x_far = ([Message(sides[side, 0], 1) for side in order] for order in (self.mate_side, self.far_side))
        self.x_lines = max(message.lines for message in self.x_mate)
        self.mate = [Message(sides[side, -1] | sides[side, 1], 1) for side in self.mate_side]
        self.far_low, self.far_high = ([Message(sides[side, end], 1) for side in self.far_side] for end in (-1, 1))
        self.mate_lines, self.far_low_lines, self.far_high_lines = (
            max(message.lines for message in messages) for messages in (self.mate, self.far_low, self.far_high)
        )

    def row(self, x, y, run=0, part=0, comp=0):
        return ((run * 6 + part * 3 + comp) * self.wide + x + STEPS) * self.ring + y % self.ring

    def rows(self, what, x, y, axis, count):
        _, _, comp, run, part = what
        start = self.row(x, y, run, part, comp)
        return pl.ds(start, count, stride=self.ring) if axis == 0 and count > 1 else pl.ds(start, count)


class State:
    def __init__(self, efield, hfield, coef):
        self.by_kind = {"E": efield, "H": hfield, "C": [coef]}

    def __call__(self, what):
        return self.by_kind[what[0]][what[1]]


def pack(plan, message, state, dx, dy, out):
    for what, x, y, count, at in message.runs:
        out[pl.ds(at, count), :] = state(what)[plan.rows(what, x + dx, y + dy, message.axis, count), :]


def by_parity(offset, body):
    parity = lax.rem(lax.axis_index("gx") + offset, 2)
    for value in (0, 1):
        pl.when(parity == value)(functools.partial(body, value))


def pack_y_kernel(plan, fwd, adj, eps, e0, h0, e1, h1, coef, z_up, sems):
    nx, ny = plan.nx, plan.ny
    own = (pl.ds(STEPS, nx), pl.ds(0, ny), slice(None))
    copies = [pltpu.make_async_copy(eps, coef.at[own], sems.at[0])]
    for run, ref in enumerate((fwd, adj)):
        for kind, array in enumerate((e0, h0)):
            for i in range(6):
                copies.append(
                    pltpu.make_async_copy(ref.at[kind * 6 + i], array.at[(run * 6 + i, *own)], sems.at[len(copies)])
                )
    for copy in copies:
        copy.start()
    copies[0].wait()
    for x in range(nx):
        coef[STEPS + x, pl.ds(0, ny), :] = (0.5 * courant) / coef[STEPS + x, pl.ds(0, ny), :]
    e0, h0, e1, h1, coef = (array.reshape((-1, array.shape[-1])) for array in (e0, h0, e1, h1, coef))
    sweeps = Sweeps(plan, [e0, e1], [h0, h1], coef, ny)
    for run in (0, 1):
        for copy in copies[1 + 12 * run : 13 + 12 * run]:
            copy.wait()
        sweeps.both(1, range(nx), range(nx - 1), runs=(run,))
    state = State([e0, e1], [h0, h1], coef)
    pack(plan, plan.y_low, state, 0, ny, z_up)


def pack_x_kernel(plan, e0, h0, e1, h1, coef, to_far, to_mate):
    state = State([e0, e1], [h0, h1], coef)

    def faces(receiver):
        pack(plan, plan.x_far[receiver], state, -plan.nx * plan.far_side[receiver], 0, to_far)
        pack(plan, plan.x_mate[receiver], state, -plan.nx * plan.mate_side[receiver], 0, to_mate)

    by_parity(1, faces)


def pack_rest_kernel(plan, e0, h0, e1, h1, coef, after, z_down, far_up, far_down):
    nx, ny = plan.nx, plan.ny
    state = State([e0, e1], [h0, h1], coef)
    pack(plan, plan.y_high, state, 0, -ny, z_down)

    def far(receiver):
        dx = -nx * plan.far_side[receiver]
        pack(plan, plan.far_low[receiver], state, dx, ny, far_up)
        pack(plan, plan.far_high[receiver], state, dx, -ny, far_down)

    by_parity(1, far)


def turns_kernel(groups, table, index, tiles, turns):
    row = index[0]
    phi_x, phi_y = table[row, 0], table[row, 1]
    at_x, at_y = lax.axis_index("gx"), lax.axis_index("gy")
    none = jnp.float32(0.0)
    ax_low = jnp.where(at_x == 0, -phi_x, none)
    ax_high = jnp.where(at_x == lax.axis_size("gx") - 1, phi_x, none)
    ay_low = jnp.where(at_y == 0, -phi_y, none)
    ay_high = jnp.where(at_y == lax.axis_size("gy") - 1, phi_y, none)
    sub = lax.broadcasted_iota(jnp.int32, (SUB, turns.shape[1]), 0)
    angles = jnp.zeros(sub.shape, jnp.float32)
    for i, angle in enumerate((ax_low, ax_high, ay_low, ay_high, ax_low + ay_low, ax_low + ay_high,
                               ax_high + ay_low, ax_high + ay_high)):
        angles = jnp.where(sub == i, angle, angles)
    turns[pl.ds(0, SUB), :] = jnp.cos(angles)
    turns[pl.ds(SUB, SUB), :] = jnp.sin(angles)
    own_tile = at_x * lax.axis_size("gy") + at_y
    chosen = tiles[0] == own_tile
    for i in range(1, tiles.shape[0]):
        chosen = jnp.logical_or(chosen, tiles[i] == own_tile)
    weight = jnp.where(chosen, jnp.float32(1.0 / groups), none)
    turns[pl.ds(2 * SUB, SUB), :] = jnp.full(sub.shape, weight, jnp.float32)


def relay_kernel(plan, z_low, z_high, after, other_after, out):
    def mate(receiver):
        dx = -plan.nx * plan.mate_side[receiver]
        for (what, x, y), row in plan.mate[receiver].at.items():
            ref, source = (z_low, plan.y_low) if y < 0 else (z_high, plan.y_high)
            out[pl.ds(row, 1), :] = ref[pl.ds(source.at[what, x + dx, y], 1), :]

    by_parity(1, mate)


def turned(real, imag, cosine, sine):
    return real * cosine - imag * sine, real * sine + imag * cosine


def unpack(plan, message, ref, which, turns, state, kinds, level, layers=None):
    axis = message.axis
    for (kind, at_level, comp, run, part), x, y, count, at in message.runs:
        if kind not in kinds or at_level != level or part == 1:
            continue
        pieces = [(x, y, count, at)]
        if layers is not None:
            pieces = [(x + i, y, 1, at + i) for i in range(count) if x + i in layers]
        for cell_x, cell_y, size, row in pieces:
            what = (kind, at_level, comp, run, 0)
            real = ref[pl.ds(row, size), :]
            if kind == "C":
                state(what)[plan.rows(what, cell_x, cell_y, axis, size), :] = real
                continue
            twin = (kind, at_level, comp, run, 1)
            imag = ref[pl.ds(message.at[twin, cell_x, cell_y], size), :]
            turn = which(y)
            cosine, sine = turns[pl.ds(turn, 1), :], turns[pl.ds(SUB + turn, 1), :]
            real, imag = turned(real, imag, cosine, sine if run == 0 else -sine)
            state(what)[plan.rows(what, cell_x, cell_y, axis, size), :] = real
            state(twin)[plan.rows(twin, cell_x, cell_y, axis, size), :] = imag


class Sweeps:
    def __init__(self, plan, efield, hfield, coef, height):
        self.plan, self.efield, self.hfield, self.coef, self.height = plan, efield, hfield, coef, height

    def rows(self, run, part, comp, x, height=None):
        return pl.ds(self.plan.row(x, 0, run, part, comp), height or self.height)

    def next_z(self, value):
        lane = lax.broadcasted_iota(jnp.int32, value.shape, 1)
        return jnp.where(lane == value.shape[1] - 1, 0.0, pltpu.roll(value, value.shape[1] - 1, 1))

    def prev_z(self, value):
        lane = lax.broadcasted_iota(jnp.int32, value.shape, 1)
        return jnp.where(lane == 0, 0.0, pltpu.roll(value, 1, 1))

    def next_y(self, value):
        return pltpu.roll(value, self.height - 1, 0)

    def prev_y(self, value):
        return pltpu.roll(value, 1, 0)

    def update_h(self, step, run, part, x):
        efield, old, new = self.efield[step - 1], self.hfield[step - 1], self.hfield[step]
        ex, ey, ez = (efield[self.rows(run, part, comp, x), :] for comp in range(3))
        ey_x, ez_x = (efield[self.rows(run, part, comp, x + 1), :] for comp in (1, 2))
        hx, hy, hz = (old[self.rows(run, part, comp, x), :] for comp in range(3))
        if step == 1:
            hx, hy, hz = hx + hx, hy + hy, hz + hz
        new[self.rows(run, part, 0, x), :] = hx - ((self.next_y(ez) - ez) - (self.next_z(ey) - ey))
        new[self.rows(run, part, 2, x), :] = hz - ((ey_x - ey) - (self.next_y(ex) - ex))
        height = self.last_height(step)
        ex, ez, ez_x, hy = (value[:height] for value in (ex, ez, ez_x, hy))
        new[self.rows(run, part, 1, x, height), :] = hy - ((self.next_z(ex) - ex) - (ez_x - ez))

    def update_e(self, step, run, part, x):
        old, new, hfield = self.efield[step - 1], self.efield[step], self.hfield[step]
        height = self.last_height(step)
        ex, ey, ez = (old[self.rows(run, part, comp, x, height), :] for comp in range(3))
        hx, hz = (hfield[self.rows(run, part, comp, x), :] for comp in (0, 2))
        hx_y, hz_y = self.prev_y(hx)[:height], self.prev_y(hz)[:height]
        hx, hz = hx[:height], hz[:height]
        hy = hfield[self.rows(run, part, 1, x, height), :]
        hy_x, hz_x = (hfield[self.rows(run, part, comp, x - 1, height), :] for comp in (1, 2))
        scale = self.coef[self.rows(0, 0, 0, x, height), :]
        new[self.rows(run, part, 0, x, height), :] = ex + scale * ((hz - hz_y) - (hy - self.prev_z(hy)))
        new[self.rows(run, part, 1, x, height), :] = ey + scale * ((hx - self.prev_z(hx)) - (hz - hz_x))
        new[self.rows(run, part, 2, x, height), :] = ez + scale * ((hy - hy_x) - (hx - hx_y))

    def last_height(self, step):
        return self.plan.ny if step == STEPS else self.height

    def both(self, step, h_layers, e_layers, after_h=None, after_e=None, runs=(0, 1)):
        for update, layers, after in ((self.update_h, h_layers, after_h), (self.update_e, e_layers, after_e)):
            for x in layers:
                for run in runs:
                    for part in (0, 1):
                        update(step, run, part, x)
            if after is not None:
                after()


def middle_kernel(plan, e0_in, h0_in, e1_in, h1_in, coef_in, z_low, z_high, turns, *arrays):
    nx = plan.nx
    efield, hfield, coef = arrays[: STEPS + 1], arrays[STEPS + 1 : 2 * STEPS + 2], arrays[-1]
    state = State(efield, hfield, coef)

    def take(kinds, level):
        unpack(plan, plan.y_low, z_low, lambda y: 2, turns, state, kinds, level)
        unpack(plan, plan.y_high, z_high, lambda y: 3, turns, state, kinds, level)

    take("EHC", 0)
    sweeps = Sweeps(plan, efield, hfield, coef, plan.ring)
    for step in range(1, STEPS + 1):
        after = [lambda: take("H", 1), lambda: take("E", 1)] if step == 1 else []
        sweeps.both(step, range(step - 1, nx - step), range(step, nx - step), *after)


def edges_kernel(plan, groups, *refs):
    nx, ny = plan.nx, plan.ny
    count = 2 * STEPS + 3
    x_far, x_mate, far_low, far_high, mate, z_low, z_high, turns, spec_f, spec_a = refs[count : count + 10]
    arrays = refs[count + 10 : 2 * count + 10]
    out_f, out_a, parts = refs[2 * count + 10 :]
    efield, hfield, coef = arrays[: STEPS + 1], arrays[STEPS + 1 : 2 * STEPS + 2], arrays[-1]
    state = State(efield, hfield, coef)

    def take(kinds, level, layers=()):

        def sides(receiver):
            for messages, ref, side in ((plan.x_far, x_far, plan.far_side), (plan.x_mate, x_mate, plan.mate_side)):
                first = 0 if side[receiver] < 0 else 1
                unpack(plan, messages[receiver], ref, lambda y: first, turns, state, kinds, level)
            for messages, ref, side in (
                (plan.far_low, far_low, plan.far_side),
                (plan.far_high, far_high, plan.far_side),
                (plan.mate, mate, plan.mate_side),
            ):
                first = 4 if side[receiver] < 0 else 6
                unpack(plan, messages[receiver], ref, lambda y: first + (y >= 0), turns, state, kinds, level)

        by_parity(0, sides)
        unpack(plan, plan.y_low, z_low, lambda y: 2, turns, state, kinds, level, layers)
        unpack(plan, plan.y_high, z_high, lambda y: 3, turns, state, kinds, level, layers)

    take("EHC", 0)
    sweeps = Sweeps(plan, efield, hfield, coef, plan.ring)
    for step in range(1, STEPS + 1):
        low, high = step - STEPS, nx - step
        h_layers = [*range(low - 1, step - 1), *range(high, nx + STEPS - step)]
        e_layers = [*range(low, step), *range(high, nx + STEPS - step)]
        after = []
        if step == 1:
            after = [functools.partial(take, "H", 1, h_layers), functools.partial(take, "E", 1, e_layers)]
        sweeps.both(step, h_layers, e_layers, *after)

    share = parts.shape[2]
    shift = lax.rem(groups - lax.axis_index("angle"), groups) * share
    weight = turns[pl.ds(2 * SUB, SUB), :]
    tiles = ny // SUB

    for i in range(nx * tiles):
        x, tile = i // tiles, i % tiles
        total = jnp.zeros(weight.shape, jnp.float32)
        for comp in range(3):
            ends = []
            for run, (spec, out) in enumerate(((spec_f, out_f), (spec_a, out_a))):
                at = [pl.ds(((part * 3 + comp) * nx + x) * ny + tile * SUB, SUB) for part in (0, 1)]
                real, imag = spec[at[0], :], spec[at[1], :]
                for step in range(1, STEPS + 1):
                    theta = omega_step * step
                    ends_e = [
                        efield[step][pl.ds(plan.row(x, tile * SUB, run, part, comp), SUB), :]
                        for part in (0, 1)
                    ]
                    more = turned(*ends_e, math.cos(theta), math.sin(theta))
                    real, imag = real + more[0], imag + more[1]
                out[at[0], :], out[at[1], :] = real, imag
                ends.append((real, imag))
            total = total + (ends[0][0] * ends[1][0] - ends[0][1] * ends[1][1])
        total = pltpu.roll(total * weight, shift, 1)
        for k in range(groups):
            parts[k, pl.ds(i * SUB, SUB), :] = total[:, k * share : (k + 1) * share]


def write_kernel(tr_f, tr_a, out_f, out_a, sems):
    copies = []
    for source, target in ((tr_f, out_f), (tr_a, out_a)):
        for i in range(source.shape[0]):
            copies.append(pltpu.make_async_copy(source.at[i], target.at[i], sems.at[len(copies)]))
    for copy in copies:
        copy.start()
    for copy in copies:
        copy.wait()


def ring_pairs(axis, offset):
    size = lax.axis_size(axis)
    return [(i, (i + offset) % size) for i in range(size)]


def mate_pairs():
    return [(i, i ^ 1) for i in range(lax.axis_size("gx"))]


def far_pairs(offset):
    size_x, size_y = lax.axis_size("gx"), lax.axis_size("gy")
    return [
        (x * size_y + y, (x + (1 if x % 2 else -1)) % size_x * size_y + (y + offset) % size_y)
        for x in range(size_x)
        for y in range(size_y)
    ]


def shards(
    forward_fields,
    adjoint_fields,
    forward_spectrum,
    adjoint_spectrum,
    permittivity,
    phase_table,
    angle_index,
    design_tiles,
):
    nx, ny, depth = permittivity.shape
    plan = Plan(nx, ny)
    groups = lax.axis_size("angle")
    wide, ring = plan.wide, plan.ring

    def array(*shape):
        return jax.ShapeDtypeStruct(shape, jnp.float32)

    def lines(count):
        return array(count, depth)

    def params(mib):
        return pltpu.CompilerParams(vmem_limit_bytes=mib * 2**20)

    def cost(size):
        return pl.CostEstimate(flops=size, bytes_accessed=size, transcendentals=0)

    assert lax.axis_size("gx") % 2 == 0
    with jax.named_scope("pack_y"):
        *first, coef, z_up = pl.pallas_call(
            functools.partial(pack_y_kernel, plan),
            out_shape=(*[array(12, wide, ring, depth)] * 4, array(wide, ring, depth), lines(plan.y_low.lines)),
            in_specs=[HBM] * 3,
            out_specs=[VMEM] * 6,
            scratch_shapes=[pltpu.SemaphoreType.DMA((25,))],
            compiler_params=params(8),
        )(*(pltpu.with_memory_space_constraint(array, pltpu.HBM) for array in (forward_fields[0], adjoint_fields[0], permittivity)))
    first = [state.reshape((-1, depth)) for state in (*first, coef)]
    with jax.named_scope("send_y_up"):
        z_low = lax.ppermute(z_up, "gy", ring_pairs("gy", 1))
    with jax.named_scope("pack_x"):
        to_far, to_mate = pl.pallas_call(
            functools.partial(pack_x_kernel, plan),
            out_shape=[lines(plan.x_lines)] * 2,
            in_specs=[VMEM] * 5,
            out_specs=[VMEM] * 2,
            compiler_params=params(8),
            cost_estimate=cost(2**10),
        )(*first)
    with jax.named_scope("send_x"):
        x_far = lax.ppermute(to_far, ("gx", "gy"), far_pairs(0))
        x_mate = lax.ppermute(to_mate, "gx", mate_pairs())
    with jax.named_scope("pack_rest"):
        z_down, far_up, far_down = pl.pallas_call(
            functools.partial(pack_rest_kernel, plan),
            out_shape=(lines(plan.y_high.lines), lines(plan.far_low_lines), lines(plan.far_high_lines)),
            in_specs=[VMEM] * 6,
            out_specs=[VMEM] * 3,
            compiler_params=params(8),
            cost_estimate=cost(2**10),
        )(*first, x_mate)
    with jax.named_scope("send_rest"):
        z_high = lax.ppermute(z_down, "gy", ring_pairs("gy", -1))
        far_low = lax.ppermute(far_up, ("gx", "gy"), far_pairs(1))
        far_high = lax.ppermute(far_down, ("gx", "gy"), far_pairs(-1))
    with jax.named_scope("turns"):
        turns = pl.pallas_call(
            functools.partial(turns_kernel, groups),
            out_shape=lines(3 * SUB),
            in_specs=[SMEM] * 3,
            out_specs=VMEM,
            compiler_params=params(4),
        )(phase_table, angle_index, design_tiles)
    with jax.named_scope("relay_corners"):
        relayed = pl.pallas_call(
            functools.partial(relay_kernel, plan),
            out_shape=lines(plan.mate_lines),
            in_specs=[VMEM] * 4,
            out_specs=VMEM,
            compiler_params=params(4),
        )(z_low, z_high, far_low, far_high)
        mate = lax.ppermute(relayed, "gx", mate_pairs())
    level = lines(12 * wide * ring)
    count = 2 * STEPS + 3
    levels = [level] * (count - 1) + [lines(wide * ring)]
    with jax.named_scope("middle"):
        state = pl.pallas_call(
            functools.partial(middle_kernel, plan),
            out_shape=levels,
            in_specs=[VMEM] * 8,
            out_specs=[VMEM] * count,
            input_output_aliases={0: 0, 1: STEPS + 1, 2: 1, 3: STEPS + 2, 4: count - 1},
            compiler_params=params(8),
            cost_estimate=cost(2**31),
        )(*first, z_low, z_high, turns)
    with jax.named_scope("edges"):
        spectra = [spectrum.reshape((-1, depth)) for spectrum in (forward_spectrum, adjoint_spectrum)]
        *_, tr_f, tr_a, parts = pl.pallas_call(
            functools.partial(edges_kernel, plan, groups),
            out_shape=[*levels, lines(6 * nx * ny), lines(6 * nx * ny), array(groups, nx * ny, depth // groups)],
            in_specs=[VMEM] * (count + 10),
            out_specs=[VMEM] * (count + 3),
            input_output_aliases={i: i for i in range(count)},
            compiler_params=params(8),
        )(*state, x_far, x_mate, far_low, far_high, mate, z_low, z_high, turns, *spectra)
    with jax.named_scope("sum_angles"):
        gradient = parts[0]
        for k in range(1, groups):
            gradient = gradient + lax.ppermute(parts[k], "angle", ring_pairs("angle", k))
    with jax.named_scope("write"):
        out_f, out_a = pl.pallas_call(
            write_kernel,
            out_shape=[array(6, nx, ny, depth)] * 2,
            in_specs=[VMEM] * 2,
            out_specs=[HBM] * 2,
            scratch_shapes=[pltpu.SemaphoreType.DMA((12,))],
            compiler_params=params(4),
        )(tr_f.reshape((6, nx, ny, depth)), tr_a.reshape((6, nx, ny, depth)))
    return (
        out_f.reshape(forward_spectrum.shape),
        out_a.reshape(adjoint_spectrum.shape),
        gradient.reshape((nx, ny, depth // groups)),
    )


def solution(mesh):
    in_specs = (
        P("angle", None, "gx", "gy", None),
        P("angle", None, "gx", "gy", None),
        P("angle", None, "gx", "gy", None),
        P("angle", None, "gx", "gy", None),
        P("gx", "gy", None),
        P(),
        P("angle"),
        P(),
    )
    out_specs = (
        P("angle", None, "gx", "gy", None),
        P("angle", None, "gx", "gy", None),
        P("gx", "gy", "angle"),
    )
    return jax.shard_map(shards, mesh=mesh, in_specs=in_specs, out_specs=out_specs, check_vma=False)
```

```python
import functools
import math

import jax
import jax.numpy as jnp
from jax import lax
from jax.experimental import pallas as pl
from jax.experimental.pallas import tpu as pltpu
from jax.sharding import PartitionSpec as P

STEPS = 3
SUB = 8

courant = 0.5
omega_step = 0.7

VMEM = pl.BlockSpec(memory_space=pltpu.VMEM)
SMEM = pl.BlockSpec(memory_space=pltpu.SMEM)
HBM = pl.BlockSpec(memory_space=pltpu.HBM)


def reads(node):
    kind, level, comp, x, y = node
    others = [c for c in range(3) if c != comp]
    if kind == "E":
        found = [("E", level - 1, comp, x, y), ("C", 0, 0, x, y)] + [("H", level, c, x, y) for c in others]
        if comp != 1:
            found.append(("H", level, 2 - comp, x, y - 1))
        if comp != 0:
            found.append(("H", level, 3 - comp, x - 1, y))
        return found
    found = [("H", level - 1, comp, x, y)] + [("E", level - 1, c, x, y) for c in others]
    if comp != 1:
        found.append(("E", level - 1, 2 - comp, x, y + 1))
    if comp != 0:
        found.append(("E", level - 1, 3 - comp, x + 1, y))
    return found


def wanted(nx, ny):
    def block(node):
        return node[3] // nx, node[4] // ny

    @functools.cache
    def alone(node):
        if node[1] == 0:
            return True
        return node[1] == 1 and all(block(other) == block(node) and alone(other) for other in reads(node))

    found, seen = set(), set()
    todo = [("E", STEPS, comp, x, y) for comp in range(3) for x in range(nx) for y in range(ny)]
    while todo:
        node = todo.pop()
        if node in seen:
            continue
        seen.add(node)
        if block(node) != (0, 0) and alone(node):
            found.add(node)
        elif node[1]:
            todo += reads(node)
    return found


class Message:
    def __init__(self, nodes, axis):
        self.axis, self.runs, self.at, self.size = axis, [], {}, 0
        stretches = []
        for node in sorted(nodes):
            before = list(node)
            before[3 + axis] -= 1
            if tuple(before) in nodes:
                continue
            count = 1
            while (*node[:3], node[3] + count * (axis == 0), node[4] + count * (axis == 1)) in nodes:
                count += 1
            stretches.append((count, node))
        for count, (kind, level, comp, x, y) in sorted(stretches, key=lambda item: (-item[0], item[1])):
            for run in (0, 1) if kind != "C" else (0,):
                for part in (0, 1) if kind != "C" else (0,):
                    what = (kind, level, comp, run, part)
                    self.runs.append((what, x, y, count, self.size))
                    for i in range(count):
                        self.at[what, x + i * (axis == 0), y + i * (axis == 1)] = self.size + i
                    self.size += count
        self.lines = -(-self.size // SUB) * SUB


class Plan:
    def __init__(self, nx, ny):
        self.nx, self.ny = nx, ny
        self.wide, self.ring = nx + 2 * STEPS, ny + SUB
        nodes = wanted(nx, ny)
        sides = {}
        for node in nodes:
            sides.setdefault((node[3] // nx, node[4] // ny), set()).add(node)

        def shifted(found, dx):
            return {(*node[:3], node[3] + dx, node[4]) for node in found}

        self.y_low, self.y_high = (
            Message(sides[0, side] | shifted(sides[-1, side], nx) | shifted(sides[1, side], -nx), 0) for side in (-1, 1)
        )
        self.mate_side, self.far_side = (1, -1), (-1, 1)
        self.x_mate, self.x_far = ([Message(sides[side, 0], 1) for side in order] for order in (self.mate_side, self.far_side))
        self.x_lines = max(message.lines for message in self.x_mate)
        self.mate, self.far = ([Message(sides[side, -1] | sides[side, 1], 1) for side in order] for order in (self.mate_side, self.far_side))
        self.corner_lines = max(message.lines for message in self.mate)

    def row(self, x, y, run=0, part=0, comp=0):
        return ((run * 6 + part * 3 + comp) * self.wide + x + STEPS) * self.ring + y % self.ring

    def rows(self, what, x, y, axis, count):
        _, _, comp, run, part = what
        start = self.row(x, y, run, part, comp)
        return pl.ds(start, count, stride=self.ring) if axis == 0 and count > 1 else pl.ds(start, count)


class State:
    def __init__(self, efield, hfield, coef):
        self.by_kind = {"E": efield, "H": hfield, "C": [coef]}

    def __call__(self, what):
        return self.by_kind[what[0]][what[1]]


def pack(plan, message, state, dx, dy, out):
    for what, x, y, count, at in message.runs:
        out[pl.ds(at, count), :] = state(what)[plan.rows(what, x + dx, y + dy, message.axis, count), :]


def by_parity(offset, body):
    parity = lax.rem(lax.axis_index("gx") + offset, 2)
    for value in (0, 1):
        pl.when(parity == value)(functools.partial(body, value))


def pack_y_kernel(plan, fwd, adj, eps, e0, h0, e1, h1, coef, z_up, sems):
    nx, ny = plan.nx, plan.ny
    own = (pl.ds(STEPS, nx), pl.ds(0, ny), slice(None))
    copies = [pltpu.make_async_copy(eps, coef.at[own], sems.at[0])]
    for run, ref in enumerate((fwd, adj)):
        for kind, array in enumerate((e0, h0)):
            for i in range(6):
                copies.append(
                    pltpu.make_async_copy(ref.at[kind * 6 + i], array.at[(run * 6 + i, *own)], sems.at[len(copies)])
                )
    for copy in copies:
        copy.start()
    copies[0].wait()
    for x in range(nx):
        coef[STEPS + x, pl.ds(0, ny), :] = (0.5 * courant) / coef[STEPS + x, pl.ds(0, ny), :]
    e0, h0, e1, h1, coef = (array.reshape((-1, array.shape[-1])) for array in (e0, h0, e1, h1, coef))
    sweeps = Sweeps(plan, [e0, e1], [h0, h1], coef, ny)
    for run in (0, 1):
        for copy in copies[1 + 12 * run : 13 + 12 * run]:
            copy.wait()
        sweeps.both(1, range(nx), range(nx - 1), runs=(run,))
    state = State([e0, e1], [h0, h1], coef)
    pack(plan, plan.y_low, state, 0, ny, z_up)


def pack_x_kernel(plan, e0, h0, e1, h1, coef, to_far, to_mate):
    state = State([e0, e1], [h0, h1], coef)

    def faces(receiver):
        pack(plan, plan.x_far[receiver], state, -plan.nx * plan.far_side[receiver], 0, to_far)
        pack(plan, plan.x_mate[receiver], state, -plan.nx * plan.mate_side[receiver], 0, to_mate)

    by_parity(1, faces)


def pack_down_kernel(plan, e0, h0, e1, h1, coef, after, z_down):
    pack(plan, plan.y_high, State([e0, e1], [h0, h1], coef), 0, -plan.ny, z_down)


def turns_kernel(groups, table, index, tiles, turns):
    row = index[0]
    phi_x, phi_y = table[row, 0], table[row, 1]
    at_x, at_y = lax.axis_index("gx"), lax.axis_index("gy")
    none = jnp.float32(0.0)
    ax_low = jnp.where(at_x == 0, -phi_x, none)
    ax_high = jnp.where(at_x == lax.axis_size("gx") - 1, phi_x, none)
    ay_low = jnp.where(at_y == 0, -phi_y, none)
    ay_high = jnp.where(at_y == lax.axis_size("gy") - 1, phi_y, none)
    sub = lax.broadcasted_iota(jnp.int32, (SUB, turns.shape[1]), 0)
    angles = jnp.zeros(sub.shape, jnp.float32)
    for i, angle in enumerate((ax_low, ax_high, ay_low, ay_high, ax_low + ay_low, ax_low + ay_high,
                               ax_high + ay_low, ax_high + ay_high)):
        angles = jnp.where(sub == i, angle, angles)
    turns[pl.ds(0, SUB), :] = jnp.cos(angles)
    turns[pl.ds(SUB, SUB), :] = jnp.sin(angles)
    own_tile = at_x * lax.axis_size("gy") + at_y
    chosen = tiles[0] == own_tile
    for i in range(1, tiles.shape[0]):
        chosen = jnp.logical_or(chosen, tiles[i] == own_tile)
    weight = jnp.where(chosen, jnp.float32(1.0 / groups), none)
    turns[pl.ds(2 * SUB, SUB), :] = jnp.full(sub.shape, weight, jnp.float32)


def relay_kernel(plan, z_low, z_high, to_far, to_mate):
    def corners(receiver):
        for messages, side, out in ((plan.far, plan.far_side, to_far), (plan.mate, plan.mate_side, to_mate)):
            dx = -plan.nx * side[receiver]
            for (what, x, y), row in messages[receiver].at.items():
                ref, source = (z_low, plan.y_low) if y < 0 else (z_high, plan.y_high)
                out[pl.ds(row, 1), :] = ref[pl.ds(source.at[what, x + dx, y], 1), :]

    by_parity(1, corners)


def turned(real, imag, cosine, sine):
    return real * cosine - imag * sine, real * sine + imag * cosine


def unpack(plan, message, ref, which, turns, state, kinds, level, layers=None):
    axis = message.axis
    for (kind, at_level, comp, run, part), x, y, count, at in message.runs:
        if kind not in kinds or at_level != level or part == 1:
            continue
        pieces = [(x, y, count, at)]
        if layers is not None:
            pieces = [(x + i, y, 1, at + i) for i in range(count) if x + i in layers]
        for cell_x, cell_y, size, row in pieces:
            what = (kind, at_level, comp, run, 0)
            real = ref[pl.ds(row, size), :]
            if kind == "C":
                state(what)[plan.rows(what, cell_x, cell_y, axis, size), :] = real
                continue
            twin = (kind, at_level, comp, run, 1)
            imag = ref[pl.ds(message.at[twin, cell_x, cell_y], size), :]
            turn = which(y)
            cosine, sine = turns[pl.ds(turn, 1), :], turns[pl.ds(SUB + turn, 1), :]
            real, imag = turned(real, imag, cosine, sine if run == 0 else -sine)
            state(what)[plan.rows(what, cell_x, cell_y, axis, size), :] = real
            state(twin)[plan.rows(twin, cell_x, cell_y, axis, size), :] = imag


class Sweeps:
    def __init__(self, plan, efield, hfield, coef, height):
        self.plan, self.efield, self.hfield, self.coef, self.height = plan, efield, hfield, coef, height

    def rows(self, run, part, comp, x, height=None):
        return pl.ds(self.plan.row(x, 0, run, part, comp), height or self.height)

    def next_z(self, value):
        lane = lax.broadcasted_iota(jnp.int32, value.shape, 1)
        return jnp.where(lane == value.shape[1] - 1, 0.0, pltpu.roll(value, value.shape[1] - 1, 1))

    def prev_z(self, value):
        lane = lax.broadcasted_iota(jnp.int32, value.shape, 1)
        return jnp.where(lane == 0, 0.0, pltpu.roll(value, 1, 1))

    def next_y(self, value):
        return pltpu.roll(value, self.height - 1, 0)

    def prev_y(self, value):
        return pltpu.roll(value, 1, 0)

    def update_h(self, step, run, part, x):
        efield, old, new = self.efield[step - 1], self.hfield[step - 1], self.hfield[step]
        ex, ey, ez = (efield[self.rows(run, part, comp, x), :] for comp in range(3))
        ey_x, ez_x = (efield[self.rows(run, part, comp, x + 1), :] for comp in (1, 2))
        hx, hy, hz = (old[self.rows(run, part, comp, x), :] for comp in range(3))
        if step == 1:
            hx, hy, hz = hx + hx, hy + hy, hz + hz
        new[self.rows(run, part, 0, x), :] = hx - ((self.next_y(ez) - ez) - (self.next_z(ey) - ey))
        new[self.rows(run, part, 2, x), :] = hz - ((ey_x - ey) - (self.next_y(ex) - ex))
        height = self.last_height(step)
        ex, ez, ez_x, hy = (value[:height] for value in (ex, ez, ez_x, hy))
        new[self.rows(run, part, 1, x, height), :] = hy - ((self.next_z(ex) - ex) - (ez_x - ez))

    def update_e(self, step, run, part, x):
        old, new, hfield = self.efield[step - 1], self.efield[step], self.hfield[step]
        height = self.last_height(step)
        ex, ey, ez = (old[self.rows(run, part, comp, x, height), :] for comp in range(3))
        hx, hz = (hfield[self.rows(run, part, comp, x), :] for comp in (0, 2))
        hx_y, hz_y = self.prev_y(hx)[:height], self.prev_y(hz)[:height]
        hx, hz = hx[:height], hz[:height]
        hy = hfield[self.rows(run, part, 1, x, height), :]
        hy_x, hz_x = (hfield[self.rows(run, part, comp, x - 1, height), :] for comp in (1, 2))
        scale = self.coef[self.rows(0, 0, 0, x, height), :]
        new[self.rows(run, part, 0, x, height), :] = ex + scale * ((hz - hz_y) - (hy - self.prev_z(hy)))
        new[self.rows(run, part, 1, x, height), :] = ey + scale * ((hx - self.prev_z(hx)) - (hz - hz_x))
        new[self.rows(run, part, 2, x, height), :] = ez + scale * ((hy - hy_x) - (hx - hx_y))

    def last_height(self, step):
        return self.plan.ny if step == STEPS else self.height

    def both(self, step, h_layers, e_layers, after_h=None, after_e=None, runs=(0, 1)):
        for update, layers, after in ((self.update_h, h_layers, after_h), (self.update_e, e_layers, after_e)):
            for x in layers:
                for run in runs:
                    for part in (0, 1):
                        update(step, run, part, x)
            if after is not None:
                after()


def middle_kernel(plan, e0_in, h0_in, e1_in, h1_in, coef_in, z_low, z_high, turns, *arrays):
    nx = plan.nx
    efield, hfield, coef = arrays[: STEPS + 1], arrays[STEPS + 1 : 2 * STEPS + 2], arrays[-1]
    state = State(efield, hfield, coef)

    def take(kinds, level):
        unpack(plan, plan.y_low, z_low, lambda y: 2, turns, state, kinds, level)
        unpack(plan, plan.y_high, z_high, lambda y: 3, turns, state, kinds, level)

    take("EHC", 0)
    sweeps = Sweeps(plan, efield, hfield, coef, plan.ring)
    for step in range(1, STEPS + 1):
        after = [lambda: take("H", 1), lambda: take("E", 1)] if step == 1 else []
        sweeps.both(step, range(step - 1, nx - step), range(step, nx - step), *after)


def edges_kernel(plan, groups, *refs):
    nx, ny = plan.nx, plan.ny
    count = 2 * STEPS + 3
    x_far, x_mate, far, mate, z_low, z_high, turns, spec_f, spec_a = refs[count : count + 9]
    arrays = refs[count + 9 : 2 * count + 9]
    out_f, out_a, parts = refs[2 * count + 9 :]
    efield, hfield, coef = arrays[: STEPS + 1], arrays[STEPS + 1 : 2 * STEPS + 2], arrays[-1]
    state = State(efield, hfield, coef)

    def take(kinds, level, layers=()):

        def sides(receiver):
            for messages, ref, side in ((plan.x_far, x_far, plan.far_side), (plan.x_mate, x_mate, plan.mate_side)):
                first = 0 if side[receiver] < 0 else 1
                unpack(plan, messages[receiver], ref, lambda y: first, turns, state, kinds, level)
            for messages, ref, side in ((plan.far, far, plan.far_side), (plan.mate, mate, plan.mate_side)):
                first = 4 if side[receiver] < 0 else 6
                unpack(plan, messages[receiver], ref, lambda y: first + (y >= 0), turns, state, kinds, level)

        by_parity(0, sides)
        unpack(plan, plan.y_low, z_low, lambda y: 2, turns, state, kinds, level, layers)
        unpack(plan, plan.y_high, z_high, lambda y: 3, turns, state, kinds, level, layers)

    take("EHC", 0)
    sweeps = Sweeps(plan, efield, hfield, coef, plan.ring)
    for step in range(1, STEPS + 1):
        low, high = step - STEPS, nx - step
        h_layers = [*range(low - 1, step - 1), *range(high, nx + STEPS - step)]
        e_layers = [*range(low, step), *range(high, nx + STEPS - step)]
        after = []
        if step == 1:
            after = [functools.partial(take, "H", 1, h_layers), functools.partial(take, "E", 1, e_layers)]
        sweeps.both(step, h_layers, e_layers, *after)

    share = parts.shape[2]
    shift = lax.rem(groups - lax.axis_index("angle"), groups) * share
    weight = turns[pl.ds(2 * SUB, SUB), :]
    tiles = ny // SUB

    for i in range(nx * tiles):
        x, tile = i // tiles, i % tiles
        total = jnp.zeros(weight.shape, jnp.float32)
        for comp in range(3):
            ends = []
            for run, (spec, out) in enumerate(((spec_f, out_f), (spec_a, out_a))):
                at = [pl.ds(((part * 3 + comp) * nx + x) * ny + tile * SUB, SUB) for part in (0, 1)]
                real, imag = spec[at[0], :], spec[at[1], :]
                for step in range(1, STEPS + 1):
                    theta = omega_step * step
                    ends_e = [
                        efield[step][pl.ds(plan.row(x, tile * SUB, run, part, comp), SUB), :]
                        for part in (0, 1)
                    ]
                    more = turned(*ends_e, math.cos(theta), math.sin(theta))
                    real, imag = real + more[0], imag + more[1]
                out[at[0], :], out[at[1], :] = real, imag
                ends.append((real, imag))
            total = total + (ends[0][0] * ends[1][0] - ends[0][1] * ends[1][1])
        total = pltpu.roll(total * weight, shift, 1)
        for k in range(groups):
            parts[k, pl.ds(i * SUB, SUB), :] = total[:, k * share : (k + 1) * share]


def write_kernel(tr_f, tr_a, out_f, out_a, sems):
    copies = []
    for source, target in ((tr_f, out_f), (tr_a, out_a)):
        for i in range(source.shape[0]):
            copies.append(pltpu.make_async_copy(source.at[i], target.at[i], sems.at[len(copies)]))
    for copy in copies:
        copy.start()
    for copy in copies:
        copy.wait()


def ring_pairs(axis, offset):
    size = lax.axis_size(axis)
    return [(i, (i + offset) % size) for i in range(size)]


def mate_pairs():
    return [(i, i ^ 1) for i in range(lax.axis_size("gx"))]


def far_pairs():
    size = lax.axis_size("gx")
    return [(i, (i + (1 if i % 2 else -1)) % size) for i in range(size)]


def shards(
    forward_fields,
    adjoint_fields,
    forward_spectrum,
    adjoint_spectrum,
    permittivity,
    phase_table,
    angle_index,
    design_tiles,
):
    nx, ny, depth = permittivity.shape
    plan = Plan(nx, ny)
    groups = lax.axis_size("angle")
    wide, ring = plan.wide, plan.ring

    def array(*shape):
        return jax.ShapeDtypeStruct(shape, jnp.float32)

    def lines(count):
        return array(count, depth)

    def params(mib):
        return pltpu.CompilerParams(vmem_limit_bytes=mib * 2**20)

    def cost(size):
        return pl.CostEstimate(flops=size, bytes_accessed=size, transcendentals=0)

    assert lax.axis_size("gx") % 2 == 0
    with jax.named_scope("pack_y"):
        *first, coef, z_up = pl.pallas_call(
            functools.partial(pack_y_kernel, plan),
            out_shape=(*[array(12, wide, ring, depth)] * 4, array(wide, ring, depth), lines(plan.y_low.lines)),
            in_specs=[HBM] * 3,
            out_specs=[VMEM] * 6,
            scratch_shapes=[pltpu.SemaphoreType.DMA((25,))],
            compiler_params=params(8),
        )(*(pltpu.with_memory_space_constraint(array, pltpu.HBM) for array in (forward_fields[0], adjoint_fields[0], permittivity)))
    first = [state.reshape((-1, depth)) for state in (*first, coef)]
    with jax.named_scope("send_y_up"):
        z_low = lax.ppermute(z_up, "gy", ring_pairs("gy", 1))
    with jax.named_scope("pack_x"):
        to_far, to_mate = pl.pallas_call(
            functools.partial(pack_x_kernel, plan),
            out_shape=[lines(plan.x_lines)] * 2,
            in_specs=[VMEM] * 5,
            out_specs=[VMEM] * 2,
            compiler_params=params(8),
        )(*first)
    with jax.named_scope("send_x"):
        x_far = lax.ppermute(to_far, "gx", far_pairs())
        x_mate = lax.ppermute(to_mate, "gx", mate_pairs())
    with jax.named_scope("pack_y_down"):
        z_down = pl.pallas_call(
            functools.partial(pack_down_kernel, plan),
            out_shape=lines(plan.y_high.lines),
            in_specs=[VMEM] * 6,
            out_specs=VMEM,
            compiler_params=params(8),
        )(*first, x_mate)
    with jax.named_scope("send_y_down"):
        z_high = lax.ppermute(z_down, "gy", ring_pairs("gy", -1))
    with jax.named_scope("turns"):
        turns = pl.pallas_call(
            functools.partial(turns_kernel, groups),
            out_shape=lines(3 * SUB),
            in_specs=[SMEM] * 3,
            out_specs=VMEM,
            compiler_params=params(4),
        )(phase_table, angle_index, design_tiles)
    with jax.named_scope("relay_corners"):
        to_far, to_mate = pl.pallas_call(
            functools.partial(relay_kernel, plan),
            out_shape=[lines(plan.corner_lines)] * 2,
            in_specs=[VMEM] * 2,
            out_specs=[VMEM] * 2,
            compiler_params=params(4),
        )(z_low, z_high)
        far = lax.ppermute(to_far, "gx", far_pairs())
        mate = lax.ppermute(to_mate, "gx", mate_pairs())
    level = lines(12 * wide * ring)
    count = 2 * STEPS + 3
    levels = [level] * (count - 1) + [lines(wide * ring)]
    with jax.named_scope("middle"):
        state = pl.pallas_call(
            functools.partial(middle_kernel, plan),
            out_shape=levels,
            in_specs=[VMEM] * 8,
            out_specs=[VMEM] * count,
            input_output_aliases={0: 0, 1: STEPS + 1, 2: 1, 3: STEPS + 2, 4: count - 1},
            compiler_params=params(8),
            cost_estimate=cost(2**31),
        )(*first, z_low, z_high, turns)
    with jax.named_scope("edges"):
        spectra = [spectrum.reshape((-1, depth)) for spectrum in (forward_spectrum, adjoint_spectrum)]
        *_, tr_f, tr_a, parts = pl.pallas_call(
            functools.partial(edges_kernel, plan, groups),
            out_shape=[*levels, lines(6 * nx * ny), lines(6 * nx * ny), array(groups, nx * ny, depth // groups)],
            in_specs=[VMEM] * (count + 9),
            out_specs=[VMEM] * (count + 3),
            input_output_aliases={i: i for i in range(count)},
            compiler_params=params(8),
        )(*state, x_far, x_mate, far, mate, z_low, z_high, turns, *spectra)
    with jax.named_scope("sum_angles"):
        gradient = parts[0]
        for k in range(1, groups):
            gradient = gradient + lax.ppermute(parts[k], "angle", ring_pairs("angle", k))
    with jax.named_scope("write"):
        out_f, out_a = pl.pallas_call(
            write_kernel,
            out_shape=[array(6, nx, ny, depth)] * 2,
            in_specs=[VMEM] * 2,
            out_specs=[HBM] * 2,
            scratch_shapes=[pltpu.SemaphoreType.DMA((12,))],
            compiler_params=params(4),
        )(tr_f.reshape((6, nx, ny, depth)), tr_a.reshape((6, nx, ny, depth)))
    return (
        out_f.reshape(forward_spectrum.shape),
        out_a.reshape(adjoint_spectrum.shape),
        gradient.reshape((nx, ny, depth // groups)),
    )


def solution(mesh):
    in_specs = (
        P("angle", None, "gx", "gy", None),
        P("angle", None, "gx", "gy", None),
        P("angle", None, "gx", "gy", None),
        P("angle", None, "gx", "gy", None),
        P("gx", "gy", None),
        P(),
        P("angle"),
        P(),
    )
    out_specs = (
        P("angle", None, "gx", "gy", None),
        P("angle", None, "gx", "gy", None),
        P("gx", "gy", "angle"),
    )
    return jax.shard_map(shards, mesh=mesh, in_specs=in_specs, out_specs=out_specs, check_vma=False)
```

```python
import functools
import math

import jax
import jax.numpy as jnp
from jax import lax
from jax.experimental import pallas as pl
from jax.experimental.pallas import tpu as pltpu
from jax.sharding import PartitionSpec as P

STEPS = 3
SUB = 8

courant = 0.5
omega_step = 0.7

VMEM = pl.BlockSpec(memory_space=pltpu.VMEM)
SMEM = pl.BlockSpec(memory_space=pltpu.SMEM)
HBM = pl.BlockSpec(memory_space=pltpu.HBM)


def reads(node):
    kind, level, comp, x, y = node
    others = [c for c in range(3) if c != comp]
    if kind == "E":
        found = [("E", level - 1, comp, x, y), ("C", 0, 0, x, y)] + [("H", level, c, x, y) for c in others]
        if comp != 1:
            found.append(("H", level, 2 - comp, x, y - 1))
        if comp != 0:
            found.append(("H", level, 3 - comp, x - 1, y))
        return found
    found = [("H", level - 1, comp, x, y)] + [("E", level - 1, c, x, y) for c in others]
    if comp != 1:
        found.append(("E", level - 1, 2 - comp, x, y + 1))
    if comp != 0:
        found.append(("E", level - 1, 3 - comp, x + 1, y))
    return found


def wanted(nx, ny):
    def block(node):
        return node[3] // nx, node[4] // ny

    @functools.cache
    def alone(node):
        if node[1] == 0:
            return True
        return node[1] == 1 and all(block(other) == block(node) and alone(other) for other in reads(node))

    found, seen = set(), set()
    todo = [("E", STEPS, comp, x, y) for comp in range(3) for x in range(nx) for y in range(ny)]
    while todo:
        node = todo.pop()
        if node in seen:
            continue
        seen.add(node)
        if block(node) != (0, 0) and alone(node):
            found.add(node)
        elif node[1]:
            todo += reads(node)
    return found


class Message:
    def __init__(self, nodes, axis):
        self.axis, self.runs, self.at, self.size = axis, [], {}, 0
        stretches = []
        for node in sorted(nodes):
            before = list(node)
            before[3 + axis] -= 1
            if tuple(before) in nodes:
                continue
            count = 1
            while (*node[:3], node[3] + count * (axis == 0), node[4] + count * (axis == 1)) in nodes:
                count += 1
            stretches.append((count, node))
        for count, (kind, level, comp, x, y) in sorted(stretches, key=lambda item: (-item[0], item[1])):
            for run in (0, 1) if kind != "C" else (0,):
                for part in (0, 1) if kind != "C" else (0,):
                    what = (kind, level, comp, run, part)
                    self.runs.append((what, x, y, count, self.size))
                    for i in range(count):
                        self.at[what, x + i * (axis == 0), y + i * (axis == 1)] = self.size + i
                    self.size += count
        self.lines = -(-self.size // SUB) * SUB


class Plan:
    def __init__(self, nx, ny):
        self.nx, self.ny = nx, ny
        self.wide, self.ring = nx + 2 * STEPS, ny + SUB
        nodes = wanted(nx, ny)
        sides = {}
        for node in nodes:
            sides.setdefault((node[3] // nx, node[4] // ny), set()).add(node)

        def shifted(found, dx):
            return {(*node[:3], node[3] + dx, node[4]) for node in found}

        self.y_low, self.y_high = (
            Message(sides[0, side] | shifted(sides[-1, side], nx) | shifted(sides[1, side], -nx), 0) for side in (-1, 1)
        )
        self.x_low, self.x_high = Message(sides[-1, 0], 1), Message(sides[1, 0], 1)
        self.mate_side, self.far_side = (1, -1), (-1, 1)
        self.mate, self.far = ([Message(sides[side, -1] | sides[side, 1], 1) for side in order] for order in (self.mate_side, self.far_side))
        self.corner_lines = max(message.lines for message in self.mate)

    def row(self, x, y, run=0, part=0, comp=0):
        return ((run * 6 + part * 3 + comp) * self.wide + x + STEPS) * self.ring + y % self.ring

    def rows(self, what, x, y, axis, count):
        _, _, comp, run, part = what
        start = self.row(x, y, run, part, comp)
        return pl.ds(start, count, stride=self.ring) if axis == 0 and count > 1 else pl.ds(start, count)


class State:
    def __init__(self, efield, hfield, coef):
        self.by_kind = {"E": efield, "H": hfield, "C": [coef]}

    def __call__(self, what):
        return self.by_kind[what[0]][what[1]]


def pack(plan, message, state, dx, dy, out):
    for what, x, y, count, at in message.runs:
        out[pl.ds(at, count), :] = state(what)[plan.rows(what, x + dx, y + dy, message.axis, count), :]


def by_parity(offset, body):
    parity = lax.rem(lax.axis_index("gx") + offset, 2)
    for value in (0, 1):
        pl.when(parity == value)(functools.partial(body, value))


def pack_y_kernel(plan, fwd, adj, eps, e0, h0, e1, h1, coef, z_up, z_down, sems):
    nx, ny = plan.nx, plan.ny
    own = (pl.ds(STEPS, nx), pl.ds(0, ny), slice(None))
    copies = [pltpu.make_async_copy(eps, coef.at[own], sems.at[0])]
    for run, ref in enumerate((fwd, adj)):
        for kind, array in enumerate((e0, h0)):
            for i in range(6):
                copies.append(
                    pltpu.make_async_copy(ref.at[kind * 6 + i], array.at[(run * 6 + i, *own)], sems.at[len(copies)])
                )
    for copy in copies:
        copy.start()
    copies[0].wait()
    for x in range(nx):
        coef[STEPS + x, pl.ds(0, ny), :] = (0.5 * courant) / coef[STEPS + x, pl.ds(0, ny), :]
    e0, h0, e1, h1, coef = (array.reshape((-1, array.shape[-1])) for array in (e0, h0, e1, h1, coef))
    sweeps = Sweeps(plan, [e0, e1], [h0, h1], coef, ny)
    for run in (0, 1):
        for copy in copies[1 + 12 * run : 13 + 12 * run]:
            copy.wait()
        sweeps.both(1, range(nx), range(nx - 1), runs=(run,))
    state = State([e0, e1], [h0, h1], coef)
    pack(plan, plan.y_low, state, 0, ny, z_up)
    pack(plan, plan.y_high, state, 0, -ny, z_down)


def pack_x_kernel(plan, e0, h0, e1, h1, coef, x_up, x_down):
    state = State([e0, e1], [h0, h1], coef)
    pack(plan, plan.x_low, state, plan.nx, 0, x_up)
    pack(plan, plan.x_high, state, -plan.nx, 0, x_down)


def turns_kernel(groups, table, index, tiles, turns):
    row = index[0]
    phi_x, phi_y = table[row, 0], table[row, 1]
    at_x, at_y = lax.axis_index("gx"), lax.axis_index("gy")
    none = jnp.float32(0.0)
    ax_low = jnp.where(at_x == 0, -phi_x, none)
    ax_high = jnp.where(at_x == lax.axis_size("gx") - 1, phi_x, none)
    ay_low = jnp.where(at_y == 0, -phi_y, none)
    ay_high = jnp.where(at_y == lax.axis_size("gy") - 1, phi_y, none)
    sub = lax.broadcasted_iota(jnp.int32, (SUB, turns.shape[1]), 0)
    angles = jnp.zeros(sub.shape, jnp.float32)
    for i, angle in enumerate((ax_low, ax_high, ay_low, ay_high, ax_low + ay_low, ax_low + ay_high,
                               ax_high + ay_low, ax_high + ay_high)):
        angles = jnp.where(sub == i, angle, angles)
    turns[pl.ds(0, SUB), :] = jnp.cos(angles)
    turns[pl.ds(SUB, SUB), :] = jnp.sin(angles)
    own_tile = at_x * lax.axis_size("gy") + at_y
    chosen = tiles[0] == own_tile
    for i in range(1, tiles.shape[0]):
        chosen = jnp.logical_or(chosen, tiles[i] == own_tile)
    weight = jnp.where(chosen, jnp.float32(1.0 / groups), none)
    turns[pl.ds(2 * SUB, SUB), :] = jnp.full(sub.shape, weight, jnp.float32)


def relay_kernel(plan, z_low, z_high, to_far, to_mate):
    def corners(receiver):
        for messages, side, out in ((plan.far, plan.far_side, to_far), (plan.mate, plan.mate_side, to_mate)):
            dx = -plan.nx * side[receiver]
            for (what, x, y), row in messages[receiver].at.items():
                ref, source = (z_low, plan.y_low) if y < 0 else (z_high, plan.y_high)
                out[pl.ds(row, 1), :] = ref[pl.ds(source.at[what, x + dx, y], 1), :]

    by_parity(1, corners)


def turned(real, imag, cosine, sine):
    return real * cosine - imag * sine, real * sine + imag * cosine


def unpack(plan, message, ref, which, turns, state, kinds, level, layers=None):
    axis = message.axis
    for (kind, at_level, comp, run, part), x, y, count, at in message.runs:
        if kind not in kinds or at_level != level or part == 1:
            continue
        pieces = [(x, y, count, at)]
        if layers is not None:
            pieces = [(x + i, y, 1, at + i) for i in range(count) if x + i in layers]
        for cell_x, cell_y, size, row in pieces:
            what = (kind, at_level, comp, run, 0)
            real = ref[pl.ds(row, size), :]
            if kind == "C":
                state(what)[plan.rows(what, cell_x, cell_y, axis, size), :] = real
                continue
            twin = (kind, at_level, comp, run, 1)
            imag = ref[pl.ds(message.at[twin, cell_x, cell_y], size), :]
            turn = which(y)
            cosine, sine = turns[pl.ds(turn, 1), :], turns[pl.ds(SUB + turn, 1), :]
            real, imag = turned(real, imag, cosine, sine if run == 0 else -sine)
            state(what)[plan.rows(what, cell_x, cell_y, axis, size), :] = real
            state(twin)[plan.rows(twin, cell_x, cell_y, axis, size), :] = imag


class Sweeps:
    def __init__(self, plan, efield, hfield, coef, height):
        self.plan, self.efield, self.hfield, self.coef, self.height = plan, efield, hfield, coef, height

    def rows(self, run, part, comp, x, height=None):
        return pl.ds(self.plan.row(x, 0, run, part, comp), height or self.height)

    def next_z(self, value):
        lane = lax.broadcasted_iota(jnp.int32, value.shape, 1)
        return jnp.where(lane == value.shape[1] - 1, 0.0, pltpu.roll(value, value.shape[1] - 1, 1))

    def prev_z(self, value):
        lane = lax.broadcasted_iota(jnp.int32, value.shape, 1)
        return jnp.where(lane == 0, 0.0, pltpu.roll(value, 1, 1))

    def next_y(self, value):
        return pltpu.roll(value, self.height - 1, 0)

    def prev_y(self, value):
        return pltpu.roll(value, 1, 0)

    def update_h(self, step, run, part, x):
        efield, old, new = self.efield[step - 1], self.hfield[step - 1], self.hfield[step]
        ex, ey, ez = (efield[self.rows(run, part, comp, x), :] for comp in range(3))
        ey_x, ez_x = (efield[self.rows(run, part, comp, x + 1), :] for comp in (1, 2))
        hx, hy, hz = (old[self.rows(run, part, comp, x), :] for comp in range(3))
        if step == 1:
            hx, hy, hz = hx + hx, hy + hy, hz + hz
        new[self.rows(run, part, 0, x), :] = hx - ((self.next_y(ez) - ez) - (self.next_z(ey) - ey))
        new[self.rows(run, part, 2, x), :] = hz - ((ey_x - ey) - (self.next_y(ex) - ex))
        height = self.last_height(step)
        ex, ez, ez_x, hy = (value[:height] for value in (ex, ez, ez_x, hy))
        new[self.rows(run, part, 1, x, height), :] = hy - ((self.next_z(ex) - ex) - (ez_x - ez))

    def update_e(self, step, run, part, x):
        old, new, hfield = self.efield[step - 1], self.efield[step], self.hfield[step]
        height = self.last_height(step)
        ex, ey, ez = (old[self.rows(run, part, comp, x, height), :] for comp in range(3))
        hx, hz = (hfield[self.rows(run, part, comp, x), :] for comp in (0, 2))
        hx_y, hz_y = self.prev_y(hx)[:height], self.prev_y(hz)[:height]
        hx, hz = hx[:height], hz[:height]
        hy = hfield[self.rows(run, part, 1, x, height), :]
        hy_x, hz_x = (hfield[self.rows(run, part, comp, x - 1, height), :] for comp in (1, 2))
        scale = self.coef[self.rows(0, 0, 0, x, height), :]
        new[self.rows(run, part, 0, x, height), :] = ex + scale * ((hz - hz_y) - (hy - self.prev_z(hy)))
        new[self.rows(run, part, 1, x, height), :] = ey + scale * ((hx - self.prev_z(hx)) - (hz - hz_x))
        new[self.rows(run, part, 2, x, height), :] = ez + scale * ((hy - hy_x) - (hx - hx_y))

    def last_height(self, step):
        return self.plan.ny if step == STEPS else self.height

    def both(self, step, h_layers, e_layers, after_h=None, after_e=None, runs=(0, 1)):
        for update, layers, after in ((self.update_h, h_layers, after_h), (self.update_e, e_layers, after_e)):
            for x in layers:
                for run in runs:
                    for part in (0, 1):
                        update(step, run, part, x)
            if after is not None:
                after()


def middle_kernel(plan, e0_in, h0_in, e1_in, h1_in, coef_in, z_low, z_high, turns, *arrays):
    nx = plan.nx
    efield, hfield, coef = arrays[: STEPS + 1], arrays[STEPS + 1 : 2 * STEPS + 2], arrays[-1]
    state = State(efield, hfield, coef)

    def take(kinds, level):
        unpack(plan, plan.y_low, z_low, lambda y: 2, turns, state, kinds, level)
        unpack(plan, plan.y_high, z_high, lambda y: 3, turns, state, kinds, level)

    take("EHC", 0)
    sweeps = Sweeps(plan, efield, hfield, coef, plan.ring)
    for step in range(1, STEPS + 1):
        after = [lambda: take("H", 1), lambda: take("E", 1)] if step == 1 else []
        sweeps.both(step, range(step - 1, nx - step), range(step, nx - step), *after)


def edges_kernel(plan, groups, *refs):
    nx, ny = plan.nx, plan.ny
    count = 2 * STEPS + 3
    x_low, x_high, far, mate, z_low, z_high, turns, spec_f, spec_a = refs[count : count + 9]
    arrays = refs[count + 9 : 2 * count + 9]
    out_f, out_a, parts = refs[2 * count + 9 :]
    efield, hfield, coef = arrays[: STEPS + 1], arrays[STEPS + 1 : 2 * STEPS + 2], arrays[-1]
    state = State(efield, hfield, coef)

    def take(kinds, level, layers=()):
        unpack(plan, plan.x_low, x_low, lambda y: 0, turns, state, kinds, level)
        unpack(plan, plan.x_high, x_high, lambda y: 1, turns, state, kinds, level)

        def corners(receiver):
            for messages, ref, side in ((plan.far, far, plan.far_side), (plan.mate, mate, plan.mate_side)):
                first = 4 if side[receiver] < 0 else 6
                unpack(plan, messages[receiver], ref, lambda y: first + (y >= 0), turns, state, kinds, level)

        by_parity(0, corners)
        unpack(plan, plan.y_low, z_low, lambda y: 2, turns, state, kinds, level, layers)
        unpack(plan, plan.y_high, z_high, lambda y: 3, turns, state, kinds, level, layers)

    take("EHC", 0)
    sweeps = Sweeps(plan, efield, hfield, coef, plan.ring)
    for step in range(1, STEPS + 1):
        low, high = step - STEPS, nx - step
        h_layers = [*range(low - 1, step - 1), *range(high, nx + STEPS - step)]
        e_layers = [*range(low, step), *range(high, nx + STEPS - step)]
        after = []
        if step == 1:
            after = [functools.partial(take, "H", 1, h_layers), functools.partial(take, "E", 1, e_layers)]
        sweeps.both(step, h_layers, e_layers, *after)

    share = parts.shape[2]
    shift = lax.rem(groups - lax.axis_index("angle"), groups) * share
    weight = turns[pl.ds(2 * SUB, SUB), :]
    tiles = ny // SUB

    for i in range(nx * tiles):
        x, tile = i // tiles, i % tiles
        total = jnp.zeros(weight.shape, jnp.float32)
        for comp in range(3):
            ends = []
            for run, (spec, out) in enumerate(((spec_f, out_f), (spec_a, out_a))):
                at = [pl.ds(((part * 3 + comp) * nx + x) * ny + tile * SUB, SUB) for part in (0, 1)]
                real, imag = spec[at[0], :], spec[at[1], :]
                for step in range(1, STEPS + 1):
                    theta = omega_step * step
                    ends_e = [
                        efield[step][pl.ds(plan.row(x, tile * SUB, run, part, comp), SUB), :]
                        for part in (0, 1)
                    ]
                    more = turned(*ends_e, math.cos(theta), math.sin(theta))
                    real, imag = real + more[0], imag + more[1]
                out[at[0], :], out[at[1], :] = real, imag
                ends.append((real, imag))
            total = total + (ends[0][0] * ends[1][0] - ends[0][1] * ends[1][1])
        total = pltpu.roll(total * weight, shift, 1)
        for k in range(groups):
            parts[k, pl.ds(i * SUB, SUB), :] = total[:, k * share : (k + 1) * share]


def write_kernel(tr_f, tr_a, out_f, out_a, sems):
    copies = []
    for source, target in ((tr_f, out_f), (tr_a, out_a)):
        for i in range(source.shape[0]):
            copies.append(pltpu.make_async_copy(source.at[i], target.at[i], sems.at[len(copies)]))
    for copy in copies:
        copy.start()
    for copy in copies:
        copy.wait()


def ring_pairs(axis, offset):
    size = lax.axis_size(axis)
    return [(i, (i + offset) % size) for i in range(size)]


def mate_pairs():
    return [(i, i ^ 1) for i in range(lax.axis_size("gx"))]


def far_pairs():
    size = lax.axis_size("gx")
    return [(i, (i + (1 if i % 2 else -1)) % size) for i in range(size)]


def shards(
    forward_fields,
    adjoint_fields,
    forward_spectrum,
    adjoint_spectrum,
    permittivity,
    phase_table,
    angle_index,
    design_tiles,
):
    nx, ny, depth = permittivity.shape
    plan = Plan(nx, ny)
    groups = lax.axis_size("angle")
    wide, ring = plan.wide, plan.ring

    def array(*shape):
        return jax.ShapeDtypeStruct(shape, jnp.float32)

    def lines(count):
        return array(count, depth)

    def params(mib):
        return pltpu.CompilerParams(vmem_limit_bytes=mib * 2**20)

    def cost(size):
        return pl.CostEstimate(flops=size, bytes_accessed=size, transcendentals=0)

    assert lax.axis_size("gx") % 2 == 0
    with jax.named_scope("pack_y"):
        *first, coef, z_up, z_down = pl.pallas_call(
            functools.partial(pack_y_kernel, plan),
            out_shape=(
                *[array(12, wide, ring, depth)] * 4,
                array(wide, ring, depth),
                lines(plan.y_low.lines),
                lines(plan.y_high.lines),
            ),
            in_specs=[HBM] * 3,
            out_specs=[VMEM] * 7,
            scratch_shapes=[pltpu.SemaphoreType.DMA((25,))],
            compiler_params=params(8),
        )(*(pltpu.with_memory_space_constraint(array, pltpu.HBM) for array in (forward_fields[0], adjoint_fields[0], permittivity)))
    e0, h0, e1, h1, coef = (state.reshape((-1, depth)) for state in (*first, coef))
    with jax.named_scope("send_y"):
        z_low = lax.ppermute(z_up, "gy", ring_pairs("gy", 1))
        z_high = lax.ppermute(z_down, "gy", ring_pairs("gy", -1))
    with jax.named_scope("pack_x"):
        x_up, x_down = pl.pallas_call(
            functools.partial(pack_x_kernel, plan),
            out_shape=(lines(plan.x_low.lines), lines(plan.x_high.lines)),
            in_specs=[VMEM] * 5,
            out_specs=[VMEM] * 2,
            compiler_params=params(8),
            cost_estimate=cost(40 * 2**20),
        )(e0, h0, e1, h1, coef)
    with jax.named_scope("send_x"):
        x_low = lax.ppermute(x_up, "gx", ring_pairs("gx", 1))
        x_high = lax.ppermute(x_down, "gx", ring_pairs("gx", -1))
    with jax.named_scope("turns"):
        turns = pl.pallas_call(
            functools.partial(turns_kernel, groups),
            out_shape=lines(3 * SUB),
            in_specs=[SMEM] * 3,
            out_specs=VMEM,
            compiler_params=params(4),
        )(phase_table, angle_index, design_tiles)
    with jax.named_scope("relay_corners"):
        to_far, to_mate = pl.pallas_call(
            functools.partial(relay_kernel, plan),
            out_shape=[lines(plan.corner_lines)] * 2,
            in_specs=[VMEM] * 2,
            out_specs=[VMEM] * 2,
            compiler_params=params(4),
        )(z_low, z_high)
        far = lax.ppermute(to_far, "gx", far_pairs())
        mate = lax.ppermute(to_mate, "gx", mate_pairs())
    level = lines(12 * wide * ring)
    count = 2 * STEPS + 3
    levels = [level] * (count - 1) + [lines(wide * ring)]
    with jax.named_scope("middle"):
        state = pl.pallas_call(
            functools.partial(middle_kernel, plan),
            out_shape=levels,
            in_specs=[VMEM] * 8,
            out_specs=[VMEM] * count,
            input_output_aliases={0: 0, 1: STEPS + 1, 2: 1, 3: STEPS + 2, 4: count - 1},
            compiler_params=params(8),
            cost_estimate=cost(2**32),
        )(e0, h0, e1, h1, coef, z_low, z_high, turns)
    with jax.named_scope("edges"):
        spectra = [spectrum.reshape((-1, depth)) for spectrum in (forward_spectrum, adjoint_spectrum)]
        *_, tr_f, tr_a, parts = pl.pallas_call(
            functools.partial(edges_kernel, plan, groups),
            out_shape=[*levels, lines(6 * nx * ny), lines(6 * nx * ny), array(groups, nx * ny, depth // groups)],
            in_specs=[VMEM] * (count + 9),
            out_specs=[VMEM] * (count + 3),
            input_output_aliases={i: i for i in range(count)},
            compiler_params=params(8),
        )(*state, x_low, x_high, far, mate, z_low, z_high, turns, *spectra)
    with jax.named_scope("sum_angles"):
        gradient = parts[0]
        for k in range(1, groups):
            gradient = gradient + lax.ppermute(parts[k], "angle", ring_pairs("angle", k))
    with jax.named_scope("write"):
        out_f, out_a = pl.pallas_call(
            write_kernel,
            out_shape=[array(6, nx, ny, depth)] * 2,
            in_specs=[VMEM] * 2,
            out_specs=[HBM] * 2,
            scratch_shapes=[pltpu.SemaphoreType.DMA((12,))],
            compiler_params=params(4),
        )(tr_f.reshape((6, nx, ny, depth)), tr_a.reshape((6, nx, ny, depth)))
    return (
        out_f.reshape(forward_spectrum.shape),
        out_a.reshape(adjoint_spectrum.shape),
        gradient.reshape((nx, ny, depth // groups)),
    )


def solution(mesh):
    in_specs = (
        P("angle", None, "gx", "gy", None),
        P("angle", None, "gx", "gy", None),
        P("angle", None, "gx", "gy", None),
        P("angle", None, "gx", "gy", None),
        P("gx", "gy", None),
        P(),
        P("angle"),
        P(),
    )
    out_specs = (
        P("angle", None, "gx", "gy", None),
        P("angle", None, "gx", "gy", None),
        P("gx", "gy", "angle"),
    )
    return jax.shard_map(shards, mesh=mesh, in_specs=in_specs, out_specs=out_specs, check_vma=False)
```

```python
import functools
import math

import jax
import jax.numpy as jnp
from jax import lax
from jax.experimental import pallas as pl
from jax.experimental.pallas import tpu as pltpu
from jax.sharding import PartitionSpec as P

STEPS = 3
SUB = 8

courant = 0.5
omega_step = 0.7

VMEM = pl.BlockSpec(memory_space=pltpu.VMEM)
SMEM = pl.BlockSpec(memory_space=pltpu.SMEM)
HBM = pl.BlockSpec(memory_space=pltpu.HBM)


def reads(node):
    kind, level, comp, x, y = node
    others = [c for c in range(3) if c != comp]
    if kind == "E":
        found = [("E", level - 1, comp, x, y), ("C", 0, 0, x, y)] + [("H", level, c, x, y) for c in others]
        if comp != 1:
            found.append(("H", level, 2 - comp, x, y - 1))
        if comp != 0:
            found.append(("H", level, 3 - comp, x - 1, y))
        return found
    found = [("H", level - 1, comp, x, y)] + [("E", level - 1, c, x, y) for c in others]
    if comp != 1:
        found.append(("E", level - 1, 2 - comp, x, y + 1))
    if comp != 0:
        found.append(("E", level - 1, 3 - comp, x + 1, y))
    return found


def wanted(nx, ny):
    def block(node):
        return node[3] // nx, node[4] // ny

    @functools.cache
    def alone(node):
        if node[1] == 0:
            return True
        return node[1] == 1 and all(block(other) == block(node) and alone(other) for other in reads(node))

    found, seen = set(), set()
    todo = [("E", STEPS, comp, x, y) for comp in range(3) for x in range(nx) for y in range(ny)]
    while todo:
        node = todo.pop()
        if node in seen:
            continue
        seen.add(node)
        if block(node) != (0, 0) and alone(node):
            found.add(node)
        elif node[1]:
            todo += reads(node)
    return found


class Message:
    def __init__(self, nodes, axis):
        self.axis, self.runs, self.at, self.size = axis, [], {}, 0
        stretches = []
        for node in sorted(nodes):
            before = list(node)
            before[3 + axis] -= 1
            if tuple(before) in nodes:
                continue
            count = 1
            while (*node[:3], node[3] + count * (axis == 0), node[4] + count * (axis == 1)) in nodes:
                count += 1
            stretches.append((count, node))
        for count, (kind, level, comp, x, y) in sorted(stretches, key=lambda item: (-item[0], item[1])):
            for run in (0, 1) if kind != "C" else (0,):
                for part in (0, 1) if kind != "C" else (0,):
                    what = (kind, level, comp, run, part)
                    self.runs.append((what, x, y, count, self.size))
                    for i in range(count):
                        self.at[what, x + i * (axis == 0), y + i * (axis == 1)] = self.size + i
                    self.size += count
        self.lines = -(-self.size // SUB) * SUB


class Plan:
    def __init__(self, nx, ny):
        self.nx, self.ny = nx, ny
        self.wide, self.ring = nx + 2 * STEPS, ny + SUB
        nodes = wanted(nx, ny)
        sides = {}
        for node in nodes:
            sides.setdefault((node[3] // nx, node[4] // ny), set()).add(node)

        def shifted(found, dx):
            return {(*node[:3], node[3] + dx, node[4]) for node in found}

        self.y_low, self.y_high = (
            Message(sides[0, side] | shifted(sides[-1, side], nx) | shifted(sides[1, side], -nx), 0) for side in (-1, 1)
        )
        self.x_low, self.x_high = Message(sides[-1, 0], 1), Message(sides[1, 0], 1)
        self.mate_side, self.far_side = (1, -1), (-1, 1)
        self.mate, self.far = ([Message(sides[side, -1] | sides[side, 1], 1) for side in order] for order in (self.mate_side, self.far_side))
        self.corner_lines = max(message.lines for message in self.mate)

    def row(self, x, y, run=0, part=0, comp=0):
        return ((run * 6 + part * 3 + comp) * self.wide + x + STEPS) * self.ring + y % self.ring

    def rows(self, what, x, y, axis, count):
        _, _, comp, run, part = what
        start = self.row(x, y, run, part, comp)
        return pl.ds(start, count, stride=self.ring) if axis == 0 and count > 1 else pl.ds(start, count)


class State:
    def __init__(self, efield, hfield, coef):
        self.by_kind = {"E": efield, "H": hfield, "C": [coef]}

    def __call__(self, what):
        return self.by_kind[what[0]][what[1]]


def pack(plan, message, state, dx, dy, out):
    for what, x, y, count, at in message.runs:
        out[pl.ds(at, count), :] = state(what)[plan.rows(what, x + dx, y + dy, message.axis, count), :]


def by_parity(offset, body):
    parity = lax.rem(lax.axis_index("gx") + offset, 2)
    for value in (0, 1):
        pl.when(parity == value)(functools.partial(body, value))


def pack_y_kernel(plan, fwd, adj, eps, e0, h0, e1, h1, coef, z_up, z_down, sems):
    nx, ny = plan.nx, plan.ny
    own = (pl.ds(STEPS, nx), pl.ds(0, ny), slice(None))
    copies = [pltpu.make_async_copy(eps, coef.at[own], sems.at[0])]
    for run, ref in enumerate((fwd, adj)):
        for kind, array in enumerate((e0, h0)):
            for i in range(6):
                copies.append(
                    pltpu.make_async_copy(ref.at[kind * 6 + i], array.at[(run * 6 + i, *own)], sems.at[len(copies)])
                )
    for copy in copies:
        copy.start()
    copies[0].wait()
    for x in range(nx):
        coef[STEPS + x, pl.ds(0, ny), :] = (0.5 * courant) / coef[STEPS + x, pl.ds(0, ny), :]
    e0, h0, e1, h1, coef = (array.reshape((-1, array.shape[-1])) for array in (e0, h0, e1, h1, coef))
    sweeps = Sweeps(plan, [e0, e1], [h0, h1], coef, ny)
    for run in (0, 1):
        for copy in copies[1 + 12 * run : 13 + 12 * run]:
            copy.wait()
        sweeps.both(1, range(nx), range(nx - 1), runs=(run,))
    state = State([e0, e1], [h0, h1], coef)
    pack(plan, plan.y_low, state, 0, ny, z_up)
    pack(plan, plan.y_high, state, 0, -ny, z_down)


def pack_x_kernel(plan, e0, h0, e1, h1, coef, x_up, x_down):
    state = State([e0, e1], [h0, h1], coef)
    pack(plan, plan.x_low, state, plan.nx, 0, x_up)
    pack(plan, plan.x_high, state, -plan.nx, 0, x_down)


def turns_kernel(groups, table, index, tiles, turns):
    row = index[0]
    phi_x, phi_y = table[row, 0], table[row, 1]
    at_x, at_y = lax.axis_index("gx"), lax.axis_index("gy")
    none = jnp.float32(0.0)
    ax_low = jnp.where(at_x == 0, -phi_x, none)
    ax_high = jnp.where(at_x == lax.axis_size("gx") - 1, phi_x, none)
    ay_low = jnp.where(at_y == 0, -phi_y, none)
    ay_high = jnp.where(at_y == lax.axis_size("gy") - 1, phi_y, none)
    sub = lax.broadcasted_iota(jnp.int32, (SUB, turns.shape[1]), 0)
    angles = jnp.zeros(sub.shape, jnp.float32)
    for i, angle in enumerate((ax_low, ax_high, ay_low, ay_high, ax_low + ay_low, ax_low + ay_high,
                               ax_high + ay_low, ax_high + ay_high)):
        angles = jnp.where(sub == i, angle, angles)
    turns[pl.ds(0, SUB), :] = jnp.cos(angles)
    turns[pl.ds(SUB, SUB), :] = jnp.sin(angles)
    own_tile = at_x * lax.axis_size("gy") + at_y
    chosen = tiles[0] == own_tile
    for i in range(1, tiles.shape[0]):
        chosen = jnp.logical_or(chosen, tiles[i] == own_tile)
    weight = jnp.where(chosen, jnp.float32(1.0 / groups), none)
    turns[pl.ds(2 * SUB, SUB), :] = jnp.full(sub.shape, weight, jnp.float32)


def relay_kernel(plan, z_low, z_high, to_far, to_mate):
    def corners(receiver):
        for messages, side, out in ((plan.far, plan.far_side, to_far), (plan.mate, plan.mate_side, to_mate)):
            dx = -plan.nx * side[receiver]
            for (what, x, y), row in messages[receiver].at.items():
                ref, source = (z_low, plan.y_low) if y < 0 else (z_high, plan.y_high)
                out[pl.ds(row, 1), :] = ref[pl.ds(source.at[what, x + dx, y], 1), :]

    by_parity(1, corners)


def turned(real, imag, cosine, sine):
    return real * cosine - imag * sine, real * sine + imag * cosine


def unpack(plan, message, ref, which, turns, state, kinds, level, layers=None):
    axis = message.axis
    for (kind, at_level, comp, run, part), x, y, count, at in message.runs:
        if kind not in kinds or at_level != level or part == 1:
            continue
        pieces = [(x, y, count, at)]
        if layers is not None:
            pieces = [(x + i, y, 1, at + i) for i in range(count) if x + i in layers]
        for cell_x, cell_y, size, row in pieces:
            what = (kind, at_level, comp, run, 0)
            real = ref[pl.ds(row, size), :]
            if kind == "C":
                state(what)[plan.rows(what, cell_x, cell_y, axis, size), :] = real
                continue
            twin = (kind, at_level, comp, run, 1)
            imag = ref[pl.ds(message.at[twin, cell_x, cell_y], size), :]
            turn = which(y)
            cosine, sine = turns[pl.ds(turn, 1), :], turns[pl.ds(SUB + turn, 1), :]
            real, imag = turned(real, imag, cosine, sine if run == 0 else -sine)
            state(what)[plan.rows(what, cell_x, cell_y, axis, size), :] = real
            state(twin)[plan.rows(twin, cell_x, cell_y, axis, size), :] = imag


class Sweeps:
    def __init__(self, plan, efield, hfield, coef, height):
        self.plan, self.efield, self.hfield, self.coef, self.height = plan, efield, hfield, coef, height

    def rows(self, run, part, comp, x, height=None):
        return pl.ds(self.plan.row(x, 0, run, part, comp), height or self.height)

    def next_z(self, value):
        lane = lax.broadcasted_iota(jnp.int32, value.shape, 1)
        return jnp.where(lane == value.shape[1] - 1, 0.0, pltpu.roll(value, value.shape[1] - 1, 1))

    def prev_z(self, value):
        lane = lax.broadcasted_iota(jnp.int32, value.shape, 1)
        return jnp.where(lane == 0, 0.0, pltpu.roll(value, 1, 1))

    def next_y(self, value):
        return pltpu.roll(value, self.height - 1, 0)

    def prev_y(self, value):
        return pltpu.roll(value, 1, 0)

    def update_h(self, step, run, part, x):
        efield, old, new = self.efield[step - 1], self.hfield[step - 1], self.hfield[step]
        ex, ey, ez = (efield[self.rows(run, part, comp, x), :] for comp in range(3))
        ey_x, ez_x = (efield[self.rows(run, part, comp, x + 1), :] for comp in (1, 2))
        hx, hy, hz = (old[self.rows(run, part, comp, x), :] for comp in range(3))
        if step == 1:
            hx, hy, hz = hx + hx, hy + hy, hz + hz
        new[self.rows(run, part, 0, x), :] = hx - ((self.next_y(ez) - ez) - (self.next_z(ey) - ey))
        new[self.rows(run, part, 2, x), :] = hz - ((ey_x - ey) - (self.next_y(ex) - ex))
        height = self.last_height(step)
        ex, ez, ez_x, hy = (value[:height] for value in (ex, ez, ez_x, hy))
        new[self.rows(run, part, 1, x, height), :] = hy - ((self.next_z(ex) - ex) - (ez_x - ez))

    def update_e(self, step, run, part, x):
        old, new, hfield = self.efield[step - 1], self.efield[step], self.hfield[step]
        height = self.last_height(step)
        ex, ey, ez = (old[self.rows(run, part, comp, x, height), :] for comp in range(3))
        hx, hz = (hfield[self.rows(run, part, comp, x), :] for comp in (0, 2))
        hx_y, hz_y = self.prev_y(hx)[:height], self.prev_y(hz)[:height]
        hx, hz = hx[:height], hz[:height]
        hy = hfield[self.rows(run, part, 1, x, height), :]
        hy_x, hz_x = (hfield[self.rows(run, part, comp, x - 1, height), :] for comp in (1, 2))
        scale = self.coef[self.rows(0, 0, 0, x, height), :]
        new[self.rows(run, part, 0, x, height), :] = ex + scale * ((hz - hz_y) - (hy - self.prev_z(hy)))
        new[self.rows(run, part, 1, x, height), :] = ey + scale * ((hx - self.prev_z(hx)) - (hz - hz_x))
        new[self.rows(run, part, 2, x, height), :] = ez + scale * ((hy - hy_x) - (hx - hx_y))

    def last_height(self, step):
        return self.plan.ny if step == STEPS else self.height

    def both(self, step, h_layers, e_layers, after_h=None, after_e=None, runs=(0, 1)):
        for update, layers, after in ((self.update_h, h_layers, after_h), (self.update_e, e_layers, after_e)):
            for x in layers:
                for run in runs:
                    for part in (0, 1):
                        update(step, run, part, x)
            if after is not None:
                after()


def middle_kernel(plan, e0_in, h0_in, e1_in, h1_in, coef_in, z_low, z_high, turns, *arrays):
    nx = plan.nx
    efield, hfield, coef = arrays[: STEPS + 1], arrays[STEPS + 1 : 2 * STEPS + 2], arrays[-1]
    state = State(efield, hfield, coef)

    def take(kinds, level):
        unpack(plan, plan.y_low, z_low, lambda y: 2, turns, state, kinds, level)
        unpack(plan, plan.y_high, z_high, lambda y: 3, turns, state, kinds, level)

    take("EHC", 0)
    sweeps = Sweeps(plan, efield, hfield, coef, plan.ring)
    for step in range(1, STEPS + 1):
        after = [lambda: take("H", 1), lambda: take("E", 1)] if step == 1 else []
        sweeps.both(step, range(step - 1, nx - step), range(step, nx - step), *after)


def edges_kernel(plan, groups, *refs):
    nx, ny = plan.nx, plan.ny
    count = 2 * STEPS + 3
    x_low, x_high, far, mate, z_low, z_high, turns, spec_f, spec_a = refs[count : count + 9]
    arrays = refs[count + 9 : 2 * count + 9]
    out_f, out_a, parts = refs[2 * count + 9 :]
    efield, hfield, coef = arrays[: STEPS + 1], arrays[STEPS + 1 : 2 * STEPS + 2], arrays[-1]
    state = State(efield, hfield, coef)

    def take(kinds, level, layers=()):
        unpack(plan, plan.x_low, x_low, lambda y: 0, turns, state, kinds, level)
        unpack(plan, plan.x_high, x_high, lambda y: 1, turns, state, kinds, level)

        def corners(receiver):
            for messages, ref, side in ((plan.far, far, plan.far_side), (plan.mate, mate, plan.mate_side)):
                first = 4 if side[receiver] < 0 else 6
                unpack(plan, messages[receiver], ref, lambda y: first + (y >= 0), turns, state, kinds, level)

        by_parity(0, corners)
        unpack(plan, plan.y_low, z_low, lambda y: 2, turns, state, kinds, level, layers)
        unpack(plan, plan.y_high, z_high, lambda y: 3, turns, state, kinds, level, layers)

    take("EHC", 0)
    sweeps = Sweeps(plan, efield, hfield, coef, plan.ring)
    for step in range(1, STEPS + 1):
        low, high = step - STEPS, nx - step
        h_layers = [*range(low - 1, step - 1), *range(high, nx + STEPS - step)]
        e_layers = [*range(low, step), *range(high, nx + STEPS - step)]
        after = []
        if step == 1:
            after = [functools.partial(take, "H", 1, h_layers), functools.partial(take, "E", 1, e_layers)]
        sweeps.both(step, h_layers, e_layers, *after)

    share = parts.shape[2]
    shift = lax.rem(groups - lax.axis_index("angle"), groups) * share
    weight = turns[pl.ds(2 * SUB, SUB), :]
    tiles = ny // SUB

    for i in range(nx * tiles):
        x, tile = i // tiles, i % tiles
        total = jnp.zeros(weight.shape, jnp.float32)
        for comp in range(3):
            ends = []
            for run, (spec, out) in enumerate(((spec_f, out_f), (spec_a, out_a))):
                at = [pl.ds(((part * 3 + comp) * nx + x) * ny + tile * SUB, SUB) for part in (0, 1)]
                real, imag = spec[at[0], :], spec[at[1], :]
                for step in range(1, STEPS + 1):
                    theta = omega_step * step
                    ends_e = [
                        efield[step][pl.ds(plan.row(x, tile * SUB, run, part, comp), SUB), :]
                        for part in (0, 1)
                    ]
                    more = turned(*ends_e, math.cos(theta), math.sin(theta))
                    real, imag = real + more[0], imag + more[1]
                out[at[0], :], out[at[1], :] = real, imag
                ends.append((real, imag))
            total = total + (ends[0][0] * ends[1][0] - ends[0][1] * ends[1][1])
        total = pltpu.roll(total * weight, shift, 1)
        for k in range(groups):
            parts[k, pl.ds(i * SUB, SUB), :] = total[:, k * share : (k + 1) * share]


def write_kernel(tr_f, tr_a, out_f, out_a, sems):
    copies = []
    for source, target in ((tr_f, out_f), (tr_a, out_a)):
        for i in range(source.shape[0]):
            copies.append(pltpu.make_async_copy(source.at[i], target.at[i], sems.at[len(copies)]))
    for copy in copies:
        copy.start()
    for copy in copies:
        copy.wait()


def ring_pairs(axis, offset):
    size = lax.axis_size(axis)
    return [(i, (i + offset) % size) for i in range(size)]


def mate_pairs():
    return [(i, i ^ 1) for i in range(lax.axis_size("gx"))]


def far_pairs():
    size = lax.axis_size("gx")
    return [(i, (i + (1 if i % 2 else -1)) % size) for i in range(size)]


def shards(
    forward_fields,
    adjoint_fields,
    forward_spectrum,
    adjoint_spectrum,
    permittivity,
    phase_table,
    angle_index,
    design_tiles,
):
    nx, ny, depth = permittivity.shape
    plan = Plan(nx, ny)
    groups = lax.axis_size("angle")
    wide, ring = plan.wide, plan.ring

    def array(*shape):
        return jax.ShapeDtypeStruct(shape, jnp.float32)

    def lines(count):
        return array(count, depth)

    def params(mib):
        return pltpu.CompilerParams(vmem_limit_bytes=mib * 2**20)

    def cost(size):
        return pl.CostEstimate(flops=size, bytes_accessed=size, transcendentals=0)

    assert lax.axis_size("gx") % 2 == 0
    with jax.named_scope("pack_y"):
        *first, coef, z_up, z_down = pl.pallas_call(
            functools.partial(pack_y_kernel, plan),
            out_shape=(
                *[array(12, wide, ring, depth)] * 4,
                array(wide, ring, depth),
                lines(plan.y_low.lines),
                lines(plan.y_high.lines),
            ),
            in_specs=[HBM] * 3,
            out_specs=[VMEM] * 7,
            scratch_shapes=[pltpu.SemaphoreType.DMA((25,))],
            compiler_params=params(8),
        )(*(pltpu.with_memory_space_constraint(array, pltpu.HBM) for array in (forward_fields[0], adjoint_fields[0], permittivity)))
    e0, h0, e1, h1, coef = (state.reshape((-1, depth)) for state in (*first, coef))
    with jax.named_scope("send_y"):
        z_low = lax.ppermute(z_up, "gy", ring_pairs("gy", 1))
        z_high = lax.ppermute(z_down, "gy", ring_pairs("gy", -1))
    with jax.named_scope("pack_x"):
        x_up, x_down = pl.pallas_call(
            functools.partial(pack_x_kernel, plan),
            out_shape=(lines(plan.x_low.lines), lines(plan.x_high.lines)),
            in_specs=[VMEM] * 5,
            out_specs=[VMEM] * 2,
            compiler_params=params(8),
            cost_estimate=cost(40 * 2**20),
        )(e0, h0, e1, h1, coef)
    with jax.named_scope("send_x"):
        x_low = lax.ppermute(x_up, "gx", ring_pairs("gx", 1))
        x_high = lax.ppermute(x_down, "gx", ring_pairs("gx", -1))
    with jax.named_scope("turns"):
        turns = pl.pallas_call(
            functools.partial(turns_kernel, groups),
            out_shape=lines(3 * SUB),
            in_specs=[SMEM] * 3,
            out_specs=VMEM,
            compiler_params=params(4),
        )(phase_table, angle_index, design_tiles)
    with jax.named_scope("relay_corners"):
        to_far, to_mate = pl.pallas_call(
            functools.partial(relay_kernel, plan),
            out_shape=[lines(plan.corner_lines)] * 2,
            in_specs=[VMEM] * 2,
            out_specs=[VMEM] * 2,
            compiler_params=params(4),
        )(z_low, z_high)
        far = lax.ppermute(to_far, "gx", far_pairs())
        mate = lax.ppermute(to_mate, "gx", mate_pairs())
    level = lines(12 * wide * ring)
    count = 2 * STEPS + 3
    levels = [level] * (count - 1) + [lines(wide * ring)]
    with jax.named_scope("middle"):
        state = pl.pallas_call(
            functools.partial(middle_kernel, plan),
            out_shape=levels,
            in_specs=[VMEM] * 8,
            out_specs=[VMEM] * count,
            input_output_aliases={0: 0, 1: STEPS + 1, 2: 1, 3: STEPS + 2, 4: count - 1},
            compiler_params=params(8),
            cost_estimate=cost(2**31),
        )(e0, h0, e1, h1, coef, z_low, z_high, turns)
    with jax.named_scope("edges"):
        spectra = [spectrum.reshape((-1, depth)) for spectrum in (forward_spectrum, adjoint_spectrum)]
        *_, tr_f, tr_a, parts = pl.pallas_call(
            functools.partial(edges_kernel, plan, groups),
            out_shape=[*levels, lines(6 * nx * ny), lines(6 * nx * ny), array(groups, nx * ny, depth // groups)],
            in_specs=[VMEM] * (count + 9),
            out_specs=[VMEM] * (count + 3),
            input_output_aliases={i: i for i in range(count)},
            compiler_params=params(8),
        )(*state, x_low, x_high, far, mate, z_low, z_high, turns, *spectra)
    with jax.named_scope("sum_angles"):
        gradient = parts[0]
        for k in range(1, groups):
            gradient = gradient + lax.ppermute(parts[k], "angle", ring_pairs("angle", k))
    with jax.named_scope("write"):
        out_f, out_a = pl.pallas_call(
            write_kernel,
            out_shape=[array(6, nx, ny, depth)] * 2,
            in_specs=[VMEM] * 2,
            out_specs=[HBM] * 2,
            scratch_shapes=[pltpu.SemaphoreType.DMA((12,))],
            compiler_params=params(4),
        )(tr_f.reshape((6, nx, ny, depth)), tr_a.reshape((6, nx, ny, depth)))
    return (
        out_f.reshape(forward_spectrum.shape),
        out_a.reshape(adjoint_spectrum.shape),
        gradient.reshape((nx, ny, depth // groups)),
    )


def solution(mesh):
    in_specs = (
        P("angle", None, "gx", "gy", None),
        P("angle", None, "gx", "gy", None),
        P("angle", None, "gx", "gy", None),
        P("angle", None, "gx", "gy", None),
        P("gx", "gy", None),
        P(),
        P("angle"),
        P(),
    )
    out_specs = (
        P("angle", None, "gx", "gy", None),
        P("angle", None, "gx", "gy", None),
        P("gx", "gy", "angle"),
    )
    return jax.shard_map(shards, mesh=mesh, in_specs=in_specs, out_specs=out_specs, check_vma=False)
```

```python
import functools
import math

import jax
import jax.numpy as jnp
from jax import lax
from jax.experimental import pallas as pl
from jax.experimental.pallas import tpu as pltpu
from jax.sharding import PartitionSpec as P

STEPS = 3
SUB = 8

courant = 0.5
omega_step = 0.7

VMEM = pl.BlockSpec(memory_space=pltpu.VMEM)
SMEM = pl.BlockSpec(memory_space=pltpu.SMEM)
HBM = pl.BlockSpec(memory_space=pltpu.HBM)


def reads(node):
    kind, level, comp, x, y = node
    others = [c for c in range(3) if c != comp]
    if kind == "E":
        found = [("E", level - 1, comp, x, y), ("C", 0, 0, x, y)] + [("H", level, c, x, y) for c in others]
        if comp != 1:
            found.append(("H", level, 2 - comp, x, y - 1))
        if comp != 0:
            found.append(("H", level, 3 - comp, x - 1, y))
        return found
    found = [("H", level - 1, comp, x, y)] + [("E", level - 1, c, x, y) for c in others]
    if comp != 1:
        found.append(("E", level - 1, 2 - comp, x, y + 1))
    if comp != 0:
        found.append(("E", level - 1, 3 - comp, x + 1, y))
    return found


def wanted(nx, ny):
    def block(node):
        return node[3] // nx, node[4] // ny

    @functools.cache
    def alone(node):
        if node[1] == 0:
            return True
        return node[1] == 1 and all(block(other) == block(node) and alone(other) for other in reads(node))

    found, made, seen = set(), set(), set()
    todo = [("E", STEPS, comp, x, y) for comp in range(3) for x in range(nx) for y in range(ny)]
    while todo:
        node = todo.pop()
        if node in seen:
            continue
        seen.add(node)
        if block(node) != (0, 0) and alone(node):
            found.add(node)
        elif node[1]:
            made.add(node)
            todo += reads(node)
    return found, made


class Message:
    def __init__(self, nodes, axis):
        self.axis, self.runs, self.at, self.size = axis, [], {}, 0
        stretches = []
        for node in sorted(nodes):
            before = list(node)
            before[3 + axis] -= 1
            if tuple(before) in nodes:
                continue
            count = 1
            while (*node[:3], node[3] + count * (axis == 0), node[4] + count * (axis == 1)) in nodes:
                count += 1
            stretches.append((count, node))
        for count, (kind, level, comp, x, y) in sorted(stretches, key=lambda item: (-item[0], item[1])):
            for run in (0, 1) if kind != "C" else (0,):
                for part in (0, 1) if kind != "C" else (0,):
                    what = (kind, level, comp, run, part)
                    self.runs.append((what, x, y, count, self.size))
                    for i in range(count):
                        self.at[what, x + i * (axis == 0), y + i * (axis == 1)] = self.size + i
                    self.size += count
        self.lines = -(-self.size // SUB) * SUB


class Plan:
    def __init__(self, nx, ny, depth):
        self.depth = depth
        self.nx, self.ny = nx, ny
        self.wide, self.ring = nx + 2 * STEPS, ny + SUB
        nodes, made = wanted(nx, ny)
        self.made = {}
        for kind, level, comp, x, y in made:
            heights = self.made.setdefault((kind, level, x), {})
            heights[comp] = max(heights.get(comp, 0), ny if 0 <= y < ny else self.ring)
        sides = {}
        for node in nodes:
            sides.setdefault((node[3] // nx, node[4] // ny), set()).add(node)

        def shifted(found, dx):
            return {(*node[:3], node[3] + dx, node[4]) for node in found}

        self.y_low, self.y_high = (
            Message(sides[0, side] | shifted(sides[-1, side], nx) | shifted(sides[1, side], -nx), 0) for side in (-1, 1)
        )
        self.x_low, self.x_high = Message(sides[-1, 0], 1), Message(sides[1, 0], 1)
        self.mate_side, self.far_side = (1, -1), (-1, 1)
        self.mate, self.far = ([Message(sides[side, -1] | sides[side, 1], 1) for side in order] for order in (self.mate_side, self.far_side))
        self.corner_lines = max(message.lines for message in self.mate)

    def row(self, x, y, run=0, part=0, comp=0):
        return ((run * 6 + part * 3 + comp) * self.wide + x + STEPS) * self.ring + y % self.ring

    def rows(self, what, x, y, axis, count):
        _, _, comp, run, part = what
        start = self.row(x, y, run, part, comp)
        return pl.ds(start, count, stride=self.ring) if axis == 0 and count > 1 else pl.ds(start, count)


class State:
    def __init__(self, efield, hfield, coef):
        self.by_kind = {"E": efield, "H": hfield, "C": [coef]}

    def __call__(self, what):
        return self.by_kind[what[0]][what[1]]


def pack(plan, message, state, dx, dy, out):
    for what, x, y, count, at in message.runs:
        out[pl.ds(at, count), :] = state(what)[plan.rows(what, x + dx, y + dy, message.axis, count), :]


def by_parity(offset, body):
    parity = lax.rem(lax.axis_index("gx") + offset, 2)
    for value in (0, 1):
        pl.when(parity == value)(functools.partial(body, value))


def pack_y_kernel(plan, fwd, adj, eps, e0, h0, e1, h1, coef, z_up, z_down, sems):
    nx, ny = plan.nx, plan.ny
    own = (pl.ds(STEPS, nx), pl.ds(0, ny), slice(None))
    copies = [pltpu.make_async_copy(eps, coef.at[own], sems.at[0])]
    for run, ref in enumerate((fwd, adj)):
        for kind, array in enumerate((e0, h0)):
            for i in range(6):
                copies.append(
                    pltpu.make_async_copy(ref.at[kind * 6 + i], array.at[(run * 6 + i, *own)], sems.at[len(copies)])
                )
    for copy in copies:
        copy.start()
    copies[0].wait()
    for x in range(nx):
        coef[STEPS + x, pl.ds(0, ny), :] = (0.5 * courant) / coef[STEPS + x, pl.ds(0, ny), :]
    e0, h0, e1, h1, coef = (array.reshape((-1, array.shape[-1])) for array in (e0, h0, e1, h1, coef))
    sweeps = Sweeps(plan, [e0, e1], [h0, h1], coef, ny)
    for run in (0, 1):
        for copy in copies[1 + 12 * run : 13 + 12 * run]:
            copy.wait()
        sweeps.both(1, range(nx), range(nx - 1), runs=(run,))
    state = State([e0, e1], [h0, h1], coef)
    pack(plan, plan.y_low, state, 0, ny, z_up)
    pack(plan, plan.y_high, state, 0, -ny, z_down)


def pack_x_kernel(plan, e0, h0, e1, h1, coef, x_up, x_down):
    state = State([e0, e1], [h0, h1], coef)
    pack(plan, plan.x_low, state, plan.nx, 0, x_up)
    pack(plan, plan.x_high, state, -plan.nx, 0, x_down)


def turns_kernel(groups, table, index, tiles, turns):
    row = index[0]
    phi_x, phi_y = table[row, 0], table[row, 1]
    at_x, at_y = lax.axis_index("gx"), lax.axis_index("gy")
    none = jnp.float32(0.0)
    ax_low = jnp.where(at_x == 0, -phi_x, none)
    ax_high = jnp.where(at_x == lax.axis_size("gx") - 1, phi_x, none)
    ay_low = jnp.where(at_y == 0, -phi_y, none)
    ay_high = jnp.where(at_y == lax.axis_size("gy") - 1, phi_y, none)
    sub = lax.broadcasted_iota(jnp.int32, (SUB, turns.shape[1]), 0)
    angles = jnp.zeros(sub.shape, jnp.float32)
    for i, angle in enumerate((ax_low, ax_high, ay_low, ay_high, ax_low + ay_low, ax_low + ay_high,
                               ax_high + ay_low, ax_high + ay_high)):
        angles = jnp.where(sub == i, angle, angles)
    turns[pl.ds(0, SUB), :] = jnp.cos(angles)
    turns[pl.ds(SUB, SUB), :] = jnp.sin(angles)
    own_tile = at_x * lax.axis_size("gy") + at_y
    chosen = tiles[0] == own_tile
    for i in range(1, tiles.shape[0]):
        chosen = jnp.logical_or(chosen, tiles[i] == own_tile)
    weight = jnp.where(chosen, jnp.float32(1.0 / groups), none)
    turns[pl.ds(2 * SUB, SUB), :] = jnp.full(sub.shape, weight, jnp.float32)


def relay_kernel(plan, z_low, z_high, to_far, to_mate):
    def corners(receiver):
        for messages, side, out in ((plan.far, plan.far_side, to_far), (plan.mate, plan.mate_side, to_mate)):
            dx = -plan.nx * side[receiver]
            for (what, x, y), row in messages[receiver].at.items():
                ref, source = (z_low, plan.y_low) if y < 0 else (z_high, plan.y_high)
                out[pl.ds(row, 1), :] = ref[pl.ds(source.at[what, x + dx, y], 1), :]

    by_parity(1, corners)


def turned(real, imag, cosine, sine):
    return real * cosine - imag * sine, real * sine + imag * cosine


def unpack(plan, message, ref, which, turns, state, kinds, level, layers=None):
    axis = message.axis
    for (kind, at_level, comp, run, part), x, y, count, at in message.runs:
        if kind not in kinds or at_level != level or part == 1:
            continue
        pieces = [(x, y, count, at)]
        if layers is not None:
            pieces = [(x + i, y, 1, at + i) for i in range(count) if x + i in layers]
        for cell_x, cell_y, size, row in pieces:
            what = (kind, at_level, comp, run, 0)
            real = ref[pl.ds(row, size), :]
            if kind == "C":
                state(what)[plan.rows(what, cell_x, cell_y, axis, size), :] = real
                continue
            twin = (kind, at_level, comp, run, 1)
            imag = ref[pl.ds(message.at[twin, cell_x, cell_y], size), :]
            turn = which(y)
            cosine, sine = turns[pl.ds(turn, 1), :], turns[pl.ds(SUB + turn, 1), :]
            real, imag = turned(real, imag, cosine, sine if run == 0 else -sine)
            state(what)[plan.rows(what, cell_x, cell_y, axis, size), :] = real
            state(twin)[plan.rows(twin, cell_x, cell_y, axis, size), :] = imag


class Sweeps:
    def __init__(self, plan, efield, hfield, coef, height):
        self.plan, self.efield, self.hfield, self.coef, self.height = plan, efield, hfield, coef, height

    def rows(self, run, part, comp, x, height):
        return pl.ds(self.plan.row(x, 0, run, part, comp), height)

    def get(self, array, run, part, comp, x):
        return array[self.rows(run, part, comp, x, self.height), :]

    def heights(self, kind, step, x):
        if self.height == self.plan.ring:
            return self.plan.made.get((kind, step, x), {})
        return dict.fromkeys(range(3), self.height)

    def next_z(self, value):
        lane = lax.broadcasted_iota(jnp.int32, value.shape, 1)
        return jnp.where(lane == value.shape[1] - 1, 0.0, pltpu.roll(value, value.shape[1] - 1, 1))

    def prev_z(self, value):
        lane = lax.broadcasted_iota(jnp.int32, value.shape, 1)
        return jnp.where(lane == 0, 0.0, pltpu.roll(value, 1, 1))

    def next_y(self, value):
        return pltpu.roll(value, self.height - 1, 0)

    def prev_y(self, value):
        return pltpu.roll(value, 1, 0)

    def update_h(self, step, run, part, x):
        efield, old, new = self.efield[step - 1], self.hfield[step - 1], self.hfield[step]
        ex, ey, ez = (self.get(efield, run, part, comp, x) for comp in range(3))
        for comp, height in self.heights("H", step, x).items():
            if comp == 0:
                curl = (self.next_y(ez) - ez)[:height] - (self.next_z(ey[:height]) - ey[:height])
            elif comp == 1:
                ez_x = self.get(efield, run, part, 2, x + 1)
                curl = (self.next_z(ex[:height]) - ex[:height]) - (ez_x - ez)[:height]
            else:
                ey_x = self.get(efield, run, part, 1, x + 1)
                curl = (ey_x - ey)[:height] - (self.next_y(ex) - ex)[:height]
            before = self.get(old, run, part, comp, x)[:height]
            if step == 1:
                before = before + before
            new[self.rows(run, part, comp, x, height), :] = before - curl

    def update_e(self, step, run, part, x):
        old, new, hfield = self.efield[step - 1], self.efield[step], self.hfield[step]
        hx, hy, hz = (self.get(hfield, run, part, comp, x) for comp in range(3))
        scale = self.get(self.coef, 0, 0, 0, x)
        for comp, height in self.heights("E", step, x).items():
            if comp == 0:
                curl = (hz - self.prev_y(hz))[:height] - (hy[:height] - self.prev_z(hy[:height]))
            elif comp == 1:
                hz_x = self.get(hfield, run, part, 2, x - 1)
                curl = (hx[:height] - self.prev_z(hx[:height])) - (hz - hz_x)[:height]
            else:
                hy_x = self.get(hfield, run, part, 1, x - 1)
                curl = (hy - hy_x)[:height] - (hx - self.prev_y(hx))[:height]
            before = self.get(old, run, part, comp, x)[:height]
            new[self.rows(run, part, comp, x, height), :] = before + scale[:height] * curl

    def both(self, step, h_layers, e_layers, after_h=None, after_e=None, runs=(0, 1)):
        for update, layers, after in ((self.update_h, h_layers, after_h), (self.update_e, e_layers, after_e)):
            for x in layers:
                for run in runs:
                    for part in (0, 1):
                        update(step, run, part, x)
            if after is not None:
                after()


def middle_kernel(plan, e0_in, h0_in, e1_in, h1_in, coef_in, z_low, z_high, turns, *arrays):
    nx = plan.nx
    efield, hfield, coef = arrays[: STEPS + 1], arrays[STEPS + 1 : 2 * STEPS + 2], arrays[-1]
    state = State(efield, hfield, coef)

    def take(kinds, level):
        unpack(plan, plan.y_low, z_low, lambda y: 2, turns, state, kinds, level)
        unpack(plan, plan.y_high, z_high, lambda y: 3, turns, state, kinds, level)

    take("EHC", 0)
    sweeps = Sweeps(plan, efield, hfield, coef, plan.ring)
    for step in range(1, STEPS + 1):
        after = [lambda: take("H", 1), lambda: take("E", 1)] if step == 1 else []
        sweeps.both(step, range(step - 1, nx - step), range(step, nx - step), *after)


def add_known(plan, efield, levels, transform, out):
    nx, ny = plan.nx, plan.ny
    for x in range(nx):
        for tile in range(ny // SUB):
            for comp in range(3):
                ends = []
                for run in (0, 1):
                    at = [pl.ds(((part * 3 + comp) * nx + x) * ny + tile * SUB, SUB) for part in (0, 1)]
                    real, imag = transform[run][at[0], :], transform[run][at[1], :]
                    for level in levels(x):
                        theta = omega_step * level
                        here = [efield[level][pl.ds(plan.row(x, tile * SUB, run, part, comp), SUB), :] for part in (0, 1)]
                        more = turned(*here, math.cos(theta), math.sin(theta))
                        real, imag = real + more[0], imag + more[1]
                    out[run][at[0], :], out[run][at[1], :] = real, imag
                    ends.append((real, imag))
                yield x, tile, comp, ends


def known(plan, x):
    return [level for level in range(1, STEPS + 1) if level <= x < plan.nx - level]


def faces_kernel(plan, *refs):
    efield, hfield, coef = refs[: STEPS + 1], refs[STEPS + 1], refs[STEPS + 2]
    x_low, x_high, turns, spec_f, spec_a = refs[STEPS + 3 : STEPS + 8]
    *_, out_f, out_a = refs
    e0, h0, coef = refs[STEPS + 8 : STEPS + 11]
    state = State([e0], [h0], coef)
    unpack(plan, plan.x_low, x_low, lambda y: 0, turns, state, "EHC", 0)
    unpack(plan, plan.x_high, x_high, lambda y: 1, turns, state, "EHC", 0)
    for _ in add_known(plan, efield, functools.partial(known, plan), (spec_f, spec_a), (out_f, out_a)):
        pass


def edges_kernel(plan, groups, *refs):
    nx, ny = plan.nx, plan.ny
    count = 2 * STEPS + 3
    x_low, x_high, far, mate, z_low, z_high, turns, part_f, part_a = refs[count : count + 9]
    arrays = refs[count + 9 : 2 * count + 9]
    out_f, out_a, *parts = refs[2 * count + 9 :]
    efield, hfield, coef = arrays[: STEPS + 1], arrays[STEPS + 1 : 2 * STEPS + 2], arrays[-1]
    state = State(efield, hfield, coef)

    def take(kinds, level, layers=()):
        if level:
            unpack(plan, plan.x_low, x_low, lambda y: 0, turns, state, kinds, level)
            unpack(plan, plan.x_high, x_high, lambda y: 1, turns, state, kinds, level)

        def corners(receiver):
            for messages, ref, side in ((plan.far, far, plan.far_side), (plan.mate, mate, plan.mate_side)):
                first = 4 if side[receiver] < 0 else 6
                unpack(plan, messages[receiver], ref, lambda y: first + (y >= 0), turns, state, kinds, level)

        by_parity(0, corners)
        unpack(plan, plan.y_low, z_low, lambda y: 2, turns, state, kinds, level, layers)
        unpack(plan, plan.y_high, z_high, lambda y: 3, turns, state, kinds, level, layers)

    take("EHC", 0)
    sweeps = Sweeps(plan, efield, hfield, coef, plan.ring)
    for step in range(1, STEPS + 1):
        low, high = step - STEPS, nx - step
        h_layers = [*range(low - 1, step - 1), *range(high, nx + STEPS - step)]
        e_layers = [*range(low, step), *range(high, nx + STEPS - step)]
        after = []
        if step == 1:
            after = [functools.partial(take, "H", 1, h_layers), functools.partial(take, "E", 1, e_layers)]
        sweeps.both(step, h_layers, e_layers, *after)

    share = plan.depth // groups
    shift = lax.rem(groups - lax.axis_index("angle"), groups) * share
    weight = turns[pl.ds(2 * SUB, SUB), :]

    def rest(x):
        return [level for level in range(1, STEPS + 1) if level not in known(plan, x)]

    totals = {}
    for x, tile, _, ends in add_known(plan, efield, rest, (part_f, part_a), (out_f, out_a)):
        term = ends[0][0] * ends[1][0] - ends[0][1] * ends[1][1]
        totals[x, tile] = totals[x, tile] + term if (x, tile) in totals else term
    block = lax.broadcasted_iota(jnp.int32, weight.shape, 1) // share
    tiles = [pltpu.roll(total * weight, shift, 1) for total in totals.values()]
    for k, part in enumerate(parts):
        for i in range(len(tiles) // groups):
            packed = jnp.zeros(weight.shape, jnp.float32)
            for t in range(groups):
                lanes = (t - k) % groups * share
                value = tiles[i * groups + t]
                packed = jnp.where(block == t, pltpu.roll(value, lanes, 1) if lanes else value, packed)
            part[pl.ds(i * SUB, SUB), :] = packed


def sum_kernel(groups, *refs):
    *parts, out = refs
    share = out.shape[1]
    for i in range(parts[0].shape[0] // SUB):
        total = parts[0][pl.ds(i * SUB, SUB), :]
        for part in parts[1:]:
            total = total + part[pl.ds(i * SUB, SUB), :]
        for t in range(groups):
            out[pl.ds((i * groups + t) * SUB, SUB), :] = total[:, t * share : (t + 1) * share]


def write_kernel(tr_f, tr_a, out_f, out_a, sems):
    copies = []
    for source, target in ((tr_f, out_f), (tr_a, out_a)):
        for i in range(source.shape[0]):
            copies.append(pltpu.make_async_copy(source.at[i], target.at[i], sems.at[len(copies)]))
    for copy in copies:
        copy.start()
    for copy in copies:
        copy.wait()


def ring_pairs(axis, offset):
    size = lax.axis_size(axis)
    return [(i, (i + offset) % size) for i in range(size)]


def mate_pairs():
    return [(i, i ^ 1) for i in range(lax.axis_size("gx"))]


def far_pairs():
    size = lax.axis_size("gx")
    return [(i, (i + (1 if i % 2 else -1)) % size) for i in range(size)]


def shards(
    forward_fields,
    adjoint_fields,
    forward_spectrum,
    adjoint_spectrum,
    permittivity,
    phase_table,
    angle_index,
    design_tiles,
):
    nx, ny, depth = permittivity.shape
    plan = Plan(nx, ny, depth)
    groups = lax.axis_size("angle")
    wide, ring = plan.wide, plan.ring

    def array(*shape):
        return jax.ShapeDtypeStruct(shape, jnp.float32)

    def lines(count):
        return array(count, depth)

    def params(mib):
        return pltpu.CompilerParams(vmem_limit_bytes=mib * 2**20)

    def cost(size):
        return pl.CostEstimate(flops=size, bytes_accessed=size, transcendentals=0)

    assert lax.axis_size("gx") % 2 == 0 and nx * ny % (groups * SUB) == 0
    with jax.named_scope("pack_y"):
        *first, coef, z_up, z_down = pl.pallas_call(
            functools.partial(pack_y_kernel, plan),
            out_shape=(
                *[array(12, wide, ring, depth)] * 4,
                array(wide, ring, depth),
                lines(plan.y_low.lines),
                lines(plan.y_high.lines),
            ),
            in_specs=[HBM] * 3,
            out_specs=[VMEM] * 7,
            scratch_shapes=[pltpu.SemaphoreType.DMA((25,))],
            compiler_params=params(8),
        )(*(pltpu.with_memory_space_constraint(array, pltpu.HBM) for array in (forward_fields[0], adjoint_fields[0], permittivity)))
    e0, h0, e1, h1, coef = (state.reshape((-1, depth)) for state in (*first, coef))
    with jax.named_scope("send_y"):
        z_low = lax.ppermute(z_up, "gy", ring_pairs("gy", 1))
        z_high = lax.ppermute(z_down, "gy", ring_pairs("gy", -1))
    with jax.named_scope("pack_x"):
        x_up, x_down = pl.pallas_call(
            functools.partial(pack_x_kernel, plan),
            out_shape=(lines(plan.x_low.lines), lines(plan.x_high.lines)),
            in_specs=[VMEM] * 5,
            out_specs=[VMEM] * 2,
            compiler_params=params(8),
            cost_estimate=cost(40 * 2**20),
        )(e0, h0, e1, h1, coef)
    with jax.named_scope("send_x"):
        x_low = lax.ppermute(x_up, "gx", ring_pairs("gx", 1))
        x_high = lax.ppermute(x_down, "gx", ring_pairs("gx", -1))
    with jax.named_scope("turns"):
        turns = pl.pallas_call(
            functools.partial(turns_kernel, groups),
            out_shape=lines(3 * SUB),
            in_specs=[SMEM] * 3,
            out_specs=VMEM,
            compiler_params=params(4),
        )(phase_table, angle_index, design_tiles)
    with jax.named_scope("relay_corners"):
        to_far, to_mate = pl.pallas_call(
            functools.partial(relay_kernel, plan),
            out_shape=[lines(plan.corner_lines)] * 2,
            in_specs=[VMEM] * 2,
            out_specs=[VMEM] * 2,
            compiler_params=params(4),
        )(z_low, z_high)
        far = lax.ppermute(to_far, "gx", far_pairs())
        mate = lax.ppermute(to_mate, "gx", mate_pairs())
    level = lines(12 * wide * ring)
    count = 2 * STEPS + 3
    levels = [level] * (count - 1) + [lines(wide * ring)]
    with jax.named_scope("middle"):
        state = pl.pallas_call(
            functools.partial(middle_kernel, plan),
            out_shape=levels,
            in_specs=[VMEM] * 8,
            out_specs=[VMEM] * count,
            input_output_aliases={0: 0, 1: STEPS + 1, 2: 1, 3: STEPS + 2, 4: count - 1},
            compiler_params=params(8),
            cost_estimate=cost(2**32),
        )(e0, h0, e1, h1, coef, z_low, z_high, turns)
    transforms = [lines(6 * nx * ny)] * 2
    with jax.named_scope("faces"):
        spectra = [spectrum.reshape((-1, depth)) for spectrum in (forward_spectrum, adjoint_spectrum)]
        e0, h0, coef, *sums = pl.pallas_call(
            functools.partial(faces_kernel, plan),
            out_shape=[level, level, levels[-1], *transforms],
            in_specs=[VMEM] * (STEPS + 8),
            out_specs=[VMEM] * 5,
            input_output_aliases={0: 0, STEPS + 1: 1, STEPS + 2: 2},
            compiler_params=params(8),
            cost_estimate=cost(2**10),
        )(*state[: STEPS + 2], state[-1], x_low, x_high, turns, *spectra)
        state = [e0, *state[1 : STEPS + 1], h0, *state[STEPS + 2 : -1], coef]
    with jax.named_scope("edges"):
        results = pl.pallas_call(
            functools.partial(edges_kernel, plan, groups),
            out_shape=[*levels, *transforms, *[lines(nx * ny // groups)] * groups],
            in_specs=[VMEM] * (count + 9),
            out_specs=[VMEM] * (count + 2 + groups),
            input_output_aliases={i: i for i in range(count)} | {count + 7: count, count + 8: count + 1},
            compiler_params=params(8),
        )(*state, x_low, x_high, far, mate, z_low, z_high, turns, *sums)
        tr_f, tr_a, own, *others = results[count:]
    with jax.named_scope("sum_angles"):
        others = [lax.ppermute(part, "angle", ring_pairs("angle", k + 1)) for k, part in enumerate(others)]
        gradient = pl.pallas_call(
            functools.partial(sum_kernel, groups),
            out_shape=array(nx * ny, depth // groups),
            in_specs=[VMEM] * groups,
            out_specs=VMEM,
            compiler_params=params(4),
        )(own, *others)
    with jax.named_scope("write"):
        out_f, out_a = pl.pallas_call(
            write_kernel,
            out_shape=[array(6, nx, ny, depth)] * 2,
            in_specs=[VMEM] * 2,
            out_specs=[HBM] * 2,
            scratch_shapes=[pltpu.SemaphoreType.DMA((12,))],
            compiler_params=params(4),
        )(tr_f.reshape((6, nx, ny, depth)), tr_a.reshape((6, nx, ny, depth)))
    return (
        out_f.reshape(forward_spectrum.shape),
        out_a.reshape(adjoint_spectrum.shape),
        gradient.reshape((nx, ny, depth // groups)),
    )


def solution(mesh):
    in_specs = (
        P("angle", None, "gx", "gy", None),
        P("angle", None, "gx", "gy", None),
        P("angle", None, "gx", "gy", None),
        P("angle", None, "gx", "gy", None),
        P("gx", "gy", None),
        P(),
        P("angle"),
        P(),
    )
    out_specs = (
        P("angle", None, "gx", "gy", None),
        P("angle", None, "gx", "gy", None),
        P("gx", "gy", "angle"),
    )
    return jax.shard_map(shards, mesh=mesh, in_specs=in_specs, out_specs=out_specs, check_vma=False)
```

```python
import functools
import math

import jax
import jax.numpy as jnp
from jax import lax
from jax.experimental import pallas as pl
from jax.experimental.pallas import tpu as pltpu
from jax.sharding import PartitionSpec as P

STEPS = 3
SUB = 8

courant = 0.5
omega_step = 0.7

VMEM = pl.BlockSpec(memory_space=pltpu.VMEM)
SMEM = pl.BlockSpec(memory_space=pltpu.SMEM)
HBM = pl.BlockSpec(memory_space=pltpu.HBM)


def reads(node):
    kind, level, comp, x, y = node
    others = [c for c in range(3) if c != comp]
    if kind == "E":
        found = [("E", level - 1, comp, x, y), ("C", 0, 0, x, y)] + [("H", level, c, x, y) for c in others]
        if comp != 1:
            found.append(("H", level, 2 - comp, x, y - 1))
        if comp != 0:
            found.append(("H", level, 3 - comp, x - 1, y))
        return found
    found = [("H", level - 1, comp, x, y)] + [("E", level - 1, c, x, y) for c in others]
    if comp != 1:
        found.append(("E", level - 1, 2 - comp, x, y + 1))
    if comp != 0:
        found.append(("E", level - 1, 3 - comp, x + 1, y))
    return found


def wanted(nx, ny):
    def block(node):
        return node[3] // nx, node[4] // ny

    @functools.cache
    def alone(node):
        if node[1] == 0:
            return True
        return node[1] == 1 and all(block(other) == block(node) and alone(other) for other in reads(node))

    found, made, seen = set(), set(), set()
    todo = [("E", STEPS, comp, x, y) for comp in range(3) for x in range(nx) for y in range(ny)]
    while todo:
        node = todo.pop()
        if node in seen:
            continue
        seen.add(node)
        if block(node) != (0, 0) and alone(node):
            found.add(node)
        elif node[1]:
            made.add(node)
            todo += reads(node)
    return found, made


class Message:
    def __init__(self, nodes, axis):
        self.axis, self.runs, self.at, self.size = axis, [], {}, 0
        stretches = []
        for node in sorted(nodes):
            before = list(node)
            before[3 + axis] -= 1
            if tuple(before) in nodes:
                continue
            count = 1
            while (*node[:3], node[3] + count * (axis == 0), node[4] + count * (axis == 1)) in nodes:
                count += 1
            stretches.append((count, node))
        for count, (kind, level, comp, x, y) in sorted(stretches, key=lambda item: (-item[0], item[1])):
            for run in (0, 1) if kind != "C" else (0,):
                for part in (0, 1) if kind != "C" else (0,):
                    what = (kind, level, comp, run, part)
                    self.runs.append((what, x, y, count, self.size))
                    for i in range(count):
                        self.at[what, x + i * (axis == 0), y + i * (axis == 1)] = self.size + i
                    self.size += count
        self.lines = -(-self.size // SUB) * SUB


class Plan:
    def __init__(self, nx, ny, depth):
        self.depth = depth
        self.nx, self.ny = nx, ny
        self.wide, self.ring = nx + 2 * STEPS, ny + SUB
        nodes, made = wanted(nx, ny)
        self.made, self.free, self.rest = {}, {}, {}
        tiles, ready = {}, set()
        for node in made:
            tiles.setdefault((node[1], "HE".index(node[0]), *node[2:4], node[4] % self.ring // SUB), []).append(node)

        def early(node):
            if node in made:
                return node in ready
            return node not in nodes or 0 <= node[3] < nx or 0 <= node[4] < ny

        for (level, order, comp, x, tile), members in sorted(tiles.items()):
            key = ("HE"[order], level, x)
            middle = level - 1 + order <= x < nx - level
            free = middle or all(early(other) for node in members for other in reads(node))
            if free:
                ready.update(members)
            for into in (self.made, self.free if free else self.rest):
                into.setdefault(key, {}).setdefault(comp, set()).add(tile)
        sides = {}
        for node in nodes:
            sides.setdefault((node[3] // nx, node[4] // ny), set()).add(node)

        def shifted(found, dx):
            return {(*node[:3], node[3] + dx, node[4]) for node in found}

        self.y_low, self.y_high = (
            Message(sides[0, side] | shifted(sides[-1, side], nx) | shifted(sides[1, side], -nx), 0) for side in (-1, 1)
        )
        self.x_low, self.x_high = Message(sides[-1, 0], 1), Message(sides[1, 0], 1)
        self.mate_side, self.far_side = (1, -1), (-1, 1)
        self.mate, self.far = ([Message(sides[side, -1] | sides[side, 1], 1) for side in order] for order in (self.mate_side, self.far_side))
        self.corner_lines = max(message.lines for message in self.mate)

    def row(self, x, y, run=0, part=0, comp=0):
        return ((run * 6 + part * 3 + comp) * self.wide + x + STEPS) * self.ring + y % self.ring

    def rows(self, what, x, y, axis, count):
        _, _, comp, run, part = what
        start = self.row(x, y, run, part, comp)
        return pl.ds(start, count, stride=self.ring) if axis == 0 and count > 1 else pl.ds(start, count)


class State:
    def __init__(self, efield, hfield, coef):
        self.by_kind = {"E": efield, "H": hfield, "C": [coef]}

    def __call__(self, what):
        return self.by_kind[what[0]][what[1]]


def pack(plan, message, state, dx, dy, out):
    for what, x, y, count, at in message.runs:
        out[pl.ds(at, count), :] = state(what)[plan.rows(what, x + dx, y + dy, message.axis, count), :]


def by_parity(offset, body):
    parity = lax.rem(lax.axis_index("gx") + offset, 2)
    for value in (0, 1):
        pl.when(parity == value)(functools.partial(body, value))


def pack_y_kernel(plan, fwd, adj, eps, e0, h0, e1, h1, coef, z_up, z_down, sems):
    nx, ny = plan.nx, plan.ny
    own = (pl.ds(STEPS, nx), pl.ds(0, ny), slice(None))
    copies = [pltpu.make_async_copy(eps, coef.at[own], sems.at[0])]
    for run, ref in enumerate((fwd, adj)):
        for kind, array in enumerate((e0, h0)):
            for i in range(6):
                copies.append(
                    pltpu.make_async_copy(ref.at[kind * 6 + i], array.at[(run * 6 + i, *own)], sems.at[len(copies)])
                )
    for copy in copies:
        copy.start()
    copies[0].wait()
    for x in range(nx):
        coef[STEPS + x, pl.ds(0, ny), :] = (0.5 * courant) / coef[STEPS + x, pl.ds(0, ny), :]
    e0, h0, e1, h1, coef = (array.reshape((-1, array.shape[-1])) for array in (e0, h0, e1, h1, coef))
    sweeps = Sweeps(plan, [e0, e1], [h0, h1], coef, ny)
    for run in (0, 1):
        for copy in copies[1 + 12 * run : 13 + 12 * run]:
            copy.wait()
        sweeps.both(1, range(nx), range(nx - 1), runs=(run,))
    state = State([e0, e1], [h0, h1], coef)
    pack(plan, plan.y_low, state, 0, ny, z_up)
    pack(plan, plan.y_high, state, 0, -ny, z_down)


def pack_x_kernel(plan, e0, h0, e1, h1, coef, x_up, x_down):
    state = State([e0, e1], [h0, h1], coef)
    pack(plan, plan.x_low, state, plan.nx, 0, x_up)
    pack(plan, plan.x_high, state, -plan.nx, 0, x_down)


def turns_kernel(groups, table, index, tiles, turns):
    row = index[0]
    phi_x, phi_y = table[row, 0], table[row, 1]
    at_x, at_y = lax.axis_index("gx"), lax.axis_index("gy")
    none = jnp.float32(0.0)
    ax_low = jnp.where(at_x == 0, -phi_x, none)
    ax_high = jnp.where(at_x == lax.axis_size("gx") - 1, phi_x, none)
    ay_low = jnp.where(at_y == 0, -phi_y, none)
    ay_high = jnp.where(at_y == lax.axis_size("gy") - 1, phi_y, none)
    sub = lax.broadcasted_iota(jnp.int32, (SUB, turns.shape[1]), 0)
    angles = jnp.zeros(sub.shape, jnp.float32)
    for i, angle in enumerate((ax_low, ax_high, ay_low, ay_high, ax_low + ay_low, ax_low + ay_high,
                               ax_high + ay_low, ax_high + ay_high)):
        angles = jnp.where(sub == i, angle, angles)
    turns[pl.ds(0, SUB), :] = jnp.cos(angles)
    turns[pl.ds(SUB, SUB), :] = jnp.sin(angles)
    own_tile = at_x * lax.axis_size("gy") + at_y
    chosen = tiles[0] == own_tile
    for i in range(1, tiles.shape[0]):
        chosen = jnp.logical_or(chosen, tiles[i] == own_tile)
    weight = jnp.where(chosen, jnp.float32(1.0 / groups), none)
    turns[pl.ds(2 * SUB, SUB), :] = jnp.full(sub.shape, weight, jnp.float32)


def relay_kernel(plan, z_low, z_high, to_far, to_mate):
    def corners(receiver):
        for messages, side, out in ((plan.far, plan.far_side, to_far), (plan.mate, plan.mate_side, to_mate)):
            dx = -plan.nx * side[receiver]
            for (what, x, y), row in messages[receiver].at.items():
                ref, source = (z_low, plan.y_low) if y < 0 else (z_high, plan.y_high)
                out[pl.ds(row, 1), :] = ref[pl.ds(source.at[what, x + dx, y], 1), :]

    by_parity(1, corners)


def turned(real, imag, cosine, sine):
    return real * cosine - imag * sine, real * sine + imag * cosine


def unpack(plan, message, ref, which, turns, state, kinds, level, layers=None):
    axis = message.axis
    for (kind, at_level, comp, run, part), x, y, count, at in message.runs:
        if kind not in kinds or at_level != level or part == 1:
            continue
        pieces = [(x, y, count, at)]
        if layers is not None:
            pieces = [(x + i, y, 1, at + i) for i in range(count) if x + i in layers]
        for cell_x, cell_y, size, row in pieces:
            what = (kind, at_level, comp, run, 0)
            real = ref[pl.ds(row, size), :]
            if kind == "C":
                state(what)[plan.rows(what, cell_x, cell_y, axis, size), :] = real
                continue
            twin = (kind, at_level, comp, run, 1)
            imag = ref[pl.ds(message.at[twin, cell_x, cell_y], size), :]
            turn = which(y)
            cosine, sine = turns[pl.ds(turn, 1), :], turns[pl.ds(SUB + turn, 1), :]
            real, imag = turned(real, imag, cosine, sine if run == 0 else -sine)
            state(what)[plan.rows(what, cell_x, cell_y, axis, size), :] = real
            state(twin)[plan.rows(twin, cell_x, cell_y, axis, size), :] = imag


class Sweeps:
    def __init__(self, plan, efield, hfield, coef, height, todo=None):
        self.plan, self.efield, self.hfield, self.coef, self.height = plan, efield, hfield, coef, height
        self.todo = todo

    def rows(self, run, part, comp, x, start, stop):
        return pl.ds(self.plan.row(x, 0, run, part, comp) + start, stop - start)

    def get(self, array, run, part, comp, x):
        return array[self.rows(run, part, comp, x, 0, self.height), :]

    def pieces(self, kind, step, x):
        if self.todo is None:
            return [(comp, 0, self.height) for comp in range(3)]
        found = []
        for comp, tiles in sorted(self.todo.get((kind, step, x), {}).items()):
            for tile in sorted(tiles):
                if found and found[-1][0] == comp and found[-1][2] == tile * SUB:
                    found[-1] = (comp, found[-1][1], (tile + 1) * SUB)
                else:
                    found.append((comp, tile * SUB, (tile + 1) * SUB))
        return found

    def next_z(self, value):
        lane = lax.broadcasted_iota(jnp.int32, value.shape, 1)
        return jnp.where(lane == value.shape[1] - 1, 0.0, pltpu.roll(value, value.shape[1] - 1, 1))

    def prev_z(self, value):
        lane = lax.broadcasted_iota(jnp.int32, value.shape, 1)
        return jnp.where(lane == 0, 0.0, pltpu.roll(value, 1, 1))

    def next_y(self, value):
        return pltpu.roll(value, self.height - 1, 0)

    def prev_y(self, value):
        return pltpu.roll(value, 1, 0)

    def update_h(self, step, run, part, x):
        efield, old, new = self.efield[step - 1], self.hfield[step - 1], self.hfield[step]
        ex, ey, ez = (self.get(efield, run, part, comp, x) for comp in range(3))
        for comp, start, stop in self.pieces("H", step, x):
            here = slice(start, stop)
            if comp == 0:
                curl = (self.next_y(ez) - ez)[here] - (self.next_z(ey[here]) - ey[here])
            elif comp == 1:
                ez_x = self.get(efield, run, part, 2, x + 1)
                curl = (self.next_z(ex[here]) - ex[here]) - (ez_x - ez)[here]
            else:
                ey_x = self.get(efield, run, part, 1, x + 1)
                curl = (ey_x - ey)[here] - (self.next_y(ex) - ex)[here]
            before = self.get(old, run, part, comp, x)[here]
            if step == 1:
                before = before + before
            new[self.rows(run, part, comp, x, start, stop), :] = before - curl

    def update_e(self, step, run, part, x):
        old, new, hfield = self.efield[step - 1], self.efield[step], self.hfield[step]
        hx, hy, hz = (self.get(hfield, run, part, comp, x) for comp in range(3))
        scale = self.get(self.coef, 0, 0, 0, x)
        for comp, start, stop in self.pieces("E", step, x):
            here = slice(start, stop)
            if comp == 0:
                curl = (hz - self.prev_y(hz))[here] - (hy[here] - self.prev_z(hy[here]))
            elif comp == 1:
                hz_x = self.get(hfield, run, part, 2, x - 1)
                curl = (hx[here] - self.prev_z(hx[here])) - (hz - hz_x)[here]
            else:
                hy_x = self.get(hfield, run, part, 1, x - 1)
                curl = (hy - hy_x)[here] - (hx - self.prev_y(hx))[here]
            before = self.get(old, run, part, comp, x)[here]
            new[self.rows(run, part, comp, x, start, stop), :] = before + scale[here] * curl

    def both(self, step, h_layers, e_layers, after_h=None, after_e=None, runs=(0, 1)):
        for update, layers, after in ((self.update_h, h_layers, after_h), (self.update_e, e_layers, after_e)):
            for x in layers:
                for run in runs:
                    for part in (0, 1):
                        update(step, run, part, x)
            if after is not None:
                after()


def middle_kernel(plan, e0_in, h0_in, e1_in, h1_in, coef_in, z_low, z_high, turns, *arrays):
    nx = plan.nx
    efield, hfield, coef = arrays[: STEPS + 1], arrays[STEPS + 1 : 2 * STEPS + 2], arrays[-1]
    state = State(efield, hfield, coef)

    def take(kinds, level):
        unpack(plan, plan.y_low, z_low, lambda y: 2, turns, state, kinds, level)
        unpack(plan, plan.y_high, z_high, lambda y: 3, turns, state, kinds, level)

    take("EHC", 0)
    sweeps = Sweeps(plan, efield, hfield, coef, plan.ring, plan.made)
    for step in range(1, STEPS + 1):
        after = [lambda: take("H", 1), lambda: take("E", 1)] if step == 1 else []
        sweeps.both(step, range(step - 1, nx - step), range(step, nx - step), *after)


def add_known(plan, efield, levels, transform, out):
    nx, ny = plan.nx, plan.ny
    for x in range(nx):
        for tile in range(ny // SUB):
            for comp in range(3):
                ends = []
                for run in (0, 1):
                    at = [pl.ds(((part * 3 + comp) * nx + x) * ny + tile * SUB, SUB) for part in (0, 1)]
                    real, imag = transform[run][at[0], :], transform[run][at[1], :]
                    for level in levels(x, tile, comp):
                        theta = omega_step * level
                        here = [efield[level][pl.ds(plan.row(x, tile * SUB, run, part, comp), SUB), :] for part in (0, 1)]
                        more = turned(*here, math.cos(theta), math.sin(theta))
                        real, imag = real + more[0], imag + more[1]
                    out[run][at[0], :], out[run][at[1], :] = real, imag
                    ends.append((real, imag))
                yield x, tile, ends


def known(plan, x, tile, comp):
    def ready(level):
        return level <= x < plan.nx - level or tile in plan.free.get(("E", level, x), {}).get(comp, ())

    return [level for level in range(1, STEPS + 1) if ready(level)]


def do_valleys(plan, sweeps, take):
    for step in range(1, STEPS + 1):
        low, high = step - STEPS, plan.nx - step
        h_layers = [*range(low - 1, step - 1), *range(high, plan.nx + STEPS - step)]
        e_layers = [*range(low, step), *range(high, plan.nx + STEPS - step)]
        after = [functools.partial(take, "H", 1, h_layers), functools.partial(take, "E", 1, e_layers)] if step == 1 else []
        sweeps.both(step, h_layers, e_layers, *after)


def faces_kernel(plan, *refs):
    count = 2 * STEPS + 3
    x_low, x_high, z_low, z_high, turns, spec_f, spec_a = refs[count : count + 7]
    arrays = refs[count + 7 : 2 * count + 7]
    out_f, out_a = refs[2 * count + 7 :]
    efield, hfield, coef = arrays[: STEPS + 1], arrays[STEPS + 1 : 2 * STEPS + 2], arrays[-1]
    state = State(efield, hfield, coef)

    def take(kinds, level, layers):
        unpack(plan, plan.x_low, x_low, lambda y: 0, turns, state, kinds, level)
        unpack(plan, plan.x_high, x_high, lambda y: 1, turns, state, kinds, level)
        unpack(plan, plan.y_low, z_low, lambda y: 2, turns, state, kinds, level, layers)
        unpack(plan, plan.y_high, z_high, lambda y: 3, turns, state, kinds, level, layers)

    take("EHC", 0, ())
    do_valleys(plan, Sweeps(plan, efield, hfield, coef, plan.ring, plan.free), take)
    for _ in add_known(plan, efield, functools.partial(known, plan), (spec_f, spec_a), (out_f, out_a)):
        pass


def edges_kernel(plan, groups, *refs):
    count = 2 * STEPS + 3
    x_low, x_high, far, mate, z_low, z_high, turns, part_f, part_a = refs[count : count + 9]
    arrays = refs[count + 9 : 2 * count + 9]
    out_f, out_a, *parts = refs[2 * count + 9 :]
    efield, hfield, coef = arrays[: STEPS + 1], arrays[STEPS + 1 : 2 * STEPS + 2], arrays[-1]
    state = State(efield, hfield, coef)

    def take(kinds, level, layers):
        if level:
            unpack(plan, plan.x_low, x_low, lambda y: 0, turns, state, kinds, level)
            unpack(plan, plan.x_high, x_high, lambda y: 1, turns, state, kinds, level)

        def corners(receiver):
            for messages, ref, side in ((plan.far, far, plan.far_side), (plan.mate, mate, plan.mate_side)):
                first = 4 if side[receiver] < 0 else 6
                unpack(plan, messages[receiver], ref, lambda y: first + (y >= 0), turns, state, kinds, level)

        by_parity(0, corners)
        unpack(plan, plan.y_low, z_low, lambda y: 2, turns, state, kinds, level, layers)
        unpack(plan, plan.y_high, z_high, lambda y: 3, turns, state, kinds, level, layers)

    take("EHC", 0, ())
    do_valleys(plan, Sweeps(plan, efield, hfield, coef, plan.ring, plan.rest), take)

    share = plan.depth // groups
    shift = lax.rem(groups - lax.axis_index("angle"), groups) * share
    weight = turns[pl.ds(2 * SUB, SUB), :]

    def rest(x, tile, comp):
        return [level for level in range(1, STEPS + 1) if level not in known(plan, x, tile, comp)]

    totals = {}
    for x, tile, ends in add_known(plan, efield, rest, (part_f, part_a), (out_f, out_a)):
        term = ends[0][0] * ends[1][0] - ends[0][1] * ends[1][1]
        totals[x, tile] = totals[x, tile] + term if (x, tile) in totals else term
    block = lax.broadcasted_iota(jnp.int32, weight.shape, 1) // share
    tiles = [pltpu.roll(total * weight, shift, 1) for total in totals.values()]
    for k, part in enumerate(parts):
        for i in range(len(tiles) // groups):
            packed = jnp.zeros(weight.shape, jnp.float32)
            for t in range(groups):
                lanes = (t - k) % groups * share
                value = tiles[i * groups + t]
                packed = jnp.where(block == t, pltpu.roll(value, lanes, 1) if lanes else value, packed)
            part[pl.ds(i * SUB, SUB), :] = packed


def sum_kernel(groups, *refs):
    *parts, out = refs
    share = out.shape[1]
    for i in range(parts[0].shape[0] // SUB):
        total = parts[0][pl.ds(i * SUB, SUB), :]
        for part in parts[1:]:
            total = total + part[pl.ds(i * SUB, SUB), :]
        for t in range(groups):
            out[pl.ds((i * groups + t) * SUB, SUB), :] = total[:, t * share : (t + 1) * share]


def write_kernel(tr_f, tr_a, out_f, out_a, sems):
    copies = []
    for source, target in ((tr_f, out_f), (tr_a, out_a)):
        for i in range(source.shape[0]):
            copies.append(pltpu.make_async_copy(source.at[i], target.at[i], sems.at[len(copies)]))
    for copy in copies:
        copy.start()
    for copy in copies:
        copy.wait()


def ring_pairs(axis, offset):
    size = lax.axis_size(axis)
    return [(i, (i + offset) % size) for i in range(size)]


def mate_pairs():
    return [(i, i ^ 1) for i in range(lax.axis_size("gx"))]


def far_pairs():
    size = lax.axis_size("gx")
    return [(i, (i + (1 if i % 2 else -1)) % size) for i in range(size)]


def shards(
    forward_fields,
    adjoint_fields,
    forward_spectrum,
    adjoint_spectrum,
    permittivity,
    phase_table,
    angle_index,
    design_tiles,
):
    nx, ny, depth = permittivity.shape
    plan = Plan(nx, ny, depth)
    groups = lax.axis_size("angle")
    wide, ring = plan.wide, plan.ring

    def array(*shape):
        return jax.ShapeDtypeStruct(shape, jnp.float32)

    def lines(count):
        return array(count, depth)

    def params(mib):
        return pltpu.CompilerParams(vmem_limit_bytes=mib * 2**20)

    def cost(size):
        return pl.CostEstimate(flops=size, bytes_accessed=size, transcendentals=0)

    assert lax.axis_size("gx") % 2 == 0 and nx * ny % (groups * SUB) == 0
    with jax.named_scope("pack_y"):
        *first, coef, z_up, z_down = pl.pallas_call(
            functools.partial(pack_y_kernel, plan),
            out_shape=(
                *[array(12, wide, ring, depth)] * 4,
                array(wide, ring, depth),
                lines(plan.y_low.lines),
                lines(plan.y_high.lines),
            ),
            in_specs=[HBM] * 3,
            out_specs=[VMEM] * 7,
            scratch_shapes=[pltpu.SemaphoreType.DMA((25,))],
            compiler_params=params(8),
        )(*(pltpu.with_memory_space_constraint(array, pltpu.HBM) for array in (forward_fields[0], adjoint_fields[0], permittivity)))
    e0, h0, e1, h1, coef = (state.reshape((-1, depth)) for state in (*first, coef))
    with jax.named_scope("send_y"):
        z_low = lax.ppermute(z_up, "gy", ring_pairs("gy", 1))
        z_high = lax.ppermute(z_down, "gy", ring_pairs("gy", -1))
    with jax.named_scope("pack_x"):
        x_up, x_down = pl.pallas_call(
            functools.partial(pack_x_kernel, plan),
            out_shape=(lines(plan.x_low.lines), lines(plan.x_high.lines)),
            in_specs=[VMEM] * 5,
            out_specs=[VMEM] * 2,
            compiler_params=params(8),
            cost_estimate=cost(40 * 2**20),
        )(e0, h0, e1, h1, coef)
    with jax.named_scope("send_x"):
        x_low = lax.ppermute(x_up, "gx", ring_pairs("gx", 1))
        x_high = lax.ppermute(x_down, "gx", ring_pairs("gx", -1))
    with jax.named_scope("turns"):
        turns = pl.pallas_call(
            functools.partial(turns_kernel, groups),
            out_shape=lines(3 * SUB),
            in_specs=[SMEM] * 3,
            out_specs=VMEM,
            compiler_params=params(4),
        )(phase_table, angle_index, design_tiles)
    with jax.named_scope("relay_corners"):
        to_far, to_mate = pl.pallas_call(
            functools.partial(relay_kernel, plan),
            out_shape=[lines(plan.corner_lines)] * 2,
            in_specs=[VMEM] * 2,
            out_specs=[VMEM] * 2,
            compiler_params=params(4),
        )(z_low, z_high)
        far = lax.ppermute(to_far, "gx", far_pairs())
        mate = lax.ppermute(to_mate, "gx", mate_pairs())
    level = lines(12 * wide * ring)
    count = 2 * STEPS + 3
    levels = [level] * (count - 1) + [lines(wide * ring)]
    with jax.named_scope("middle"):
        state = pl.pallas_call(
            functools.partial(middle_kernel, plan),
            out_shape=levels,
            in_specs=[VMEM] * 8,
            out_specs=[VMEM] * count,
            input_output_aliases={0: 0, 1: STEPS + 1, 2: 1, 3: STEPS + 2, 4: count - 1},
            compiler_params=params(8),
            cost_estimate=cost(2**32),
        )(e0, h0, e1, h1, coef, z_low, z_high, turns)
    transforms = [lines(6 * nx * ny)] * 2
    with jax.named_scope("faces"):
        spectra = [spectrum.reshape((-1, depth)) for spectrum in (forward_spectrum, adjoint_spectrum)]
        results = pl.pallas_call(
            functools.partial(faces_kernel, plan),
            out_shape=[*levels, *transforms],
            in_specs=[VMEM] * (count + 7),
            out_specs=[VMEM] * (count + 2),
            input_output_aliases={i: i for i in range(count)},
            compiler_params=params(8),
        )(*state, x_low, x_high, z_low, z_high, turns, *spectra)
        state, sums = results[:count], results[count:]
    with jax.named_scope("edges"):
        results = pl.pallas_call(
            functools.partial(edges_kernel, plan, groups),
            out_shape=[*levels, *transforms, *[lines(nx * ny // groups)] * groups],
            in_specs=[VMEM] * (count + 9),
            out_specs=[VMEM] * (count + 2 + groups),
            input_output_aliases={i: i for i in range(count)} | {count + 7: count, count + 8: count + 1},
            compiler_params=params(8),
        )(*state, x_low, x_high, far, mate, z_low, z_high, turns, *sums)
        tr_f, tr_a, own, *others = results[count:]
    with jax.named_scope("sum_angles"):
        others = [lax.ppermute(part, "angle", ring_pairs("angle", k + 1)) for k, part in enumerate(others)]
        gradient = pl.pallas_call(
            functools.partial(sum_kernel, groups),
            out_shape=array(nx * ny, depth // groups),
            in_specs=[VMEM] * groups,
            out_specs=VMEM,
            compiler_params=params(4),
        )(own, *others)
    with jax.named_scope("write"):
        out_f, out_a = pl.pallas_call(
            write_kernel,
            out_shape=[array(6, nx, ny, depth)] * 2,
            in_specs=[VMEM] * 2,
            out_specs=[HBM] * 2,
            scratch_shapes=[pltpu.SemaphoreType.DMA((12,))],
            compiler_params=params(4),
        )(tr_f.reshape((6, nx, ny, depth)), tr_a.reshape((6, nx, ny, depth)))
    return (
        out_f.reshape(forward_spectrum.shape),
        out_a.reshape(adjoint_spectrum.shape),
        gradient.reshape((nx, ny, depth // groups)),
    )


def solution(mesh):
    in_specs = (
        P("angle", None, "gx", "gy", None),
        P("angle", None, "gx", "gy", None),
        P("angle", None, "gx", "gy", None),
        P("angle", None, "gx", "gy", None),
        P("gx", "gy", None),
        P(),
        P("angle"),
        P(),
    )
    out_specs = (
        P("angle", None, "gx", "gy", None),
        P("angle", None, "gx", "gy", None),
        P("gx", "gy", "angle"),
    )
    return jax.shard_map(shards, mesh=mesh, in_specs=in_specs, out_specs=out_specs, check_vma=False)
```

```python
import functools
import math

import jax
import jax.numpy as jnp
from jax import lax
from jax.experimental import pallas as pl
from jax.experimental.pallas import tpu as pltpu
from jax.sharding import PartitionSpec as P

STEPS = 3
SUB = 8

courant = 0.5
omega_step = 0.7

VMEM = pl.BlockSpec(memory_space=pltpu.VMEM)
SMEM = pl.BlockSpec(memory_space=pltpu.SMEM)
HBM = pl.BlockSpec(memory_space=pltpu.HBM)


def reads(node):
    kind, level, comp, x, y = node
    others = [c for c in range(3) if c != comp]
    if kind == "E":
        found = [("E", level - 1, comp, x, y), ("C", 0, 0, x, y)] + [("H", level, c, x, y) for c in others]
        if comp != 1:
            found.append(("H", level, 2 - comp, x, y - 1))
        if comp != 0:
            found.append(("H", level, 3 - comp, x - 1, y))
        return found
    found = [("H", level - 1, comp, x, y)] + [("E", level - 1, c, x, y) for c in others]
    if comp != 1:
        found.append(("E", level - 1, 2 - comp, x, y + 1))
    if comp != 0:
        found.append(("E", level - 1, 3 - comp, x + 1, y))
    return found


def wanted(nx, ny):
    def block(node):
        return node[3] // nx, node[4] // ny

    @functools.cache
    def alone(node):
        if node[1] == 0:
            return True
        return node[1] == 1 and all(block(other) == block(node) and alone(other) for other in reads(node))

    found, made, seen = set(), set(), set()
    todo = [("E", STEPS, comp, x, y) for comp in range(3) for x in range(nx) for y in range(ny)]
    while todo:
        node = todo.pop()
        if node in seen:
            continue
        seen.add(node)
        if block(node) != (0, 0) and alone(node):
            found.add(node)
        elif node[1]:
            made.add(node)
            todo += reads(node)
    return found, made


class Message:
    def __init__(self, nodes, axis, folded=()):
        self.axis, self.runs, self.at, self.size = axis, [], {}, 0
        assert nodes.issuperset(folded)
        self.zeros = Message(set(folded), axis).runs if folded else []
        nodes = nodes - set(folded)
        stretches = []
        for node in sorted(nodes):
            before = list(node)
            before[3 + axis] -= 1
            if tuple(before) in nodes:
                continue
            count = 1
            while (*node[:3], node[3] + count * (axis == 0), node[4] + count * (axis == 1)) in nodes:
                count += 1
            stretches.append((count, node))
        for count, (kind, level, comp, x, y) in sorted(stretches, key=lambda item: (-item[0], item[1])):
            for run in (0, 1) if kind != "C" else (0,):
                for part in (0, 1) if kind != "C" else (0,):
                    what = (kind, level, comp, run, part)
                    self.runs.append((what, x, y, count, self.size))
                    for i in range(count):
                        self.at[what, x + i * (axis == 0), y + i * (axis == 1)] = self.size + i
                    self.size += count
        self.lines = -(-self.size // SUB) * SUB


class Plan:
    def __init__(self, nx, ny, depth):
        self.depth = depth
        self.nx, self.ny = nx, ny
        self.wide, self.ring = nx + 2 * STEPS, ny + SUB
        nodes, made = wanted(nx, ny)
        self.made, self.free, self.rest = {}, {}, {}
        tiles, ready = {}, set()
        for node in made:
            tiles.setdefault((node[1], "HE".index(node[0]), *node[2:4], node[4] % self.ring // SUB), []).append(node)

        def early(node):
            if node in made:
                return node in ready
            return node not in nodes or 0 <= node[3] < nx or 0 <= node[4] < ny

        for (level, order, comp, x, tile), members in sorted(tiles.items()):
            key = ("HE"[order], level, x)
            middle = level - 1 + order <= x < nx - level
            free = middle or all(early(other) for node in members for other in reads(node))
            if free:
                ready.update(members)
            for into in (self.made, self.free if free else self.rest):
                into.setdefault(key, {}).setdefault(comp, set()).add(tile)
        sides = {}
        for node in nodes:
            sides.setdefault((node[3] // nx, node[4] // ny), set()).add(node)

        def shifted(found, dx):
            return {(*node[:3], node[3] + dx, node[4]) for node in found}

        y_low, y_high = (sides[0, side] | shifted(sides[-1, side], nx) | shifted(sides[1, side], -nx) for side in (-1, 1))
        self.x_folds = (1, ny - 2), (2, ny - 2)
        self.y_folds = (2, nx - 2), (3, nx - 2)
        x_folded = [("E", 1, comp, -2, y) for comp in range(3) for y in range(*self.x_folds[comp == 0])]
        y_folded = [("E", 1, comp, x, -2) for comp in range(3) for x in range(*self.y_folds[comp == 1])]
        self.y_low, self.y_high = Message(y_low, 0, y_folded), Message(y_high, 0)
        self.x_low, self.x_high = Message(sides[-1, 0], 1, x_folded), Message(sides[1, 0], 1)
        self.mate_side, self.far_side = (1, -1), (-1, 1)
        self.mate, self.far = ([Message(sides[side, -1] | sides[side, 1], 1) for side in order] for order in (self.mate_side, self.far_side))
        self.corner_lines = max(message.lines for message in self.mate)

    def row(self, x, y, run=0, part=0, comp=0):
        return ((run * 6 + part * 3 + comp) * self.wide + x + STEPS) * self.ring + y % self.ring

    def rows(self, what, x, y, axis, count):
        _, _, comp, run, part = what
        start = self.row(x, y, run, part, comp)
        return pl.ds(start, count, stride=self.ring) if axis == 0 and count > 1 else pl.ds(start, count)


class State:
    def __init__(self, efield, hfield, coef):
        self.by_kind = {"E": efield, "H": hfield, "C": [coef]}

    def __call__(self, what):
        return self.by_kind[what[0]][what[1]]


def pack(plan, message, state, dx, dy, out, changed=None):
    for what, x, y, count, at in message.runs:
        layer, first = (y, x) if message.axis == 0 else (x, y)
        if changed and (what, layer) in changed:
            ref, row = changed[what, layer]
            value = ref[pl.ds(row + first, count), :]
        else:
            value = state(what)[plan.rows(what, x + dx, y + dy, message.axis, count), :]
        out[pl.ds(at, count), :] = value


def fold(plan, state, axis, scratch):
    nx, ny = plan.nx, plan.ny
    size, normal = (nx, 1) if axis == 0 else (ny, 0)
    before, after = ((0, 2) if axis == 0 else (1, 2))
    cell = lax.broadcasted_iota(jnp.int32, (size, scratch.shape[1]), 0)
    lane = lax.broadcasted_iota(jnp.int32, cell.shape, 1)
    folds = plan.y_folds if axis == 0 else plan.x_folds
    changed = {}

    def lines(what, layer):
        place = (0, ny + layer) if axis == 0 else (nx + layer, 0)
        return state(what)[plan.rows(what, *place, axis, size), :]

    def inside(value, fold):
        return jnp.where((cell >= fold[0]) & (cell < fold[1]), value, 0.0)

    for run in (0, 1):
        for part in (0, 1):

            def get(kind, level, comp, layer):
                return lines((kind, level, comp, run, part), layer)

            def put(kind, level, comp, layer, value):
                row = len(changed) * size
                scratch[pl.ds(row, size), :] = value
                changed[(kind, level, comp, run, part), layer] = scratch, row

            low, high = (inside(get("E", 1, comp, -2), folds[0]) for comp in (before, after))
            along = inside(get("E", 1, normal, -2), folds[1])
            along_z = jnp.where(lane == lane.shape[1] - 1, 0.0, pltpu.roll(along, lane.shape[1] - 1, 1)) - along
            along_next = pltpu.roll(along, size - 1, 0) - along
            sign = 1.0 if axis == 0 else -1.0
            d_before = sign * (high + along_z)
            d_after = -sign * (low + along_next)
            scale = lines(("C", 0, 0, 0, 0), -1)
            put("H", 1, before, -2, get("H", 1, before, -2) + d_before)
            put("H", 1, after, -2, get("H", 1, after, -2) + d_after)
            put("E", 0, before, -1, get("E", 0, before, -1) + sign * scale * d_after)
            put("E", 0, after, -1, get("E", 0, after, -1) - sign * scale * d_before)
            put("H", 0, before, -1, get("H", 0, before, -1) + 0.5 * scale * d_before)
            put("H", 0, after, -1, get("H", 0, after, -1) + 0.5 * scale * d_after)
    return changed


def by_parity(offset, body):
    parity = lax.rem(lax.axis_index("gx") + offset, 2)
    for value in (0, 1):
        pl.when(parity == value)(functools.partial(body, value))


def pack_y_kernel(plan, fwd, adj, eps, e0, h0, e1, h1, coef, z_up, z_down, sems, scratch):
    nx, ny = plan.nx, plan.ny
    own = (pl.ds(STEPS, nx), pl.ds(0, ny), slice(None))
    copies = [pltpu.make_async_copy(eps, coef.at[own], sems.at[0])]
    for run, ref in enumerate((fwd, adj)):
        for kind, array in enumerate((e0, h0)):
            for i in range(6):
                copies.append(
                    pltpu.make_async_copy(ref.at[kind * 6 + i], array.at[(run * 6 + i, *own)], sems.at[len(copies)])
                )
    for copy in copies:
        copy.start()
    copies[0].wait()
    for x in range(nx):
        coef[STEPS + x, pl.ds(0, ny), :] = (0.5 * courant) / coef[STEPS + x, pl.ds(0, ny), :]
    e0, h0, e1, h1, coef = (array.reshape((-1, array.shape[-1])) for array in (e0, h0, e1, h1, coef))
    sweeps = Sweeps(plan, [e0, e1], [h0, h1], coef, ny)
    for run in (0, 1):
        for copy in copies[1 + 12 * run : 13 + 12 * run]:
            copy.wait()
        sweeps.both(1, range(nx), range(nx - 1), runs=(run,))
    state = State([e0, e1], [h0, h1], coef)
    pack(plan, plan.y_low, state, 0, ny, z_up, fold(plan, state, 0, scratch))
    pack(plan, plan.y_high, state, 0, -ny, z_down)


def pack_x_kernel(plan, e0, h0, e1, h1, coef, x_up, x_down, scratch):
    state = State([e0, e1], [h0, h1], coef)
    pack(plan, plan.x_low, state, plan.nx, 0, x_up, fold(plan, state, 1, scratch))
    pack(plan, plan.x_high, state, -plan.nx, 0, x_down)


def turns_kernel(groups, table, index, tiles, turns):
    row = index[0]
    phi_x, phi_y = table[row, 0], table[row, 1]
    at_x, at_y = lax.axis_index("gx"), lax.axis_index("gy")
    none = jnp.float32(0.0)
    ax_low = jnp.where(at_x == 0, -phi_x, none)
    ax_high = jnp.where(at_x == lax.axis_size("gx") - 1, phi_x, none)
    ay_low = jnp.where(at_y == 0, -phi_y, none)
    ay_high = jnp.where(at_y == lax.axis_size("gy") - 1, phi_y, none)
    sub = lax.broadcasted_iota(jnp.int32, (SUB, turns.shape[1]), 0)
    angles = jnp.zeros(sub.shape, jnp.float32)
    for i, angle in enumerate((ax_low, ax_high, ay_low, ay_high, ax_low + ay_low, ax_low + ay_high,
                               ax_high + ay_low, ax_high + ay_high)):
        angles = jnp.where(sub == i, angle, angles)
    turns[pl.ds(0, SUB), :] = jnp.cos(angles)
    turns[pl.ds(SUB, SUB), :] = jnp.sin(angles)
    own_tile = at_x * lax.axis_size("gy") + at_y
    chosen = tiles[0] == own_tile
    for i in range(1, tiles.shape[0]):
        chosen = jnp.logical_or(chosen, tiles[i] == own_tile)
    weight = jnp.where(chosen, jnp.float32(1.0 / groups), none)
    turns[pl.ds(2 * SUB, SUB), :] = jnp.full(sub.shape, weight, jnp.float32)


def relay_kernel(plan, z_low, z_high, to_far, to_mate):
    def corners(receiver):
        for messages, side, out in ((plan.far, plan.far_side, to_far), (plan.mate, plan.mate_side, to_mate)):
            dx = -plan.nx * side[receiver]
            for (what, x, y), row in messages[receiver].at.items():
                ref, source = (z_low, plan.y_low) if y < 0 else (z_high, plan.y_high)
                out[pl.ds(row, 1), :] = ref[pl.ds(source.at[what, x + dx, y], 1), :]

    by_parity(1, corners)


def turned(real, imag, cosine, sine):
    return real * cosine - imag * sine, real * sine + imag * cosine


def unpack(plan, message, ref, which, turns, state, kinds, level, layers=None):
    axis = message.axis
    for (kind, at_level, comp, run, part), x, y, count, at in message.runs:
        if kind not in kinds or at_level != level or part == 1:
            continue
        pieces = [(x, y, count, at)]
        if layers is not None:
            pieces = [(x + i, y, 1, at + i) for i in range(count) if x + i in layers]
        for cell_x, cell_y, size, row in pieces:
            what = (kind, at_level, comp, run, 0)
            real = ref[pl.ds(row, size), :]
            if kind == "C":
                state(what)[plan.rows(what, cell_x, cell_y, axis, size), :] = real
                continue
            twin = (kind, at_level, comp, run, 1)
            imag = ref[pl.ds(message.at[twin, cell_x, cell_y], size), :]
            turn = which(y)
            cosine, sine = turns[pl.ds(turn, 1), :], turns[pl.ds(SUB + turn, 1), :]
            real, imag = turned(real, imag, cosine, sine if run == 0 else -sine)
            state(what)[plan.rows(what, cell_x, cell_y, axis, size), :] = real
            state(twin)[plan.rows(twin, cell_x, cell_y, axis, size), :] = imag
    for what, x, y, count, _ in message.zeros:
        if what[0] in kinds and what[1] == level and layers is None:
            state(what)[plan.rows(what, x, y, axis, count), :] = jnp.zeros((count, ref.shape[1]), jnp.float32)


class Sweeps:
    def __init__(self, plan, efield, hfield, coef, height, todo=None):
        self.plan, self.efield, self.hfield, self.coef, self.height = plan, efield, hfield, coef, height
        self.todo = todo

    def rows(self, run, part, comp, x, start, stop):
        return pl.ds(self.plan.row(x, 0, run, part, comp) + start, stop - start)

    def get(self, array, run, part, comp, x):
        return array[self.rows(run, part, comp, x, 0, self.height), :]

    def pieces(self, kind, step, x):
        if self.todo is None:
            return [(comp, 0, self.height) for comp in range(3)]
        found = []
        for comp, tiles in sorted(self.todo.get((kind, step, x), {}).items()):
            for tile in sorted(tiles):
                if found and found[-1][0] == comp and found[-1][2] == tile * SUB:
                    found[-1] = (comp, found[-1][1], (tile + 1) * SUB)
                else:
                    found.append((comp, tile * SUB, (tile + 1) * SUB))
        return found

    def next_z(self, value):
        lane = lax.broadcasted_iota(jnp.int32, value.shape, 1)
        return jnp.where(lane == value.shape[1] - 1, 0.0, pltpu.roll(value, value.shape[1] - 1, 1))

    def prev_z(self, value):
        lane = lax.broadcasted_iota(jnp.int32, value.shape, 1)
        return jnp.where(lane == 0, 0.0, pltpu.roll(value, 1, 1))

    def next_y(self, value):
        return pltpu.roll(value, self.height - 1, 0)

    def prev_y(self, value):
        return pltpu.roll(value, 1, 0)

    def update_h(self, step, run, part, x):
        efield, old, new = self.efield[step - 1], self.hfield[step - 1], self.hfield[step]
        ex, ey, ez = (self.get(efield, run, part, comp, x) for comp in range(3))
        for comp, start, stop in self.pieces("H", step, x):
            here = slice(start, stop)
            if comp == 0:
                curl = (self.next_y(ez) - ez)[here] - (self.next_z(ey[here]) - ey[here])
            elif comp == 1:
                ez_x = self.get(efield, run, part, 2, x + 1)
                curl = (self.next_z(ex[here]) - ex[here]) - (ez_x - ez)[here]
            else:
                ey_x = self.get(efield, run, part, 1, x + 1)
                curl = (ey_x - ey)[here] - (self.next_y(ex) - ex)[here]
            before = self.get(old, run, part, comp, x)[here]
            if step == 1:
                before = before + before
            new[self.rows(run, part, comp, x, start, stop), :] = before - curl

    def update_e(self, step, run, part, x):
        old, new, hfield = self.efield[step - 1], self.efield[step], self.hfield[step]
        hx, hy, hz = (self.get(hfield, run, part, comp, x) for comp in range(3))
        scale = self.get(self.coef, 0, 0, 0, x)
        for comp, start, stop in self.pieces("E", step, x):
            here = slice(start, stop)
            if comp == 0:
                curl = (hz - self.prev_y(hz))[here] - (hy[here] - self.prev_z(hy[here]))
            elif comp == 1:
                hz_x = self.get(hfield, run, part, 2, x - 1)
                curl = (hx[here] - self.prev_z(hx[here])) - (hz - hz_x)[here]
            else:
                hy_x = self.get(hfield, run, part, 1, x - 1)
                curl = (hy - hy_x)[here] - (hx - self.prev_y(hx))[here]
            before = self.get(old, run, part, comp, x)[here]
            new[self.rows(run, part, comp, x, start, stop), :] = before + scale[here] * curl

    def both(self, step, h_layers, e_layers, after_h=None, after_e=None, runs=(0, 1)):
        for update, layers, after in ((self.update_h, h_layers, after_h), (self.update_e, e_layers, after_e)):
            for x in layers:
                for run in runs:
                    for part in (0, 1):
                        update(step, run, part, x)
            if after is not None:
                after()


def middle_kernel(plan, e0_in, h0_in, e1_in, h1_in, coef_in, z_low, z_high, turns, *arrays):
    nx = plan.nx
    efield, hfield, coef = arrays[: STEPS + 1], arrays[STEPS + 1 : 2 * STEPS + 2], arrays[-1]
    state = State(efield, hfield, coef)

    def take(kinds, level):
        unpack(plan, plan.y_low, z_low, lambda y: 2, turns, state, kinds, level)
        unpack(plan, plan.y_high, z_high, lambda y: 3, turns, state, kinds, level)

    take("EHC", 0)
    sweeps = Sweeps(plan, efield, hfield, coef, plan.ring, plan.made)
    for step in range(1, STEPS + 1):
        after = [lambda: take("H", 1), lambda: take("E", 1)] if step == 1 else []
        sweeps.both(step, range(step - 1, nx - step), range(step, nx - step), *after)


def add_known(plan, efield, levels, transform, out):
    nx, ny = plan.nx, plan.ny
    for x in range(nx):
        for tile in range(ny // SUB):
            for comp in range(3):
                ends = []
                for run in (0, 1):
                    at = [pl.ds(((part * 3 + comp) * nx + x) * ny + tile * SUB, SUB) for part in (0, 1)]
                    real, imag = transform[run][at[0], :], transform[run][at[1], :]
                    for level in levels(x, tile, comp):
                        theta = omega_step * level
                        here = [efield[level][pl.ds(plan.row(x, tile * SUB, run, part, comp), SUB), :] for part in (0, 1)]
                        more = turned(*here, math.cos(theta), math.sin(theta))
                        real, imag = real + more[0], imag + more[1]
                    out[run][at[0], :], out[run][at[1], :] = real, imag
                    ends.append((real, imag))
                yield x, tile, ends


def known(plan, x, tile, comp):
    def ready(level):
        return level <= x < plan.nx - level or tile in plan.free.get(("E", level, x), {}).get(comp, ())

    return [level for level in range(1, STEPS + 1) if ready(level)]


def do_valleys(plan, sweeps, take):
    for step in range(1, STEPS + 1):
        low, high = step - STEPS, plan.nx - step
        h_layers = [*range(low - 1, step - 1), *range(high, plan.nx + STEPS - step)]
        e_layers = [*range(low, step), *range(high, plan.nx + STEPS - step)]
        after = [functools.partial(take, "H", 1, h_layers), functools.partial(take, "E", 1, e_layers)] if step == 1 else []
        sweeps.both(step, h_layers, e_layers, *after)


def faces_kernel(plan, *refs):
    count = 2 * STEPS + 3
    x_low, x_high, z_low, z_high, turns, spec_f, spec_a = refs[count : count + 7]
    arrays = refs[count + 7 : 2 * count + 7]
    out_f, out_a = refs[2 * count + 7 :]
    efield, hfield, coef = arrays[: STEPS + 1], arrays[STEPS + 1 : 2 * STEPS + 2], arrays[-1]
    state = State(efield, hfield, coef)

    def take(kinds, level, layers):
        unpack(plan, plan.x_low, x_low, lambda y: 0, turns, state, kinds, level)
        unpack(plan, plan.x_high, x_high, lambda y: 1, turns, state, kinds, level)
        unpack(plan, plan.y_low, z_low, lambda y: 2, turns, state, kinds, level, layers)
        unpack(plan, plan.y_high, z_high, lambda y: 3, turns, state, kinds, level, layers)

    take("EHC", 0, ())
    do_valleys(plan, Sweeps(plan, efield, hfield, coef, plan.ring, plan.free), take)
    for _ in add_known(plan, efield, functools.partial(known, plan), (spec_f, spec_a), (out_f, out_a)):
        pass


def edges_kernel(plan, groups, *refs):
    count = 2 * STEPS + 3
    x_low, x_high, far, mate, z_low, z_high, turns, part_f, part_a = refs[count : count + 9]
    arrays = refs[count + 9 : 2 * count + 9]
    out_f, out_a, *parts = refs[2 * count + 9 :]
    efield, hfield, coef = arrays[: STEPS + 1], arrays[STEPS + 1 : 2 * STEPS + 2], arrays[-1]
    state = State(efield, hfield, coef)

    def take(kinds, level, layers):
        if level:
            unpack(plan, plan.x_low, x_low, lambda y: 0, turns, state, kinds, level)
            unpack(plan, plan.x_high, x_high, lambda y: 1, turns, state, kinds, level)

        def corners(receiver):
            for messages, ref, side in ((plan.far, far, plan.far_side), (plan.mate, mate, plan.mate_side)):
                first = 4 if side[receiver] < 0 else 6
                unpack(plan, messages[receiver], ref, lambda y: first + (y >= 0), turns, state, kinds, level)

        by_parity(0, corners)
        unpack(plan, plan.y_low, z_low, lambda y: 2, turns, state, kinds, level, layers)
        unpack(plan, plan.y_high, z_high, lambda y: 3, turns, state, kinds, level, layers)

    take("EHC", 0, ())
    do_valleys(plan, Sweeps(plan, efield, hfield, coef, plan.ring, plan.rest), take)

    share = plan.depth // groups
    shift = lax.rem(groups - lax.axis_index("angle"), groups) * share
    weight = turns[pl.ds(2 * SUB, SUB), :]

    def rest(x, tile, comp):
        return [level for level in range(1, STEPS + 1) if level not in known(plan, x, tile, comp)]

    totals = {}
    for x, tile, ends in add_known(plan, efield, rest, (part_f, part_a), (out_f, out_a)):
        term = ends[0][0] * ends[1][0] - ends[0][1] * ends[1][1]
        totals[x, tile] = totals[x, tile] + term if (x, tile) in totals else term
    block = lax.broadcasted_iota(jnp.int32, weight.shape, 1) // share
    tiles = [pltpu.roll(total * weight, shift, 1) for total in totals.values()]
    for k, part in enumerate(parts):
        for i in range(len(tiles) // groups):
            packed = jnp.zeros(weight.shape, jnp.float32)
            for t in range(groups):
                lanes = (t - k) % groups * share
                value = tiles[i * groups + t]
                packed = jnp.where(block == t, pltpu.roll(value, lanes, 1) if lanes else value, packed)
            part[pl.ds(i * SUB, SUB), :] = packed


def sum_kernel(groups, *refs):
    *parts, out = refs
    share = out.shape[1]
    for i in range(parts[0].shape[0] // SUB):
        total = parts[0][pl.ds(i * SUB, SUB), :]
        for part in parts[1:]:
            total = total + part[pl.ds(i * SUB, SUB), :]
        for t in range(groups):
            out[pl.ds((i * groups + t) * SUB, SUB), :] = total[:, t * share : (t + 1) * share]


def write_kernel(tr_f, tr_a, out_f, out_a, sems):
    copies = []
    for source, target in ((tr_f, out_f), (tr_a, out_a)):
        for i in range(source.shape[0]):
            copies.append(pltpu.make_async_copy(source.at[i], target.at[i], sems.at[len(copies)]))
    for copy in copies:
        copy.start()
    for copy in copies:
        copy.wait()


def ring_pairs(axis, offset):
    size = lax.axis_size(axis)
    return [(i, (i + offset) % size) for i in range(size)]


def mate_pairs():
    return [(i, i ^ 1) for i in range(lax.axis_size("gx"))]


def far_pairs():
    size = lax.axis_size("gx")
    return [(i, (i + (1 if i % 2 else -1)) % size) for i in range(size)]


def shards(
    forward_fields,
    adjoint_fields,
    forward_spectrum,
    adjoint_spectrum,
    permittivity,
    phase_table,
    angle_index,
    design_tiles,
):
    nx, ny, depth = permittivity.shape
    plan = Plan(nx, ny, depth)
    groups = lax.axis_size("angle")
    wide, ring = plan.wide, plan.ring

    def array(*shape):
        return jax.ShapeDtypeStruct(shape, jnp.float32)

    def lines(count):
        return array(count, depth)

    def params(mib):
        return pltpu.CompilerParams(vmem_limit_bytes=mib * 2**20)

    def cost(size):
        return pl.CostEstimate(flops=size, bytes_accessed=size, transcendentals=0)

    assert lax.axis_size("gx") % 2 == 0 and nx * ny % (groups * SUB) == 0
    with jax.named_scope("pack_y"):
        *first, coef, z_up, z_down = pl.pallas_call(
            functools.partial(pack_y_kernel, plan),
            out_shape=(
                *[array(12, wide, ring, depth)] * 4,
                array(wide, ring, depth),
                lines(plan.y_low.lines),
                lines(plan.y_high.lines),
            ),
            in_specs=[HBM] * 3,
            out_specs=[VMEM] * 7,
            scratch_shapes=[pltpu.SemaphoreType.DMA((25,)), pltpu.VMEM((24 * nx, depth), jnp.float32)],
            compiler_params=params(8),
        )(*(pltpu.with_memory_space_constraint(array, pltpu.HBM) for array in (forward_fields[0], adjoint_fields[0], permittivity)))
    e0, h0, e1, h1, coef = (state.reshape((-1, depth)) for state in (*first, coef))
    with jax.named_scope("send_y"):
        z_low = lax.ppermute(z_up, "gy", ring_pairs("gy", 1))
        z_high = lax.ppermute(z_down, "gy", ring_pairs("gy", -1))
    with jax.named_scope("pack_x"):
        x_up, x_down = pl.pallas_call(
            functools.partial(pack_x_kernel, plan),
            out_shape=(lines(plan.x_low.lines), lines(plan.x_high.lines)),
            in_specs=[VMEM] * 5,
            out_specs=[VMEM] * 2,
            scratch_shapes=[pltpu.VMEM((24 * ny, depth), jnp.float32)],
            compiler_params=params(8),
            cost_estimate=cost(40 * 2**20),
        )(e0, h0, e1, h1, coef)
    with jax.named_scope("send_x"):
        x_low = lax.ppermute(x_up, "gx", ring_pairs("gx", 1))
        x_high = lax.ppermute(x_down, "gx", ring_pairs("gx", -1))
    with jax.named_scope("turns"):
        turns = pl.pallas_call(
            functools.partial(turns_kernel, groups),
            out_shape=lines(3 * SUB),
            in_specs=[SMEM] * 3,
            out_specs=VMEM,
            compiler_params=params(4),
        )(phase_table, angle_index, design_tiles)
    with jax.named_scope("relay_corners"):
        to_far, to_mate = pl.pallas_call(
            functools.partial(relay_kernel, plan),
            out_shape=[lines(plan.corner_lines)] * 2,
            in_specs=[VMEM] * 2,
            out_specs=[VMEM] * 2,
            compiler_params=params(4),
        )(z_low, z_high)
        far = lax.ppermute(to_far, "gx", far_pairs())
        mate = lax.ppermute(to_mate, "gx", mate_pairs())
    level = lines(12 * wide * ring)
    count = 2 * STEPS + 3
    levels = [level] * (count - 1) + [lines(wide * ring)]
    with jax.named_scope("middle"):
        state = pl.pallas_call(
            functools.partial(middle_kernel, plan),
            out_shape=levels,
            in_specs=[VMEM] * 8,
            out_specs=[VMEM] * count,
            input_output_aliases={0: 0, 1: STEPS + 1, 2: 1, 3: STEPS + 2, 4: count - 1},
            compiler_params=params(8),
            cost_estimate=cost(2**32),
        )(e0, h0, e1, h1, coef, z_low, z_high, turns)
    transforms = [lines(6 * nx * ny)] * 2
    with jax.named_scope("faces"):
        spectra = [spectrum.reshape((-1, depth)) for spectrum in (forward_spectrum, adjoint_spectrum)]
        results = pl.pallas_call(
            functools.partial(faces_kernel, plan),
            out_shape=[*levels, *transforms],
            in_specs=[VMEM] * (count + 7),
            out_specs=[VMEM] * (count + 2),
            input_output_aliases={i: i for i in range(count)},
            compiler_params=params(8),
        )(*state, x_low, x_high, z_low, z_high, turns, *spectra)
        state, sums = results[:count], results[count:]
    with jax.named_scope("edges"):
        results = pl.pallas_call(
            functools.partial(edges_kernel, plan, groups),
            out_shape=[*levels, *transforms, *[lines(nx * ny // groups)] * groups],
            in_specs=[VMEM] * (count + 9),
            out_specs=[VMEM] * (count + 2 + groups),
            input_output_aliases={i: i for i in range(count)} | {count + 7: count, count + 8: count + 1},
            compiler_params=params(8),
        )(*state, x_low, x_high, far, mate, z_low, z_high, turns, *sums)
        tr_f, tr_a, own, *others = results[count:]
    with jax.named_scope("sum_angles"):
        others = [lax.ppermute(part, "angle", ring_pairs("angle", k + 1)) for k, part in enumerate(others)]
        gradient = pl.pallas_call(
            functools.partial(sum_kernel, groups),
            out_shape=array(nx * ny, depth // groups),
            in_specs=[VMEM] * groups,
            out_specs=VMEM,
            compiler_params=params(4),
        )(own, *others)
    with jax.named_scope("write"):
        out_f, out_a = pl.pallas_call(
            write_kernel,
            out_shape=[array(6, nx, ny, depth)] * 2,
            in_specs=[VMEM] * 2,
            out_specs=[HBM] * 2,
            scratch_shapes=[pltpu.SemaphoreType.DMA((12,))],
            compiler_params=params(4),
        )(tr_f.reshape((6, nx, ny, depth)), tr_a.reshape((6, nx, ny, depth)))
    return (
        out_f.reshape(forward_spectrum.shape),
        out_a.reshape(adjoint_spectrum.shape),
        gradient.reshape((nx, ny, depth // groups)),
    )


def solution(mesh):
    in_specs = (
        P("angle", None, "gx", "gy", None),
        P("angle", None, "gx", "gy", None),
        P("angle", None, "gx", "gy", None),
        P("angle", None, "gx", "gy", None),
        P("gx", "gy", None),
        P(),
        P("angle"),
        P(),
    )
    out_specs = (
        P("angle", None, "gx", "gy", None),
        P("angle", None, "gx", "gy", None),
        P("gx", "gy", "angle"),
    )
    return jax.shard_map(shards, mesh=mesh, in_specs=in_specs, out_specs=out_specs, check_vma=False)
```

```python
import functools
import math

import jax
import jax.numpy as jnp
from jax import lax
from jax.experimental import pallas as pl
from jax.experimental.pallas import tpu as pltpu
from jax.sharding import PartitionSpec as P

STEPS = 3
SUB = 8

courant = 0.5
omega_step = 0.7

VMEM = pl.BlockSpec(memory_space=pltpu.VMEM)
SMEM = pl.BlockSpec(memory_space=pltpu.SMEM)
HBM = pl.BlockSpec(memory_space=pltpu.HBM)


def reads(node):
    kind, level, comp, x, y = node
    others = [c for c in range(3) if c != comp]
    if kind == "E":
        found = [("E", level - 1, comp, x, y), ("C", 0, 0, x, y)] + [("H", level, c, x, y) for c in others]
        if comp != 1:
            found.append(("H", level, 2 - comp, x, y - 1))
        if comp != 0:
            found.append(("H", level, 3 - comp, x - 1, y))
        return found
    found = [("H", level - 1, comp, x, y)] + [("E", level - 1, c, x, y) for c in others]
    if comp != 1:
        found.append(("E", level - 1, 2 - comp, x, y + 1))
    if comp != 0:
        found.append(("E", level - 1, 3 - comp, x + 1, y))
    return found


def wanted(nx, ny):
    def block(node):
        return node[3] // nx, node[4] // ny

    @functools.cache
    def alone(node):
        if node[1] == 0:
            return True
        return node[1] == 1 and all(block(other) == block(node) and alone(other) for other in reads(node))

    found, made, seen = set(), set(), set()
    todo = [("E", STEPS, comp, x, y) for comp in range(3) for x in range(nx) for y in range(ny)]
    while todo:
        node = todo.pop()
        if node in seen:
            continue
        seen.add(node)
        if block(node) != (0, 0) and alone(node):
            found.add(node)
        elif node[1]:
            made.add(node)
            todo += reads(node)
    return found, made


class Message:
    def __init__(self, nodes, axis, folded=()):
        self.axis, self.runs, self.at, self.size = axis, [], {}, 0
        assert nodes.issuperset(folded)
        self.zeros = Message(set(folded), axis).runs if folded else []
        nodes = nodes - set(folded)
        stretches = []
        for node in sorted(nodes):
            before = list(node)
            before[3 + axis] -= 1
            if tuple(before) in nodes:
                continue
            count = 1
            while (*node[:3], node[3] + count * (axis == 0), node[4] + count * (axis == 1)) in nodes:
                count += 1
            stretches.append((count, node))
        for count, (kind, level, comp, x, y) in sorted(stretches, key=lambda item: (-item[0], item[1])):
            for run in (0, 1) if kind != "C" else (0,):
                for part in (0, 1) if kind != "C" else (0,):
                    what = (kind, level, comp, run, part)
                    self.runs.append((what, x, y, count, self.size))
                    for i in range(count):
                        self.at[what, x + i * (axis == 0), y + i * (axis == 1)] = self.size + i
                    self.size += count
        self.lines = -(-self.size // SUB) * SUB


class Plan:
    def __init__(self, nx, ny, depth):
        self.depth = depth
        self.nx, self.ny = nx, ny
        self.wide, self.ring = nx + 2 * STEPS, ny + SUB
        nodes, made = wanted(nx, ny)
        self.made, self.free, self.rest = {}, {}, {}
        tiles, ready = {}, set()
        for node in made:
            tiles.setdefault((node[1], "HE".index(node[0]), *node[2:4], node[4] % self.ring // SUB), []).append(node)

        def early(node):
            if node in made:
                return node in ready
            return node not in nodes or 0 <= node[3] < nx or 0 <= node[4] < ny

        for (level, order, comp, x, tile), members in sorted(tiles.items()):
            key = ("HE"[order], level, x)
            middle = level - 1 + order <= x < nx - level
            free = middle or all(early(other) for node in members for other in reads(node))
            if free:
                ready.update(members)
            for into in (self.made, self.free if free else self.rest):
                into.setdefault(key, {}).setdefault(comp, set()).add(tile)
        sides = {}
        for node in nodes:
            sides.setdefault((node[3] // nx, node[4] // ny), set()).add(node)

        def shifted(found, dx):
            return {(*node[:3], node[3] + dx, node[4]) for node in found}

        y_low, y_high = (sides[0, side] | shifted(sides[-1, side], nx) | shifted(sides[1, side], -nx) for side in (-1, 1))
        self.x_folds = (1, ny - 2), (2, ny - 2)
        self.y_folds = (2, nx - 2), (3, nx - 2)
        x_folded = [("E", 1, comp, -2, y) for comp in range(3) for y in range(*self.x_folds[comp == 0])]
        y_folded = [("E", 1, comp, x, -2) for comp in range(3) for x in range(*self.y_folds[comp == 1])]
        self.y_low, self.y_high = Message(y_low, 0, y_folded), Message(y_high, 0)
        self.x_low, self.x_high = Message(sides[-1, 0], 1, x_folded), Message(sides[1, 0], 1)
        self.mate_side, self.far_side = (1, -1), (-1, 1)
        self.mate = [Message(sides[side, -1] | sides[side, 1], 1) for side in self.mate_side]
        self.far_low, self.far_high = ([Message(sides[side, end], 1) for side in self.far_side] for end in (-1, 1))

    def row(self, x, y, run=0, part=0, comp=0):
        return ((run * 6 + part * 3 + comp) * self.wide + x + STEPS) * self.ring + y % self.ring

    def rows(self, what, x, y, axis, count):
        _, _, comp, run, part = what
        start = self.row(x, y, run, part, comp)
        return pl.ds(start, count, stride=self.ring) if axis == 0 and count > 1 else pl.ds(start, count)


class State:
    def __init__(self, efield, hfield, coef):
        self.by_kind = {"E": efield, "H": hfield, "C": [coef]}

    def __call__(self, what):
        return self.by_kind[what[0]][what[1]]


def pack(plan, message, state, dx, dy, out, changed=None):
    for what, x, y, count, at in message.runs:
        layer, first = (y, x) if message.axis == 0 else (x, y)
        if changed and (what, layer) in changed:
            ref, row = changed[what, layer]
            value = ref[pl.ds(row + first, count), :]
        else:
            value = state(what)[plan.rows(what, x + dx, y + dy, message.axis, count), :]
        out[pl.ds(at, count), :] = value


def fold(plan, state, axis, scratch):
    nx, ny = plan.nx, plan.ny
    size, normal = (nx, 1) if axis == 0 else (ny, 0)
    before, after = ((0, 2) if axis == 0 else (1, 2))
    cell = lax.broadcasted_iota(jnp.int32, (size, scratch.shape[1]), 0)
    lane = lax.broadcasted_iota(jnp.int32, cell.shape, 1)
    folds = plan.y_folds if axis == 0 else plan.x_folds
    changed = {}

    def lines(what, layer):
        place = (0, ny + layer) if axis == 0 else (nx + layer, 0)
        return state(what)[plan.rows(what, *place, axis, size), :]

    def inside(value, fold):
        return jnp.where((cell >= fold[0]) & (cell < fold[1]), value, 0.0)

    for run in (0, 1):
        for part in (0, 1):

            def get(kind, level, comp, layer):
                return lines((kind, level, comp, run, part), layer)

            def put(kind, level, comp, layer, value):
                row = len(changed) * size
                scratch[pl.ds(row, size), :] = value
                changed[(kind, level, comp, run, part), layer] = scratch, row

            low, high = (inside(get("E", 1, comp, -2), folds[0]) for comp in (before, after))
            along = inside(get("E", 1, normal, -2), folds[1])
            along_z = jnp.where(lane == lane.shape[1] - 1, 0.0, pltpu.roll(along, lane.shape[1] - 1, 1)) - along
            along_next = pltpu.roll(along, size - 1, 0) - along
            sign = 1.0 if axis == 0 else -1.0
            d_before = sign * (high + along_z)
            d_after = -sign * (low + along_next)
            scale = lines(("C", 0, 0, 0, 0), -1)
            put("H", 1, before, -2, get("H", 1, before, -2) + d_before)
            put("H", 1, after, -2, get("H", 1, after, -2) + d_after)
            put("E", 0, before, -1, get("E", 0, before, -1) + sign * scale * d_after)
            put("E", 0, after, -1, get("E", 0, after, -1) - sign * scale * d_before)
            put("H", 0, before, -1, get("H", 0, before, -1) + 0.5 * scale * d_before)
            put("H", 0, after, -1, get("H", 0, after, -1) + 0.5 * scale * d_after)
    return changed


def by_parity(offset, body):
    parity = lax.rem(lax.axis_index("gx") + offset, 2)
    for value in (0, 1):
        pl.when(parity == value)(functools.partial(body, value))


def pack_y_kernel(plan, fwd, adj, eps, e0, h0, e1, h1, coef, z_up, z_down, sems, scratch):
    nx, ny = plan.nx, plan.ny
    own = (pl.ds(STEPS, nx), pl.ds(0, ny), slice(None))
    copies = [pltpu.make_async_copy(eps, coef.at[own], sems.at[0])]
    for run, ref in enumerate((fwd, adj)):
        for kind, array in enumerate((e0, h0)):
            for i in range(6):
                copies.append(
                    pltpu.make_async_copy(ref.at[kind * 6 + i], array.at[(run * 6 + i, *own)], sems.at[len(copies)])
                )
    for copy in copies:
        copy.start()
    copies[0].wait()
    for x in range(nx):
        coef[STEPS + x, pl.ds(0, ny), :] = (0.5 * courant) / coef[STEPS + x, pl.ds(0, ny), :]
    e0, h0, e1, h1, coef = (array.reshape((-1, array.shape[-1])) for array in (e0, h0, e1, h1, coef))
    sweeps = Sweeps(plan, [e0, e1], [h0, h1], coef, ny)
    for run in (0, 1):
        for copy in copies[1 + 12 * run : 13 + 12 * run]:
            copy.wait()
        sweeps.both(1, range(nx), range(nx - 1), runs=(run,))
    state = State([e0, e1], [h0, h1], coef)
    pack(plan, plan.y_low, state, 0, ny, z_up, fold(plan, state, 0, scratch))
    pack(plan, plan.y_high, state, 0, -ny, z_down)


def pack_x_kernel(plan, e0, h0, e1, h1, coef, x_up, x_down, scratch):
    state = State([e0, e1], [h0, h1], coef)
    pack(plan, plan.x_low, state, plan.nx, 0, x_up, fold(plan, state, 1, scratch))
    pack(plan, plan.x_high, state, -plan.nx, 0, x_down)


def turns_kernel(groups, table, index, tiles, turns):
    row = index[0]
    phi_x, phi_y = table[row, 0], table[row, 1]
    at_x, at_y = lax.axis_index("gx"), lax.axis_index("gy")
    none = jnp.float32(0.0)
    ax_low = jnp.where(at_x == 0, -phi_x, none)
    ax_high = jnp.where(at_x == lax.axis_size("gx") - 1, phi_x, none)
    ay_low = jnp.where(at_y == 0, -phi_y, none)
    ay_high = jnp.where(at_y == lax.axis_size("gy") - 1, phi_y, none)
    sub = lax.broadcasted_iota(jnp.int32, (SUB, turns.shape[1]), 0)
    angles = jnp.zeros(sub.shape, jnp.float32)
    for i, angle in enumerate((ax_low, ax_high, ay_low, ay_high, ax_low + ay_low, ax_low + ay_high,
                               ax_high + ay_low, ax_high + ay_high)):
        angles = jnp.where(sub == i, angle, angles)
    turns[pl.ds(0, SUB), :] = jnp.cos(angles)
    turns[pl.ds(SUB, SUB), :] = jnp.sin(angles)
    own_tile = at_x * lax.axis_size("gy") + at_y
    chosen = tiles[0] == own_tile
    for i in range(1, tiles.shape[0]):
        chosen = jnp.logical_or(chosen, tiles[i] == own_tile)
    weight = jnp.where(chosen, jnp.float32(1.0 / groups), none)
    turns[pl.ds(2 * SUB, SUB), :] = jnp.full(sub.shape, weight, jnp.float32)


def relay_kernel(plan, jobs, *refs):
    faces, outs = refs[: len(refs) - len(jobs)], refs[len(refs) - len(jobs) :]

    def corners(receiver):
        for (messages, side), out in zip(jobs, outs, strict=True):
            dx = -plan.nx * side[receiver]
            for (what, x, y), row in messages[receiver].at.items():
                ref, source = (faces[0], plan.y_low) if y < 0 else (faces[1], plan.y_high)
                out[pl.ds(row, 1), :] = ref[pl.ds(source.at[what, x + dx, y], 1), :]

    by_parity(1, corners)


def turned(real, imag, cosine, sine):
    return real * cosine - imag * sine, real * sine + imag * cosine


def unpack(plan, message, ref, which, turns, state, kinds, level, layers=None):
    axis = message.axis
    for (kind, at_level, comp, run, part), x, y, count, at in message.runs:
        if kind not in kinds or at_level != level or part == 1:
            continue
        pieces = [(x, y, count, at)]
        if layers is not None:
            pieces = [(x + i, y, 1, at + i) for i in range(count) if x + i in layers]
        for cell_x, cell_y, size, row in pieces:
            what = (kind, at_level, comp, run, 0)
            real = ref[pl.ds(row, size), :]
            if kind == "C":
                state(what)[plan.rows(what, cell_x, cell_y, axis, size), :] = real
                continue
            twin = (kind, at_level, comp, run, 1)
            imag = ref[pl.ds(message.at[twin, cell_x, cell_y], size), :]
            turn = which(y)
            cosine, sine = turns[pl.ds(turn, 1), :], turns[pl.ds(SUB + turn, 1), :]
            real, imag = turned(real, imag, cosine, sine if run == 0 else -sine)
            state(what)[plan.rows(what, cell_x, cell_y, axis, size), :] = real
            state(twin)[plan.rows(twin, cell_x, cell_y, axis, size), :] = imag
    for what, x, y, count, _ in message.zeros:
        if what[0] in kinds and what[1] == level and layers is None:
            state(what)[plan.rows(what, x, y, axis, count), :] = jnp.zeros((count, ref.shape[1]), jnp.float32)


class Sweeps:
    def __init__(self, plan, efield, hfield, coef, height, todo=None):
        self.plan, self.efield, self.hfield, self.coef, self.height = plan, efield, hfield, coef, height
        self.todo = todo

    def rows(self, run, part, comp, x, start, stop):
        return pl.ds(self.plan.row(x, 0, run, part, comp) + start, stop - start)

    def get(self, array, run, part, comp, x):
        return array[self.rows(run, part, comp, x, 0, self.height), :]

    def pieces(self, kind, step, x):
        if self.todo is None:
            return [(comp, 0, self.height) for comp in range(3)]
        found = []
        for comp, tiles in sorted(self.todo.get((kind, step, x), {}).items()):
            for tile in sorted(tiles):
                if found and found[-1][0] == comp and found[-1][2] == tile * SUB:
                    found[-1] = (comp, found[-1][1], (tile + 1) * SUB)
                else:
                    found.append((comp, tile * SUB, (tile + 1) * SUB))
        return found

    def next_z(self, value):
        lane = lax.broadcasted_iota(jnp.int32, value.shape, 1)
        return jnp.where(lane == value.shape[1] - 1, 0.0, pltpu.roll(value, value.shape[1] - 1, 1))

    def prev_z(self, value):
        lane = lax.broadcasted_iota(jnp.int32, value.shape, 1)
        return jnp.where(lane == 0, 0.0, pltpu.roll(value, 1, 1))

    def next_y(self, value):
        return pltpu.roll(value, self.height - 1, 0)

    def prev_y(self, value):
        return pltpu.roll(value, 1, 0)

    def update_h(self, step, run, part, x):
        efield, old, new = self.efield[step - 1], self.hfield[step - 1], self.hfield[step]
        ex, ey, ez = (self.get(efield, run, part, comp, x) for comp in range(3))
        for comp, start, stop in self.pieces("H", step, x):
            here = slice(start, stop)
            if comp == 0:
                curl = (self.next_y(ez) - ez)[here] - (self.next_z(ey[here]) - ey[here])
            elif comp == 1:
                ez_x = self.get(efield, run, part, 2, x + 1)
                curl = (self.next_z(ex[here]) - ex[here]) - (ez_x - ez)[here]
            else:
                ey_x = self.get(efield, run, part, 1, x + 1)
                curl = (ey_x - ey)[here] - (self.next_y(ex) - ex)[here]
            before = self.get(old, run, part, comp, x)[here]
            if step == 1:
                before = before + before
            new[self.rows(run, part, comp, x, start, stop), :] = before - curl

    def update_e(self, step, run, part, x):
        old, new, hfield = self.efield[step - 1], self.efield[step], self.hfield[step]
        hx, hy, hz = (self.get(hfield, run, part, comp, x) for comp in range(3))
        scale = self.get(self.coef, 0, 0, 0, x)
        for comp, start, stop in self.pieces("E", step, x):
            here = slice(start, stop)
            if comp == 0:
                curl = (hz - self.prev_y(hz))[here] - (hy[here] - self.prev_z(hy[here]))
            elif comp == 1:
                hz_x = self.get(hfield, run, part, 2, x - 1)
                curl = (hx[here] - self.prev_z(hx[here])) - (hz - hz_x)[here]
            else:
                hy_x = self.get(hfield, run, part, 1, x - 1)
                curl = (hy - hy_x)[here] - (hx - self.prev_y(hx))[here]
            before = self.get(old, run, part, comp, x)[here]
            new[self.rows(run, part, comp, x, start, stop), :] = before + scale[here] * curl

    def both(self, step, h_layers, e_layers, after_h=None, after_e=None, runs=(0, 1)):
        for update, layers, after in ((self.update_h, h_layers, after_h), (self.update_e, e_layers, after_e)):
            for x in layers:
                for run in runs:
                    for part in (0, 1):
                        update(step, run, part, x)
            if after is not None:
                after()


def middle_kernel(plan, e0_in, h0_in, e1_in, h1_in, coef_in, z_low, z_high, turns, *arrays):
    nx = plan.nx
    efield, hfield, coef = arrays[: STEPS + 1], arrays[STEPS + 1 : 2 * STEPS + 2], arrays[-1]
    state = State(efield, hfield, coef)

    def take(kinds, level):
        unpack(plan, plan.y_low, z_low, lambda y: 2, turns, state, kinds, level)
        unpack(plan, plan.y_high, z_high, lambda y: 3, turns, state, kinds, level)

    take("EHC", 0)
    sweeps = Sweeps(plan, efield, hfield, coef, plan.ring, plan.made)
    for step in range(1, STEPS + 1):
        after = [lambda: take("H", 1), lambda: take("E", 1)] if step == 1 else []
        sweeps.both(step, range(step - 1, nx - step), range(step, nx - step), *after)


def add_known(plan, efield, levels, transform, out):
    nx, ny = plan.nx, plan.ny
    for x in range(nx):
        for tile in range(ny // SUB):
            for comp in range(3):
                ends = []
                for run in (0, 1):
                    at = [pl.ds(((part * 3 + comp) * nx + x) * ny + tile * SUB, SUB) for part in (0, 1)]
                    real, imag = transform[run][at[0], :], transform[run][at[1], :]
                    for level in levels(x, tile, comp):
                        theta = omega_step * level
                        here = [efield[level][pl.ds(plan.row(x, tile * SUB, run, part, comp), SUB), :] for part in (0, 1)]
                        more = turned(*here, math.cos(theta), math.sin(theta))
                        real, imag = real + more[0], imag + more[1]
                    out[run][at[0], :], out[run][at[1], :] = real, imag
                    ends.append((real, imag))
                yield x, tile, ends


def known(plan, x, tile, comp):
    def ready(level):
        return level <= x < plan.nx - level or tile in plan.free.get(("E", level, x), {}).get(comp, ())

    return [level for level in range(1, STEPS + 1) if ready(level)]


def do_valleys(plan, sweeps, take):
    for step in range(1, STEPS + 1):
        low, high = step - STEPS, plan.nx - step
        h_layers = [*range(low - 1, step - 1), *range(high, plan.nx + STEPS - step)]
        e_layers = [*range(low, step), *range(high, plan.nx + STEPS - step)]
        after = [functools.partial(take, "H", 1, h_layers), functools.partial(take, "E", 1, e_layers)] if step == 1 else []
        sweeps.both(step, h_layers, e_layers, *after)


def faces_kernel(plan, *refs):
    count = 2 * STEPS + 3
    x_low, x_high, z_low, z_high, turns, spec_f, spec_a = refs[count : count + 7]
    arrays = refs[count + 7 : 2 * count + 7]
    out_f, out_a = refs[2 * count + 7 :]
    efield, hfield, coef = arrays[: STEPS + 1], arrays[STEPS + 1 : 2 * STEPS + 2], arrays[-1]
    state = State(efield, hfield, coef)

    def take(kinds, level, layers):
        unpack(plan, plan.x_low, x_low, lambda y: 0, turns, state, kinds, level)
        unpack(plan, plan.x_high, x_high, lambda y: 1, turns, state, kinds, level)
        unpack(plan, plan.y_low, z_low, lambda y: 2, turns, state, kinds, level, layers)
        unpack(plan, plan.y_high, z_high, lambda y: 3, turns, state, kinds, level, layers)

    take("EHC", 0, ())
    do_valleys(plan, Sweeps(plan, efield, hfield, coef, plan.ring, plan.free), take)
    for _ in add_known(plan, efield, functools.partial(known, plan), (spec_f, spec_a), (out_f, out_a)):
        pass


def edges_kernel(plan, groups, *refs):
    count = 2 * STEPS + 3
    x_low, x_high, far_low, far_high, mate, z_low, z_high, turns, part_f, part_a = refs[count : count + 10]
    arrays = refs[count + 10 : 2 * count + 10]
    out_f, out_a, *parts = refs[2 * count + 10 :]
    efield, hfield, coef = arrays[: STEPS + 1], arrays[STEPS + 1 : 2 * STEPS + 2], arrays[-1]
    state = State(efield, hfield, coef)

    def take(kinds, level, layers):
        if level:
            unpack(plan, plan.x_low, x_low, lambda y: 0, turns, state, kinds, level)
            unpack(plan, plan.x_high, x_high, lambda y: 1, turns, state, kinds, level)

        def corners(receiver):
            for messages, ref, side in (
                (plan.far_low, far_low, plan.far_side),
                (plan.far_high, far_high, plan.far_side),
                (plan.mate, mate, plan.mate_side),
            ):
                first = 4 if side[receiver] < 0 else 6
                unpack(plan, messages[receiver], ref, lambda y: first + (y >= 0), turns, state, kinds, level)

        by_parity(0, corners)
        unpack(plan, plan.y_low, z_low, lambda y: 2, turns, state, kinds, level, layers)
        unpack(plan, plan.y_high, z_high, lambda y: 3, turns, state, kinds, level, layers)

    take("EHC", 0, ())
    do_valleys(plan, Sweeps(plan, efield, hfield, coef, plan.ring, plan.rest), take)

    share = plan.depth // groups
    shift = lax.rem(groups - lax.axis_index("angle"), groups) * share
    weight = turns[pl.ds(2 * SUB, SUB), :]

    def rest(x, tile, comp):
        return [level for level in range(1, STEPS + 1) if level not in known(plan, x, tile, comp)]

    totals = {}
    for x, tile, ends in add_known(plan, efield, rest, (part_f, part_a), (out_f, out_a)):
        term = ends[0][0] * ends[1][0] - ends[0][1] * ends[1][1]
        totals[x, tile] = totals[x, tile] + term if (x, tile) in totals else term
    block = lax.broadcasted_iota(jnp.int32, weight.shape, 1) // share
    tiles = [pltpu.roll(total * weight, shift, 1) for total in totals.values()]
    for k, part in enumerate(parts):
        for i in range(len(tiles) // groups):
            packed = jnp.zeros(weight.shape, jnp.float32)
            for t in range(groups):
                lanes = (t - k) % groups * share
                value = tiles[i * groups + t]
                packed = jnp.where(block == t, pltpu.roll(value, lanes, 1) if lanes else value, packed)
            part[pl.ds(i * SUB, SUB), :] = packed


def sum_kernel(groups, *refs):
    *parts, out = refs
    share = out.shape[1]
    for i in range(parts[0].shape[0] // SUB):
        total = parts[0][pl.ds(i * SUB, SUB), :]
        for part in parts[1:]:
            total = total + part[pl.ds(i * SUB, SUB), :]
        for t in range(groups):
            out[pl.ds((i * groups + t) * SUB, SUB), :] = total[:, t * share : (t + 1) * share]


def write_kernel(tr_f, tr_a, out_f, out_a, sems):
    copies = []
    for source, target in ((tr_f, out_f), (tr_a, out_a)):
        for i in range(source.shape[0]):
            copies.append(pltpu.make_async_copy(source.at[i], target.at[i], sems.at[len(copies)]))
    for copy in copies:
        copy.start()
    for copy in copies:
        copy.wait()


def ring_pairs(axis, offset):
    size = lax.axis_size(axis)
    return [(i, (i + offset) % size) for i in range(size)]


def mate_pairs():
    return [(i, i ^ 1) for i in range(lax.axis_size("gx"))]


def far_pairs():
    size = lax.axis_size("gx")
    return [(i, (i + (1 if i % 2 else -1)) % size) for i in range(size)]


def shards(
    forward_fields,
    adjoint_fields,
    forward_spectrum,
    adjoint_spectrum,
    permittivity,
    phase_table,
    angle_index,
    design_tiles,
):
    nx, ny, depth = permittivity.shape
    plan = Plan(nx, ny, depth)
    groups = lax.axis_size("angle")
    wide, ring = plan.wide, plan.ring

    def array(*shape):
        return jax.ShapeDtypeStruct(shape, jnp.float32)

    def lines(count):
        return array(count, depth)

    def params(mib):
        return pltpu.CompilerParams(vmem_limit_bytes=mib * 2**20)

    def cost(size):
        return pl.CostEstimate(flops=size, bytes_accessed=size, transcendentals=0)

    assert lax.axis_size("gx") % 2 == 0 and nx * ny % (groups * SUB) == 0
    with jax.named_scope("pack_y"):
        *first, coef, z_up, z_down = pl.pallas_call(
            functools.partial(pack_y_kernel, plan),
            out_shape=(
                *[array(12, wide, ring, depth)] * 4,
                array(wide, ring, depth),
                lines(plan.y_low.lines),
                lines(plan.y_high.lines),
            ),
            in_specs=[HBM] * 3,
            out_specs=[VMEM] * 7,
            scratch_shapes=[pltpu.SemaphoreType.DMA((25,)), pltpu.VMEM((24 * nx, depth), jnp.float32)],
            compiler_params=params(8),
        )(*(pltpu.with_memory_space_constraint(array, pltpu.HBM) for array in (forward_fields[0], adjoint_fields[0], permittivity)))
    e0, h0, e1, h1, coef = (state.reshape((-1, depth)) for state in (*first, coef))
    with jax.named_scope("send_y"):
        z_low = lax.ppermute(z_up, "gy", ring_pairs("gy", 1))
        z_high = lax.ppermute(z_down, "gy", ring_pairs("gy", -1))
    with jax.named_scope("pack_x"):
        x_up, x_down = pl.pallas_call(
            functools.partial(pack_x_kernel, plan),
            out_shape=(lines(plan.x_low.lines), lines(plan.x_high.lines)),
            in_specs=[VMEM] * 5,
            out_specs=[VMEM] * 2,
            scratch_shapes=[pltpu.VMEM((24 * ny, depth), jnp.float32)],
            compiler_params=params(8),
            cost_estimate=cost(40 * 2**20),
        )(e0, h0, e1, h1, coef)
    with jax.named_scope("send_x"):
        x_low = lax.ppermute(x_up, "gx", ring_pairs("gx", 1))
        x_high = lax.ppermute(x_down, "gx", ring_pairs("gx", -1))
    with jax.named_scope("turns"):
        turns = pl.pallas_call(
            functools.partial(turns_kernel, groups),
            out_shape=lines(3 * SUB),
            in_specs=[SMEM] * 3,
            out_specs=VMEM,
            compiler_params=params(4),
        )(phase_table, angle_index, design_tiles)
    def relay(jobs, *faces):
        return pl.pallas_call(
            functools.partial(relay_kernel, plan, jobs),
            out_shape=[lines(max(message.lines for message in messages)) for messages, _ in jobs],
            in_specs=[VMEM] * len(faces),
            out_specs=[VMEM] * len(jobs),
            compiler_params=params(4),
            cost_estimate=cost(2**10),
        )(*faces)

    with jax.named_scope("relay_low_corners"):
        (to_far,) = relay([(plan.far_low, plan.far_side)], z_low)
        far_low = lax.ppermute(to_far, "gx", far_pairs())
    with jax.named_scope("relay_corners"):
        to_far, to_mate = relay([(plan.far_high, plan.far_side), (plan.mate, plan.mate_side)], z_low, z_high)
        far_high = lax.ppermute(to_far, "gx", far_pairs())
        mate = lax.ppermute(to_mate, "gx", mate_pairs())
    level = lines(12 * wide * ring)
    count = 2 * STEPS + 3
    levels = [level] * (count - 1) + [lines(wide * ring)]
    with jax.named_scope("middle"):
        state = pl.pallas_call(
            functools.partial(middle_kernel, plan),
            out_shape=levels,
            in_specs=[VMEM] * 8,
            out_specs=[VMEM] * count,
            input_output_aliases={0: 0, 1: STEPS + 1, 2: 1, 3: STEPS + 2, 4: count - 1},
            compiler_params=params(8),
            cost_estimate=cost(2**32),
        )(e0, h0, e1, h1, coef, z_low, z_high, turns)
    transforms = [lines(6 * nx * ny)] * 2
    with jax.named_scope("faces"):
        spectra = [spectrum.reshape((-1, depth)) for spectrum in (forward_spectrum, adjoint_spectrum)]
        results = pl.pallas_call(
            functools.partial(faces_kernel, plan),
            out_shape=[*levels, *transforms],
            in_specs=[VMEM] * (count + 7),
            out_specs=[VMEM] * (count + 2),
            input_output_aliases={i: i for i in range(count)},
            compiler_params=params(8),
        )(*state, x_low, x_high, z_low, z_high, turns, *spectra)
        state, sums = results[:count], results[count:]
    with jax.named_scope("edges"):
        results = pl.pallas_call(
            functools.partial(edges_kernel, plan, groups),
            out_shape=[*levels, *transforms, *[lines(nx * ny // groups)] * groups],
            in_specs=[VMEM] * (count + 10),
            out_specs=[VMEM] * (count + 2 + groups),
            input_output_aliases={i: i for i in range(count)} | {count + 8: count, count + 9: count + 1},
            compiler_params=params(8),
        )(*state, x_low, x_high, far_low, far_high, mate, z_low, z_high, turns, *sums)
        tr_f, tr_a, own, *others = results[count:]
    with jax.named_scope("sum_angles"):
        others = [lax.ppermute(part, "angle", ring_pairs("angle", k + 1)) for k, part in enumerate(others)]
        gradient = pl.pallas_call(
            functools.partial(sum_kernel, groups),
            out_shape=array(nx * ny, depth // groups),
            in_specs=[VMEM] * groups,
            out_specs=VMEM,
            compiler_params=params(4),
        )(own, *others)
    with jax.named_scope("write"):
        out_f, out_a = pl.pallas_call(
            write_kernel,
            out_shape=[array(6, nx, ny, depth)] * 2,
            in_specs=[VMEM] * 2,
            out_specs=[HBM] * 2,
            scratch_shapes=[pltpu.SemaphoreType.DMA((12,))],
            compiler_params=params(4),
        )(tr_f.reshape((6, nx, ny, depth)), tr_a.reshape((6, nx, ny, depth)))
    return (
        out_f.reshape(forward_spectrum.shape),
        out_a.reshape(adjoint_spectrum.shape),
        gradient.reshape((nx, ny, depth // groups)),
    )


def solution(mesh):
    in_specs = (
        P("angle", None, "gx", "gy", None),
        P("angle", None, "gx", "gy", None),
        P("angle", None, "gx", "gy", None),
        P("angle", None, "gx", "gy", None),
        P("gx", "gy", None),
        P(),
        P("angle"),
        P(),
    )
    out_specs = (
        P("angle", None, "gx", "gy", None),
        P("angle", None, "gx", "gy", None),
        P("gx", "gy", "angle"),
    )
    return jax.shard_map(shards, mesh=mesh, in_specs=in_specs, out_specs=out_specs, check_vma=False)
```

```python
import functools
import math

import jax
import jax.numpy as jnp
from jax import lax
from jax.experimental import pallas as pl
from jax.experimental.pallas import tpu as pltpu
from jax.sharding import PartitionSpec as P

STEPS = 3
SUB = 8

courant = 0.5
omega_step = 0.7

VMEM = pl.BlockSpec(memory_space=pltpu.VMEM)
SMEM = pl.BlockSpec(memory_space=pltpu.SMEM)
HBM = pl.BlockSpec(memory_space=pltpu.HBM)


def reads(node):
    kind, level, comp, x, y = node
    others = [c for c in range(3) if c != comp]
    if kind == "E":
        found = [("E", level - 1, comp, x, y), ("C", 0, 0, x, y)] + [("H", level, c, x, y) for c in others]
        if comp != 1:
            found.append(("H", level, 2 - comp, x, y - 1))
        if comp != 0:
            found.append(("H", level, 3 - comp, x - 1, y))
        return found
    found = [("H", level - 1, comp, x, y)] + [("E", level - 1, c, x, y) for c in others]
    if comp != 1:
        found.append(("E", level - 1, 2 - comp, x, y + 1))
    if comp != 0:
        found.append(("E", level - 1, 3 - comp, x + 1, y))
    return found


def wanted(nx, ny):
    def block(node):
        return node[3] // nx, node[4] // ny

    @functools.cache
    def alone(node):
        if node[1] == 0:
            return True
        return node[1] == 1 and all(block(other) == block(node) and alone(other) for other in reads(node))

    found, made, seen = set(), set(), set()
    todo = [("E", STEPS, comp, x, y) for comp in range(3) for x in range(nx) for y in range(ny)]
    while todo:
        node = todo.pop()
        if node in seen:
            continue
        seen.add(node)
        if block(node) != (0, 0) and alone(node):
            found.add(node)
        elif node[1]:
            made.add(node)
            todo += reads(node)
    return found, made


class Message:
    def __init__(self, nodes, axis, folded=()):
        self.axis, self.runs, self.at, self.size = axis, [], {}, 0
        assert nodes.issuperset(folded)
        self.zeros = Message(set(folded), axis).runs if folded else []
        nodes = nodes - set(folded)
        stretches = []
        for node in sorted(nodes):
            before = list(node)
            before[3 + axis] -= 1
            if tuple(before) in nodes:
                continue
            count = 1
            while (*node[:3], node[3] + count * (axis == 0), node[4] + count * (axis == 1)) in nodes:
                count += 1
            stretches.append((count, node))
        for count, (kind, level, comp, x, y) in sorted(stretches, key=lambda item: (-item[0], item[1])):
            for run in (0, 1) if kind != "C" else (0,):
                for part in (0, 1) if kind != "C" else (0,):
                    what = (kind, level, comp, run, part)
                    self.runs.append((what, x, y, count, self.size))
                    for i in range(count):
                        self.at[what, x + i * (axis == 0), y + i * (axis == 1)] = self.size + i
                    self.size += count
        self.lines = -(-self.size // SUB) * SUB


class Plan:
    def __init__(self, nx, ny, depth):
        self.depth = depth
        self.nx, self.ny = nx, ny
        self.wide, self.ring = nx + 2 * STEPS, ny + SUB
        nodes, made = wanted(nx, ny)
        self.made, self.free, self.rest = {}, {}, {}
        tiles, ready = {}, set()
        for node in made:
            tiles.setdefault((node[1], "HE".index(node[0]), *node[2:4], node[4] % self.ring // SUB), []).append(node)

        def early(node):
            if node in made:
                return node in ready
            return node not in nodes or 0 <= node[3] < nx or 0 <= node[4] < ny

        for (level, order, comp, x, tile), members in sorted(tiles.items()):
            key = ("HE"[order], level, x)
            middle = level - 1 + order <= x < nx - level
            free = middle or all(early(other) for node in members for other in reads(node))
            if free:
                ready.update(members)
            for into in (self.made, self.free if free else self.rest):
                into.setdefault(key, {}).setdefault(comp, set()).add(tile)
        sides = {}
        for node in nodes:
            sides.setdefault((node[3] // nx, node[4] // ny), set()).add(node)

        def shifted(found, dx):
            return {(*node[:3], node[3] + dx, node[4]) for node in found}

        y_low, y_high = (sides[0, side] | shifted(sides[-1, side], nx) | shifted(sides[1, side], -nx) for side in (-1, 1))
        self.x_folds = (1, ny - 2), (2, ny - 2)
        self.y_folds = (2, nx - 2), (3, nx - 2)
        x_folded = [("E", 1, comp, -2, y) for comp in range(3) for y in range(*self.x_folds[comp == 0])]
        y_folded = [("E", 1, comp, x, -2) for comp in range(3) for x in range(*self.y_folds[comp == 1])]
        self.y_low, self.y_high = Message(y_low, 0, y_folded), Message(y_high, 0)
        self.x_low, self.x_high = Message(sides[-1, 0], 1, x_folded), Message(sides[1, 0], 1)
        self.mate_side, self.far_side = (1, -1), (-1, 1)
        self.mate = [Message(sides[side, -1] | sides[side, 1], 1) for side in self.mate_side]
        self.far_low, self.far_high = ([Message(sides[side, end], 1) for side in self.far_side] for end in (-1, 1))

    def row(self, x, y, run=0, part=0, comp=0):
        return ((run * 6 + part * 3 + comp) * self.wide + x + STEPS) * self.ring + y % self.ring

    def rows(self, what, x, y, axis, count):
        _, _, comp, run, part = what
        start = self.row(x, y, run, part, comp)
        return pl.ds(start, count, stride=self.ring) if axis == 0 and count > 1 else pl.ds(start, count)


class State:
    def __init__(self, efield, hfield, coef):
        self.by_kind = {"E": efield, "H": hfield, "C": [coef]}

    def __call__(self, what):
        return self.by_kind[what[0]][what[1]]


def pack(plan, message, state, dx, dy, out, changed=None):
    for what, x, y, count, at in message.runs:
        layer, first = (y, x) if message.axis == 0 else (x, y)
        if changed and (what, layer) in changed:
            ref, row = changed[what, layer]
            value = ref[pl.ds(row + first, count), :]
        else:
            value = state(what)[plan.rows(what, x + dx, y + dy, message.axis, count), :]
        out[pl.ds(at, count), :] = value


def fold(plan, state, axis, scratch):
    nx, ny = plan.nx, plan.ny
    size, normal = (nx, 1) if axis == 0 else (ny, 0)
    before, after = ((0, 2) if axis == 0 else (1, 2))
    cell = lax.broadcasted_iota(jnp.int32, (size, scratch.shape[1]), 0)
    lane = lax.broadcasted_iota(jnp.int32, cell.shape, 1)
    folds = plan.y_folds if axis == 0 else plan.x_folds
    changed = {}

    def lines(what, layer):
        place = (0, ny + layer) if axis == 0 else (nx + layer, 0)
        return state(what)[plan.rows(what, *place, axis, size), :]

    def inside(value, fold):
        return jnp.where((cell >= fold[0]) & (cell < fold[1]), value, 0.0)

    for run in (0, 1):
        for part in (0, 1):

            def get(kind, level, comp, layer):
                return lines((kind, level, comp, run, part), layer)

            def put(kind, level, comp, layer, value):
                row = len(changed) * size
                scratch[pl.ds(row, size), :] = value
                changed[(kind, level, comp, run, part), layer] = scratch, row

            low, high = (inside(get("E", 1, comp, -2), folds[0]) for comp in (before, after))
            along = inside(get("E", 1, normal, -2), folds[1])
            along_z = jnp.where(lane == lane.shape[1] - 1, 0.0, pltpu.roll(along, lane.shape[1] - 1, 1)) - along
            along_next = pltpu.roll(along, size - 1, 0) - along
            sign = 1.0 if axis == 0 else -1.0
            d_before = sign * (high + along_z)
            d_after = -sign * (low + along_next)
            scale = lines(("C", 0, 0, 0, 0), -1)
            put("H", 1, before, -2, get("H", 1, before, -2) + d_before)
            put("H", 1, after, -2, get("H", 1, after, -2) + d_after)
            put("E", 0, before, -1, get("E", 0, before, -1) + sign * scale * d_after)
            put("E", 0, after, -1, get("E", 0, after, -1) - sign * scale * d_before)
            put("H", 0, before, -1, get("H", 0, before, -1) + 0.5 * scale * d_before)
            put("H", 0, after, -1, get("H", 0, after, -1) + 0.5 * scale * d_after)
    return changed


def by_parity(offset, body):
    parity = lax.rem(lax.axis_index("gx") + offset, 2)
    for value in (0, 1):
        pl.when(parity == value)(functools.partial(body, value))


def pack_y_kernel(plan, fwd, adj, eps, e0, h0, e1, h1, coef, z_up, z_down, sems, scratch):
    nx, ny = plan.nx, plan.ny
    own = (pl.ds(STEPS, nx), pl.ds(0, ny), slice(None))
    copies = [pltpu.make_async_copy(eps, coef.at[own], sems.at[0])]
    for run, ref in enumerate((fwd, adj)):
        for kind, array in enumerate((e0, h0)):
            for i in range(6):
                copies.append(
                    pltpu.make_async_copy(ref.at[kind * 6 + i], array.at[(run * 6 + i, *own)], sems.at[len(copies)])
                )
    for copy in copies:
        copy.start()
    copies[0].wait()
    for x in range(nx):
        coef[STEPS + x, pl.ds(0, ny), :] = (0.5 * courant) / coef[STEPS + x, pl.ds(0, ny), :]
    e0, h0, e1, h1, coef = (array.reshape((-1, array.shape[-1])) for array in (e0, h0, e1, h1, coef))
    sweeps = Sweeps(plan, [e0, e1], [h0, h1], coef, ny)
    for run in (0, 1):
        for copy in copies[1 + 12 * run : 13 + 12 * run]:
            copy.wait()
        sweeps.both(1, range(nx), range(nx - 1), runs=(run,))
    state = State([e0, e1], [h0, h1], coef)
    pack(plan, plan.y_low, state, 0, ny, z_up, fold(plan, state, 0, scratch))
    pack(plan, plan.y_high, state, 0, -ny, z_down)


def pack_x_kernel(plan, e0, h0, e1, h1, coef, x_up, x_down, scratch):
    state = State([e0, e1], [h0, h1], coef)
    pack(plan, plan.x_low, state, plan.nx, 0, x_up, fold(plan, state, 1, scratch))
    pack(plan, plan.x_high, state, -plan.nx, 0, x_down)


def pack_diagonal_kernel(plan, e0, h0, e1, h1, coef, after, diagonal):
    state = State([e0, e1], [h0, h1], coef)

    def corners(receiver):
        pack(plan, plan.far_high[receiver], state, -plan.nx * plan.far_side[receiver], -plan.ny, diagonal)

    by_parity(1, corners)


def turns_kernel(groups, table, index, tiles, turns):
    row = index[0]
    phi_x, phi_y = table[row, 0], table[row, 1]
    at_x, at_y = lax.axis_index("gx"), lax.axis_index("gy")
    none = jnp.float32(0.0)
    ax_low = jnp.where(at_x == 0, -phi_x, none)
    ax_high = jnp.where(at_x == lax.axis_size("gx") - 1, phi_x, none)
    ay_low = jnp.where(at_y == 0, -phi_y, none)
    ay_high = jnp.where(at_y == lax.axis_size("gy") - 1, phi_y, none)
    sub = lax.broadcasted_iota(jnp.int32, (SUB, turns.shape[1]), 0)
    angles = jnp.zeros(sub.shape, jnp.float32)
    for i, angle in enumerate((ax_low, ax_high, ay_low, ay_high, ax_low + ay_low, ax_low + ay_high,
                               ax_high + ay_low, ax_high + ay_high)):
        angles = jnp.where(sub == i, angle, angles)
    turns[pl.ds(0, SUB), :] = jnp.cos(angles)
    turns[pl.ds(SUB, SUB), :] = jnp.sin(angles)
    own_tile = at_x * lax.axis_size("gy") + at_y
    chosen = tiles[0] == own_tile
    for i in range(1, tiles.shape[0]):
        chosen = jnp.logical_or(chosen, tiles[i] == own_tile)
    weight = jnp.where(chosen, jnp.float32(1.0 / groups), none)
    turns[pl.ds(2 * SUB, SUB), :] = jnp.full(sub.shape, weight, jnp.float32)


def relay_kernel(plan, jobs, *refs):
    faces, outs = refs[: len(refs) - len(jobs)], refs[len(refs) - len(jobs) :]

    def corners(receiver):
        for (messages, side), out in zip(jobs, outs, strict=True):
            dx = -plan.nx * side[receiver]
            for (what, x, y), row in messages[receiver].at.items():
                ref, source = (faces[0], plan.y_low) if y < 0 else (faces[1], plan.y_high)
                out[pl.ds(row, 1), :] = ref[pl.ds(source.at[what, x + dx, y], 1), :]

    by_parity(1, corners)


def turned(real, imag, cosine, sine):
    return real * cosine - imag * sine, real * sine + imag * cosine


def unpack(plan, message, ref, which, turns, state, kinds, level, layers=None):
    axis = message.axis
    for (kind, at_level, comp, run, part), x, y, count, at in message.runs:
        if kind not in kinds or at_level != level or part == 1:
            continue
        pieces = [(x, y, count, at)]
        if layers is not None:
            pieces = [(x + i, y, 1, at + i) for i in range(count) if x + i in layers]
        for cell_x, cell_y, size, row in pieces:
            what = (kind, at_level, comp, run, 0)
            real = ref[pl.ds(row, size), :]
            if kind == "C":
                state(what)[plan.rows(what, cell_x, cell_y, axis, size), :] = real
                continue
            twin = (kind, at_level, comp, run, 1)
            imag = ref[pl.ds(message.at[twin, cell_x, cell_y], size), :]
            turn = which(y)
            cosine, sine = turns[pl.ds(turn, 1), :], turns[pl.ds(SUB + turn, 1), :]
            real, imag = turned(real, imag, cosine, sine if run == 0 else -sine)
            state(what)[plan.rows(what, cell_x, cell_y, axis, size), :] = real
            state(twin)[plan.rows(twin, cell_x, cell_y, axis, size), :] = imag
    for what, x, y, count, _ in message.zeros:
        if what[0] in kinds and what[1] == level and layers is None:
            state(what)[plan.rows(what, x, y, axis, count), :] = jnp.zeros((count, ref.shape[1]), jnp.float32)


class Sweeps:
    def __init__(self, plan, efield, hfield, coef, height, todo=None):
        self.plan, self.efield, self.hfield, self.coef, self.height = plan, efield, hfield, coef, height
        self.todo = todo

    def rows(self, run, part, comp, x, start, stop):
        return pl.ds(self.plan.row(x, 0, run, part, comp) + start, stop - start)

    def get(self, array, run, part, comp, x):
        return array[self.rows(run, part, comp, x, 0, self.height), :]

    def pieces(self, kind, step, x):
        if self.todo is None:
            return [(comp, 0, self.height) for comp in range(3)]
        found = []
        for comp, tiles in sorted(self.todo.get((kind, step, x), {}).items()):
            for tile in sorted(tiles):
                if found and found[-1][0] == comp and found[-1][2] == tile * SUB:
                    found[-1] = (comp, found[-1][1], (tile + 1) * SUB)
                else:
                    found.append((comp, tile * SUB, (tile + 1) * SUB))
        return found

    def next_z(self, value):
        lane = lax.broadcasted_iota(jnp.int32, value.shape, 1)
        return jnp.where(lane == value.shape[1] - 1, 0.0, pltpu.roll(value, value.shape[1] - 1, 1))

    def prev_z(self, value):
        lane = lax.broadcasted_iota(jnp.int32, value.shape, 1)
        return jnp.where(lane == 0, 0.0, pltpu.roll(value, 1, 1))

    def next_y(self, value):
        return pltpu.roll(value, self.height - 1, 0)

    def prev_y(self, value):
        return pltpu.roll(value, 1, 0)

    def update_h(self, step, run, part, x):
        efield, old, new = self.efield[step - 1], self.hfield[step - 1], self.hfield[step]
        ex, ey, ez = (self.get(efield, run, part, comp, x) for comp in range(3))
        for comp, start, stop in self.pieces("H", step, x):
            here = slice(start, stop)
            if comp == 0:
                curl = (self.next_y(ez) - ez)[here] - (self.next_z(ey[here]) - ey[here])
            elif comp == 1:
                ez_x = self.get(efield, run, part, 2, x + 1)
                curl = (self.next_z(ex[here]) - ex[here]) - (ez_x - ez)[here]
            else:
                ey_x = self.get(efield, run, part, 1, x + 1)
                curl = (ey_x - ey)[here] - (self.next_y(ex) - ex)[here]
            before = self.get(old, run, part, comp, x)[here]
            if step == 1:
                before = before + before
            new[self.rows(run, part, comp, x, start, stop), :] = before - curl

    def update_e(self, step, run, part, x):
        old, new, hfield = self.efield[step - 1], self.efield[step], self.hfield[step]
        hx, hy, hz = (self.get(hfield, run, part, comp, x) for comp in range(3))
        scale = self.get(self.coef, 0, 0, 0, x)
        for comp, start, stop in self.pieces("E", step, x):
            here = slice(start, stop)
            if comp == 0:
                curl = (hz - self.prev_y(hz))[here] - (hy[here] - self.prev_z(hy[here]))
            elif comp == 1:
                hz_x = self.get(hfield, run, part, 2, x - 1)
                curl = (hx[here] - self.prev_z(hx[here])) - (hz - hz_x)[here]
            else:
                hy_x = self.get(hfield, run, part, 1, x - 1)
                curl = (hy - hy_x)[here] - (hx - self.prev_y(hx))[here]
            before = self.get(old, run, part, comp, x)[here]
            new[self.rows(run, part, comp, x, start, stop), :] = before + scale[here] * curl

    def both(self, step, h_layers, e_layers, after_h=None, after_e=None, runs=(0, 1)):
        for update, layers, after in ((self.update_h, h_layers, after_h), (self.update_e, e_layers, after_e)):
            for x in layers:
                for run in runs:
                    for part in (0, 1):
                        update(step, run, part, x)
            if after is not None:
                after()


def middle_kernel(plan, e0_in, h0_in, e1_in, h1_in, coef_in, z_low, z_high, turns, *arrays):
    nx = plan.nx
    efield, hfield, coef = arrays[: STEPS + 1], arrays[STEPS + 1 : 2 * STEPS + 2], arrays[-1]
    state = State(efield, hfield, coef)

    def take(kinds, level):
        unpack(plan, plan.y_low, z_low, lambda y: 2, turns, state, kinds, level)
        unpack(plan, plan.y_high, z_high, lambda y: 3, turns, state, kinds, level)

    take("EHC", 0)
    sweeps = Sweeps(plan, efield, hfield, coef, plan.ring, plan.made)
    for step in range(1, STEPS + 1):
        after = [lambda: take("H", 1), lambda: take("E", 1)] if step == 1 else []
        sweeps.both(step, range(step - 1, nx - step), range(step, nx - step), *after)


def add_known(plan, efield, levels, transform, out):
    nx, ny = plan.nx, plan.ny
    for x in range(nx):
        for tile in range(ny // SUB):
            for comp in range(3):
                ends = []
                for run in (0, 1):
                    at = [pl.ds(((part * 3 + comp) * nx + x) * ny + tile * SUB, SUB) for part in (0, 1)]
                    real, imag = transform[run][at[0], :], transform[run][at[1], :]
                    for level in levels(x, tile, comp):
                        theta = omega_step * level
                        here = [efield[level][pl.ds(plan.row(x, tile * SUB, run, part, comp), SUB), :] for part in (0, 1)]
                        more = turned(*here, math.cos(theta), math.sin(theta))
                        real, imag = real + more[0], imag + more[1]
                    out[run][at[0], :], out[run][at[1], :] = real, imag
                    ends.append((real, imag))
                yield x, tile, ends


def known(plan, x, tile, comp):
    def ready(level):
        return level <= x < plan.nx - level or tile in plan.free.get(("E", level, x), {}).get(comp, ())

    return [level for level in range(1, STEPS + 1) if ready(level)]


def do_valleys(plan, sweeps, take):
    for step in range(1, STEPS + 1):
        low, high = step - STEPS, plan.nx - step
        h_layers = [*range(low - 1, step - 1), *range(high, plan.nx + STEPS - step)]
        e_layers = [*range(low, step), *range(high, plan.nx + STEPS - step)]
        after = [functools.partial(take, "H", 1, h_layers), functools.partial(take, "E", 1, e_layers)] if step == 1 else []
        sweeps.both(step, h_layers, e_layers, *after)


def faces_kernel(plan, *refs):
    count = 2 * STEPS + 3
    x_low, x_high, z_low, z_high, turns, spec_f, spec_a = refs[count : count + 7]
    arrays = refs[count + 7 : 2 * count + 7]
    out_f, out_a = refs[2 * count + 7 :]
    efield, hfield, coef = arrays[: STEPS + 1], arrays[STEPS + 1 : 2 * STEPS + 2], arrays[-1]
    state = State(efield, hfield, coef)

    def take(kinds, level, layers):
        unpack(plan, plan.x_low, x_low, lambda y: 0, turns, state, kinds, level)
        unpack(plan, plan.x_high, x_high, lambda y: 1, turns, state, kinds, level)
        unpack(plan, plan.y_low, z_low, lambda y: 2, turns, state, kinds, level, layers)
        unpack(plan, plan.y_high, z_high, lambda y: 3, turns, state, kinds, level, layers)

    take("EHC", 0, ())
    do_valleys(plan, Sweeps(plan, efield, hfield, coef, plan.ring, plan.free), take)
    for _ in add_known(plan, efield, functools.partial(known, plan), (spec_f, spec_a), (out_f, out_a)):
        pass


def edges_kernel(plan, groups, *refs):
    count = 2 * STEPS + 3
    x_low, x_high, far_low, far_high, mate, z_low, z_high, turns, part_f, part_a = refs[count : count + 10]
    arrays = refs[count + 10 : 2 * count + 10]
    out_f, out_a, *parts = refs[2 * count + 10 :]
    efield, hfield, coef = arrays[: STEPS + 1], arrays[STEPS + 1 : 2 * STEPS + 2], arrays[-1]
    state = State(efield, hfield, coef)

    def take(kinds, level, layers):
        if level:
            unpack(plan, plan.x_low, x_low, lambda y: 0, turns, state, kinds, level)
            unpack(plan, plan.x_high, x_high, lambda y: 1, turns, state, kinds, level)

        def corners(receiver):
            for messages, ref, side in (
                (plan.far_low, far_low, plan.far_side),
                (plan.far_high, far_high, plan.far_side),
                (plan.mate, mate, plan.mate_side),
            ):
                first = 4 if side[receiver] < 0 else 6
                unpack(plan, messages[receiver], ref, lambda y: first + (y >= 0), turns, state, kinds, level)

        by_parity(0, corners)
        unpack(plan, plan.y_low, z_low, lambda y: 2, turns, state, kinds, level, layers)
        unpack(plan, plan.y_high, z_high, lambda y: 3, turns, state, kinds, level, layers)

    take("EHC", 0, ())
    do_valleys(plan, Sweeps(plan, efield, hfield, coef, plan.ring, plan.rest), take)

    share = plan.depth // groups
    shift = lax.rem(groups - lax.axis_index("angle"), groups) * share
    weight = turns[pl.ds(2 * SUB, SUB), :]

    def rest(x, tile, comp):
        return [level for level in range(1, STEPS + 1) if level not in known(plan, x, tile, comp)]

    totals = {}
    for x, tile, ends in add_known(plan, efield, rest, (part_f, part_a), (out_f, out_a)):
        term = ends[0][0] * ends[1][0] - ends[0][1] * ends[1][1]
        totals[x, tile] = totals[x, tile] + term if (x, tile) in totals else term
    block = lax.broadcasted_iota(jnp.int32, weight.shape, 1) // share
    tiles = [pltpu.roll(total * weight, shift, 1) for total in totals.values()]
    for k, part in enumerate(parts):
        for i in range(len(tiles) // groups):
            packed = jnp.zeros(weight.shape, jnp.float32)
            for t in range(groups):
                lanes = (t - k) % groups * share
                value = tiles[i * groups + t]
                packed = jnp.where(block == t, pltpu.roll(value, lanes, 1) if lanes else value, packed)
            part[pl.ds(i * SUB, SUB), :] = packed


def sum_kernel(groups, *refs):
    *parts, out = refs
    share = out.shape[1]
    for i in range(parts[0].shape[0] // SUB):
        total = parts[0][pl.ds(i * SUB, SUB), :]
        for part in parts[1:]:
            total = total + part[pl.ds(i * SUB, SUB), :]
        for t in range(groups):
            out[pl.ds((i * groups + t) * SUB, SUB), :] = total[:, t * share : (t + 1) * share]


def write_kernel(tr_f, tr_a, out_f, out_a, sems):
    copies = []
    for source, target in ((tr_f, out_f), (tr_a, out_a)):
        for i in range(source.shape[0]):
            copies.append(pltpu.make_async_copy(source.at[i], target.at[i], sems.at[len(copies)]))
    for copy in copies:
        copy.start()
    for copy in copies:
        copy.wait()


def ring_pairs(axis, offset):
    size = lax.axis_size(axis)
    return [(i, (i + offset) % size) for i in range(size)]


def mate_pairs():
    return [(i, i ^ 1) for i in range(lax.axis_size("gx"))]


def far_pairs():
    size = lax.axis_size("gx")
    return [(i, (i + (1 if i % 2 else -1)) % size) for i in range(size)]


def diagonal_pairs():
    size = lax.axis_size("gy")
    return [(x * size + y, far * size + (y - 1) % size) for x, far in far_pairs() for y in range(size)]


def shards(
    forward_fields,
    adjoint_fields,
    forward_spectrum,
    adjoint_spectrum,
    permittivity,
    phase_table,
    angle_index,
    design_tiles,
):
    nx, ny, depth = permittivity.shape
    plan = Plan(nx, ny, depth)
    groups = lax.axis_size("angle")
    wide, ring = plan.wide, plan.ring

    def array(*shape):
        return jax.ShapeDtypeStruct(shape, jnp.float32)

    def lines(count):
        return array(count, depth)

    def params(mib):
        return pltpu.CompilerParams(vmem_limit_bytes=mib * 2**20)

    def cost(size):
        return pl.CostEstimate(flops=size, bytes_accessed=size, transcendentals=0)

    assert lax.axis_size("gx") % 2 == 0 and nx * ny % (groups * SUB) == 0
    with jax.named_scope("pack_y"):
        *first, coef, z_up, z_down = pl.pallas_call(
            functools.partial(pack_y_kernel, plan),
            out_shape=(
                *[array(12, wide, ring, depth)] * 4,
                array(wide, ring, depth),
                lines(plan.y_low.lines),
                lines(plan.y_high.lines),
            ),
            in_specs=[HBM] * 3,
            out_specs=[VMEM] * 7,
            scratch_shapes=[pltpu.SemaphoreType.DMA((25,)), pltpu.VMEM((24 * nx, depth), jnp.float32)],
            compiler_params=params(8),
        )(*(pltpu.with_memory_space_constraint(array, pltpu.HBM) for array in (forward_fields[0], adjoint_fields[0], permittivity)))
    e0, h0, e1, h1, coef = (state.reshape((-1, depth)) for state in (*first, coef))
    with jax.named_scope("send_y"):
        z_low = lax.ppermute(z_up, "gy", ring_pairs("gy", 1))
        z_high = lax.ppermute(z_down, "gy", ring_pairs("gy", -1))
    with jax.named_scope("pack_x"):
        x_up, x_down = pl.pallas_call(
            functools.partial(pack_x_kernel, plan),
            out_shape=[lines(plan.x_low.lines), lines(plan.x_high.lines)],
            in_specs=[VMEM] * 5,
            out_specs=[VMEM] * 2,
            scratch_shapes=[pltpu.VMEM((24 * ny, depth), jnp.float32)],
            compiler_params=params(8),
            cost_estimate=cost(40 * 2**20),
        )(e0, h0, e1, h1, coef)
    with jax.named_scope("send_x"):
        x_low = lax.ppermute(x_up, "gx", ring_pairs("gx", 1))
        x_high = lax.ppermute(x_down, "gx", ring_pairs("gx", -1))
    with jax.named_scope("turns"):
        turns = pl.pallas_call(
            functools.partial(turns_kernel, groups),
            out_shape=lines(3 * SUB),
            in_specs=[SMEM] * 3,
            out_specs=VMEM,
            compiler_params=params(4),
        )(phase_table, angle_index, design_tiles)
    with jax.named_scope("diagonal_corners"):
        to_diagonal = pl.pallas_call(
            functools.partial(pack_diagonal_kernel, plan),
            out_shape=lines(max(message.lines for message in plan.far_high)),
            in_specs=[VMEM] * 6,
            out_specs=VMEM,
            compiler_params=params(4),
        )(e0, h0, e1, h1, coef, x_up)
        far_high = lax.ppermute(to_diagonal, ("gx", "gy"), diagonal_pairs())

    def relay(jobs, *faces):
        return pl.pallas_call(
            functools.partial(relay_kernel, plan, jobs),
            out_shape=[lines(max(message.lines for message in messages)) for messages, _ in jobs],
            in_specs=[VMEM] * len(faces),
            out_specs=[VMEM] * len(jobs),
            compiler_params=params(4),
            cost_estimate=cost(2**10),
        )(*faces)

    with jax.named_scope("relay_low_corners"):
        (to_far,) = relay([(plan.far_low, plan.far_side)], z_low)
        far_low = lax.ppermute(to_far, "gx", far_pairs())
    with jax.named_scope("relay_corners"):
        (to_mate,) = relay([(plan.mate, plan.mate_side)], z_low, z_high)
        mate = lax.ppermute(to_mate, "gx", mate_pairs())
    level = lines(12 * wide * ring)
    count = 2 * STEPS + 3
    levels = [level] * (count - 1) + [lines(wide * ring)]
    with jax.named_scope("middle"):
        state = pl.pallas_call(
            functools.partial(middle_kernel, plan),
            out_shape=levels,
            in_specs=[VMEM] * 8,
            out_specs=[VMEM] * count,
            input_output_aliases={0: 0, 1: STEPS + 1, 2: 1, 3: STEPS + 2, 4: count - 1},
            compiler_params=params(8),
            cost_estimate=cost(5 * 2**29),
        )(e0, h0, e1, h1, coef, z_low, z_high, turns)
    transforms = [lines(6 * nx * ny)] * 2
    with jax.named_scope("faces"):
        spectra = [spectrum.reshape((-1, depth)) for spectrum in (forward_spectrum, adjoint_spectrum)]
        results = pl.pallas_call(
            functools.partial(faces_kernel, plan),
            out_shape=[*levels, *transforms],
            in_specs=[VMEM] * (count + 7),
            out_specs=[VMEM] * (count + 2),
            input_output_aliases={i: i for i in range(count)},
            compiler_params=params(8),
        )(*state, x_low, x_high, z_low, z_high, turns, *spectra)
        state, sums = results[:count], results[count:]
    with jax.named_scope("edges"):
        results = pl.pallas_call(
            functools.partial(edges_kernel, plan, groups),
            out_shape=[*levels, *transforms, *[lines(nx * ny // groups)] * groups],
            in_specs=[VMEM] * (count + 10),
            out_specs=[VMEM] * (count + 2 + groups),
            input_output_aliases={i: i for i in range(count)} | {count + 8: count, count + 9: count + 1},
            compiler_params=params(8),
        )(*state, x_low, x_high, far_low, far_high, mate, z_low, z_high, turns, *sums)
        tr_f, tr_a, own, *others = results[count:]
    with jax.named_scope("sum_angles"):
        others = [lax.ppermute(part, "angle", ring_pairs("angle", k + 1)) for k, part in enumerate(others)]
        gradient = pl.pallas_call(
            functools.partial(sum_kernel, groups),
            out_shape=array(nx * ny, depth // groups),
            in_specs=[VMEM] * groups,
            out_specs=VMEM,
            compiler_params=params(4),
        )(own, *others)
    with jax.named_scope("write"):
        out_f, out_a = pl.pallas_call(
            write_kernel,
            out_shape=[array(6, nx, ny, depth)] * 2,
            in_specs=[VMEM] * 2,
            out_specs=[HBM] * 2,
            scratch_shapes=[pltpu.SemaphoreType.DMA((12,))],
            compiler_params=params(4),
        )(tr_f.reshape((6, nx, ny, depth)), tr_a.reshape((6, nx, ny, depth)))
    return (
        out_f.reshape(forward_spectrum.shape),
        out_a.reshape(adjoint_spectrum.shape),
        gradient.reshape((nx, ny, depth // groups)),
    )


def solution(mesh):
    in_specs = (
        P("angle", None, "gx", "gy", None),
        P("angle", None, "gx", "gy", None),
        P("angle", None, "gx", "gy", None),
        P("angle", None, "gx", "gy", None),
        P("gx", "gy", None),
        P(),
        P("angle"),
        P(),
    )
    out_specs = (
        P("angle", None, "gx", "gy", None),
        P("angle", None, "gx", "gy", None),
        P("gx", "gy", "angle"),
    )
    return jax.shard_map(shards, mesh=mesh, in_specs=in_specs, out_specs=out_specs, check_vma=False)
```

```python
import functools
import math

import jax
import jax.numpy as jnp
from jax import lax
from jax.experimental import pallas as pl
from jax.experimental.pallas import tpu as pltpu
from jax.sharding import PartitionSpec as P

STEPS = 3
SUB = 8

courant = 0.5
omega_step = 0.7

VMEM = pl.BlockSpec(memory_space=pltpu.VMEM)
SMEM = pl.BlockSpec(memory_space=pltpu.SMEM)
HBM = pl.BlockSpec(memory_space=pltpu.HBM)


def reads(node):
    kind, level, comp, x, y = node
    others = [c for c in range(3) if c != comp]
    if kind == "E":
        found = [("E", level - 1, comp, x, y), ("C", 0, 0, x, y)] + [("H", level, c, x, y) for c in others]
        if comp != 1:
            found.append(("H", level, 2 - comp, x, y - 1))
        if comp != 0:
            found.append(("H", level, 3 - comp, x - 1, y))
        return found
    found = [("H", level - 1, comp, x, y)] + [("E", level - 1, c, x, y) for c in others]
    if comp != 1:
        found.append(("E", level - 1, 2 - comp, x, y + 1))
    if comp != 0:
        found.append(("E", level - 1, 3 - comp, x + 1, y))
    return found


def wanted(nx, ny):
    def block(node):
        return node[3] // nx, node[4] // ny

    @functools.cache
    def alone(node):
        if node[1] == 0:
            return True
        return node[1] == 1 and all(block(other) == block(node) and alone(other) for other in reads(node))

    found, made, seen = set(), set(), set()
    todo = [("E", STEPS, comp, x, y) for comp in range(3) for x in range(nx) for y in range(ny)]
    while todo:
        node = todo.pop()
        if node in seen:
            continue
        seen.add(node)
        if block(node) != (0, 0) and alone(node):
            found.add(node)
        elif node[1]:
            made.add(node)
            todo += reads(node)
    return found, made


class Message:
    def __init__(self, nodes, axis, folded=()):
        self.axis, self.runs, self.at, self.size = axis, [], {}, 0
        assert nodes.issuperset(folded)
        self.zeros = Message(set(folded), axis).runs if folded else []
        nodes = nodes - set(folded)
        stretches = []
        for node in sorted(nodes):
            before = list(node)
            before[3 + axis] -= 1
            if tuple(before) in nodes:
                continue
            count = 1
            while (*node[:3], node[3] + count * (axis == 0), node[4] + count * (axis == 1)) in nodes:
                count += 1
            stretches.append((count, node))
        for count, (kind, level, comp, x, y) in sorted(stretches, key=lambda item: (-item[0], item[1])):
            for run in (0, 1) if kind != "C" else (0,):
                for part in (0, 1) if kind != "C" else (0,):
                    what = (kind, level, comp, run, part)
                    self.runs.append((what, x, y, count, self.size))
                    for i in range(count):
                        self.at[what, x + i * (axis == 0), y + i * (axis == 1)] = self.size + i
                    self.size += count
        self.lines = -(-self.size // SUB) * SUB


class Plan:
    def __init__(self, nx, ny, depth):
        self.depth = depth
        self.nx, self.ny = nx, ny
        self.wide, self.ring = nx + 2 * STEPS, ny + SUB
        nodes, made = wanted(nx, ny)
        self.made, self.free, self.rest = {}, {}, {}
        tiles, ready = {}, set()
        for node in made:
            tiles.setdefault((node[1], "HE".index(node[0]), *node[2:4], node[4] % self.ring // SUB), []).append(node)

        def early(node):
            if node in made:
                return node in ready
            return node not in nodes or 0 <= node[3] < nx or 0 <= node[4] < ny

        for (level, order, comp, x, tile), members in sorted(tiles.items()):
            key = ("HE"[order], level, x)
            middle = level - 1 + order <= x < nx - level
            free = middle or all(early(other) for node in members for other in reads(node))
            if free:
                ready.update(members)
            for into in (self.made, self.free if free else self.rest):
                into.setdefault(key, {}).setdefault(comp, set()).add(tile)
        sides = {}
        for node in nodes:
            sides.setdefault((node[3] // nx, node[4] // ny), set()).add(node)

        def shifted(found, dx):
            return {(*node[:3], node[3] + dx, node[4]) for node in found}

        y_low, y_high = (sides[0, side] | shifted(sides[-1, side], nx) | shifted(sides[1, side], -nx) for side in (-1, 1))
        self.x_folds = (1, ny - 2), (2, ny - 2)
        self.y_folds = (2, nx - 2), (3, nx - 2)
        x_folded = [("E", 1, comp, -2, y) for comp in range(3) for y in range(*self.x_folds[comp == 0])]
        y_folded = [("E", 1, comp, x, -2) for comp in range(3) for x in range(*self.y_folds[comp == 1])]
        self.y_low, self.y_high = Message(y_low, 0, y_folded), Message(y_high, 0)
        self.x_low, self.x_high = Message(sides[-1, 0], 1, x_folded), Message(sides[1, 0], 1)
        self.mate_side, self.far_side = (1, -1), (-1, 1)
        self.mate = [Message(sides[side, -1] | sides[side, 1], 1) for side in self.mate_side]
        self.far_low, self.far_high = ([Message(sides[side, end], 1) for side in self.far_side] for end in (-1, 1))

    def row(self, x, y, run=0, part=0, comp=0):
        return ((run * 6 + part * 3 + comp) * self.wide + x + STEPS) * self.ring + y % self.ring

    def rows(self, what, x, y, axis, count):
        _, _, comp, run, part = what
        start = self.row(x, y, run, part, comp)
        return pl.ds(start, count, stride=self.ring) if axis == 0 and count > 1 else pl.ds(start, count)


class State:
    def __init__(self, efield, hfield, coef):
        self.by_kind = {"E": efield, "H": hfield, "C": [coef]}

    def __call__(self, what):
        return self.by_kind[what[0]][what[1]]


def pack(plan, message, state, dx, dy, out, changed=None):
    for what, x, y, count, at in message.runs:
        layer, first = (y, x) if message.axis == 0 else (x, y)
        if changed and (what, layer) in changed:
            ref, row = changed[what, layer]
            value = ref[pl.ds(row + first, count), :]
        else:
            value = state(what)[plan.rows(what, x + dx, y + dy, message.axis, count), :]
        out[pl.ds(at, count), :] = value


def fold(plan, state, axis, scratch):
    nx, ny = plan.nx, plan.ny
    size, normal = (nx, 1) if axis == 0 else (ny, 0)
    before, after = ((0, 2) if axis == 0 else (1, 2))
    cell = lax.broadcasted_iota(jnp.int32, (size, scratch.shape[1]), 0)
    lane = lax.broadcasted_iota(jnp.int32, cell.shape, 1)
    folds = plan.y_folds if axis == 0 else plan.x_folds
    changed = {}

    def lines(what, layer):
        place = (0, ny + layer) if axis == 0 else (nx + layer, 0)
        return state(what)[plan.rows(what, *place, axis, size), :]

    def inside(value, fold):
        return jnp.where((cell >= fold[0]) & (cell < fold[1]), value, 0.0)

    for run in (0, 1):
        for part in (0, 1):

            def get(kind, level, comp, layer):
                return lines((kind, level, comp, run, part), layer)

            def put(kind, level, comp, layer, value):
                row = len(changed) * size
                scratch[pl.ds(row, size), :] = value
                changed[(kind, level, comp, run, part), layer] = scratch, row

            low, high = (inside(get("E", 1, comp, -2), folds[0]) for comp in (before, after))
            along = inside(get("E", 1, normal, -2), folds[1])
            along_z = jnp.where(lane == lane.shape[1] - 1, 0.0, pltpu.roll(along, lane.shape[1] - 1, 1)) - along
            along_next = pltpu.roll(along, size - 1, 0) - along
            sign = 1.0 if axis == 0 else -1.0
            d_before = sign * (high + along_z)
            d_after = -sign * (low + along_next)
            scale = lines(("C", 0, 0, 0, 0), -1)
            put("H", 1, before, -2, get("H", 1, before, -2) + d_before)
            put("H", 1, after, -2, get("H", 1, after, -2) + d_after)
            put("E", 0, before, -1, get("E", 0, before, -1) + sign * scale * d_after)
            put("E", 0, after, -1, get("E", 0, after, -1) - sign * scale * d_before)
            put("H", 0, before, -1, get("H", 0, before, -1) + 0.5 * scale * d_before)
            put("H", 0, after, -1, get("H", 0, after, -1) + 0.5 * scale * d_after)
    return changed


def by_parity(offset, body):
    parity = lax.rem(lax.axis_index("gx") + offset, 2)
    for value in (0, 1):
        pl.when(parity == value)(functools.partial(body, value))


def pack_y_kernel(plan, fwd, adj, eps, e0, h0, e1, h1, coef, z_up, z_down, sems, scratch):
    nx, ny = plan.nx, plan.ny
    own = (pl.ds(STEPS, nx), pl.ds(0, ny), slice(None))
    copies = [pltpu.make_async_copy(eps, coef.at[own], sems.at[0])]
    for run, ref in enumerate((fwd, adj)):
        for kind, array in enumerate((e0, h0)):
            for i in range(6):
                copies.append(
                    pltpu.make_async_copy(ref.at[kind * 6 + i], array.at[(run * 6 + i, *own)], sems.at[len(copies)])
                )
    for copy in copies:
        copy.start()
    copies[0].wait()
    for x in range(nx):
        coef[STEPS + x, pl.ds(0, ny), :] = (0.5 * courant) / coef[STEPS + x, pl.ds(0, ny), :]
    e0, h0, e1, h1, coef = (array.reshape((-1, array.shape[-1])) for array in (e0, h0, e1, h1, coef))
    sweeps = Sweeps(plan, [e0, e1], [h0, h1], coef, ny)
    for run in (0, 1):
        for copy in copies[1 + 12 * run : 13 + 12 * run]:
            copy.wait()
        sweeps.both(1, range(nx), range(nx - 1), runs=(run,))
    state = State([e0, e1], [h0, h1], coef)
    pack(plan, plan.y_low, state, 0, ny, z_up, fold(plan, state, 0, scratch))
    pack(plan, plan.y_high, state, 0, -ny, z_down)


def pack_x_kernel(plan, e0, h0, e1, h1, coef, x_up, x_down, scratch):
    state = State([e0, e1], [h0, h1], coef)
    pack(plan, plan.x_low, state, plan.nx, 0, x_up, fold(plan, state, 1, scratch))
    pack(plan, plan.x_high, state, -plan.nx, 0, x_down)


def pack_diagonal_kernel(plan, e0, h0, e1, h1, coef, after, diagonal):
    state = State([e0, e1], [h0, h1], coef)

    def corners(receiver):
        pack(plan, plan.far_high[receiver], state, -plan.nx * plan.far_side[receiver], -plan.ny, diagonal)

    by_parity(1, corners)


def turns_kernel(groups, table, index, tiles, turns):
    row = index[0]
    phi_x, phi_y = table[row, 0], table[row, 1]
    at_x, at_y = lax.axis_index("gx"), lax.axis_index("gy")
    none = jnp.float32(0.0)
    ax_low = jnp.where(at_x == 0, -phi_x, none)
    ax_high = jnp.where(at_x == lax.axis_size("gx") - 1, phi_x, none)
    ay_low = jnp.where(at_y == 0, -phi_y, none)
    ay_high = jnp.where(at_y == lax.axis_size("gy") - 1, phi_y, none)
    sub = lax.broadcasted_iota(jnp.int32, (SUB, turns.shape[1]), 0)
    angles = jnp.zeros(sub.shape, jnp.float32)
    for i, angle in enumerate((ax_low, ax_high, ay_low, ay_high, ax_low + ay_low, ax_low + ay_high,
                               ax_high + ay_low, ax_high + ay_high)):
        angles = jnp.where(sub == i, angle, angles)
    turns[pl.ds(0, SUB), :] = jnp.cos(angles)
    turns[pl.ds(SUB, SUB), :] = jnp.sin(angles)
    own_tile = at_x * lax.axis_size("gy") + at_y
    chosen = tiles[0] == own_tile
    for i in range(1, tiles.shape[0]):
        chosen = jnp.logical_or(chosen, tiles[i] == own_tile)
    weight = jnp.where(chosen, jnp.float32(1.0 / groups), none)
    turns[pl.ds(2 * SUB, SUB), :] = jnp.full(sub.shape, weight, jnp.float32)


def relay_kernel(plan, jobs, *refs):
    faces, outs = refs[: len(refs) - len(jobs)], refs[len(refs) - len(jobs) :]

    def corners(receiver):
        for (messages, side), out in zip(jobs, outs, strict=True):
            dx = -plan.nx * side[receiver]
            for (what, x, y), row in messages[receiver].at.items():
                ref, source = (faces[0], plan.y_low) if y < 0 else (faces[1], plan.y_high)
                out[pl.ds(row, 1), :] = ref[pl.ds(source.at[what, x + dx, y], 1), :]

    by_parity(1, corners)


def turned(real, imag, cosine, sine):
    return real * cosine - imag * sine, real * sine + imag * cosine


def unpack(plan, message, ref, which, turns, state, kinds, level, layers=None):
    axis = message.axis
    for (kind, at_level, comp, run, part), x, y, count, at in message.runs:
        if kind not in kinds or at_level != level or part == 1:
            continue
        pieces = [(x, y, count, at)]
        if layers is not None:
            pieces = [(x + i, y, 1, at + i) for i in range(count) if x + i in layers]
        for cell_x, cell_y, size, row in pieces:
            what = (kind, at_level, comp, run, 0)
            real = ref[pl.ds(row, size), :]
            if kind == "C":
                state(what)[plan.rows(what, cell_x, cell_y, axis, size), :] = real
                continue
            twin = (kind, at_level, comp, run, 1)
            imag = ref[pl.ds(message.at[twin, cell_x, cell_y], size), :]
            turn = which(y)
            cosine, sine = turns[pl.ds(turn, 1), :], turns[pl.ds(SUB + turn, 1), :]
            real, imag = turned(real, imag, cosine, sine if run == 0 else -sine)
            state(what)[plan.rows(what, cell_x, cell_y, axis, size), :] = real
            state(twin)[plan.rows(twin, cell_x, cell_y, axis, size), :] = imag
    for what, x, y, count, _ in message.zeros:
        if what[0] in kinds and what[1] == level and layers is None:
            state(what)[plan.rows(what, x, y, axis, count), :] = jnp.zeros((count, ref.shape[1]), jnp.float32)


class Sweeps:
    def __init__(self, plan, efield, hfield, coef, height, todo=None):
        self.plan, self.efield, self.hfield, self.coef, self.height = plan, efield, hfield, coef, height
        self.todo = todo

    def rows(self, run, part, comp, x, start, stop):
        return pl.ds(self.plan.row(x, 0, run, part, comp) + start, stop - start)

    def get(self, array, run, part, comp, x):
        return array[self.rows(run, part, comp, x, 0, self.height), :]

    def pieces(self, kind, step, x):
        if self.todo is None:
            return [(comp, 0, self.height) for comp in range(3)]
        found = []
        for comp, tiles in sorted(self.todo.get((kind, step, x), {}).items()):
            for tile in sorted(tiles):
                if found and found[-1][0] == comp and found[-1][2] == tile * SUB:
                    found[-1] = (comp, found[-1][1], (tile + 1) * SUB)
                else:
                    found.append((comp, tile * SUB, (tile + 1) * SUB))
        return found

    def next_z(self, value):
        lane = lax.broadcasted_iota(jnp.int32, value.shape, 1)
        return jnp.where(lane == value.shape[1] - 1, 0.0, pltpu.roll(value, value.shape[1] - 1, 1))

    def prev_z(self, value):
        lane = lax.broadcasted_iota(jnp.int32, value.shape, 1)
        return jnp.where(lane == 0, 0.0, pltpu.roll(value, 1, 1))

    def next_y(self, value):
        return pltpu.roll(value, self.height - 1, 0)

    def prev_y(self, value):
        return pltpu.roll(value, 1, 0)

    def update_h(self, step, run, part, x):
        efield, old, new = self.efield[step - 1], self.hfield[step - 1], self.hfield[step]
        ex, ey, ez = (self.get(efield, run, part, comp, x) for comp in range(3))
        for comp, start, stop in self.pieces("H", step, x):
            here = slice(start, stop)
            if comp == 0:
                curl = (self.next_y(ez) - ez)[here] - (self.next_z(ey[here]) - ey[here])
            elif comp == 1:
                ez_x = self.get(efield, run, part, 2, x + 1)
                curl = (self.next_z(ex[here]) - ex[here]) - (ez_x - ez)[here]
            else:
                ey_x = self.get(efield, run, part, 1, x + 1)
                curl = (ey_x - ey)[here] - (self.next_y(ex) - ex)[here]
            before = self.get(old, run, part, comp, x)[here]
            if step == 1:
                before = before + before
            new[self.rows(run, part, comp, x, start, stop), :] = before - curl

    def update_e(self, step, run, part, x):
        old, new, hfield = self.efield[step - 1], self.efield[step], self.hfield[step]
        hx, hy, hz = (self.get(hfield, run, part, comp, x) for comp in range(3))
        scale = self.get(self.coef, 0, 0, 0, x)
        for comp, start, stop in self.pieces("E", step, x):
            here = slice(start, stop)
            if comp == 0:
                curl = (hz - self.prev_y(hz))[here] - (hy[here] - self.prev_z(hy[here]))
            elif comp == 1:
                hz_x = self.get(hfield, run, part, 2, x - 1)
                curl = (hx[here] - self.prev_z(hx[here])) - (hz - hz_x)[here]
            else:
                hy_x = self.get(hfield, run, part, 1, x - 1)
                curl = (hy - hy_x)[here] - (hx - self.prev_y(hx))[here]
            before = self.get(old, run, part, comp, x)[here]
            new[self.rows(run, part, comp, x, start, stop), :] = before + scale[here] * curl

    def both(self, step, h_layers, e_layers, after_h=None, after_e=None, runs=(0, 1)):
        for update, layers, after in ((self.update_h, h_layers, after_h), (self.update_e, e_layers, after_e)):
            for x in layers:
                for run in runs:
                    for part in (0, 1):
                        update(step, run, part, x)
            if after is not None:
                after()


def middle_kernel(plan, e0_in, h0_in, e1_in, h1_in, coef_in, z_low, z_high, turns, *arrays):
    nx = plan.nx
    efield, hfield, coef = arrays[: STEPS + 1], arrays[STEPS + 1 : 2 * STEPS + 2], arrays[-1]
    state = State(efield, hfield, coef)

    def take(kinds, level):
        unpack(plan, plan.y_low, z_low, lambda y: 2, turns, state, kinds, level)
        unpack(plan, plan.y_high, z_high, lambda y: 3, turns, state, kinds, level)

    take("EHC", 0)
    sweeps = Sweeps(plan, efield, hfield, coef, plan.ring, plan.made)
    for step in range(1, STEPS + 1):
        after = [lambda: take("H", 1), lambda: take("E", 1)] if step == 1 else []
        sweeps.both(step, range(step - 1, nx - step), range(step, nx - step), *after)


def add_known(plan, efield, levels, transform, out):
    nx, ny = plan.nx, plan.ny
    for x in range(nx):
        for tile in range(ny // SUB):
            for comp in range(3):
                ends = []
                for run in (0, 1):
                    at = [pl.ds(((part * 3 + comp) * nx + x) * ny + tile * SUB, SUB) for part in (0, 1)]
                    real, imag = transform[run][at[0], :], transform[run][at[1], :]
                    for level in levels(x, tile, comp):
                        theta = omega_step * level
                        here = [efield[level][pl.ds(plan.row(x, tile * SUB, run, part, comp), SUB), :] for part in (0, 1)]
                        more = turned(*here, math.cos(theta), math.sin(theta))
                        real, imag = real + more[0], imag + more[1]
                    out[run][at[0], :], out[run][at[1], :] = real, imag
                    ends.append((real, imag))
                yield x, tile, ends


def known(plan, x, tile, comp):
    def ready(level):
        return level <= x < plan.nx - level or tile in plan.free.get(("E", level, x), {}).get(comp, ())

    return [level for level in range(1, STEPS + 1) if ready(level)]


def do_valleys(plan, sweeps, take):
    for step in range(1, STEPS + 1):
        low, high = step - STEPS, plan.nx - step
        h_layers = [*range(low - 1, step - 1), *range(high, plan.nx + STEPS - step)]
        e_layers = [*range(low, step), *range(high, plan.nx + STEPS - step)]
        after = [functools.partial(take, "H", 1, h_layers), functools.partial(take, "E", 1, e_layers)] if step == 1 else []
        sweeps.both(step, h_layers, e_layers, *after)


def faces_kernel(plan, *refs):
    count = 2 * STEPS + 3
    x_low, x_high, z_low, z_high, turns, spec_f, spec_a = refs[count : count + 7]
    arrays = refs[count + 7 : 2 * count + 7]
    out_f, out_a = refs[2 * count + 7 :]
    efield, hfield, coef = arrays[: STEPS + 1], arrays[STEPS + 1 : 2 * STEPS + 2], arrays[-1]
    state = State(efield, hfield, coef)

    def take(kinds, level, layers):
        unpack(plan, plan.x_low, x_low, lambda y: 0, turns, state, kinds, level)
        unpack(plan, plan.x_high, x_high, lambda y: 1, turns, state, kinds, level)
        unpack(plan, plan.y_low, z_low, lambda y: 2, turns, state, kinds, level, layers)
        unpack(plan, plan.y_high, z_high, lambda y: 3, turns, state, kinds, level, layers)

    take("EHC", 0, ())
    do_valleys(plan, Sweeps(plan, efield, hfield, coef, plan.ring, plan.free), take)
    for _ in add_known(plan, efield, functools.partial(known, plan), (spec_f, spec_a), (out_f, out_a)):
        pass


def edges_kernel(plan, groups, *refs):
    count = 2 * STEPS + 3
    x_low, x_high, far_low, far_high, mate, z_low, z_high, turns, part_f, part_a = refs[count : count + 10]
    arrays = refs[count + 10 : 2 * count + 10]
    out_f, out_a, *parts = refs[2 * count + 10 :]
    efield, hfield, coef = arrays[: STEPS + 1], arrays[STEPS + 1 : 2 * STEPS + 2], arrays[-1]
    state = State(efield, hfield, coef)

    def take(kinds, level, layers):
        if level:
            unpack(plan, plan.x_low, x_low, lambda y: 0, turns, state, kinds, level)
            unpack(plan, plan.x_high, x_high, lambda y: 1, turns, state, kinds, level)

        def corners(receiver):
            for messages, ref, side in (
                (plan.far_low, far_low, plan.far_side),
                (plan.far_high, far_high, plan.far_side),
                (plan.mate, mate, plan.mate_side),
            ):
                first = 4 if side[receiver] < 0 else 6
                unpack(plan, messages[receiver], ref, lambda y: first + (y >= 0), turns, state, kinds, level)

        by_parity(0, corners)
        unpack(plan, plan.y_low, z_low, lambda y: 2, turns, state, kinds, level, layers)
        unpack(plan, plan.y_high, z_high, lambda y: 3, turns, state, kinds, level, layers)

    take("EHC", 0, ())
    do_valleys(plan, Sweeps(plan, efield, hfield, coef, plan.ring, plan.rest), take)

    share = plan.depth // groups
    shift = lax.rem(groups - lax.axis_index("angle"), groups) * share
    weight = turns[pl.ds(2 * SUB, SUB), :]

    def rest(x, tile, comp):
        return [level for level in range(1, STEPS + 1) if level not in known(plan, x, tile, comp)]

    totals = {}
    for x, tile, ends in add_known(plan, efield, rest, (part_f, part_a), (out_f, out_a)):
        term = ends[0][0] * ends[1][0] - ends[0][1] * ends[1][1]
        totals[x, tile] = totals[x, tile] + term if (x, tile) in totals else term
    block = lax.broadcasted_iota(jnp.int32, weight.shape, 1) // share
    tiles = [pltpu.roll(total * weight, shift, 1) for total in totals.values()]
    for k, part in enumerate(parts):
        for i in range(len(tiles) // groups):
            packed = jnp.zeros(weight.shape, jnp.float32)
            for t in range(groups):
                lanes = (t - k) % groups * share
                value = tiles[i * groups + t]
                packed = jnp.where(block == t, pltpu.roll(value, lanes, 1) if lanes else value, packed)
            part[pl.ds(i * SUB, SUB), :] = packed


def sum_kernel(groups, *refs):
    *parts, out = refs
    share = out.shape[1]
    for i in range(parts[0].shape[0] // SUB):
        total = parts[0][pl.ds(i * SUB, SUB), :]
        for part in parts[1:]:
            total = total + part[pl.ds(i * SUB, SUB), :]
        for t in range(groups):
            out[pl.ds((i * groups + t) * SUB, SUB), :] = total[:, t * share : (t + 1) * share]


def write_kernel(tr_f, tr_a, out_f, out_a, sems):
    copies = []
    for source, target in ((tr_f, out_f), (tr_a, out_a)):
        for i in range(source.shape[0]):
            copies.append(pltpu.make_async_copy(source.at[i], target.at[i], sems.at[len(copies)]))
    for copy in copies:
        copy.start()
    for copy in copies:
        copy.wait()


def ring_pairs(axis, offset):
    size = lax.axis_size(axis)
    return [(i, (i + offset) % size) for i in range(size)]


def mate_pairs():
    return [(i, i ^ 1) for i in range(lax.axis_size("gx"))]


def far_pairs():
    size = lax.axis_size("gx")
    return [(i, (i + (1 if i % 2 else -1)) % size) for i in range(size)]


def diagonal_pairs():
    size = lax.axis_size("gy")
    return [(x * size + y, far * size + (y - 1) % size) for x, far in far_pairs() for y in range(size)]


def shards(
    forward_fields,
    adjoint_fields,
    forward_spectrum,
    adjoint_spectrum,
    permittivity,
    phase_table,
    angle_index,
    design_tiles,
):
    nx, ny, depth = permittivity.shape
    plan = Plan(nx, ny, depth)
    groups = lax.axis_size("angle")
    wide, ring = plan.wide, plan.ring

    def array(*shape):
        return jax.ShapeDtypeStruct(shape, jnp.float32)

    def lines(count):
        return array(count, depth)

    def params(mib):
        return pltpu.CompilerParams(vmem_limit_bytes=mib * 2**20)

    def cost(size):
        return pl.CostEstimate(flops=size, bytes_accessed=size, transcendentals=0)

    assert lax.axis_size("gx") % 2 == 0 and nx * ny % (groups * SUB) == 0
    with jax.named_scope("pack_y"):
        *first, coef, z_up, z_down = pl.pallas_call(
            functools.partial(pack_y_kernel, plan),
            out_shape=(
                *[array(12, wide, ring, depth)] * 4,
                array(wide, ring, depth),
                lines(plan.y_low.lines),
                lines(plan.y_high.lines),
            ),
            in_specs=[HBM] * 3,
            out_specs=[VMEM] * 7,
            scratch_shapes=[pltpu.SemaphoreType.DMA((25,)), pltpu.VMEM((24 * nx, depth), jnp.float32)],
            compiler_params=params(8),
        )(*(pltpu.with_memory_space_constraint(array, pltpu.HBM) for array in (forward_fields[0], adjoint_fields[0], permittivity)))
    e0, h0, e1, h1, coef = (state.reshape((-1, depth)) for state in (*first, coef))
    with jax.named_scope("send_y"):
        z_low = lax.ppermute(z_up, "gy", ring_pairs("gy", 1))
        z_high = lax.ppermute(z_down, "gy", ring_pairs("gy", -1))
    with jax.named_scope("pack_x"):
        x_up, x_down = pl.pallas_call(
            functools.partial(pack_x_kernel, plan),
            out_shape=[lines(plan.x_low.lines), lines(plan.x_high.lines)],
            in_specs=[VMEM] * 5,
            out_specs=[VMEM] * 2,
            scratch_shapes=[pltpu.VMEM((24 * ny, depth), jnp.float32)],
            compiler_params=params(8),
            cost_estimate=cost(40 * 2**20),
        )(e0, h0, e1, h1, coef)
    with jax.named_scope("send_x"):
        x_low = lax.ppermute(x_up, "gx", ring_pairs("gx", 1))
        x_high = lax.ppermute(x_down, "gx", ring_pairs("gx", -1))
    with jax.named_scope("turns"):
        turns = pl.pallas_call(
            functools.partial(turns_kernel, groups),
            out_shape=lines(3 * SUB),
            in_specs=[SMEM] * 3,
            out_specs=VMEM,
            compiler_params=params(4),
        )(phase_table, angle_index, design_tiles)
    with jax.named_scope("diagonal_corners"):
        to_diagonal = pl.pallas_call(
            functools.partial(pack_diagonal_kernel, plan),
            out_shape=lines(max(message.lines for message in plan.far_high)),
            in_specs=[VMEM] * 6,
            out_specs=VMEM,
            compiler_params=params(4),
        )(e0, h0, e1, h1, coef, x_up)
        far_high = lax.ppermute(to_diagonal, ("gx", "gy"), diagonal_pairs())

    def relay(jobs, *faces):
        return pl.pallas_call(
            functools.partial(relay_kernel, plan, jobs),
            out_shape=[lines(max(message.lines for message in messages)) for messages, _ in jobs],
            in_specs=[VMEM] * len(faces),
            out_specs=[VMEM] * len(jobs),
            compiler_params=params(4),
            cost_estimate=cost(2**10),
        )(*faces)

    with jax.named_scope("relay_low_corners"):
        (to_far,) = relay([(plan.far_low, plan.far_side)], z_low)
        far_low = lax.ppermute(to_far, "gx", far_pairs())
    with jax.named_scope("relay_corners"):
        (to_mate,) = relay([(plan.mate, plan.mate_side)], z_low, z_high)
        mate = lax.ppermute(to_mate, "gx", mate_pairs())
    level = lines(12 * wide * ring)
    count = 2 * STEPS + 3
    levels = [level] * (count - 1) + [lines(wide * ring)]
    with jax.named_scope("middle"):
        state = pl.pallas_call(
            functools.partial(middle_kernel, plan),
            out_shape=levels,
            in_specs=[VMEM] * 8,
            out_specs=[VMEM] * count,
            input_output_aliases={0: 0, 1: STEPS + 1, 2: 1, 3: STEPS + 2, 4: count - 1},
            compiler_params=params(8),
            cost_estimate=cost(3 * 2**29),
        )(e0, h0, e1, h1, coef, z_low, z_high, turns)
    transforms = [lines(6 * nx * ny)] * 2
    with jax.named_scope("faces"):
        spectra = [spectrum.reshape((-1, depth)) for spectrum in (forward_spectrum, adjoint_spectrum)]
        results = pl.pallas_call(
            functools.partial(faces_kernel, plan),
            out_shape=[*levels, *transforms],
            in_specs=[VMEM] * (count + 7),
            out_specs=[VMEM] * (count + 2),
            input_output_aliases={i: i for i in range(count)},
            compiler_params=params(8),
        )(*state, x_low, x_high, z_low, z_high, turns, *spectra)
        state, sums = results[:count], results[count:]
    with jax.named_scope("edges"):
        results = pl.pallas_call(
            functools.partial(edges_kernel, plan, groups),
            out_shape=[*levels, *transforms, *[lines(nx * ny // groups)] * groups],
            in_specs=[VMEM] * (count + 10),
            out_specs=[VMEM] * (count + 2 + groups),
            input_output_aliases={i: i for i in range(count)} | {count + 8: count, count + 9: count + 1},
            compiler_params=params(8),
        )(*state, x_low, x_high, far_low, far_high, mate, z_low, z_high, turns, *sums)
        tr_f, tr_a, own, *others = results[count:]
    with jax.named_scope("sum_angles"):
        others = [lax.ppermute(part, "angle", ring_pairs("angle", k + 1)) for k, part in enumerate(others)]
        gradient = pl.pallas_call(
            functools.partial(sum_kernel, groups),
            out_shape=array(nx * ny, depth // groups),
            in_specs=[VMEM] * groups,
            out_specs=VMEM,
            compiler_params=params(4),
        )(own, *others)
    with jax.named_scope("write"):
        out_f, out_a = pl.pallas_call(
            write_kernel,
            out_shape=[array(6, nx, ny, depth)] * 2,
            in_specs=[VMEM] * 2,
            out_specs=[HBM] * 2,
            scratch_shapes=[pltpu.SemaphoreType.DMA((12,))],
            compiler_params=params(4),
        )(tr_f.reshape((6, nx, ny, depth)), tr_a.reshape((6, nx, ny, depth)))
    return (
        out_f.reshape(forward_spectrum.shape),
        out_a.reshape(adjoint_spectrum.shape),
        gradient.reshape((nx, ny, depth // groups)),
    )


def solution(mesh):
    in_specs = (
        P("angle", None, "gx", "gy", None),
        P("angle", None, "gx", "gy", None),
        P("angle", None, "gx", "gy", None),
        P("angle", None, "gx", "gy", None),
        P("gx", "gy", None),
        P(),
        P("angle"),
        P(),
    )
    out_specs = (
        P("angle", None, "gx", "gy", None),
        P("angle", None, "gx", "gy", None),
        P("gx", "gy", "angle"),
    )
    return jax.shard_map(shards, mesh=mesh, in_specs=in_specs, out_specs=out_specs, check_vma=False)
```

```python
import functools
import math

import jax
import jax.numpy as jnp
from jax import lax
from jax.experimental import pallas as pl
from jax.experimental.pallas import tpu as pltpu
from jax.sharding import PartitionSpec as P

STEPS = 3
SUB = 8

courant = 0.5
omega_step = 0.7

VMEM = pl.BlockSpec(memory_space=pltpu.VMEM)
SMEM = pl.BlockSpec(memory_space=pltpu.SMEM)
HBM = pl.BlockSpec(memory_space=pltpu.HBM)


def reads(node):
    kind, level, comp, x, y = node
    others = [c for c in range(3) if c != comp]
    if kind == "E":
        found = [("E", level - 1, comp, x, y), ("C", 0, 0, x, y)] + [("H", level, c, x, y) for c in others]
        if comp != 1:
            found.append(("H", level, 2 - comp, x, y - 1))
        if comp != 0:
            found.append(("H", level, 3 - comp, x - 1, y))
        return found
    found = [("H", level - 1, comp, x, y)] + [("E", level - 1, c, x, y) for c in others]
    if comp != 1:
        found.append(("E", level - 1, 2 - comp, x, y + 1))
    if comp != 0:
        found.append(("E", level - 1, 3 - comp, x + 1, y))
    return found


def wanted(nx, ny):
    def block(node):
        return node[3] // nx, node[4] // ny

    @functools.cache
    def alone(node):
        if node[1] == 0:
            return True
        return node[1] == 1 and all(block(other) == block(node) and alone(other) for other in reads(node))

    found, made, seen = set(), set(), set()
    todo = [("E", STEPS, comp, x, y) for comp in range(3) for x in range(nx) for y in range(ny)]
    while todo:
        node = todo.pop()
        if node in seen:
            continue
        seen.add(node)
        if block(node) != (0, 0) and alone(node):
            found.add(node)
        elif node[1]:
            made.add(node)
            todo += reads(node)
    return found, made


class Message:
    def __init__(self, nodes, axis, folded=()):
        self.axis, self.runs, self.at, self.size = axis, [], {}, 0
        assert nodes.issuperset(folded)
        self.zeros = Message(set(folded), axis).runs if folded else []
        nodes = nodes - set(folded)
        stretches = []
        for node in sorted(nodes):
            before = list(node)
            before[3 + axis] -= 1
            if tuple(before) in nodes:
                continue
            count = 1
            while (*node[:3], node[3] + count * (axis == 0), node[4] + count * (axis == 1)) in nodes:
                count += 1
            stretches.append((count, node))
        for count, (kind, level, comp, x, y) in sorted(stretches, key=lambda item: (-item[0], item[1])):
            for run in (0, 1) if kind != "C" else (0,):
                for part in (0, 1) if kind != "C" else (0,):
                    what = (kind, level, comp, run, part)
                    self.runs.append((what, x, y, count, self.size))
                    for i in range(count):
                        self.at[what, x + i * (axis == 0), y + i * (axis == 1)] = self.size + i
                    self.size += count
        self.lines = -(-self.size // SUB) * SUB


class Plan:
    def __init__(self, nx, ny, depth):
        self.depth = depth
        self.nx, self.ny = nx, ny
        self.wide, self.ring = nx + 2 * STEPS, ny + SUB
        nodes, made = wanted(nx, ny)
        self.made, self.free, self.rest = {}, {}, {}
        tiles, ready = {}, set()
        for node in made:
            tiles.setdefault((node[1], "HE".index(node[0]), *node[2:4], node[4] % self.ring // SUB), []).append(node)

        def early(node):
            if node in made:
                return node in ready
            return node not in nodes or 0 <= node[3] < nx or 0 <= node[4] < ny

        for (level, order, comp, x, tile), members in sorted(tiles.items()):
            key = ("HE"[order], level, x)
            middle = level - 1 + order <= x < nx - level
            free = middle or all(early(other) for node in members for other in reads(node))
            if free:
                ready.update(members)
            for into in (self.made, self.free if free else self.rest):
                into.setdefault(key, {}).setdefault(comp, set()).add(tile)
        self.late = {
            key: {comp: {tile for tile in found if (tile + 1) * SUB + STEPS > ny} for comp, found in comps.items()}
            for key, comps in self.made.items()
        }
        sides = {}
        for node in nodes:
            sides.setdefault((node[3] // nx, node[4] // ny), set()).add(node)

        def shifted(found, dx):
            return {(*node[:3], node[3] + dx, node[4]) for node in found}

        y_low, y_high = (sides[0, side] | shifted(sides[-1, side], nx) | shifted(sides[1, side], -nx) for side in (-1, 1))
        self.x_folds = (1, ny - 2), (2, ny - 2)
        self.y_folds = (2, nx - 2), (3, nx - 2)
        x_folded = [("E", 1, comp, -2, y) for comp in range(3) for y in range(*self.x_folds[comp == 0])]
        y_folded = [("E", 1, comp, x, -2) for comp in range(3) for x in range(*self.y_folds[comp == 1])]
        self.y_low, self.y_high = Message(y_low, 0, y_folded), Message(y_high, 0)
        self.x_low, self.x_high = Message(sides[-1, 0], 1, x_folded), Message(sides[1, 0], 1)
        self.mate_side, self.far_side = (1, -1), (-1, 1)
        self.mate = [Message(sides[side, -1] | sides[side, 1], 1) for side in self.mate_side]
        self.far_low, self.far_high = ([Message(sides[side, end], 1) for side in self.far_side] for end in (-1, 1))

    def row(self, x, y, run=0, part=0, comp=0):
        return ((run * 6 + part * 3 + comp) * self.wide + x + STEPS) * self.ring + y % self.ring

    def rows(self, what, x, y, axis, count):
        _, _, comp, run, part = what
        start = self.row(x, y, run, part, comp)
        return pl.ds(start, count, stride=self.ring) if axis == 0 and count > 1 else pl.ds(start, count)


class State:
    def __init__(self, efield, hfield, coef):
        self.by_kind = {"E": efield, "H": hfield, "C": [coef]}

    def __call__(self, what):
        return self.by_kind[what[0]][what[1]]


def pack(plan, message, state, dx, dy, out, changed=None):
    for what, x, y, count, at in message.runs:
        layer, first = (y, x) if message.axis == 0 else (x, y)
        if changed and (what, layer) in changed:
            ref, row = changed[what, layer]
            value = ref[pl.ds(row + first, count), :]
        else:
            value = state(what)[plan.rows(what, x + dx, y + dy, message.axis, count), :]
        out[pl.ds(at, count), :] = value


def fold(plan, state, axis, scratch):
    nx, ny = plan.nx, plan.ny
    size, normal = (nx, 1) if axis == 0 else (ny, 0)
    before, after = ((0, 2) if axis == 0 else (1, 2))
    cell = lax.broadcasted_iota(jnp.int32, (size, scratch.shape[1]), 0)
    lane = lax.broadcasted_iota(jnp.int32, cell.shape, 1)
    folds = plan.y_folds if axis == 0 else plan.x_folds
    changed = {}

    def lines(what, layer):
        place = (0, ny + layer) if axis == 0 else (nx + layer, 0)
        return state(what)[plan.rows(what, *place, axis, size), :]

    def inside(value, fold):
        return jnp.where((cell >= fold[0]) & (cell < fold[1]), value, 0.0)

    for run in (0, 1):
        for part in (0, 1):

            def get(kind, level, comp, layer):
                return lines((kind, level, comp, run, part), layer)

            def put(kind, level, comp, layer, value):
                row = len(changed) * size
                scratch[pl.ds(row, size), :] = value
                changed[(kind, level, comp, run, part), layer] = scratch, row

            low, high = (inside(get("E", 1, comp, -2), folds[0]) for comp in (before, after))
            along = inside(get("E", 1, normal, -2), folds[1])
            along_z = jnp.where(lane == lane.shape[1] - 1, 0.0, pltpu.roll(along, lane.shape[1] - 1, 1)) - along
            along_next = pltpu.roll(along, size - 1, 0) - along
            sign = 1.0 if axis == 0 else -1.0
            d_before = sign * (high + along_z)
            d_after = -sign * (low + along_next)
            scale = lines(("C", 0, 0, 0, 0), -1)
            put("H", 1, before, -2, get("H", 1, before, -2) + d_before)
            put("H", 1, after, -2, get("H", 1, after, -2) + d_after)
            put("E", 0, before, -1, get("E", 0, before, -1) + sign * scale * d_after)
            put("E", 0, after, -1, get("E", 0, after, -1) - sign * scale * d_before)
            put("H", 0, before, -1, get("H", 0, before, -1) + 0.5 * scale * d_before)
            put("H", 0, after, -1, get("H", 0, after, -1) + 0.5 * scale * d_after)
    return changed


def by_parity(offset, body):
    parity = lax.rem(lax.axis_index("gx") + offset, 2)
    for value in (0, 1):
        pl.when(parity == value)(functools.partial(body, value))


def pack_y_kernel(plan, fwd, adj, eps, e0, h0, e1, h1, coef, z_up, z_down, sems, scratch):
    nx, ny = plan.nx, plan.ny
    own = (pl.ds(STEPS, nx), pl.ds(0, ny), slice(None))
    copies = [pltpu.make_async_copy(eps, coef.at[own], sems.at[0])]
    for run, ref in enumerate((fwd, adj)):
        for kind, array in enumerate((e0, h0)):
            for i in range(6):
                copies.append(
                    pltpu.make_async_copy(ref.at[kind * 6 + i], array.at[(run * 6 + i, *own)], sems.at[len(copies)])
                )
    for copy in copies:
        copy.start()
    copies[0].wait()
    for x in range(nx):
        coef[STEPS + x, pl.ds(0, ny), :] = (0.5 * courant) / coef[STEPS + x, pl.ds(0, ny), :]
    e0, h0, e1, h1, coef = (array.reshape((-1, array.shape[-1])) for array in (e0, h0, e1, h1, coef))
    sweeps = Sweeps(plan, [e0, e1], [h0, h1], coef, ny)
    for run in (0, 1):
        for copy in copies[1 + 12 * run : 13 + 12 * run]:
            copy.wait()
        sweeps.both(1, range(nx), range(nx - 1), runs=(run,))
    state = State([e0, e1], [h0, h1], coef)
    pack(plan, plan.y_low, state, 0, ny, z_up, fold(plan, state, 0, scratch))
    pack(plan, plan.y_high, state, 0, -ny, z_down)


def pack_x_kernel(plan, e0, h0, e1, h1, coef, x_up, x_down, scratch):
    state = State([e0, e1], [h0, h1], coef)
    pack(plan, plan.x_low, state, plan.nx, 0, x_up, fold(plan, state, 1, scratch))
    pack(plan, plan.x_high, state, -plan.nx, 0, x_down)


def pack_diagonal_kernel(plan, e0, h0, e1, h1, coef, after, diagonal):
    state = State([e0, e1], [h0, h1], coef)

    def corners(receiver):
        pack(plan, plan.far_high[receiver], state, -plan.nx * plan.far_side[receiver], -plan.ny, diagonal)

    by_parity(1, corners)


def turns_kernel(groups, table, index, tiles, turns):
    row = index[0]
    phi_x, phi_y = table[row, 0], table[row, 1]
    at_x, at_y = lax.axis_index("gx"), lax.axis_index("gy")
    none = jnp.float32(0.0)
    ax_low = jnp.where(at_x == 0, -phi_x, none)
    ax_high = jnp.where(at_x == lax.axis_size("gx") - 1, phi_x, none)
    ay_low = jnp.where(at_y == 0, -phi_y, none)
    ay_high = jnp.where(at_y == lax.axis_size("gy") - 1, phi_y, none)
    sub = lax.broadcasted_iota(jnp.int32, (SUB, turns.shape[1]), 0)
    angles = jnp.zeros(sub.shape, jnp.float32)
    for i, angle in enumerate((ax_low, ax_high, ay_low, ay_high, ax_low + ay_low, ax_low + ay_high,
                               ax_high + ay_low, ax_high + ay_high)):
        angles = jnp.where(sub == i, angle, angles)
    turns[pl.ds(0, SUB), :] = jnp.cos(angles)
    turns[pl.ds(SUB, SUB), :] = jnp.sin(angles)
    own_tile = at_x * lax.axis_size("gy") + at_y
    chosen = tiles[0] == own_tile
    for i in range(1, tiles.shape[0]):
        chosen = jnp.logical_or(chosen, tiles[i] == own_tile)
    weight = jnp.where(chosen, jnp.float32(1.0 / groups), none)
    turns[pl.ds(2 * SUB, SUB), :] = jnp.full(sub.shape, weight, jnp.float32)


def relay_kernel(plan, jobs, *refs):
    faces, outs = refs[: len(refs) - len(jobs)], refs[len(refs) - len(jobs) :]

    def corners(receiver):
        for (messages, side), out in zip(jobs, outs, strict=True):
            dx = -plan.nx * side[receiver]
            for (what, x, y), row in messages[receiver].at.items():
                ref, source = (faces[0], plan.y_low) if y < 0 else (faces[1], plan.y_high)
                out[pl.ds(row, 1), :] = ref[pl.ds(source.at[what, x + dx, y], 1), :]

    by_parity(1, corners)


def turned(real, imag, cosine, sine):
    return real * cosine - imag * sine, real * sine + imag * cosine


def unpack(plan, message, ref, which, turns, state, kinds, level, layers=None):
    axis = message.axis
    for (kind, at_level, comp, run, part), x, y, count, at in message.runs:
        if kind not in kinds or at_level != level or part == 1:
            continue
        pieces = [(x, y, count, at)]
        if layers is not None:
            pieces = [(x + i, y, 1, at + i) for i in range(count) if x + i in layers]
        for cell_x, cell_y, size, row in pieces:
            what = (kind, at_level, comp, run, 0)
            real = ref[pl.ds(row, size), :]
            if kind == "C":
                state(what)[plan.rows(what, cell_x, cell_y, axis, size), :] = real
                continue
            twin = (kind, at_level, comp, run, 1)
            imag = ref[pl.ds(message.at[twin, cell_x, cell_y], size), :]
            turn = which(y)
            cosine, sine = turns[pl.ds(turn, 1), :], turns[pl.ds(SUB + turn, 1), :]
            real, imag = turned(real, imag, cosine, sine if run == 0 else -sine)
            state(what)[plan.rows(what, cell_x, cell_y, axis, size), :] = real
            state(twin)[plan.rows(twin, cell_x, cell_y, axis, size), :] = imag
    for what, x, y, count, _ in message.zeros:
        if what[0] in kinds and what[1] == level and layers is None:
            state(what)[plan.rows(what, x, y, axis, count), :] = jnp.zeros((count, ref.shape[1]), jnp.float32)


class Sweeps:
    def __init__(self, plan, efield, hfield, coef, height, todo=None):
        self.plan, self.efield, self.hfield, self.coef, self.height = plan, efield, hfield, coef, height
        self.todo = todo

    def rows(self, run, part, comp, x, start, stop):
        return pl.ds(self.plan.row(x, 0, run, part, comp) + start, stop - start)

    def get(self, array, run, part, comp, x):
        return array[self.rows(run, part, comp, x, 0, self.height), :]

    def pieces(self, kind, step, x):
        if self.todo is None:
            return [(comp, 0, self.height) for comp in range(3)]
        found = []
        for comp, tiles in sorted(self.todo.get((kind, step, x), {}).items()):
            for tile in sorted(tiles):
                if found and found[-1][0] == comp and found[-1][2] == tile * SUB:
                    found[-1] = (comp, found[-1][1], (tile + 1) * SUB)
                else:
                    found.append((comp, tile * SUB, (tile + 1) * SUB))
        return found

    def next_z(self, value):
        lane = lax.broadcasted_iota(jnp.int32, value.shape, 1)
        return jnp.where(lane == value.shape[1] - 1, 0.0, pltpu.roll(value, value.shape[1] - 1, 1))

    def prev_z(self, value):
        lane = lax.broadcasted_iota(jnp.int32, value.shape, 1)
        return jnp.where(lane == 0, 0.0, pltpu.roll(value, 1, 1))

    def next_y(self, value):
        return pltpu.roll(value, self.height - 1, 0)

    def prev_y(self, value):
        return pltpu.roll(value, 1, 0)

    def update_h(self, step, run, part, x):
        efield, old, new = self.efield[step - 1], self.hfield[step - 1], self.hfield[step]
        ex, ey, ez = (self.get(efield, run, part, comp, x) for comp in range(3))
        for comp, start, stop in self.pieces("H", step, x):
            here = slice(start, stop)
            if comp == 0:
                curl = (self.next_y(ez) - ez)[here] - (self.next_z(ey[here]) - ey[here])
            elif comp == 1:
                ez_x = self.get(efield, run, part, 2, x + 1)
                curl = (self.next_z(ex[here]) - ex[here]) - (ez_x - ez)[here]
            else:
                ey_x = self.get(efield, run, part, 1, x + 1)
                curl = (ey_x - ey)[here] - (self.next_y(ex) - ex)[here]
            before = self.get(old, run, part, comp, x)[here]
            if step == 1:
                before = before + before
            new[self.rows(run, part, comp, x, start, stop), :] = before - curl

    def update_e(self, step, run, part, x):
        old, new, hfield = self.efield[step - 1], self.efield[step], self.hfield[step]
        hx, hy, hz = (self.get(hfield, run, part, comp, x) for comp in range(3))
        scale = self.get(self.coef, 0, 0, 0, x)
        for comp, start, stop in self.pieces("E", step, x):
            here = slice(start, stop)
            if comp == 0:
                curl = (hz - self.prev_y(hz))[here] - (hy[here] - self.prev_z(hy[here]))
            elif comp == 1:
                hz_x = self.get(hfield, run, part, 2, x - 1)
                curl = (hx[here] - self.prev_z(hx[here])) - (hz - hz_x)[here]
            else:
                hy_x = self.get(hfield, run, part, 1, x - 1)
                curl = (hy - hy_x)[here] - (hx - self.prev_y(hx))[here]
            before = self.get(old, run, part, comp, x)[here]
            new[self.rows(run, part, comp, x, start, stop), :] = before + scale[here] * curl

    def both(self, step, h_layers, e_layers, after_h=None, after_e=None, runs=(0, 1)):
        for update, layers, after in ((self.update_h, h_layers, after_h), (self.update_e, e_layers, after_e)):
            for x in layers:
                for run in runs:
                    for part in (0, 1):
                        update(step, run, part, x)
            if after is not None:
                after()


def do_middle(plan, arrays, todo, take):
    nx = plan.nx
    sweeps = Sweeps(plan, arrays[: STEPS + 1], arrays[STEPS + 1 : 2 * STEPS + 2], arrays[-1], plan.ring, todo)
    for step in range(1, STEPS + 1):
        after = [functools.partial(take, "H", 1), functools.partial(take, "E", 1)] if step == 1 else []
        sweeps.both(step, range(step - 1, nx - step), range(step, nx - step), *after)


def early_kernel(plan, e0_in, h0_in, e1_in, h1_in, coef_in, z_low, turns, *arrays):
    state = State(arrays[: STEPS + 1], arrays[STEPS + 1 : 2 * STEPS + 2], arrays[-1])

    def take(kinds, level):
        unpack(plan, plan.y_low, z_low, lambda y: 2, turns, state, kinds, level)

    take("EHC", 0)
    do_middle(plan, arrays, plan.made, take)


def middle_kernel(plan, *refs):
    count = 2 * STEPS + 3
    z_low, z_high, turns = refs[count : count + 3]
    arrays = refs[count + 3 :]
    state = State(arrays[: STEPS + 1], arrays[STEPS + 1 : 2 * STEPS + 2], arrays[-1])

    def take(kinds, level):
        if level:
            unpack(plan, plan.y_low, z_low, lambda y: 2, turns, state, kinds, level)
        unpack(plan, plan.y_high, z_high, lambda y: 3, turns, state, kinds, level)

    take("EHC", 0)
    do_middle(plan, arrays, plan.late, take)


def add_known(plan, efield, levels, transform, out):
    nx, ny = plan.nx, plan.ny
    for x in range(nx):
        for tile in range(ny // SUB):
            for comp in range(3):
                ends = []
                for run in (0, 1):
                    at = [pl.ds(((part * 3 + comp) * nx + x) * ny + tile * SUB, SUB) for part in (0, 1)]
                    real, imag = transform[run][at[0], :], transform[run][at[1], :]
                    for level in levels(x, tile, comp):
                        theta = omega_step * level
                        here = [efield[level][pl.ds(plan.row(x, tile * SUB, run, part, comp), SUB), :] for part in (0, 1)]
                        more = turned(*here, math.cos(theta), math.sin(theta))
                        real, imag = real + more[0], imag + more[1]
                    out[run][at[0], :], out[run][at[1], :] = real, imag
                    ends.append((real, imag))
                yield x, tile, ends


def known(plan, x, tile, comp):
    def ready(level):
        return level <= x < plan.nx - level or tile in plan.free.get(("E", level, x), {}).get(comp, ())

    return [level for level in range(1, STEPS + 1) if ready(level)]


def do_valleys(plan, sweeps, take):
    for step in range(1, STEPS + 1):
        low, high = step - STEPS, plan.nx - step
        h_layers = [*range(low - 1, step - 1), *range(high, plan.nx + STEPS - step)]
        e_layers = [*range(low, step), *range(high, plan.nx + STEPS - step)]
        after = [functools.partial(take, "H", 1, h_layers), functools.partial(take, "E", 1, e_layers)] if step == 1 else []
        sweeps.both(step, h_layers, e_layers, *after)


def faces_kernel(plan, *refs):
    count = 2 * STEPS + 3
    x_low, x_high, z_low, z_high, turns, spec_f, spec_a = refs[count : count + 7]
    arrays = refs[count + 7 : 2 * count + 7]
    out_f, out_a = refs[2 * count + 7 :]
    efield, hfield, coef = arrays[: STEPS + 1], arrays[STEPS + 1 : 2 * STEPS + 2], arrays[-1]
    state = State(efield, hfield, coef)

    def take(kinds, level, layers):
        unpack(plan, plan.x_low, x_low, lambda y: 0, turns, state, kinds, level)
        unpack(plan, plan.x_high, x_high, lambda y: 1, turns, state, kinds, level)
        unpack(plan, plan.y_low, z_low, lambda y: 2, turns, state, kinds, level, layers)
        unpack(plan, plan.y_high, z_high, lambda y: 3, turns, state, kinds, level, layers)

    take("EHC", 0, ())
    do_valleys(plan, Sweeps(plan, efield, hfield, coef, plan.ring, plan.free), take)
    for _ in add_known(plan, efield, functools.partial(known, plan), (spec_f, spec_a), (out_f, out_a)):
        pass


def edges_kernel(plan, groups, *refs):
    count = 2 * STEPS + 3
    x_low, x_high, far_low, far_high, mate, z_low, z_high, turns, part_f, part_a = refs[count : count + 10]
    arrays = refs[count + 10 : 2 * count + 10]
    out_f, out_a, *parts = refs[2 * count + 10 :]
    efield, hfield, coef = arrays[: STEPS + 1], arrays[STEPS + 1 : 2 * STEPS + 2], arrays[-1]
    state = State(efield, hfield, coef)

    def take(kinds, level, layers):
        if level:
            unpack(plan, plan.x_low, x_low, lambda y: 0, turns, state, kinds, level)
            unpack(plan, plan.x_high, x_high, lambda y: 1, turns, state, kinds, level)

        def corners(receiver):
            for messages, ref, side in (
                (plan.far_low, far_low, plan.far_side),
                (plan.far_high, far_high, plan.far_side),
                (plan.mate, mate, plan.mate_side),
            ):
                first = 4 if side[receiver] < 0 else 6
                unpack(plan, messages[receiver], ref, lambda y: first + (y >= 0), turns, state, kinds, level)

        by_parity(0, corners)
        unpack(plan, plan.y_low, z_low, lambda y: 2, turns, state, kinds, level, layers)
        unpack(plan, plan.y_high, z_high, lambda y: 3, turns, state, kinds, level, layers)

    take("EHC", 0, ())
    do_valleys(plan, Sweeps(plan, efield, hfield, coef, plan.ring, plan.rest), take)

    share = plan.depth // groups
    shift = lax.rem(groups - lax.axis_index("angle"), groups) * share
    weight = turns[pl.ds(2 * SUB, SUB), :]

    def rest(x, tile, comp):
        return [level for level in range(1, STEPS + 1) if level not in known(plan, x, tile, comp)]

    totals = {}
    for x, tile, ends in add_known(plan, efield, rest, (part_f, part_a), (out_f, out_a)):
        term = ends[0][0] * ends[1][0] - ends[0][1] * ends[1][1]
        totals[x, tile] = totals[x, tile] + term if (x, tile) in totals else term
    block = lax.broadcasted_iota(jnp.int32, weight.shape, 1) // share
    tiles = [pltpu.roll(total * weight, shift, 1) for total in totals.values()]
    for k, part in enumerate(parts):
        for i in range(len(tiles) // groups):
            packed = jnp.zeros(weight.shape, jnp.float32)
            for t in range(groups):
                lanes = (t - k) % groups * share
                value = tiles[i * groups + t]
                packed = jnp.where(block == t, pltpu.roll(value, lanes, 1) if lanes else value, packed)
            part[pl.ds(i * SUB, SUB), :] = packed


def sum_kernel(groups, *refs):
    *parts, out = refs
    share = out.shape[1]
    for i in range(parts[0].shape[0] // SUB):
        total = parts[0][pl.ds(i * SUB, SUB), :]
        for part in parts[1:]:
            total = total + part[pl.ds(i * SUB, SUB), :]
        for t in range(groups):
            out[pl.ds((i * groups + t) * SUB, SUB), :] = total[:, t * share : (t + 1) * share]


def write_kernel(tr_f, tr_a, out_f, out_a, sems):
    copies = []
    for source, target in ((tr_f, out_f), (tr_a, out_a)):
        for i in range(source.shape[0]):
            copies.append(pltpu.make_async_copy(source.at[i], target.at[i], sems.at[len(copies)]))
    for copy in copies:
        copy.start()
    for copy in copies:
        copy.wait()


def ring_pairs(axis, offset):
    size = lax.axis_size(axis)
    return [(i, (i + offset) % size) for i in range(size)]


def mate_pairs():
    return [(i, i ^ 1) for i in range(lax.axis_size("gx"))]


def far_pairs():
    size = lax.axis_size("gx")
    return [(i, (i + (1 if i % 2 else -1)) % size) for i in range(size)]


def diagonal_pairs():
    size = lax.axis_size("gy")
    return [(x * size + y, far * size + (y - 1) % size) for x, far in far_pairs() for y in range(size)]


def shards(
    forward_fields,
    adjoint_fields,
    forward_spectrum,
    adjoint_spectrum,
    permittivity,
    phase_table,
    angle_index,
    design_tiles,
):
    nx, ny, depth = permittivity.shape
    plan = Plan(nx, ny, depth)
    groups = lax.axis_size("angle")
    wide, ring = plan.wide, plan.ring

    def array(*shape):
        return jax.ShapeDtypeStruct(shape, jnp.float32)

    def lines(count):
        return array(count, depth)

    def params(mib):
        return pltpu.CompilerParams(vmem_limit_bytes=mib * 2**20)

    def cost(size):
        return pl.CostEstimate(flops=size, bytes_accessed=size, transcendentals=0)

    assert lax.axis_size("gx") % 2 == 0 and nx * ny % (groups * SUB) == 0
    with jax.named_scope("pack_y"):
        *first, coef, z_up, z_down = pl.pallas_call(
            functools.partial(pack_y_kernel, plan),
            out_shape=(
                *[array(12, wide, ring, depth)] * 4,
                array(wide, ring, depth),
                lines(plan.y_low.lines),
                lines(plan.y_high.lines),
            ),
            in_specs=[HBM] * 3,
            out_specs=[VMEM] * 7,
            scratch_shapes=[pltpu.SemaphoreType.DMA((25,)), pltpu.VMEM((24 * nx, depth), jnp.float32)],
            compiler_params=params(8),
        )(*(pltpu.with_memory_space_constraint(array, pltpu.HBM) for array in (forward_fields[0], adjoint_fields[0], permittivity)))
    e0, h0, e1, h1, coef = (state.reshape((-1, depth)) for state in (*first, coef))
    with jax.named_scope("send_y"):
        z_low = lax.ppermute(z_up, "gy", ring_pairs("gy", 1))
        z_high = lax.ppermute(z_down, "gy", ring_pairs("gy", -1))
    with jax.named_scope("pack_x"):
        x_up, x_down = pl.pallas_call(
            functools.partial(pack_x_kernel, plan),
            out_shape=[lines(plan.x_low.lines), lines(plan.x_high.lines)],
            in_specs=[VMEM] * 5,
            out_specs=[VMEM] * 2,
            scratch_shapes=[pltpu.VMEM((24 * ny, depth), jnp.float32)],
            compiler_params=params(8),
            cost_estimate=cost(40 * 2**20),
        )(e0, h0, e1, h1, coef)
    with jax.named_scope("send_x"):
        x_low = lax.ppermute(x_up, "gx", ring_pairs("gx", 1))
        x_high = lax.ppermute(x_down, "gx", ring_pairs("gx", -1))
    with jax.named_scope("turns"):
        turns = pl.pallas_call(
            functools.partial(turns_kernel, groups),
            out_shape=lines(3 * SUB),
            in_specs=[SMEM] * 3,
            out_specs=VMEM,
            compiler_params=params(4),
        )(phase_table, angle_index, design_tiles)
    with jax.named_scope("diagonal_corners"):
        to_diagonal = pl.pallas_call(
            functools.partial(pack_diagonal_kernel, plan),
            out_shape=lines(max(message.lines for message in plan.far_high)),
            in_specs=[VMEM] * 6,
            out_specs=VMEM,
            compiler_params=params(4),
        )(e0, h0, e1, h1, coef, x_up)
        far_high = lax.ppermute(to_diagonal, ("gx", "gy"), diagonal_pairs())

    def relay(jobs, *faces):
        return pl.pallas_call(
            functools.partial(relay_kernel, plan, jobs),
            out_shape=[lines(max(message.lines for message in messages)) for messages, _ in jobs],
            in_specs=[VMEM] * len(faces),
            out_specs=[VMEM] * len(jobs),
            compiler_params=params(4),
            cost_estimate=cost(2**10),
        )(*faces)

    with jax.named_scope("relay_low_corners"):
        (to_far,) = relay([(plan.far_low, plan.far_side)], z_low)
        far_low = lax.ppermute(to_far, "gx", far_pairs())
    level = lines(12 * wide * ring)
    count = 2 * STEPS + 3
    levels = [level] * (count - 1) + [lines(wide * ring)]
    with jax.named_scope("early"):
        state = pl.pallas_call(
            functools.partial(early_kernel, plan),
            out_shape=levels,
            in_specs=[VMEM] * 7,
            out_specs=[VMEM] * count,
            input_output_aliases={0: 0, 1: STEPS + 1, 2: 1, 3: STEPS + 2, 4: count - 1},
            compiler_params=params(8),
            cost_estimate=cost(2**10),
        )(e0, h0, e1, h1, coef, z_low, turns)
    with jax.named_scope("relay_corners"):
        (to_mate,) = relay([(plan.mate, plan.mate_side)], z_low, z_high, state[-1])
        mate = lax.ppermute(to_mate, "gx", mate_pairs())
    with jax.named_scope("middle"):
        state = pl.pallas_call(
            functools.partial(middle_kernel, plan),
            out_shape=levels,
            in_specs=[VMEM] * (count + 3),
            out_specs=[VMEM] * count,
            input_output_aliases={i: i for i in range(count)},
            compiler_params=params(8),
            cost_estimate=cost(3 * 2**29),
        )(*state, z_low, z_high, turns)
    transforms = [lines(6 * nx * ny)] * 2
    with jax.named_scope("faces"):
        spectra = [spectrum.reshape((-1, depth)) for spectrum in (forward_spectrum, adjoint_spectrum)]
        results = pl.pallas_call(
            functools.partial(faces_kernel, plan),
            out_shape=[*levels, *transforms],
            in_specs=[VMEM] * (count + 7),
            out_specs=[VMEM] * (count + 2),
            input_output_aliases={i: i for i in range(count)},
            compiler_params=params(8),
        )(*state, x_low, x_high, z_low, z_high, turns, *spectra)
        state, sums = results[:count], results[count:]
    with jax.named_scope("edges"):
        results = pl.pallas_call(
            functools.partial(edges_kernel, plan, groups),
            out_shape=[*levels, *transforms, *[lines(nx * ny // groups)] * groups],
            in_specs=[VMEM] * (count + 10),
            out_specs=[VMEM] * (count + 2 + groups),
            input_output_aliases={i: i for i in range(count)} | {count + 8: count, count + 9: count + 1},
            compiler_params=params(8),
        )(*state, x_low, x_high, far_low, far_high, mate, z_low, z_high, turns, *sums)
        tr_f, tr_a, own, *others = results[count:]
    with jax.named_scope("sum_angles"):
        others = [lax.ppermute(part, "angle", ring_pairs("angle", k + 1)) for k, part in enumerate(others)]
        gradient = pl.pallas_call(
            functools.partial(sum_kernel, groups),
            out_shape=array(nx * ny, depth // groups),
            in_specs=[VMEM] * groups,
            out_specs=VMEM,
            compiler_params=params(4),
        )(own, *others)
    with jax.named_scope("write"):
        out_f, out_a = pl.pallas_call(
            write_kernel,
            out_shape=[array(6, nx, ny, depth)] * 2,
            in_specs=[VMEM] * 2,
            out_specs=[HBM] * 2,
            scratch_shapes=[pltpu.SemaphoreType.DMA((12,))],
            compiler_params=params(4),
        )(tr_f.reshape((6, nx, ny, depth)), tr_a.reshape((6, nx, ny, depth)))
    return (
        out_f.reshape(forward_spectrum.shape),
        out_a.reshape(adjoint_spectrum.shape),
        gradient.reshape((nx, ny, depth // groups)),
    )


def solution(mesh):
    in_specs = (
        P("angle", None, "gx", "gy", None),
        P("angle", None, "gx", "gy", None),
        P("angle", None, "gx", "gy", None),
        P("angle", None, "gx", "gy", None),
        P("gx", "gy", None),
        P(),
        P("angle"),
        P(),
    )
    out_specs = (
        P("angle", None, "gx", "gy", None),
        P("angle", None, "gx", "gy", None),
        P("gx", "gy", "angle"),
    )
    return jax.shard_map(shards, mesh=mesh, in_specs=in_specs, out_specs=out_specs, check_vma=False)
```

```python
import functools
import math

import jax
import jax.numpy as jnp
from jax import lax
from jax.experimental import pallas as pl
from jax.experimental.pallas import tpu as pltpu
from jax.sharding import PartitionSpec as P

STEPS = 3
SUB = 8

courant = 0.5
omega_step = 0.7

VMEM = pl.BlockSpec(memory_space=pltpu.VMEM)
SMEM = pl.BlockSpec(memory_space=pltpu.SMEM)
HBM = pl.BlockSpec(memory_space=pltpu.HBM)


def reads(node):
    kind, level, comp, x, y = node
    others = [c for c in range(3) if c != comp]
    if kind == "E":
        found = [("E", level - 1, comp, x, y), ("C", 0, 0, x, y)] + [("H", level, c, x, y) for c in others]
        if comp != 1:
            found.append(("H", level, 2 - comp, x, y - 1))
        if comp != 0:
            found.append(("H", level, 3 - comp, x - 1, y))
        return found
    found = [("H", level - 1, comp, x, y)] + [("E", level - 1, c, x, y) for c in others]
    if comp != 1:
        found.append(("E", level - 1, 2 - comp, x, y + 1))
    if comp != 0:
        found.append(("E", level - 1, 3 - comp, x + 1, y))
    return found


def wanted(nx, ny):
    def block(node):
        return node[3] // nx, node[4] // ny

    @functools.cache
    def alone(node):
        if node[1] == 0:
            return True
        return node[1] == 1 and all(block(other) == block(node) and alone(other) for other in reads(node))

    found, made, seen = set(), set(), set()
    todo = [("E", STEPS, comp, x, y) for comp in range(3) for x in range(nx) for y in range(ny)]
    while todo:
        node = todo.pop()
        if node in seen:
            continue
        seen.add(node)
        if block(node) != (0, 0) and alone(node):
            found.add(node)
        elif node[1]:
            made.add(node)
            todo += reads(node)
    return found, made


class Message:
    def __init__(self, nodes, axis, folded=()):
        self.axis, self.runs, self.at, self.size = axis, [], {}, 0
        assert nodes.issuperset(folded)
        self.zeros = Message(set(folded), axis).runs if folded else []
        nodes = nodes - set(folded)
        stretches = []
        for node in sorted(nodes):
            before = list(node)
            before[3 + axis] -= 1
            if tuple(before) in nodes:
                continue
            count = 1
            while (*node[:3], node[3] + count * (axis == 0), node[4] + count * (axis == 1)) in nodes:
                count += 1
            stretches.append((count, node))
        for count, (kind, level, comp, x, y) in sorted(stretches, key=lambda item: (-item[0], item[1])):
            for run in (0, 1) if kind != "C" else (0,):
                for part in (0, 1) if kind != "C" else (0,):
                    what = (kind, level, comp, run, part)
                    self.runs.append((what, x, y, count, self.size))
                    for i in range(count):
                        self.at[what, x + i * (axis == 0), y + i * (axis == 1)] = self.size + i
                    self.size += count
        self.lines = -(-self.size // SUB) * SUB


class Plan:
    def __init__(self, nx, ny, depth):
        self.depth = depth
        self.nx, self.ny = nx, ny
        self.wide, self.ring = nx + 2 * STEPS, ny + SUB
        nodes, made = wanted(nx, ny)
        self.made = {}
        for kind, level, comp, x, y in made:
            self.made.setdefault((kind, level, x), {}).setdefault(comp, set()).add(y % self.ring // SUB)
        sides = {}
        for node in nodes:
            sides.setdefault((node[3] // nx, node[4] // ny), set()).add(node)

        def shifted(found, dx):
            return {(*node[:3], node[3] + dx, node[4]) for node in found}

        y_low, y_high = (sides[0, side] | shifted(sides[-1, side], nx) | shifted(sides[1, side], -nx) for side in (-1, 1))
        self.x_folds = (1, ny - 2), (2, ny - 2)
        self.y_folds = (2, nx - 2), (3, nx - 2)
        x_folded = [("E", 1, comp, -2, y) for comp in range(3) for y in range(*self.x_folds[comp == 0])]
        y_folded = [("E", 1, comp, x, -2) for comp in range(3) for x in range(*self.y_folds[comp == 1])]
        self.y_low, self.y_high = Message(y_low, 0, y_folded), Message(y_high, 0)
        self.x_low, self.x_high = Message(sides[-1, 0], 1, x_folded), Message(sides[1, 0], 1)
        self.mate_side, self.far_side = (1, -1), (-1, 1)
        self.mate = [Message(sides[side, -1] | sides[side, 1], 1) for side in self.mate_side]
        self.far_low, self.far_high = ([Message(sides[side, end], 1) for side in self.far_side] for end in (-1, 1))

    def row(self, x, y, run=0, part=0, comp=0):
        return ((run * 6 + part * 3 + comp) * self.wide + x + STEPS) * self.ring + y % self.ring

    def rows(self, what, x, y, axis, count):
        _, _, comp, run, part = what
        start = self.row(x, y, run, part, comp)
        return pl.ds(start, count, stride=self.ring) if axis == 0 and count > 1 else pl.ds(start, count)


class State:
    def __init__(self, efield, hfield, coef):
        self.by_kind = {"E": efield, "H": hfield, "C": [coef]}

    def __call__(self, what):
        return self.by_kind[what[0]][what[1]]


def pack(plan, message, state, dx, dy, out, changed=None):
    for what, x, y, count, at in message.runs:
        layer, first = (y, x) if message.axis == 0 else (x, y)
        if changed and (what, layer) in changed:
            ref, row = changed[what, layer]
            value = ref[pl.ds(row + first, count), :]
        else:
            value = state(what)[plan.rows(what, x + dx, y + dy, message.axis, count), :]
        out[pl.ds(at, count), :] = value


def fold(plan, state, axis, scratch):
    nx, ny = plan.nx, plan.ny
    size, normal = (nx, 1) if axis == 0 else (ny, 0)
    before, after = ((0, 2) if axis == 0 else (1, 2))
    cell = lax.broadcasted_iota(jnp.int32, (size, scratch.shape[1]), 0)
    lane = lax.broadcasted_iota(jnp.int32, cell.shape, 1)
    folds = plan.y_folds if axis == 0 else plan.x_folds
    changed = {}

    def lines(what, layer):
        place = (0, ny + layer) if axis == 0 else (nx + layer, 0)
        return state(what)[plan.rows(what, *place, axis, size), :]

    def inside(value, fold):
        return jnp.where((cell >= fold[0]) & (cell < fold[1]), value, 0.0)

    for run in (0, 1):
        for part in (0, 1):

            def get(kind, level, comp, layer):
                return lines((kind, level, comp, run, part), layer)

            def put(kind, level, comp, layer, value):
                row = len(changed) * size
                scratch[pl.ds(row, size), :] = value
                changed[(kind, level, comp, run, part), layer] = scratch, row

            low, high = (inside(get("E", 1, comp, -2), folds[0]) for comp in (before, after))
            along = inside(get("E", 1, normal, -2), folds[1])
            along_z = jnp.where(lane == lane.shape[1] - 1, 0.0, pltpu.roll(along, lane.shape[1] - 1, 1)) - along
            along_next = pltpu.roll(along, size - 1, 0) - along
            sign = 1.0 if axis == 0 else -1.0
            d_before = sign * (high + along_z)
            d_after = -sign * (low + along_next)
            scale = lines(("C", 0, 0, 0, 0), -1)
            put("H", 1, before, -2, get("H", 1, before, -2) + d_before)
            put("H", 1, after, -2, get("H", 1, after, -2) + d_after)
            put("E", 0, before, -1, get("E", 0, before, -1) + sign * scale * d_after)
            put("E", 0, after, -1, get("E", 0, after, -1) - sign * scale * d_before)
            put("H", 0, before, -1, get("H", 0, before, -1) + 0.5 * scale * d_before)
            put("H", 0, after, -1, get("H", 0, after, -1) + 0.5 * scale * d_after)
    return changed


def by_parity(offset, body):
    parity = lax.rem(lax.axis_index("gx") + offset, 2)
    for value in (0, 1):
        pl.when(parity == value)(functools.partial(body, value))


def pack_y_kernel(plan, fwd, adj, eps, e0, h0, e1, h1, coef, z_up, z_down, sems, scratch):
    nx, ny = plan.nx, plan.ny
    own = (pl.ds(STEPS, nx), pl.ds(0, ny), slice(None))
    copies = [pltpu.make_async_copy(eps, coef.at[own], sems.at[0])]
    for run, ref in enumerate((fwd, adj)):
        for kind, array in enumerate((e0, h0)):
            for i in range(6):
                copies.append(
                    pltpu.make_async_copy(ref.at[kind * 6 + i], array.at[(run * 6 + i, *own)], sems.at[len(copies)])
                )
    for copy in copies:
        copy.start()
    copies[0].wait()
    for x in range(nx):
        coef[STEPS + x, pl.ds(0, ny), :] = (0.5 * courant) / coef[STEPS + x, pl.ds(0, ny), :]
    e0, h0, e1, h1, coef = (array.reshape((-1, array.shape[-1])) for array in (e0, h0, e1, h1, coef))
    sweeps = Sweeps(plan, [e0, e1], [h0, h1], coef, ny)
    for run in (0, 1):
        for copy in copies[1 + 12 * run : 13 + 12 * run]:
            copy.wait()
        sweeps.both(1, range(nx), range(nx - 1), runs=(run,))
    state = State([e0, e1], [h0, h1], coef)
    pack(plan, plan.y_low, state, 0, ny, z_up, fold(plan, state, 0, scratch))
    pack(plan, plan.y_high, state, 0, -ny, z_down)


def pack_x_kernel(plan, e0, h0, e1, h1, coef, x_up, x_down, scratch):
    state = State([e0, e1], [h0, h1], coef)
    pack(plan, plan.x_low, state, plan.nx, 0, x_up, fold(plan, state, 1, scratch))
    pack(plan, plan.x_high, state, -plan.nx, 0, x_down)


def pack_diagonal_kernel(plan, e0, h0, e1, h1, coef, after, diagonal):
    state = State([e0, e1], [h0, h1], coef)

    def corners(receiver):
        pack(plan, plan.far_high[receiver], state, -plan.nx * plan.far_side[receiver], -plan.ny, diagonal)

    by_parity(1, corners)


def turns_kernel(groups, table, index, tiles, turns):
    row = index[0]
    phi_x, phi_y = table[row, 0], table[row, 1]
    at_x, at_y = lax.axis_index("gx"), lax.axis_index("gy")
    none = jnp.float32(0.0)
    ax_low = jnp.where(at_x == 0, -phi_x, none)
    ax_high = jnp.where(at_x == lax.axis_size("gx") - 1, phi_x, none)
    ay_low = jnp.where(at_y == 0, -phi_y, none)
    ay_high = jnp.where(at_y == lax.axis_size("gy") - 1, phi_y, none)
    sub = lax.broadcasted_iota(jnp.int32, (SUB, turns.shape[1]), 0)
    angles = jnp.zeros(sub.shape, jnp.float32)
    for i, angle in enumerate((ax_low, ax_high, ay_low, ay_high, ax_low + ay_low, ax_low + ay_high,
                               ax_high + ay_low, ax_high + ay_high)):
        angles = jnp.where(sub == i, angle, angles)
    turns[pl.ds(0, SUB), :] = jnp.cos(angles)
    turns[pl.ds(SUB, SUB), :] = jnp.sin(angles)
    own_tile = at_x * lax.axis_size("gy") + at_y
    chosen = tiles[0] == own_tile
    for i in range(1, tiles.shape[0]):
        chosen = jnp.logical_or(chosen, tiles[i] == own_tile)
    weight = jnp.where(chosen, jnp.float32(1.0 / groups), none)
    turns[pl.ds(2 * SUB, SUB), :] = jnp.full(sub.shape, weight, jnp.float32)


def relay_kernel(plan, jobs, *refs):
    faces, outs = refs[: len(refs) - len(jobs)], refs[len(refs) - len(jobs) :]

    def corners(receiver):
        for (messages, side), out in zip(jobs, outs, strict=True):
            dx = -plan.nx * side[receiver]
            for (what, x, y), row in messages[receiver].at.items():
                ref, source = (faces[0], plan.y_low) if y < 0 else (faces[1], plan.y_high)
                out[pl.ds(row, 1), :] = ref[pl.ds(source.at[what, x + dx, y], 1), :]

    by_parity(1, corners)


def turned(real, imag, cosine, sine):
    return real * cosine - imag * sine, real * sine + imag * cosine


def unpack(plan, message, ref, which, turns, state, kinds, level, layers=None):
    axis = message.axis
    for (kind, at_level, comp, run, part), x, y, count, at in message.runs:
        if kind not in kinds or at_level != level or part == 1:
            continue
        pieces = [(x, y, count, at)]
        if layers is not None:
            pieces = [(x + i, y, 1, at + i) for i in range(count) if x + i in layers]
        for cell_x, cell_y, size, row in pieces:
            what = (kind, at_level, comp, run, 0)
            real = ref[pl.ds(row, size), :]
            if kind == "C":
                state(what)[plan.rows(what, cell_x, cell_y, axis, size), :] = real
                continue
            twin = (kind, at_level, comp, run, 1)
            imag = ref[pl.ds(message.at[twin, cell_x, cell_y], size), :]
            turn = which(y)
            cosine, sine = turns[pl.ds(turn, 1), :], turns[pl.ds(SUB + turn, 1), :]
            real, imag = turned(real, imag, cosine, sine if run == 0 else -sine)
            state(what)[plan.rows(what, cell_x, cell_y, axis, size), :] = real
            state(twin)[plan.rows(twin, cell_x, cell_y, axis, size), :] = imag
    for what, x, y, count, _ in message.zeros:
        if what[0] in kinds and what[1] == level and layers is None:
            state(what)[plan.rows(what, x, y, axis, count), :] = jnp.zeros((count, ref.shape[1]), jnp.float32)


class Sweeps:
    def __init__(self, plan, efield, hfield, coef, height, todo=None):
        self.plan, self.efield, self.hfield, self.coef, self.height = plan, efield, hfield, coef, height
        self.todo = todo

    def rows(self, run, part, comp, x, start, stop):
        return pl.ds(self.plan.row(x, 0, run, part, comp) + start, stop - start)

    def get(self, array, run, part, comp, x):
        return array[self.rows(run, part, comp, x, 0, self.height), :]

    def pieces(self, kind, step, x):
        if self.todo is None:
            return [(comp, 0, self.height) for comp in range(3)]
        found = []
        for comp, tiles in sorted(self.todo.get((kind, step, x), {}).items()):
            for tile in sorted(tiles):
                if found and found[-1][0] == comp and found[-1][2] == tile * SUB:
                    found[-1] = (comp, found[-1][1], (tile + 1) * SUB)
                else:
                    found.append((comp, tile * SUB, (tile + 1) * SUB))
        return found

    def next_z(self, value):
        lane = lax.broadcasted_iota(jnp.int32, value.shape, 1)
        return jnp.where(lane == value.shape[1] - 1, 0.0, pltpu.roll(value, value.shape[1] - 1, 1))

    def prev_z(self, value):
        lane = lax.broadcasted_iota(jnp.int32, value.shape, 1)
        return jnp.where(lane == 0, 0.0, pltpu.roll(value, 1, 1))

    def next_y(self, value):
        return pltpu.roll(value, self.height - 1, 0)

    def prev_y(self, value):
        return pltpu.roll(value, 1, 0)

    def update_h(self, step, run, part, x):
        efield, old, new = self.efield[step - 1], self.hfield[step - 1], self.hfield[step]
        ex, ey, ez = (self.get(efield, run, part, comp, x) for comp in range(3))
        for comp, start, stop in self.pieces("H", step, x):
            here = slice(start, stop)
            if comp == 0:
                curl = (self.next_y(ez) - ez)[here] - (self.next_z(ey[here]) - ey[here])
            elif comp == 1:
                ez_x = self.get(efield, run, part, 2, x + 1)
                curl = (self.next_z(ex[here]) - ex[here]) - (ez_x - ez)[here]
            else:
                ey_x = self.get(efield, run, part, 1, x + 1)
                curl = (ey_x - ey)[here] - (self.next_y(ex) - ex)[here]
            before = self.get(old, run, part, comp, x)[here]
            if step == 1:
                before = before + before
            new[self.rows(run, part, comp, x, start, stop), :] = before - curl

    def update_e(self, step, run, part, x):
        old, new, hfield = self.efield[step - 1], self.efield[step], self.hfield[step]
        hx, hy, hz = (self.get(hfield, run, part, comp, x) for comp in range(3))
        scale = self.get(self.coef, 0, 0, 0, x)
        for comp, start, stop in self.pieces("E", step, x):
            here = slice(start, stop)
            if comp == 0:
                curl = (hz - self.prev_y(hz))[here] - (hy[here] - self.prev_z(hy[here]))
            elif comp == 1:
                hz_x = self.get(hfield, run, part, 2, x - 1)
                curl = (hx[here] - self.prev_z(hx[here])) - (hz - hz_x)[here]
            else:
                hy_x = self.get(hfield, run, part, 1, x - 1)
                curl = (hy - hy_x)[here] - (hx - self.prev_y(hx))[here]
            before = self.get(old, run, part, comp, x)[here]
            new[self.rows(run, part, comp, x, start, stop), :] = before + scale[here] * curl

    def both(self, step, h_layers, e_layers, after_h=None, after_e=None, runs=(0, 1)):
        for update, layers, after in ((self.update_h, h_layers, after_h), (self.update_e, e_layers, after_e)):
            for x in layers:
                for run in runs:
                    for part in (0, 1):
                        update(step, run, part, x)
            if after is not None:
                after()


def middle_kernel(plan, e0_in, h0_in, e1_in, h1_in, coef_in, z_low, z_high, turns, *arrays):
    nx = plan.nx
    efield, hfield, coef = arrays[: STEPS + 1], arrays[STEPS + 1 : 2 * STEPS + 2], arrays[-1]
    state = State(efield, hfield, coef)

    def take(kinds, level):
        unpack(plan, plan.y_low, z_low, lambda y: 2, turns, state, kinds, level)
        unpack(plan, plan.y_high, z_high, lambda y: 3, turns, state, kinds, level)

    take("EHC", 0)
    sweeps = Sweeps(plan, efield, hfield, coef, plan.ring, plan.made)
    for step in range(1, STEPS + 1):
        after = [lambda: take("H", 1), lambda: take("E", 1)] if step == 1 else []
        sweeps.both(step, range(step - 1, nx - step), range(step, nx - step), *after)


def add_up(plan, efield, transform, out):
    nx, ny = plan.nx, plan.ny
    for x in range(nx):
        for tile in range(ny // SUB):
            for comp in range(3):
                ends = []
                for run in (0, 1):
                    at = [pl.ds(((part * 3 + comp) * nx + x) * ny + tile * SUB, SUB) for part in (0, 1)]
                    real, imag = transform[run][at[0], :], transform[run][at[1], :]
                    for level in range(1, STEPS + 1):
                        theta = omega_step * level
                        here = [efield[level][pl.ds(plan.row(x, tile * SUB, run, part, comp), SUB), :] for part in (0, 1)]
                        more = turned(*here, math.cos(theta), math.sin(theta))
                        real, imag = real + more[0], imag + more[1]
                    out[run][at[0], :], out[run][at[1], :] = real, imag
                    ends.append((real, imag))
                yield x, tile, ends


def do_valleys(plan, sweeps, take):
    for step in range(1, STEPS + 1):
        low, high = step - STEPS, plan.nx - step
        h_layers = [*range(low - 1, step - 1), *range(high, plan.nx + STEPS - step)]
        e_layers = [*range(low, step), *range(high, plan.nx + STEPS - step)]
        after = [functools.partial(take, "H", 1, h_layers), functools.partial(take, "E", 1, e_layers)] if step == 1 else []
        sweeps.both(step, h_layers, e_layers, *after)


def edges_kernel(plan, groups, *refs):
    count = 2 * STEPS + 3
    x_low, x_high, far_low, far_high, mate, z_low, z_high, turns, spec_f, spec_a = refs[count : count + 10]
    arrays = refs[count + 10 : 2 * count + 10]
    out_f, out_a, *parts = refs[2 * count + 10 :]
    efield, hfield, coef = arrays[: STEPS + 1], arrays[STEPS + 1 : 2 * STEPS + 2], arrays[-1]
    state = State(efield, hfield, coef)

    def take(kinds, level, layers):
        unpack(plan, plan.x_low, x_low, lambda y: 0, turns, state, kinds, level)
        unpack(plan, plan.x_high, x_high, lambda y: 1, turns, state, kinds, level)

        def corners(receiver):
            for messages, ref, side in (
                (plan.far_low, far_low, plan.far_side),
                (plan.far_high, far_high, plan.far_side),
                (plan.mate, mate, plan.mate_side),
            ):
                first = 4 if side[receiver] < 0 else 6
                unpack(plan, messages[receiver], ref, lambda y: first + (y >= 0), turns, state, kinds, level)

        by_parity(0, corners)
        unpack(plan, plan.y_low, z_low, lambda y: 2, turns, state, kinds, level, layers)
        unpack(plan, plan.y_high, z_high, lambda y: 3, turns, state, kinds, level, layers)

    take("EHC", 0, ())
    do_valleys(plan, Sweeps(plan, efield, hfield, coef, plan.ring, plan.made), take)

    share = plan.depth // groups
    shift = lax.rem(groups - lax.axis_index("angle"), groups) * share
    weight = turns[pl.ds(2 * SUB, SUB), :]

    totals = {}
    for x, tile, ends in add_up(plan, efield, (spec_f, spec_a), (out_f, out_a)):
        term = ends[0][0] * ends[1][0] - ends[0][1] * ends[1][1]
        totals[x, tile] = totals[x, tile] + term if (x, tile) in totals else term
    block = lax.broadcasted_iota(jnp.int32, weight.shape, 1) // share
    tiles = [pltpu.roll(total * weight, shift, 1) for total in totals.values()]
    for k, part in enumerate(parts):
        for i in range(len(tiles) // groups):
            packed = jnp.zeros(weight.shape, jnp.float32)
            for t in range(groups):
                lanes = (t - k) % groups * share
                value = tiles[i * groups + t]
                packed = jnp.where(block == t, pltpu.roll(value, lanes, 1) if lanes else value, packed)
            part[pl.ds(i * SUB, SUB), :] = packed


def sum_kernel(groups, *refs):
    *parts, out = refs
    share = out.shape[1]
    for i in range(parts[0].shape[0] // SUB):
        total = parts[0][pl.ds(i * SUB, SUB), :]
        for part in parts[1:]:
            total = total + part[pl.ds(i * SUB, SUB), :]
        for t in range(groups):
            out[pl.ds((i * groups + t) * SUB, SUB), :] = total[:, t * share : (t + 1) * share]


def write_kernel(tr_f, tr_a, out_f, out_a, sems):
    copies = []
    for source, target in ((tr_f, out_f), (tr_a, out_a)):
        for i in range(source.shape[0]):
            copies.append(pltpu.make_async_copy(source.at[i], target.at[i], sems.at[len(copies)]))
    for copy in copies:
        copy.start()
    for copy in copies:
        copy.wait()


def ring_pairs(axis, offset):
    size = lax.axis_size(axis)
    return [(i, (i + offset) % size) for i in range(size)]


def mate_pairs():
    return [(i, i ^ 1) for i in range(lax.axis_size("gx"))]


def far_pairs():
    size = lax.axis_size("gx")
    return [(i, (i + (1 if i % 2 else -1)) % size) for i in range(size)]


def diagonal_pairs():
    size = lax.axis_size("gy")
    return [(x * size + y, far * size + (y - 1) % size) for x, far in far_pairs() for y in range(size)]


def shards(
    forward_fields,
    adjoint_fields,
    forward_spectrum,
    adjoint_spectrum,
    permittivity,
    phase_table,
    angle_index,
    design_tiles,
):
    nx, ny, depth = permittivity.shape
    plan = Plan(nx, ny, depth)
    groups = lax.axis_size("angle")
    wide, ring = plan.wide, plan.ring

    def array(*shape):
        return jax.ShapeDtypeStruct(shape, jnp.float32)

    def lines(count):
        return array(count, depth)

    def params(mib):
        return pltpu.CompilerParams(vmem_limit_bytes=mib * 2**20)

    def cost(size):
        return pl.CostEstimate(flops=size, bytes_accessed=size, transcendentals=0)

    assert lax.axis_size("gx") % 2 == 0 and nx * ny % (groups * SUB) == 0
    with jax.named_scope("pack_y"):
        *first, coef, z_up, z_down = pl.pallas_call(
            functools.partial(pack_y_kernel, plan),
            out_shape=(
                *[array(12, wide, ring, depth)] * 4,
                array(wide, ring, depth),
                lines(plan.y_low.lines),
                lines(plan.y_high.lines),
            ),
            in_specs=[HBM] * 3,
            out_specs=[VMEM] * 7,
            scratch_shapes=[pltpu.SemaphoreType.DMA((25,)), pltpu.VMEM((24 * nx, depth), jnp.float32)],
            compiler_params=params(8),
        )(*(pltpu.with_memory_space_constraint(array, pltpu.HBM) for array in (forward_fields[0], adjoint_fields[0], permittivity)))
    e0, h0, e1, h1, coef = (state.reshape((-1, depth)) for state in (*first, coef))
    with jax.named_scope("send_y"):
        z_low = lax.ppermute(z_up, "gy", ring_pairs("gy", 1))
        z_high = lax.ppermute(z_down, "gy", ring_pairs("gy", -1))
    with jax.named_scope("pack_x"):
        x_up, x_down = pl.pallas_call(
            functools.partial(pack_x_kernel, plan),
            out_shape=[lines(plan.x_low.lines), lines(plan.x_high.lines)],
            in_specs=[VMEM] * 5,
            out_specs=[VMEM] * 2,
            scratch_shapes=[pltpu.VMEM((24 * ny, depth), jnp.float32)],
            compiler_params=params(8),
            cost_estimate=cost(40 * 2**20),
        )(e0, h0, e1, h1, coef)
    with jax.named_scope("send_x"):
        x_low = lax.ppermute(x_up, "gx", ring_pairs("gx", 1))
        x_high = lax.ppermute(x_down, "gx", ring_pairs("gx", -1))
    with jax.named_scope("turns"):
        turns = pl.pallas_call(
            functools.partial(turns_kernel, groups),
            out_shape=lines(3 * SUB),
            in_specs=[SMEM] * 3,
            out_specs=VMEM,
            compiler_params=params(4),
        )(phase_table, angle_index, design_tiles)
    with jax.named_scope("diagonal_corners"):
        to_diagonal = pl.pallas_call(
            functools.partial(pack_diagonal_kernel, plan),
            out_shape=lines(max(message.lines for message in plan.far_high)),
            in_specs=[VMEM] * 6,
            out_specs=VMEM,
            compiler_params=params(4),
        )(e0, h0, e1, h1, coef, x_up)
        far_high = lax.ppermute(to_diagonal, ("gx", "gy"), diagonal_pairs())

    def relay(jobs, *faces):
        return pl.pallas_call(
            functools.partial(relay_kernel, plan, jobs),
            out_shape=[lines(max(message.lines for message in messages)) for messages, _ in jobs],
            in_specs=[VMEM] * len(faces),
            out_specs=[VMEM] * len(jobs),
            compiler_params=params(4),
            cost_estimate=cost(2**10),
        )(*faces)

    with jax.named_scope("relay_low_corners"):
        (to_far,) = relay([(plan.far_low, plan.far_side)], z_low)
        far_low = lax.ppermute(to_far, "gx", far_pairs())
    with jax.named_scope("relay_corners"):
        (to_mate,) = relay([(plan.mate, plan.mate_side)], z_low, z_high)
        mate = lax.ppermute(to_mate, "gx", mate_pairs())
    level = lines(12 * wide * ring)
    count = 2 * STEPS + 3
    levels = [level] * (count - 1) + [lines(wide * ring)]
    with jax.named_scope("middle"):
        state = pl.pallas_call(
            functools.partial(middle_kernel, plan),
            out_shape=levels,
            in_specs=[VMEM] * 8,
            out_specs=[VMEM] * count,
            input_output_aliases={0: 0, 1: STEPS + 1, 2: 1, 3: STEPS + 2, 4: count - 1},
            compiler_params=params(8),
            cost_estimate=cost(3 * 2**29),
        )(e0, h0, e1, h1, coef, z_low, z_high, turns)
    transforms = [lines(6 * nx * ny)] * 2
    with jax.named_scope("edges"):
        spectra = [spectrum.reshape((-1, depth)) for spectrum in (forward_spectrum, adjoint_spectrum)]
        results = pl.pallas_call(
            functools.partial(edges_kernel, plan, groups),
            out_shape=[*levels, *transforms, *[lines(nx * ny // groups)] * groups],
            in_specs=[VMEM] * (count + 10),
            out_specs=[VMEM] * (count + 2 + groups),
            input_output_aliases={i: i for i in range(count)},
            compiler_params=params(8),
        )(*state, x_low, x_high, far_low, far_high, mate, z_low, z_high, turns, *spectra)
        tr_f, tr_a, own, *others = results[count:]
    with jax.named_scope("sum_angles"):
        others = [lax.ppermute(part, "angle", ring_pairs("angle", k + 1)) for k, part in enumerate(others)]
        gradient = pl.pallas_call(
            functools.partial(sum_kernel, groups),
            out_shape=array(nx * ny, depth // groups),
            in_specs=[VMEM] * groups,
            out_specs=VMEM,
            compiler_params=params(4),
        )(own, *others)
    with jax.named_scope("write"):
        out_f, out_a = pl.pallas_call(
            write_kernel,
            out_shape=[array(6, nx, ny, depth)] * 2,
            in_specs=[VMEM] * 2,
            out_specs=[HBM] * 2,
            scratch_shapes=[pltpu.SemaphoreType.DMA((12,))],
            compiler_params=params(4),
        )(tr_f.reshape((6, nx, ny, depth)), tr_a.reshape((6, nx, ny, depth)))
    return (
        out_f.reshape(forward_spectrum.shape),
        out_a.reshape(adjoint_spectrum.shape),
        gradient.reshape((nx, ny, depth // groups)),
    )


def solution(mesh):
    in_specs = (
        P("angle", None, "gx", "gy", None),
        P("angle", None, "gx", "gy", None),
        P("angle", None, "gx", "gy", None),
        P("angle", None, "gx", "gy", None),
        P("gx", "gy", None),
        P(),
        P("angle"),
        P(),
    )
    out_specs = (
        P("angle", None, "gx", "gy", None),
        P("angle", None, "gx", "gy", None),
        P("gx", "gy", "angle"),
    )
    return jax.shard_map(shards, mesh=mesh, in_specs=in_specs, out_specs=out_specs, check_vma=False)
```

```python
import functools
import math

import jax
import jax.numpy as jnp
from jax import lax
from jax.experimental import pallas as pl
from jax.experimental.pallas import tpu as pltpu
from jax.sharding import PartitionSpec as P

STEPS = 3
SUB = 8

courant = 0.5
omega_step = 0.7

VMEM = pl.BlockSpec(memory_space=pltpu.VMEM)
SMEM = pl.BlockSpec(memory_space=pltpu.SMEM)
HBM = pl.BlockSpec(memory_space=pltpu.HBM)


def reads(node):
    kind, level, comp, x, y = node
    others = [c for c in range(3) if c != comp]
    if kind == "E":
        found = [("E", level - 1, comp, x, y), ("C", 0, 0, x, y)] + [("H", level, c, x, y) for c in others]
        if comp != 1:
            found.append(("H", level, 2 - comp, x, y - 1))
        if comp != 0:
            found.append(("H", level, 3 - comp, x - 1, y))
        return found
    found = [("H", level - 1, comp, x, y)] + [("E", level - 1, c, x, y) for c in others]
    if comp != 1:
        found.append(("E", level - 1, 2 - comp, x, y + 1))
    if comp != 0:
        found.append(("E", level - 1, 3 - comp, x + 1, y))
    return found


def wanted(nx, ny):
    def block(node):
        return node[3] // nx, node[4] // ny

    @functools.cache
    def alone(node):
        if node[1] == 0:
            return True
        return node[1] == 1 and all(block(other) == block(node) and alone(other) for other in reads(node))

    found, made, seen = set(), set(), set()
    todo = [("E", STEPS, comp, x, y) for comp in range(3) for x in range(nx) for y in range(ny)]
    while todo:
        node = todo.pop()
        if node in seen:
            continue
        seen.add(node)
        if block(node) != (0, 0) and alone(node):
            found.add(node)
        elif node[1]:
            made.add(node)
            todo += reads(node)
    return found, made


class Message:
    def __init__(self, nodes, axis, folded=()):
        self.axis, self.runs, self.at, self.size = axis, [], {}, 0
        assert nodes.issuperset(folded)
        self.zeros = Message(set(folded), axis).runs if folded else []
        nodes = nodes - set(folded)
        stretches = []
        for node in sorted(nodes):
            before = list(node)
            before[3 + axis] -= 1
            if tuple(before) in nodes:
                continue
            count = 1
            while (*node[:3], node[3] + count * (axis == 0), node[4] + count * (axis == 1)) in nodes:
                count += 1
            stretches.append((count, node))
        for count, (kind, level, comp, x, y) in sorted(stretches, key=lambda item: (-item[0], item[1])):
            for run in (0, 1) if kind != "C" else (0,):
                for part in (0, 1) if kind != "C" else (0,):
                    what = (kind, level, comp, run, part)
                    self.runs.append((what, x, y, count, self.size))
                    for i in range(count):
                        self.at[what, x + i * (axis == 0), y + i * (axis == 1)] = self.size + i
                    self.size += count
        self.lines = -(-self.size // SUB) * SUB


class Plan:
    def __init__(self, nx, ny, depth):
        self.depth = depth
        self.nx, self.ny = nx, ny
        self.wide, self.ring = nx + 2 * STEPS, ny + SUB
        nodes, made = wanted(nx, ny)
        self.made = {}
        for kind, level, comp, x, y in made:
            self.made.setdefault((kind, level, x), {}).setdefault(comp, set()).add(y % self.ring // SUB)
        sides = {}
        for node in nodes:
            sides.setdefault((node[3] // nx, node[4] // ny), set()).add(node)

        def shifted(found, dx):
            return {(*node[:3], node[3] + dx, node[4]) for node in found}

        y_low, y_high = (sides[0, side] | shifted(sides[-1, side], nx) | shifted(sides[1, side], -nx) for side in (-1, 1))
        self.x_folds = (1, ny - 2), (2, ny - 2)
        self.y_folds = (2, nx - 2), (3, nx - 2)
        x_folded = [("E", 1, comp, -2, y) for comp in range(3) for y in range(*self.x_folds[comp == 0])]
        y_folded = [("E", 1, comp, x, -2) for comp in range(3) for x in range(*self.y_folds[comp == 1])]
        self.y_low, self.y_high = Message(y_low, 0, y_folded), Message(y_high, 0)
        self.x_low, self.x_high = Message(sides[-1, 0], 1, x_folded), Message(sides[1, 0], 1)
        self.mate_side, self.far_side = (1, -1), (-1, 1)
        self.mate = [Message(sides[side, -1] | sides[side, 1], 1) for side in self.mate_side]
        self.far_low, self.far_high = ([Message(sides[side, end], 1) for side in self.far_side] for end in (-1, 1))

    def row(self, x, y, run=0, part=0, comp=0):
        return ((run * 6 + part * 3 + comp) * self.wide + x + STEPS) * self.ring + y % self.ring

    def rows(self, what, x, y, axis, count):
        _, _, comp, run, part = what
        start = self.row(x, y, run, part, comp)
        return pl.ds(start, count, stride=self.ring) if axis == 0 and count > 1 else pl.ds(start, count)


class State:
    def __init__(self, efield, hfield, coef):
        self.by_kind = {"E": efield, "H": hfield, "C": [coef]}

    def __call__(self, what):
        return self.by_kind[what[0]][what[1]]


def pack(plan, message, state, dx, dy, out, changed=None):
    for what, x, y, count, at in message.runs:
        layer, first = (y, x) if message.axis == 0 else (x, y)
        if changed and (what, layer) in changed:
            ref, row = changed[what, layer]
            value = ref[pl.ds(row + first, count), :]
        else:
            value = state(what)[plan.rows(what, x + dx, y + dy, message.axis, count), :]
        out[pl.ds(at, count), :] = value


def fold(plan, state, axis, scratch):
    nx, ny = plan.nx, plan.ny
    size, normal = (nx, 1) if axis == 0 else (ny, 0)
    before, after = ((0, 2) if axis == 0 else (1, 2))
    cell = lax.broadcasted_iota(jnp.int32, (size, scratch.shape[1]), 0)
    lane = lax.broadcasted_iota(jnp.int32, cell.shape, 1)
    folds = plan.y_folds if axis == 0 else plan.x_folds
    changed = {}

    def lines(what, layer):
        place = (0, ny + layer) if axis == 0 else (nx + layer, 0)
        return state(what)[plan.rows(what, *place, axis, size), :]

    def inside(value, fold):
        return jnp.where((cell >= fold[0]) & (cell < fold[1]), value, 0.0)

    for run in (0, 1):
        for part in (0, 1):

            def get(kind, level, comp, layer):
                return lines((kind, level, comp, run, part), layer)

            def put(kind, level, comp, layer, value):
                row = len(changed) * size
                scratch[pl.ds(row, size), :] = value
                changed[(kind, level, comp, run, part), layer] = scratch, row

            low, high = (inside(get("E", 1, comp, -2), folds[0]) for comp in (before, after))
            along = inside(get("E", 1, normal, -2), folds[1])
            along_z = jnp.where(lane == lane.shape[1] - 1, 0.0, pltpu.roll(along, lane.shape[1] - 1, 1)) - along
            along_next = pltpu.roll(along, size - 1, 0) - along
            sign = 1.0 if axis == 0 else -1.0
            d_before = sign * (high + along_z)
            d_after = -sign * (low + along_next)
            scale = lines(("C", 0, 0, 0, 0), -1)
            put("H", 1, before, -2, get("H", 1, before, -2) + d_before)
            put("H", 1, after, -2, get("H", 1, after, -2) + d_after)
            put("E", 0, before, -1, get("E", 0, before, -1) + sign * scale * d_after)
            put("E", 0, after, -1, get("E", 0, after, -1) - sign * scale * d_before)
            put("H", 0, before, -1, get("H", 0, before, -1) + 0.5 * scale * d_before)
            put("H", 0, after, -1, get("H", 0, after, -1) + 0.5 * scale * d_after)
    return changed


def by_parity(offset, body):
    parity = lax.rem(lax.axis_index("gx") + offset, 2)
    for value in (0, 1):
        pl.when(parity == value)(functools.partial(body, value))


def pack_y_kernel(plan, fwd, adj, eps, e0, h0, e1, h1, coef, z_up, z_down, sems, scratch):
    nx, ny = plan.nx, plan.ny
    own = (pl.ds(STEPS, nx), pl.ds(0, ny), slice(None))
    copies = [pltpu.make_async_copy(eps, coef.at[own], sems.at[0])]
    for run, ref in enumerate((fwd, adj)):
        for kind, array in enumerate((e0, h0)):
            for i in range(6):
                copies.append(
                    pltpu.make_async_copy(ref.at[kind * 6 + i], array.at[(run * 6 + i, *own)], sems.at[len(copies)])
                )
    for copy in copies:
        copy.start()
    copies[0].wait()
    for x in range(nx):
        coef[STEPS + x, pl.ds(0, ny), :] = (0.5 * courant) / coef[STEPS + x, pl.ds(0, ny), :]
    e0, h0, e1, h1, coef = (array.reshape((-1, array.shape[-1])) for array in (e0, h0, e1, h1, coef))
    sweeps = Sweeps(plan, [e0, e1], [h0, h1], coef, ny)
    for run in (0, 1):
        for copy in copies[1 + 12 * run : 13 + 12 * run]:
            copy.wait()
        sweeps.both(1, range(nx), range(nx - 1), runs=(run,))
    state = State([e0, e1], [h0, h1], coef)
    pack(plan, plan.y_low, state, 0, ny, z_up, fold(plan, state, 0, scratch))
    pack(plan, plan.y_high, state, 0, -ny, z_down)


def pack_x_kernel(plan, e0, h0, e1, h1, coef, x_up, x_down, scratch):
    state = State([e0, e1], [h0, h1], coef)
    pack(plan, plan.x_low, state, plan.nx, 0, x_up, fold(plan, state, 1, scratch))
    pack(plan, plan.x_high, state, -plan.nx, 0, x_down)


def pack_diagonal_kernel(plan, e0, h0, e1, h1, coef, after, diagonal):
    state = State([e0, e1], [h0, h1], coef)

    def corners(receiver):
        pack(plan, plan.far_high[receiver], state, -plan.nx * plan.far_side[receiver], -plan.ny, diagonal)

    by_parity(1, corners)


def turns_kernel(groups, table, index, tiles, turns):
    row = index[0]
    phi_x, phi_y = table[row, 0], table[row, 1]
    at_x, at_y = lax.axis_index("gx"), lax.axis_index("gy")
    none = jnp.float32(0.0)
    ax_low = jnp.where(at_x == 0, -phi_x, none)
    ax_high = jnp.where(at_x == lax.axis_size("gx") - 1, phi_x, none)
    ay_low = jnp.where(at_y == 0, -phi_y, none)
    ay_high = jnp.where(at_y == lax.axis_size("gy") - 1, phi_y, none)
    sub = lax.broadcasted_iota(jnp.int32, (SUB, turns.shape[1]), 0)
    angles = jnp.zeros(sub.shape, jnp.float32)
    for i, angle in enumerate((ax_low, ax_high, ay_low, ay_high, ax_low + ay_low, ax_low + ay_high,
                               ax_high + ay_low, ax_high + ay_high)):
        angles = jnp.where(sub == i, angle, angles)
    turns[pl.ds(0, SUB), :] = jnp.cos(angles)
    turns[pl.ds(SUB, SUB), :] = jnp.sin(angles)
    own_tile = at_x * lax.axis_size("gy") + at_y
    chosen = tiles[0] == own_tile
    for i in range(1, tiles.shape[0]):
        chosen = jnp.logical_or(chosen, tiles[i] == own_tile)
    weight = jnp.where(chosen, jnp.float32(1.0 / groups), none)
    turns[pl.ds(2 * SUB, SUB), :] = jnp.full(sub.shape, weight, jnp.float32)


def relay_kernel(plan, jobs, *refs):
    faces, outs = refs[: len(refs) - len(jobs)], refs[len(refs) - len(jobs) :]

    def corners(receiver):
        for (messages, side), out in zip(jobs, outs, strict=True):
            dx = -plan.nx * side[receiver]
            for (what, x, y), row in messages[receiver].at.items():
                ref, source = (faces[0], plan.y_low) if y < 0 else (faces[1], plan.y_high)
                out[pl.ds(row, 1), :] = ref[pl.ds(source.at[what, x + dx, y], 1), :]

    by_parity(1, corners)


def turned(real, imag, cosine, sine):
    return real * cosine - imag * sine, real * sine + imag * cosine


def unpack(plan, message, ref, which, turns, state, kinds, level, layers=None):
    axis = message.axis
    for (kind, at_level, comp, run, part), x, y, count, at in message.runs:
        if kind not in kinds or at_level != level or part == 1:
            continue
        pieces = [(x, y, count, at)]
        if layers is not None:
            pieces = [(x + i, y, 1, at + i) for i in range(count) if x + i in layers]
        for cell_x, cell_y, size, row in pieces:
            what = (kind, at_level, comp, run, 0)
            real = ref[pl.ds(row, size), :]
            if kind == "C":
                state(what)[plan.rows(what, cell_x, cell_y, axis, size), :] = real
                continue
            twin = (kind, at_level, comp, run, 1)
            imag = ref[pl.ds(message.at[twin, cell_x, cell_y], size), :]
            turn = which(y)
            cosine, sine = turns[pl.ds(turn, 1), :], turns[pl.ds(SUB + turn, 1), :]
            real, imag = turned(real, imag, cosine, sine if run == 0 else -sine)
            state(what)[plan.rows(what, cell_x, cell_y, axis, size), :] = real
            state(twin)[plan.rows(twin, cell_x, cell_y, axis, size), :] = imag
    for what, x, y, count, _ in message.zeros:
        if what[0] in kinds and what[1] == level and layers is None:
            state(what)[plan.rows(what, x, y, axis, count), :] = jnp.zeros((count, ref.shape[1]), jnp.float32)


class Sweeps:
    def __init__(self, plan, efield, hfield, coef, height, todo=None):
        self.plan, self.efield, self.hfield, self.coef, self.height = plan, efield, hfield, coef, height
        self.todo = todo

    def rows(self, run, part, comp, x, start, stop):
        return pl.ds(self.plan.row(x, 0, run, part, comp) + start, stop - start)

    def get(self, array, run, part, comp, x):
        return array[self.rows(run, part, comp, x, 0, self.height), :]

    def pieces(self, kind, step, x):
        if self.todo is None:
            return [(comp, 0, self.height) for comp in range(3)]
        found = []
        for comp, tiles in sorted(self.todo.get((kind, step, x), {}).items()):
            for tile in sorted(tiles):
                if found and found[-1][0] == comp and found[-1][2] == tile * SUB:
                    found[-1] = (comp, found[-1][1], (tile + 1) * SUB)
                else:
                    found.append((comp, tile * SUB, (tile + 1) * SUB))
        return found

    def next_z(self, value):
        lane = lax.broadcasted_iota(jnp.int32, value.shape, 1)
        return jnp.where(lane == value.shape[1] - 1, 0.0, pltpu.roll(value, value.shape[1] - 1, 1))

    def prev_z(self, value):
        lane = lax.broadcasted_iota(jnp.int32, value.shape, 1)
        return jnp.where(lane == 0, 0.0, pltpu.roll(value, 1, 1))

    def next_y(self, value):
        return pltpu.roll(value, self.height - 1, 0)

    def prev_y(self, value):
        return pltpu.roll(value, 1, 0)

    def update_h(self, step, run, part, x):
        efield, old, new = self.efield[step - 1], self.hfield[step - 1], self.hfield[step]
        ex, ey, ez = (self.get(efield, run, part, comp, x) for comp in range(3))
        for comp, start, stop in self.pieces("H", step, x):
            here = slice(start, stop)
            if comp == 0:
                curl = (self.next_y(ez) - ez)[here] - (self.next_z(ey[here]) - ey[here])
            elif comp == 1:
                ez_x = self.get(efield, run, part, 2, x + 1)
                curl = (self.next_z(ex[here]) - ex[here]) - (ez_x - ez)[here]
            else:
                ey_x = self.get(efield, run, part, 1, x + 1)
                curl = (ey_x - ey)[here] - (self.next_y(ex) - ex)[here]
            before = self.get(old, run, part, comp, x)[here]
            if step == 1:
                before = before + before
            new[self.rows(run, part, comp, x, start, stop), :] = before - curl

    def update_e(self, step, run, part, x):
        old, new, hfield = self.efield[step - 1], self.efield[step], self.hfield[step]
        hx, hy, hz = (self.get(hfield, run, part, comp, x) for comp in range(3))
        scale = self.get(self.coef, 0, 0, 0, x)
        for comp, start, stop in self.pieces("E", step, x):
            here = slice(start, stop)
            if comp == 0:
                curl = (hz - self.prev_y(hz))[here] - (hy[here] - self.prev_z(hy[here]))
            elif comp == 1:
                hz_x = self.get(hfield, run, part, 2, x - 1)
                curl = (hx[here] - self.prev_z(hx[here])) - (hz - hz_x)[here]
            else:
                hy_x = self.get(hfield, run, part, 1, x - 1)
                curl = (hy - hy_x)[here] - (hx - self.prev_y(hx))[here]
            before = self.get(old, run, part, comp, x)[here]
            new[self.rows(run, part, comp, x, start, stop), :] = before + scale[here] * curl

    def both(self, step, h_layers, e_layers, after_h=None, after_e=None, runs=(0, 1)):
        for update, layers, after in ((self.update_h, h_layers, after_h), (self.update_e, e_layers, after_e)):
            for x in layers:
                for run in runs:
                    for part in (0, 1):
                        update(step, run, part, x)
            if after is not None:
                after()


def middle_kernel(plan, e0_in, h0_in, e1_in, h1_in, coef_in, z_low, z_high, turns, spec_f, spec_a, *refs):
    *arrays, out_f, out_a = refs
    nx = plan.nx
    efield, hfield, coef = arrays[: STEPS + 1], arrays[STEPS + 1 : 2 * STEPS + 2], arrays[-1]
    state = State(efield, hfield, coef)

    def take(kinds, level):
        unpack(plan, plan.y_low, z_low, lambda y: 2, turns, state, kinds, level)
        unpack(plan, plan.y_high, z_high, lambda y: 3, turns, state, kinds, level)

    take("EHC", 0)
    sweeps = Sweeps(plan, efield, hfield, coef, plan.ring, plan.made)
    for step in range(1, STEPS + 1):
        after = [lambda: take("H", 1), lambda: take("E", 1)] if step == 1 else []
        sweeps.both(step, range(step - 1, nx - step), range(step, nx - step), *after)
    for _ in add_up(plan, efield, functools.partial(in_middle, plan), (spec_f, spec_a), (out_f, out_a)):
        pass


def add_up(plan, efield, levels, transform, out):
    nx, ny = plan.nx, plan.ny
    for x in range(nx):
        for tile in range(ny // SUB):
            for comp in range(3):
                ends = []
                for run in (0, 1):
                    at = [pl.ds(((part * 3 + comp) * nx + x) * ny + tile * SUB, SUB) for part in (0, 1)]
                    real, imag = transform[run][at[0], :], transform[run][at[1], :]
                    for level in levels(x):
                        theta = omega_step * level
                        here = [efield[level][pl.ds(plan.row(x, tile * SUB, run, part, comp), SUB), :] for part in (0, 1)]
                        more = turned(*here, math.cos(theta), math.sin(theta))
                        real, imag = real + more[0], imag + more[1]
                    out[run][at[0], :], out[run][at[1], :] = real, imag
                    ends.append((real, imag))
                yield x, tile, ends


def in_middle(plan, x):
    return [level for level in range(1, STEPS + 1) if level <= x < plan.nx - level]


def do_valleys(plan, sweeps, take):
    for step in range(1, STEPS + 1):
        low, high = step - STEPS, plan.nx - step
        h_layers = [*range(low - 1, step - 1), *range(high, plan.nx + STEPS - step)]
        e_layers = [*range(low, step), *range(high, plan.nx + STEPS - step)]
        after = [functools.partial(take, "H", 1, h_layers), functools.partial(take, "E", 1, e_layers)] if step == 1 else []
        sweeps.both(step, h_layers, e_layers, *after)


def edges_kernel(plan, groups, *refs):
    count = 2 * STEPS + 3
    x_low, x_high, far_low, far_high, mate, z_low, z_high, turns, part_f, part_a = refs[count : count + 10]
    arrays = refs[count + 10 : 2 * count + 10]
    out_f, out_a, *parts = refs[2 * count + 10 :]
    efield, hfield, coef = arrays[: STEPS + 1], arrays[STEPS + 1 : 2 * STEPS + 2], arrays[-1]
    state = State(efield, hfield, coef)

    def take(kinds, level, layers):
        unpack(plan, plan.x_low, x_low, lambda y: 0, turns, state, kinds, level)
        unpack(plan, plan.x_high, x_high, lambda y: 1, turns, state, kinds, level)

        def corners(receiver):
            for messages, ref, side in (
                (plan.far_low, far_low, plan.far_side),
                (plan.far_high, far_high, plan.far_side),
                (plan.mate, mate, plan.mate_side),
            ):
                first = 4 if side[receiver] < 0 else 6
                unpack(plan, messages[receiver], ref, lambda y: first + (y >= 0), turns, state, kinds, level)

        by_parity(0, corners)
        unpack(plan, plan.y_low, z_low, lambda y: 2, turns, state, kinds, level, layers)
        unpack(plan, plan.y_high, z_high, lambda y: 3, turns, state, kinds, level, layers)

    take("EHC", 0, ())
    do_valleys(plan, Sweeps(plan, efield, hfield, coef, plan.ring, plan.made), take)

    share = plan.depth // groups
    shift = lax.rem(groups - lax.axis_index("angle"), groups) * share
    weight = turns[pl.ds(2 * SUB, SUB), :]

    def rest(x):
        return [level for level in range(1, STEPS + 1) if level not in in_middle(plan, x)]

    totals = {}
    for x, tile, ends in add_up(plan, efield, rest, (part_f, part_a), (out_f, out_a)):
        term = ends[0][0] * ends[1][0] - ends[0][1] * ends[1][1]
        totals[x, tile] = totals[x, tile] + term if (x, tile) in totals else term
    block = lax.broadcasted_iota(jnp.int32, weight.shape, 1) // share
    tiles = [pltpu.roll(total * weight, shift, 1) for total in totals.values()]
    for k, part in enumerate(parts):
        for i in range(len(tiles) // groups):
            packed = jnp.zeros(weight.shape, jnp.float32)
            for t in range(groups):
                lanes = (t - k) % groups * share
                value = tiles[i * groups + t]
                packed = jnp.where(block == t, pltpu.roll(value, lanes, 1) if lanes else value, packed)
            part[pl.ds(i * SUB, SUB), :] = packed


def sum_kernel(groups, *refs):
    *parts, out = refs
    share = out.shape[1]
    for i in range(parts[0].shape[0] // SUB):
        total = parts[0][pl.ds(i * SUB, SUB), :]
        for part in parts[1:]:
            total = total + part[pl.ds(i * SUB, SUB), :]
        for t in range(groups):
            out[pl.ds((i * groups + t) * SUB, SUB), :] = total[:, t * share : (t + 1) * share]


def write_kernel(tr_f, tr_a, out_f, out_a, sems):
    copies = []
    for source, target in ((tr_f, out_f), (tr_a, out_a)):
        for i in range(source.shape[0]):
            copies.append(pltpu.make_async_copy(source.at[i], target.at[i], sems.at[len(copies)]))
    for copy in copies:
        copy.start()
    for copy in copies:
        copy.wait()


def ring_pairs(axis, offset):
    size = lax.axis_size(axis)
    return [(i, (i + offset) % size) for i in range(size)]


def mate_pairs():
    return [(i, i ^ 1) for i in range(lax.axis_size("gx"))]


def far_pairs():
    size = lax.axis_size("gx")
    return [(i, (i + (1 if i % 2 else -1)) % size) for i in range(size)]


def diagonal_pairs():
    size = lax.axis_size("gy")
    return [(x * size + y, far * size + (y - 1) % size) for x, far in far_pairs() for y in range(size)]


def shards(
    forward_fields,
    adjoint_fields,
    forward_spectrum,
    adjoint_spectrum,
    permittivity,
    phase_table,
    angle_index,
    design_tiles,
):
    nx, ny, depth = permittivity.shape
    plan = Plan(nx, ny, depth)
    groups = lax.axis_size("angle")
    wide, ring = plan.wide, plan.ring

    def array(*shape):
        return jax.ShapeDtypeStruct(shape, jnp.float32)

    def lines(count):
        return array(count, depth)

    def params(mib):
        return pltpu.CompilerParams(vmem_limit_bytes=mib * 2**20)

    def cost(size):
        return pl.CostEstimate(flops=size, bytes_accessed=size, transcendentals=0)

    assert lax.axis_size("gx") % 2 == 0 and nx * ny % (groups * SUB) == 0
    with jax.named_scope("pack_y"):
        *first, coef, z_up, z_down = pl.pallas_call(
            functools.partial(pack_y_kernel, plan),
            out_shape=(
                *[array(12, wide, ring, depth)] * 4,
                array(wide, ring, depth),
                lines(plan.y_low.lines),
                lines(plan.y_high.lines),
            ),
            in_specs=[HBM] * 3,
            out_specs=[VMEM] * 7,
            scratch_shapes=[pltpu.SemaphoreType.DMA((25,)), pltpu.VMEM((24 * nx, depth), jnp.float32)],
            compiler_params=params(8),
        )(*(pltpu.with_memory_space_constraint(array, pltpu.HBM) for array in (forward_fields[0], adjoint_fields[0], permittivity)))
    e0, h0, e1, h1, coef = (state.reshape((-1, depth)) for state in (*first, coef))
    with jax.named_scope("send_y"):
        z_low = lax.ppermute(z_up, "gy", ring_pairs("gy", 1))
        z_high = lax.ppermute(z_down, "gy", ring_pairs("gy", -1))
    with jax.named_scope("pack_x"):
        x_up, x_down = pl.pallas_call(
            functools.partial(pack_x_kernel, plan),
            out_shape=[lines(plan.x_low.lines), lines(plan.x_high.lines)],
            in_specs=[VMEM] * 5,
            out_specs=[VMEM] * 2,
            scratch_shapes=[pltpu.VMEM((24 * ny, depth), jnp.float32)],
            compiler_params=params(8),
            cost_estimate=cost(40 * 2**20),
        )(e0, h0, e1, h1, coef)
    with jax.named_scope("send_x"):
        x_low = lax.ppermute(x_up, "gx", ring_pairs("gx", 1))
        x_high = lax.ppermute(x_down, "gx", ring_pairs("gx", -1))
    with jax.named_scope("turns"):
        turns = pl.pallas_call(
            functools.partial(turns_kernel, groups),
            out_shape=lines(3 * SUB),
            in_specs=[SMEM] * 3,
            out_specs=VMEM,
            compiler_params=params(4),
        )(phase_table, angle_index, design_tiles)
    with jax.named_scope("diagonal_corners"):
        to_diagonal = pl.pallas_call(
            functools.partial(pack_diagonal_kernel, plan),
            out_shape=lines(max(message.lines for message in plan.far_high)),
            in_specs=[VMEM] * 6,
            out_specs=VMEM,
            compiler_params=params(4),
        )(e0, h0, e1, h1, coef, x_up)
        far_high = lax.ppermute(to_diagonal, ("gx", "gy"), diagonal_pairs())

    def relay(jobs, *faces):
        return pl.pallas_call(
            functools.partial(relay_kernel, plan, jobs),
            out_shape=[lines(max(message.lines for message in messages)) for messages, _ in jobs],
            in_specs=[VMEM] * len(faces),
            out_specs=[VMEM] * len(jobs),
            compiler_params=params(4),
            cost_estimate=cost(2**10),
        )(*faces)

    with jax.named_scope("relay_low_corners"):
        (to_far,) = relay([(plan.far_low, plan.far_side)], z_low)
        far_low = lax.ppermute(to_far, "gx", far_pairs())
    with jax.named_scope("relay_corners"):
        (to_mate,) = relay([(plan.mate, plan.mate_side)], z_low, z_high)
        mate = lax.ppermute(to_mate, "gx", mate_pairs())
    level = lines(12 * wide * ring)
    count = 2 * STEPS + 3
    levels = [level] * (count - 1) + [lines(wide * ring)]
    transforms = [lines(6 * nx * ny)] * 2
    with jax.named_scope("middle"):
        spectra = [spectrum.reshape((-1, depth)) for spectrum in (forward_spectrum, adjoint_spectrum)]
        results = pl.pallas_call(
            functools.partial(middle_kernel, plan),
            out_shape=[*levels, *transforms],
            in_specs=[VMEM] * 10,
            out_specs=[VMEM] * (count + 2),
            input_output_aliases={0: 0, 1: STEPS + 1, 2: 1, 3: STEPS + 2, 4: count - 1},
            compiler_params=params(8),
            cost_estimate=cost(3 * 2**29),
        )(e0, h0, e1, h1, coef, z_low, z_high, turns, *spectra)
        state, sums = results[:count], results[count:]
    with jax.named_scope("edges"):
        results = pl.pallas_call(
            functools.partial(edges_kernel, plan, groups),
            out_shape=[*levels, *transforms, *[lines(nx * ny // groups)] * groups],
            in_specs=[VMEM] * (count + 10),
            out_specs=[VMEM] * (count + 2 + groups),
            input_output_aliases={i: i for i in range(count)} | {count + 8: count, count + 9: count + 1},
            compiler_params=params(8),
        )(*state, x_low, x_high, far_low, far_high, mate, z_low, z_high, turns, *sums)
        tr_f, tr_a, own, *others = results[count:]
    with jax.named_scope("sum_angles"):
        others = [lax.ppermute(part, "angle", ring_pairs("angle", k + 1)) for k, part in enumerate(others)]
        gradient = pl.pallas_call(
            functools.partial(sum_kernel, groups),
            out_shape=array(nx * ny, depth // groups),
            in_specs=[VMEM] * groups,
            out_specs=VMEM,
            compiler_params=params(4),
        )(own, *others)
    with jax.named_scope("write"):
        out_f, out_a = pl.pallas_call(
            write_kernel,
            out_shape=[array(6, nx, ny, depth)] * 2,
            in_specs=[VMEM] * 2,
            out_specs=[HBM] * 2,
            scratch_shapes=[pltpu.SemaphoreType.DMA((12,))],
            compiler_params=params(4),
        )(tr_f.reshape((6, nx, ny, depth)), tr_a.reshape((6, nx, ny, depth)))
    return (
        out_f.reshape(forward_spectrum.shape),
        out_a.reshape(adjoint_spectrum.shape),
        gradient.reshape((nx, ny, depth // groups)),
    )


def solution(mesh):
    in_specs = (
        P("angle", None, "gx", "gy", None),
        P("angle", None, "gx", "gy", None),
        P("angle", None, "gx", "gy", None),
        P("angle", None, "gx", "gy", None),
        P("gx", "gy", None),
        P(),
        P("angle"),
        P(),
    )
    out_specs = (
        P("angle", None, "gx", "gy", None),
        P("angle", None, "gx", "gy", None),
        P("gx", "gy", "angle"),
    )
    return jax.shard_map(shards, mesh=mesh, in_specs=in_specs, out_specs=out_specs, check_vma=False)
```

```python
import functools
import math

import jax
import jax.numpy as jnp
from jax import lax
from jax.experimental import pallas as pl
from jax.experimental.pallas import tpu as pltpu
from jax.sharding import PartitionSpec as P

STEPS = 3
SUB = 8

courant = 0.5
omega_step = 0.7

VMEM = pl.BlockSpec(memory_space=pltpu.VMEM)
SMEM = pl.BlockSpec(memory_space=pltpu.SMEM)
HBM = pl.BlockSpec(memory_space=pltpu.HBM)


def reads(node):
    kind, level, comp, x, y = node
    others = [c for c in range(3) if c != comp]
    if kind == "E":
        found = [("E", level - 1, comp, x, y), ("C", 0, 0, x, y)] + [("H", level, c, x, y) for c in others]
        if comp != 1:
            found.append(("H", level, 2 - comp, x, y - 1))
        if comp != 0:
            found.append(("H", level, 3 - comp, x - 1, y))
        return found
    found = [("H", level - 1, comp, x, y)] + [("E", level - 1, c, x, y) for c in others]
    if comp != 1:
        found.append(("E", level - 1, 2 - comp, x, y + 1))
    if comp != 0:
        found.append(("E", level - 1, 3 - comp, x + 1, y))
    return found


def wanted(nx, ny):
    def block(node):
        return node[3] // nx, node[4] // ny

    @functools.cache
    def alone(node):
        if node[1] == 0:
            return True
        return node[1] == 1 and all(block(other) == block(node) and alone(other) for other in reads(node))

    found, made, seen = set(), set(), set()
    todo = [("E", STEPS, comp, x, y) for comp in range(3) for x in range(nx) for y in range(ny)]
    while todo:
        node = todo.pop()
        if node in seen:
            continue
        seen.add(node)
        if block(node) != (0, 0) and alone(node):
            found.add(node)
        elif node[1]:
            made.add(node)
            todo += reads(node)
    return found, made


class Message:
    def __init__(self, nodes, axis, folded=()):
        self.axis, self.runs, self.at, self.size = axis, [], {}, 0
        assert nodes.issuperset(folded)
        self.zeros = Message(set(folded), axis).runs if folded else []
        nodes = nodes - set(folded)
        stretches = []
        for node in sorted(nodes):
            before = list(node)
            before[3 + axis] -= 1
            if tuple(before) in nodes:
                continue
            count = 1
            while (*node[:3], node[3] + count * (axis == 0), node[4] + count * (axis == 1)) in nodes:
                count += 1
            stretches.append((count, node))
        for count, (kind, level, comp, x, y) in sorted(stretches, key=lambda item: (-item[0], item[1])):
            for run in (0, 1) if kind != "C" else (0,):
                for part in (0, 1) if kind != "C" else (0,):
                    what = (kind, level, comp, run, part)
                    self.runs.append((what, x, y, count, self.size))
                    for i in range(count):
                        self.at[what, x + i * (axis == 0), y + i * (axis == 1)] = self.size + i
                    self.size += count
        self.lines = -(-self.size // SUB) * SUB


class Plan:
    def __init__(self, nx, ny, depth):
        self.depth = depth
        self.nx, self.ny = nx, ny
        self.wide, self.ring = nx + 2 * STEPS, ny + SUB
        nodes, made = wanted(nx, ny)
        self.made = {}
        for kind, level, comp, x, y in made:
            self.made.setdefault((kind, level, x), {}).setdefault(comp, set()).add(y % self.ring // SUB)
        sides = {}
        for node in nodes:
            sides.setdefault((node[3] // nx, node[4] // ny), set()).add(node)

        def shifted(found, dx):
            return {(*node[:3], node[3] + dx, node[4]) for node in found}

        y_low, y_high = (sides[0, side] | shifted(sides[-1, side], nx) | shifted(sides[1, side], -nx) for side in (-1, 1))
        self.x_folds = (1, ny - 2), (2, ny - 2)
        self.y_folds = (2, nx - 2), (3, nx - 2)
        x_folded = [("E", 1, comp, -2, y) for comp in range(3) for y in range(*self.x_folds[comp == 0])]
        y_folded = [("E", 1, comp, x, -2) for comp in range(3) for x in range(*self.y_folds[comp == 1])]
        self.y_low, self.y_high = Message(y_low, 0, y_folded), Message(y_high, 0)
        self.x_low, self.x_high = Message(sides[-1, 0], 1, x_folded), Message(sides[1, 0], 1)
        self.mate_side, self.far_side = (1, -1), (-1, 1)
        self.mate = [Message(sides[side, -1] | sides[side, 1], 1) for side in self.mate_side]
        self.far_low, self.far_high = ([Message(sides[side, end], 1) for side in self.far_side] for end in (-1, 1))

    def row(self, x, y, run=0, part=0, comp=0):
        return ((run * 6 + part * 3 + comp) * self.wide + x + STEPS) * self.ring + y % self.ring

    def rows(self, what, x, y, axis, count):
        _, _, comp, run, part = what
        start = self.row(x, y, run, part, comp)
        return pl.ds(start, count, stride=self.ring) if axis == 0 and count > 1 else pl.ds(start, count)


class State:
    def __init__(self, efield, hfield, coef):
        self.by_kind = {"E": efield, "H": hfield, "C": [coef]}

    def __call__(self, what):
        return self.by_kind[what[0]][what[1]]


def pack(plan, message, state, dx, dy, out, changed=None):
    for what, x, y, count, at in message.runs:
        layer, first = (y, x) if message.axis == 0 else (x, y)
        if changed and (what, layer) in changed:
            ref, row = changed[what, layer]
            value = ref[pl.ds(row + first, count), :]
        else:
            value = state(what)[plan.rows(what, x + dx, y + dy, message.axis, count), :]
        out[pl.ds(at, count), :] = value


def fold(plan, state, axis, scratch):
    nx, ny = plan.nx, plan.ny
    size, normal = (nx, 1) if axis == 0 else (ny, 0)
    before, after = ((0, 2) if axis == 0 else (1, 2))
    cell = lax.broadcasted_iota(jnp.int32, (size, scratch.shape[1]), 0)
    lane = lax.broadcasted_iota(jnp.int32, cell.shape, 1)
    folds = plan.y_folds if axis == 0 else plan.x_folds
    changed = {}

    def lines(what, layer):
        place = (0, ny + layer) if axis == 0 else (nx + layer, 0)
        return state(what)[plan.rows(what, *place, axis, size), :]

    def inside(value, fold):
        return jnp.where((cell >= fold[0]) & (cell < fold[1]), value, 0.0)

    for run in (0, 1):
        for part in (0, 1):

            def get(kind, level, comp, layer):
                return lines((kind, level, comp, run, part), layer)

            def put(kind, level, comp, layer, value):
                row = len(changed) * size
                scratch[pl.ds(row, size), :] = value
                changed[(kind, level, comp, run, part), layer] = scratch, row

            low, high = (inside(get("E", 1, comp, -2), folds[0]) for comp in (before, after))
            along = inside(get("E", 1, normal, -2), folds[1])
            along_z = jnp.where(lane == lane.shape[1] - 1, 0.0, pltpu.roll(along, lane.shape[1] - 1, 1)) - along
            along_next = pltpu.roll(along, size - 1, 0) - along
            sign = 1.0 if axis == 0 else -1.0
            d_before = sign * (high + along_z)
            d_after = -sign * (low + along_next)
            scale = lines(("C", 0, 0, 0, 0), -1)
            put("H", 1, before, -2, get("H", 1, before, -2) + d_before)
            put("H", 1, after, -2, get("H", 1, after, -2) + d_after)
            put("E", 0, before, -1, get("E", 0, before, -1) + sign * scale * d_after)
            put("E", 0, after, -1, get("E", 0, after, -1) - sign * scale * d_before)
            put("H", 0, before, -1, get("H", 0, before, -1) + 0.5 * scale * d_before)
            put("H", 0, after, -1, get("H", 0, after, -1) + 0.5 * scale * d_after)
    return changed


def by_parity(offset, body):
    parity = lax.rem(lax.axis_index("gx") + offset, 2)
    for value in (0, 1):
        pl.when(parity == value)(functools.partial(body, value))


def pack_y_kernel(plan, fwd, adj, eps, e0, h0, e1, h1, coef, z_up, sems, scratch):
    nx, ny = plan.nx, plan.ny
    own = (pl.ds(STEPS, nx), pl.ds(0, ny), slice(None))
    copies = [pltpu.make_async_copy(eps, coef.at[own], sems.at[0])]
    for run, ref in enumerate((fwd, adj)):
        for kind, array in enumerate((e0, h0)):
            for i in range(6):
                copies.append(
                    pltpu.make_async_copy(ref.at[kind * 6 + i], array.at[(run * 6 + i, *own)], sems.at[len(copies)])
                )
    for copy in copies:
        copy.start()
    copies[0].wait()
    for x in range(nx):
        coef[STEPS + x, pl.ds(0, ny), :] = (0.5 * courant) / coef[STEPS + x, pl.ds(0, ny), :]
    e0, h0, e1, h1, coef = (array.reshape((-1, array.shape[-1])) for array in (e0, h0, e1, h1, coef))
    sweeps = Sweeps(plan, [e0, e1], [h0, h1], coef, ny)
    for run in (0, 1):
        for copy in copies[1 + 12 * run : 13 + 12 * run]:
            copy.wait()
        sweeps.both(1, range(nx), range(nx - 1), runs=(run,))
    state = State([e0, e1], [h0, h1], coef)
    pack(plan, plan.y_low, state, 0, ny, z_up, fold(plan, state, 0, scratch))


def pack_x_kernel(plan, e0, h0, e1, h1, coef, x_up, x_down, z_down, scratch):
    state = State([e0, e1], [h0, h1], coef)
    pack(plan, plan.x_low, state, plan.nx, 0, x_up, fold(plan, state, 1, scratch))
    pack(plan, plan.x_high, state, -plan.nx, 0, x_down)
    pack(plan, plan.y_high, state, 0, -plan.ny, z_down)


def pack_diagonal_kernel(plan, e0, h0, e1, h1, coef, after, diagonal):
    state = State([e0, e1], [h0, h1], coef)

    def corners(receiver):
        pack(plan, plan.far_high[receiver], state, -plan.nx * plan.far_side[receiver], -plan.ny, diagonal)

    by_parity(1, corners)


def turns_kernel(groups, table, index, tiles, turns):
    row = index[0]
    phi_x, phi_y = table[row, 0], table[row, 1]
    at_x, at_y = lax.axis_index("gx"), lax.axis_index("gy")
    none = jnp.float32(0.0)
    ax_low = jnp.where(at_x == 0, -phi_x, none)
    ax_high = jnp.where(at_x == lax.axis_size("gx") - 1, phi_x, none)
    ay_low = jnp.where(at_y == 0, -phi_y, none)
    ay_high = jnp.where(at_y == lax.axis_size("gy") - 1, phi_y, none)
    sub = lax.broadcasted_iota(jnp.int32, (SUB, turns.shape[1]), 0)
    angles = jnp.zeros(sub.shape, jnp.float32)
    for i, angle in enumerate((ax_low, ax_high, ay_low, ay_high, ax_low + ay_low, ax_low + ay_high,
                               ax_high + ay_low, ax_high + ay_high)):
        angles = jnp.where(sub == i, angle, angles)
    turns[pl.ds(0, SUB), :] = jnp.cos(angles)
    turns[pl.ds(SUB, SUB), :] = jnp.sin(angles)
    own_tile = at_x * lax.axis_size("gy") + at_y
    chosen = tiles[0] == own_tile
    for i in range(1, tiles.shape[0]):
        chosen = jnp.logical_or(chosen, tiles[i] == own_tile)
    weight = jnp.where(chosen, jnp.float32(1.0 / groups), none)
    turns[pl.ds(2 * SUB, SUB), :] = jnp.full(sub.shape, weight, jnp.float32)


def relay_kernel(plan, jobs, *refs):
    faces, outs = refs[: len(refs) - len(jobs)], refs[len(refs) - len(jobs) :]

    def corners(receiver):
        for (messages, side), out in zip(jobs, outs, strict=True):
            dx = -plan.nx * side[receiver]
            for (what, x, y), row in messages[receiver].at.items():
                ref, source = (faces[0], plan.y_low) if y < 0 else (faces[1], plan.y_high)
                out[pl.ds(row, 1), :] = ref[pl.ds(source.at[what, x + dx, y], 1), :]

    by_parity(1, corners)


def turned(real, imag, cosine, sine):
    return real * cosine - imag * sine, real * sine + imag * cosine


def unpack(plan, message, ref, which, turns, state, kinds, level, layers=None):
    axis = message.axis
    for (kind, at_level, comp, run, part), x, y, count, at in message.runs:
        if kind not in kinds or at_level != level or part == 1:
            continue
        pieces = [(x, y, count, at)]
        if layers is not None:
            pieces = [(x + i, y, 1, at + i) for i in range(count) if x + i in layers]
        for cell_x, cell_y, size, row in pieces:
            what = (kind, at_level, comp, run, 0)
            real = ref[pl.ds(row, size), :]
            if kind == "C":
                state(what)[plan.rows(what, cell_x, cell_y, axis, size), :] = real
                continue
            twin = (kind, at_level, comp, run, 1)
            imag = ref[pl.ds(message.at[twin, cell_x, cell_y], size), :]
            turn = which(y)
            cosine, sine = turns[pl.ds(turn, 1), :], turns[pl.ds(SUB + turn, 1), :]
            real, imag = turned(real, imag, cosine, sine if run == 0 else -sine)
            state(what)[plan.rows(what, cell_x, cell_y, axis, size), :] = real
            state(twin)[plan.rows(twin, cell_x, cell_y, axis, size), :] = imag
    for what, x, y, count, _ in message.zeros:
        if what[0] in kinds and what[1] == level and layers is None:
            state(what)[plan.rows(what, x, y, axis, count), :] = jnp.zeros((count, ref.shape[1]), jnp.float32)


class Sweeps:
    def __init__(self, plan, efield, hfield, coef, height, todo=None):
        self.plan, self.efield, self.hfield, self.coef, self.height = plan, efield, hfield, coef, height
        self.todo = todo

    def rows(self, run, part, comp, x, start, stop):
        return pl.ds(self.plan.row(x, 0, run, part, comp) + start, stop - start)

    def get(self, array, run, part, comp, x):
        return array[self.rows(run, part, comp, x, 0, self.height), :]

    def pieces(self, kind, step, x):
        if self.todo is None:
            return [(comp, 0, self.height) for comp in range(3)]
        found = []
        for comp, tiles in sorted(self.todo.get((kind, step, x), {}).items()):
            for tile in sorted(tiles):
                if found and found[-1][0] == comp and found[-1][2] == tile * SUB:
                    found[-1] = (comp, found[-1][1], (tile + 1) * SUB)
                else:
                    found.append((comp, tile * SUB, (tile + 1) * SUB))
        return found

    def next_z(self, value):
        lane = lax.broadcasted_iota(jnp.int32, value.shape, 1)
        return jnp.where(lane == value.shape[1] - 1, 0.0, pltpu.roll(value, value.shape[1] - 1, 1))

    def prev_z(self, value):
        lane = lax.broadcasted_iota(jnp.int32, value.shape, 1)
        return jnp.where(lane == 0, 0.0, pltpu.roll(value, 1, 1))

    def next_y(self, value):
        return pltpu.roll(value, self.height - 1, 0)

    def prev_y(self, value):
        return pltpu.roll(value, 1, 0)

    def update_h(self, step, run, part, x):
        efield, old, new = self.efield[step - 1], self.hfield[step - 1], self.hfield[step]
        ex, ey, ez = (self.get(efield, run, part, comp, x) for comp in range(3))
        for comp, start, stop in self.pieces("H", step, x):
            here = slice(start, stop)
            if comp == 0:
                curl = (self.next_y(ez) - ez)[here] - (self.next_z(ey[here]) - ey[here])
            elif comp == 1:
                ez_x = self.get(efield, run, part, 2, x + 1)
                curl = (self.next_z(ex[here]) - ex[here]) - (ez_x - ez)[here]
            else:
                ey_x = self.get(efield, run, part, 1, x + 1)
                curl = (ey_x - ey)[here] - (self.next_y(ex) - ex)[here]
            before = self.get(old, run, part, comp, x)[here]
            if step == 1:
                before = before + before
            new[self.rows(run, part, comp, x, start, stop), :] = before - curl

    def update_e(self, step, run, part, x):
        old, new, hfield = self.efield[step - 1], self.efield[step], self.hfield[step]
        hx, hy, hz = (self.get(hfield, run, part, comp, x) for comp in range(3))
        scale = self.get(self.coef, 0, 0, 0, x)
        for comp, start, stop in self.pieces("E", step, x):
            here = slice(start, stop)
            if comp == 0:
                curl = (hz - self.prev_y(hz))[here] - (hy[here] - self.prev_z(hy[here]))
            elif comp == 1:
                hz_x = self.get(hfield, run, part, 2, x - 1)
                curl = (hx[here] - self.prev_z(hx[here])) - (hz - hz_x)[here]
            else:
                hy_x = self.get(hfield, run, part, 1, x - 1)
                curl = (hy - hy_x)[here] - (hx - self.prev_y(hx))[here]
            before = self.get(old, run, part, comp, x)[here]
            new[self.rows(run, part, comp, x, start, stop), :] = before + scale[here] * curl

    def both(self, step, h_layers, e_layers, after_h=None, after_e=None, runs=(0, 1)):
        for update, layers, after in ((self.update_h, h_layers, after_h), (self.update_e, e_layers, after_e)):
            for x in layers:
                for run in runs:
                    for part in (0, 1):
                        update(step, run, part, x)
            if after is not None:
                after()


def middle_kernel(plan, e0_in, h0_in, e1_in, h1_in, coef_in, z_low, z_high, turns, spec_f, spec_a, *refs):
    *arrays, out_f, out_a = refs
    nx = plan.nx
    efield, hfield, coef = arrays[: STEPS + 1], arrays[STEPS + 1 : 2 * STEPS + 2], arrays[-1]
    state = State(efield, hfield, coef)

    def take(kinds, level):
        unpack(plan, plan.y_low, z_low, lambda y: 2, turns, state, kinds, level)
        unpack(plan, plan.y_high, z_high, lambda y: 3, turns, state, kinds, level)

    take("EHC", 0)
    sweeps = Sweeps(plan, efield, hfield, coef, plan.ring, plan.made)
    for step in range(1, STEPS + 1):
        after = [lambda: take("H", 1), lambda: take("E", 1)] if step == 1 else []
        sweeps.both(step, range(step - 1, nx - step), range(step, nx - step), *after)
    for _ in add_up(plan, efield, functools.partial(in_middle, plan), (spec_f, spec_a), (out_f, out_a)):
        pass


def add_up(plan, efield, levels, transform, out):
    nx, ny = plan.nx, plan.ny
    for x in range(nx):
        for tile in range(ny // SUB):
            for comp in range(3):
                ends = []
                for run in (0, 1):
                    at = [pl.ds(((part * 3 + comp) * nx + x) * ny + tile * SUB, SUB) for part in (0, 1)]
                    real, imag = transform[run][at[0], :], transform[run][at[1], :]
                    for level in levels(x):
                        theta = omega_step * level
                        here = [efield[level][pl.ds(plan.row(x, tile * SUB, run, part, comp), SUB), :] for part in (0, 1)]
                        more = turned(*here, math.cos(theta), math.sin(theta))
                        real, imag = real + more[0], imag + more[1]
                    out[run][at[0], :], out[run][at[1], :] = real, imag
                    ends.append((real, imag))
                yield x, tile, ends


def in_middle(plan, x):
    return [level for level in range(1, STEPS + 1) if level <= x < plan.nx - level]


def do_valleys(plan, sweeps, take):
    for step in range(1, STEPS + 1):
        low, high = step - STEPS, plan.nx - step
        h_layers = [*range(low - 1, step - 1), *range(high, plan.nx + STEPS - step)]
        e_layers = [*range(low, step), *range(high, plan.nx + STEPS - step)]
        after = [functools.partial(take, "H", 1, h_layers), functools.partial(take, "E", 1, e_layers)] if step == 1 else []
        sweeps.both(step, h_layers, e_layers, *after)


def edges_kernel(plan, groups, *refs):
    count = 2 * STEPS + 3
    x_low, x_high, far_low, far_high, mate, z_low, z_high, turns, part_f, part_a = refs[count : count + 10]
    arrays = refs[count + 10 : 2 * count + 10]
    out_f, out_a, *parts = refs[2 * count + 10 :]
    efield, hfield, coef = arrays[: STEPS + 1], arrays[STEPS + 1 : 2 * STEPS + 2], arrays[-1]
    state = State(efield, hfield, coef)

    def take(kinds, level, layers):
        unpack(plan, plan.x_low, x_low, lambda y: 0, turns, state, kinds, level)
        unpack(plan, plan.x_high, x_high, lambda y: 1, turns, state, kinds, level)

        def corners(receiver):
            for messages, ref, side in (
                (plan.far_low, far_low, plan.far_side),
                (plan.far_high, far_high, plan.far_side),
                (plan.mate, mate, plan.mate_side),
            ):
                first = 4 if side[receiver] < 0 else 6
                unpack(plan, messages[receiver], ref, lambda y: first + (y >= 0), turns, state, kinds, level)

        by_parity(0, corners)
        unpack(plan, plan.y_low, z_low, lambda y: 2, turns, state, kinds, level, layers)
        unpack(plan, plan.y_high, z_high, lambda y: 3, turns, state, kinds, level, layers)

    take("EHC", 0, ())
    do_valleys(plan, Sweeps(plan, efield, hfield, coef, plan.ring, plan.made), take)

    share = plan.depth // groups
    shift = lax.rem(groups - lax.axis_index("angle"), groups) * share
    weight = turns[pl.ds(2 * SUB, SUB), :]

    def rest(x):
        return [level for level in range(1, STEPS + 1) if level not in in_middle(plan, x)]

    totals = {}
    for x, tile, ends in add_up(plan, efield, rest, (part_f, part_a), (out_f, out_a)):
        term = ends[0][0] * ends[1][0] - ends[0][1] * ends[1][1]
        totals[x, tile] = totals[x, tile] + term if (x, tile) in totals else term
    block = lax.broadcasted_iota(jnp.int32, weight.shape, 1) // share
    tiles = [pltpu.roll(total * weight, shift, 1) for total in totals.values()]
    for k, part in enumerate(parts):
        for i in range(len(tiles) // groups):
            packed = jnp.zeros(weight.shape, jnp.float32)
            for t in range(groups):
                lanes = (t - k) % groups * share
                value = tiles[i * groups + t]
                packed = jnp.where(block == t, pltpu.roll(value, lanes, 1) if lanes else value, packed)
            part[pl.ds(i * SUB, SUB), :] = packed


def sum_kernel(groups, *refs):
    *parts, out = refs
    share = out.shape[1]
    for i in range(parts[0].shape[0] // SUB):
        total = parts[0][pl.ds(i * SUB, SUB), :]
        for part in parts[1:]:
            total = total + part[pl.ds(i * SUB, SUB), :]
        for t in range(groups):
            out[pl.ds((i * groups + t) * SUB, SUB), :] = total[:, t * share : (t + 1) * share]


def write_kernel(tr_f, tr_a, out_f, out_a, sems):
    copies = []
    for source, target in ((tr_f, out_f), (tr_a, out_a)):
        for i in range(source.shape[0]):
            copies.append(pltpu.make_async_copy(source.at[i], target.at[i], sems.at[len(copies)]))
    for copy in copies:
        copy.start()
    for copy in copies:
        copy.wait()


def ring_pairs(axis, offset):
    size = lax.axis_size(axis)
    return [(i, (i + offset) % size) for i in range(size)]


def mate_pairs():
    return [(i, i ^ 1) for i in range(lax.axis_size("gx"))]


def far_pairs():
    size = lax.axis_size("gx")
    return [(i, (i + (1 if i % 2 else -1)) % size) for i in range(size)]


def diagonal_pairs():
    size = lax.axis_size("gy")
    return [(x * size + y, far * size + (y - 1) % size) for x, far in far_pairs() for y in range(size)]


def shards(
    forward_fields,
    adjoint_fields,
    forward_spectrum,
    adjoint_spectrum,
    permittivity,
    phase_table,
    angle_index,
    design_tiles,
):
    nx, ny, depth = permittivity.shape
    plan = Plan(nx, ny, depth)
    groups = lax.axis_size("angle")
    wide, ring = plan.wide, plan.ring

    def array(*shape):
        return jax.ShapeDtypeStruct(shape, jnp.float32)

    def lines(count):
        return array(count, depth)

    def params(mib):
        return pltpu.CompilerParams(vmem_limit_bytes=mib * 2**20)

    def cost(size):
        return pl.CostEstimate(flops=size, bytes_accessed=size, transcendentals=0)

    assert lax.axis_size("gx") % 2 == 0 and nx * ny % (groups * SUB) == 0
    with jax.named_scope("pack_y"):
        *first, coef, z_up = pl.pallas_call(
            functools.partial(pack_y_kernel, plan),
            out_shape=(
                *[array(12, wide, ring, depth)] * 4,
                array(wide, ring, depth),
                lines(plan.y_low.lines),
            ),
            in_specs=[HBM] * 3,
            out_specs=[VMEM] * 6,
            scratch_shapes=[pltpu.SemaphoreType.DMA((25,)), pltpu.VMEM((24 * nx, depth), jnp.float32)],
            compiler_params=params(8),
        )(*(pltpu.with_memory_space_constraint(array, pltpu.HBM) for array in (forward_fields[0], adjoint_fields[0], permittivity)))
    e0, h0, e1, h1, coef = (state.reshape((-1, depth)) for state in (*first, coef))
    with jax.named_scope("send_y"):
        z_low = lax.ppermute(z_up, "gy", ring_pairs("gy", 1))
    with jax.named_scope("pack_x"):
        x_up, x_down, z_down = pl.pallas_call(
            functools.partial(pack_x_kernel, plan),
            out_shape=[lines(plan.x_low.lines), lines(plan.x_high.lines), lines(plan.y_high.lines)],
            in_specs=[VMEM] * 5,
            out_specs=[VMEM] * 3,
            scratch_shapes=[pltpu.VMEM((24 * ny, depth), jnp.float32)],
            compiler_params=params(8),
            cost_estimate=cost(40 * 2**20),
        )(e0, h0, e1, h1, coef)
    with jax.named_scope("send_x"):
        x_low = lax.ppermute(x_up, "gx", ring_pairs("gx", 1))
        z_high = lax.ppermute(z_down, "gy", ring_pairs("gy", -1))
        x_high = lax.ppermute(x_down, "gx", ring_pairs("gx", -1))
    with jax.named_scope("turns"):
        turns = pl.pallas_call(
            functools.partial(turns_kernel, groups),
            out_shape=lines(3 * SUB),
            in_specs=[SMEM] * 3,
            out_specs=VMEM,
            compiler_params=params(4),
        )(phase_table, angle_index, design_tiles)
    with jax.named_scope("diagonal_corners"):
        to_diagonal = pl.pallas_call(
            functools.partial(pack_diagonal_kernel, plan),
            out_shape=lines(max(message.lines for message in plan.far_high)),
            in_specs=[VMEM] * 6,
            out_specs=VMEM,
            compiler_params=params(4),
        )(e0, h0, e1, h1, coef, x_up)
        far_high = lax.ppermute(to_diagonal, ("gx", "gy"), diagonal_pairs())

    def relay(jobs, *faces):
        return pl.pallas_call(
            functools.partial(relay_kernel, plan, jobs),
            out_shape=[lines(max(message.lines for message in messages)) for messages, _ in jobs],
            in_specs=[VMEM] * len(faces),
            out_specs=[VMEM] * len(jobs),
            compiler_params=params(4),
            cost_estimate=cost(2**10),
        )(*faces)

    with jax.named_scope("relay_low_corners"):
        (to_far,) = relay([(plan.far_low, plan.far_side)], z_low)
        far_low = lax.ppermute(to_far, "gx", far_pairs())
    with jax.named_scope("relay_corners"):
        (to_mate,) = relay([(plan.mate, plan.mate_side)], z_low, z_high)
        mate = lax.ppermute(to_mate, "gx", mate_pairs())
    level = lines(12 * wide * ring)
    count = 2 * STEPS + 3
    levels = [level] * (count - 1) + [lines(wide * ring)]
    transforms = [lines(6 * nx * ny)] * 2
    with jax.named_scope("middle"):
        spectra = [spectrum.reshape((-1, depth)) for spectrum in (forward_spectrum, adjoint_spectrum)]
        results = pl.pallas_call(
            functools.partial(middle_kernel, plan),
            out_shape=[*levels, *transforms],
            in_specs=[VMEM] * 10,
            out_specs=[VMEM] * (count + 2),
            input_output_aliases={0: 0, 1: STEPS + 1, 2: 1, 3: STEPS + 2, 4: count - 1},
            compiler_params=params(8),
            cost_estimate=cost(3 * 2**29),
        )(e0, h0, e1, h1, coef, z_low, z_high, turns, *spectra)
        state, sums = results[:count], results[count:]
    with jax.named_scope("edges"):
        results = pl.pallas_call(
            functools.partial(edges_kernel, plan, groups),
            out_shape=[*levels, *transforms, *[lines(nx * ny // groups)] * groups],
            in_specs=[VMEM] * (count + 10),
            out_specs=[VMEM] * (count + 2 + groups),
            input_output_aliases={i: i for i in range(count)} | {count + 8: count, count + 9: count + 1},
            compiler_params=params(8),
        )(*state, x_low, x_high, far_low, far_high, mate, z_low, z_high, turns, *sums)
        tr_f, tr_a, own, *others = results[count:]
    with jax.named_scope("sum_angles"):
        others = [lax.ppermute(part, "angle", ring_pairs("angle", k + 1)) for k, part in enumerate(others)]
        gradient = pl.pallas_call(
            functools.partial(sum_kernel, groups),
            out_shape=array(nx * ny, depth // groups),
            in_specs=[VMEM] * groups,
            out_specs=VMEM,
            compiler_params=params(4),
        )(own, *others)
    with jax.named_scope("write"):
        out_f, out_a = pl.pallas_call(
            write_kernel,
            out_shape=[array(6, nx, ny, depth)] * 2,
            in_specs=[VMEM] * 2,
            out_specs=[HBM] * 2,
            scratch_shapes=[pltpu.SemaphoreType.DMA((12,))],
            compiler_params=params(4),
        )(tr_f.reshape((6, nx, ny, depth)), tr_a.reshape((6, nx, ny, depth)))
    return (
        out_f.reshape(forward_spectrum.shape),
        out_a.reshape(adjoint_spectrum.shape),
        gradient.reshape((nx, ny, depth // groups)),
    )


def solution(mesh):
    in_specs = (
        P("angle", None, "gx", "gy", None),
        P("angle", None, "gx", "gy", None),
        P("angle", None, "gx", "gy", None),
        P("angle", None, "gx", "gy", None),
        P("gx", "gy", None),
        P(),
        P("angle"),
        P(),
    )
    out_specs = (
        P("angle", None, "gx", "gy", None),
        P("angle", None, "gx", "gy", None),
        P("gx", "gy", "angle"),
    )
    return jax.shard_map(shards, mesh=mesh, in_specs=in_specs, out_specs=out_specs, check_vma=False)
```
